32 devices in a mesh: dp: 8 (over y, x, core), tensor: 4 (over z).
Axes of the slice: x: 2, y: 2, z: 4, core: 2. Of those that a mesh axis runs over, the one named last changes fastest.
Arguments:
- frames: float32 [8000, 768], P('dp'), may hold values from -6 to 6
- cotangent: float32 [8000, 768], P('dp'), may hold values from -6 to 6
- w_attn: float32 [2, 4, 768, 768], P(None, None, None, 'tensor'), may hold values from -4 to 4, as said below
- w_mlp: float32 [2, 2, 768, 3072], P(None, None, None, 'tensor'), may hold values from -4 to 4, as said below
- vectors: float32 [2, 6, 768], replicated, may hold values from -2 to 2, as said below
- head_bias: float32 [2, 2, 12, 64], P(None, None, 'tensor'), may hold values from -4 to 4
- up_bias: float32 [2, 48, 64], P(None, 'tensor'), may hold values from -4 to 4
- moment_attn: float32 [2, 4, 768, 768], P(None, None, 'dp', 'tensor')
- square_attn: float32 [2, 4, 768, 768], P(None, None, 'dp', 'tensor'), as said below
- moment_mlp: float32 [2, 2, 768, 3072], P(None, None, 'dp', 'tensor')
- square_mlp: float32 [2, 2, 768, 3072], P(None, None, 'dp', 'tensor'), as said below
- moment_vectors: float32 [2, 6, 768], P(None, None, 'dp')
- square_vectors: float32 [2, 6, 768], P(None, None, 'dp'), as said below
- moment_head: float32 [2, 2, 12, 64], P(None, None, 'tensor', 'dp')
- square_head: float32 [2, 2, 12, 64], P(None, None, 'tensor', 'dp'), as said below
- moment_up: float32 [2, 48, 64], P(None, 'tensor', 'dp')
- square_up: float32 [2, 48, 64], P(None, 'tensor', 'dp'), as said below
Outputs:
- layer_outputs: float32 [2, 8000, 768], P(None, 'dp')
- input_grad: float32 [8000, 768], P('dp')
- attn_new: float32 [2, 4, 768, 768], P(None, None, 'dp', 'tensor')
- attn_first: float32 [2, 4, 768, 768], P(None, None, 'dp', 'tensor')
- attn_second: float32 [2, 4, 768, 768], P(None, None, 'dp', 'tensor')
- mlp_new: float32 [2, 2, 768, 3072], P(None, None, 'dp', 'tensor')
- mlp_first: float32 [2, 2, 768, 3072], P(None, None, 'dp', 'tensor')
- mlp_second: float32 [2, 2, 768, 3072], P(None, None, 'dp', 'tensor')
- vectors_new: float32 [2, 6, 768], P(None, None, 'dp')
- vectors_first: float32 [2, 6, 768], P(None, None, 'dp')
- vectors_second: float32 [2, 6, 768], P(None, None, 'dp')
- head_new: float32 [2, 2, 12, 64], P(None, None, 'tensor', 'dp')
- head_first: float32 [2, 2, 12, 64], P(None, None, 'tensor', 'dp')
- head_second: float32 [2, 2, 12, 64], P(None, None, 'tensor', 'dp')
- up_new: float32 [2, 48, 64], P(None, 'tensor', 'dp')
- up_first: float32 [2, 48, 64], P(None, 'tensor', 'dp')
- up_second: float32 [2, 48, 64], P(None, 'tensor', 'dp')
The draws below stay inside these ranges and needn't reach their ends.
Inputs may be any that keep to these rules, and one draw needn't show every extreme that they name: `w_attn`: independent entries. `w_mlp`: independent entries. `vectors`: gains near one, shifts and biases near zero. `square_attn`: positive. `square_mlp`: positive. `square_vectors`: positive. `square_head`: positive. `square_up`: positive.
All inputs are finite; a program needn't handle non-finite values.
Results may differ from the reference program's by a relative error of at most 0.019.
The reference program's roundings to bfloat16 on the way count: a program that leaves them out, or rounds other values in their place, can miss the bound.
Values sent between devices are 32-bit elements; how exact they have to be, the bound alone decides.
A program may use at most 192 MiB of HBM per device.

```python
import math
import jax
import jax.numpy as jnp
from jax import lax

D = 768
HEADS = 12
HEAD_DIM = 64
FF = 3072
FRAMES = 500
LAYERS = 2
STEP = 10
CLIPS = 16
TOKENS = 8000


first_share = 0.1 / 0.9


second_share = 0.001 / 0.999


attn_levels = [0.6, 0.6, 0.6, 0.15]


attn_square_levels = [1.5, 1.5, 1.5, 0.375]


mlp_levels = [0.4, 0.6]


vector_levels = [1.5, 1.5, 0.8, 0.8, 1.0, 1.0]


vector_square_levels = [2.7, 2.7, 1.44, 1.44, 1.8, 1.8]


head_levels = [0.8, 0.8]


up_levels = [0.4]


def slot_factor(extent, slot_scales):
    return jnp.asarray(slot_scales, jnp.float32).reshape((1, len(slot_scales)) + (1,) * (len(extent) - 2))


def signed_block(key, extent, slot_scales):
    values = jnp.clip(jax.random.normal(key, extent, jnp.float32), -4.0, 4.0)
    return values * slot_factor(extent, slot_scales)


def positive_block(key, extent, slot_scales):
    exponent = jax.random.uniform(key, extent, jnp.float32, math.log(0.5), math.log(8.0))
    return jnp.exp(exponent) * slot_factor(extent, slot_scales)


def moment_scales(levels):
    return [first_share * factor_one * math.sqrt(TOKENS) for factor_one in levels]


def square_scales(levels):
    return [second_share * factor_one * factor_one * TOKENS for factor_one in levels]


def draw_w_attn(key, part):
    key = jax.random.fold_in(key, 11)
    root = math.sqrt(D)
    return signed_block(key, (LAYERS, 4, D, D), [1.5 / root, 1.5 / root, 1.0 / root, 6.0 / root])


def draw_w_mlp(key, part):
    key = jax.random.fold_in(key, 12)
    return signed_block(key, (LAYERS, 2, D, FF), [1.0 / math.sqrt(D), 1.5 / math.sqrt(FF)])


def draw_vectors(key, part):
    key = jax.random.fold_in(key, 13)
    values = signed_block(key, (LAYERS, 6, D), [0.15, 0.3, 0.15, 0.3, 0.3, 0.3])
    return values + slot_factor((LAYERS, 6, D), [1.0, 0.0, 1.0, 0.0, 0.0, 0.0])


def draw_moment_attn(key, part):
    key = jax.random.fold_in(key, 21)
    return signed_block(key, (LAYERS, 4, D, D), moment_scales(attn_levels))


def draw_square_attn(key, part):
    key = jax.random.fold_in(key, 22)
    return positive_block(key, (LAYERS, 4, D, D), square_scales(attn_square_levels))


def draw_moment_mlp(key, part):
    key = jax.random.fold_in(key, 23)
    return signed_block(key, (LAYERS, 2, D, FF), moment_scales(mlp_levels))


def draw_square_mlp(key, part):
    key = jax.random.fold_in(key, 24)
    return positive_block(key, (LAYERS, 2, D, FF), square_scales(mlp_levels))


def draw_moment_vectors(key, part):
    key = jax.random.fold_in(key, 25)
    return signed_block(key, (LAYERS, 6, D), moment_scales(vector_levels))


def draw_square_vectors(key, part):
    key = jax.random.fold_in(key, 26)
    return positive_block(key, (LAYERS, 6, D), square_scales(vector_square_levels))


def draw_moment_head(key, part):
    key = jax.random.fold_in(key, 27)
    return signed_block(key, (LAYERS, 2, HEADS, HEAD_DIM), moment_scales(head_levels))


def draw_square_head(key, part):
    key = jax.random.fold_in(key, 28)
    return positive_block(key, (LAYERS, 2, HEADS, HEAD_DIM), square_scales(head_levels))


def draw_moment_up(key, part):
    key = jax.random.fold_in(key, 29)
    return signed_block(key, (LAYERS, FF // HEAD_DIM, HEAD_DIM), moment_scales(up_levels))


def draw_square_up(key, part):
    key = jax.random.fold_in(key, 30)
    return positive_block(key, (LAYERS, FF // HEAD_DIM, HEAD_DIM), square_scales(up_levels))


def spiked(values, rng, source, target, parts, factor):
    def block_of(axis_at):
        return (jnp.arange(values.shape[axis_at]) // (values.shape[axis_at] // parts)).reshape((-1,) + (1,) * (values.ndim - 1 - axis_at))

    one_side = jax.random.permutation(rng, parts)[block_of(target)]
    other_side = (block_of(target) + parts // 2) % parts
    return jnp.where((block_of(source) == one_side) | (block_of(source) == other_side), factor * values, values)


def level_of(rng, shape, cuts, low, largest):
    level = 1.0
    for position, parts in cuts:
        steps = jax.random.uniform(jax.random.fold_in(jax.random.fold_in(rng, 6), position), (parts,), jnp.float32, low / len(cuts), largest / len(cuts))
        level = level * jnp.repeat(jnp.exp(steps), shape[position] // parts).reshape((-1,) + (1,) * (len(shape) - 1 - position))
    return level


def bell_draw(own_key, shape, width, bound, pieces=(), held_as=jnp.bfloat16):
    loudness = level_of(own_key, shape, pieces, -0.22, 0.18) if pieces else 1.0
    values = jax.random.normal(own_key, shape, jnp.float32) * width * loudness
    return jnp.minimum(jnp.maximum(values, -bound), bound).astype(held_as)


def bell_draw_with(own_key, shape, deviation, reach, pieces, heavy, kind=jnp.bfloat16):
    values = deviation * jax.random.normal(own_key, shape, jnp.float32)
    if pieces:
        values = values * level_of(own_key, shape, pieces, -0.22, 0.18)
    return jnp.clip(spiked(values, jax.random.fold_in(own_key, 3), *heavy), -reach, reach).astype(kind)


def setup_inputs(seed: int = 0) -> dict:
    streams_of = jax.random.split(jax.random.key(seed), 18)
    frames = bell_draw(streams_of[0], (TOKENS, D), 1.0, 6.0, ((0, 8),), jnp.float32)
    cotangent = bell_draw_with(streams_of[1], (TOKENS, D), 1.0, 6.0, ((0, 8),), (0, 1, 8, 2.0), jnp.float32)
    w_attn = draw_w_attn(jax.random.fold_in(streams_of[17], 71), 0)
    w_mlp = draw_w_mlp(jax.random.fold_in(streams_of[17], 71), 0)
    vectors = draw_vectors(jax.random.fold_in(streams_of[17], 71), 0)
    head_bias = bell_draw(streams_of[5], (LAYERS, 2, HEADS, HEAD_DIM), 0.3, 4.0, ((2, 4),), jnp.float32)
    up_bias = bell_draw(streams_of[6], (LAYERS, FF // HEAD_DIM, HEAD_DIM), 0.3, 4.0, ((1, 4),), jnp.float32)
    moment_attn = draw_moment_attn(jax.random.fold_in(streams_of[17], 71), 0)
    square_attn = draw_square_attn(jax.random.fold_in(streams_of[17], 71), 0)
    moment_mlp = draw_moment_mlp(jax.random.fold_in(streams_of[17], 71), 0)
    square_mlp = draw_square_mlp(jax.random.fold_in(streams_of[17], 71), 0)
    moment_vectors = draw_moment_vectors(jax.random.fold_in(streams_of[17], 71), 0)
    square_vectors = draw_square_vectors(jax.random.fold_in(streams_of[17], 71), 0)
    moment_head = draw_moment_head(jax.random.fold_in(streams_of[17], 71), 0)
    square_head = draw_square_head(jax.random.fold_in(streams_of[17], 71), 0)
    moment_up = draw_moment_up(jax.random.fold_in(streams_of[17], 71), 0)
    square_up = draw_square_up(jax.random.fold_in(streams_of[17], 71), 0)
    return {"frames": frames, "cotangent": cotangent, "w_attn": w_attn, "w_mlp": w_mlp, "vectors": vectors, "head_bias": head_bias, "up_bias": up_bias, "moment_attn": moment_attn, "square_attn": square_attn, "moment_mlp": moment_mlp, "square_mlp": square_mlp, "moment_vectors": moment_vectors, "square_vectors": square_vectors, "moment_head": moment_head, "square_head": square_head, "moment_up": moment_up, "square_up": square_up}


@jax.custom_vjp
def low(v):
    return lax.optimization_barrier(v.astype(jnp.bfloat16)).astype(jnp.float32)

@jax.custom_vjp
def low_back(v):
    return v

def low_keep(v):
    return (low(v), None)

def low_pass(kept, grad):
    return (grad,)

def back_keep(v):
    return (v, None)

def back_low(kept, grad):
    return (low(grad),)
low.defvjp(low_keep, low_pass)
low_back.defvjp(back_keep, back_low)
ln_eps = 1e-05
beta_one = 0.9
beta_two = 0.999
adam_eps = 1e-08
decay_rate = 0.01
rate_matrix = 0.05
rate_vector = 0.2
highest = lax.Precision.HIGHEST

def matmul(left, right):
    return jnp.dot(left, right, precision=highest, preferred_element_type=jnp.float32)

def normalize(inputs, gain, shift):
    centre = lax.optimization_barrier(jnp.mean(inputs, axis=-1, keepdims=True))
    centred = inputs - centre
    spread = lax.optimization_barrier(jnp.mean(centred * centred, axis=-1, keepdims=True))
    return centred * lax.rsqrt(spread + ln_eps) * gain + shift

def attend_clip(operands):
    queries, keys_all, values_all = operands
    queries = queries.reshape(FRAMES, HEADS, HEAD_DIM)
    keys_all = keys_all.reshape(FRAMES, HEADS, HEAD_DIM)
    values_all = values_all.reshape(FRAMES, HEADS, HEAD_DIM)
    scores = jnp.einsum('qhd,khd->hqk', queries, keys_all, precision=highest) * (1.0 / math.sqrt(HEAD_DIM))
    scores = low_back(scores)
    weights = low(jax.nn.softmax(scores, axis=-1))
    mixture = jnp.einsum('hqk,khd->qhd', weights, values_all, precision=highest)
    return mixture.reshape(FRAMES, HEADS * HEAD_DIM)

def encoder(frames, w_attn, w_mlp, vectors, head_bias, up_bias):
    hidden = frames
    sections = []
    for layer_index in range(LAYERS):
        row_params = vectors[layer_index]
        attn_low = low(w_attn[layer_index])
        mlp_low = low(w_mlp[layer_index])
        normed = low(normalize(hidden, row_params[0], row_params[1]))
        queries = low(low_back(matmul(normed, attn_low[0]) + head_bias[layer_index, 0].reshape(D)))
        keys_all = low(low_back(matmul(normed, attn_low[1])))
        values_all = low(low_back(matmul(normed, attn_low[2]) + head_bias[layer_index, 1].reshape(D)))
        mixture = lax.map(jax.checkpoint(attend_clip), (queries.reshape(CLIPS, FRAMES, D), keys_all.reshape(CLIPS, FRAMES, D), values_all.reshape(CLIPS, FRAMES, D)))
        mixture = low(low_back(mixture.reshape(TOKENS, D)))
        hidden = hidden + low_back(matmul(mixture, attn_low[3].T) + row_params[4])
        normed_two = low(normalize(hidden, row_params[2], row_params[3]))
        before = low_back(matmul(normed_two, mlp_low[0]) + up_bias[layer_index].reshape(FF))
        activated = low(jax.nn.gelu(before, approximate=False))
        hidden = hidden + low_back(matmul(activated, mlp_low[1].T) + row_params[5])
        sections.append(hidden)
    return (hidden, jnp.stack(sections))

def adamw_update(param, gradient, first, second, rate):
    first_new = beta_one * first + (1.0 - beta_one) * gradient
    second_new = beta_two * second + (1.0 - beta_two) * gradient * gradient
    ratio = first_new / (1.0 - beta_one ** STEP) / (jnp.sqrt(second_new / (1.0 - beta_two ** STEP)) + adam_eps)
    return (param - rate * (ratio + decay_rate * param), first_new, second_new)

def reference(frames, cotangent, w_attn, w_mlp, vectors, head_bias, up_bias, moment_attn, square_attn, moment_mlp, square_mlp, moment_vectors, square_vectors, moment_head, square_head, moment_up, square_up):
    final_state, pullback, sections = jax.vjp(encoder, frames, w_attn, w_mlp, vectors, head_bias, up_bias, has_aux=True)
    gradients = pullback(cotangent)
    attn = adamw_update(w_attn, gradients[1], moment_attn, square_attn, rate_matrix)
    mlp = adamw_update(w_mlp, gradients[2], moment_mlp, square_mlp, rate_matrix)
    vector_new = adamw_update(vectors, gradients[3], moment_vectors, square_vectors, rate_vector)
    head = adamw_update(head_bias, gradients[4], moment_head, square_head, rate_vector)
    upper = adamw_update(up_bias, gradients[5], moment_up, square_up, rate_vector)
    return (sections, gradients[0], attn[0], attn[1], attn[2], mlp[0], mlp[1], mlp[2], vector_new[0], vector_new[1], vector_new[2], head[0], head[1], head[2], upper[0], upper[1], upper[2])
```

```python
import math
from types import SimpleNamespace

import jax
import jax.numpy as jnp
from jax import lax
from jax.experimental import pallas as pl
from jax.experimental.pallas import tpu as pltpu
from jax.sharding import PartitionSpec as P

HEAD_DIM = 64
FRAMES = 500
ROWS = 512
LAYERS = 2
STEP = 10
WIDTH = 768
BLOCK = 384
UNITS = 6
TOTAL = LAYERS * UNITS
GROUP = 8
HEADS_HERE = 3
SLOTS = 4

ln_eps = 1e-05
beta_one = 0.9
beta_two = 0.999
adam_eps = 1e-08
decay_rate = 0.01
rate_matrix = 0.05
rate_vector = 0.2
score_scale = 1.0 / math.sqrt(HEAD_DIM)
MESH = pl.DeviceIdType.MESH
f32 = jnp.float32
bf16 = jnp.bfloat16
ANY = pl.BlockSpec(memory_space=pl.ANY)
VMEM = pl.BlockSpec(memory_space=pltpu.VMEM)


def product(left, right):
    return jnp.dot(left, right, preferred_element_type=f32)


def contract_last(left, right):
    return lax.dot_general(left, right, (((1,), (1,)), ((), ())), preferred_element_type=f32)


def contract_rows(left, right):
    return lax.dot_general(left, right, (((0,), (0,)), ((), ())), preferred_element_type=f32)


def normalize_parts(inputs):
    centre = jnp.mean(inputs, axis=-1, keepdims=True)
    centred = inputs - centre
    inverse = lax.rsqrt(jnp.mean(centred * centred, axis=-1, keepdims=True) + ln_eps)
    return centred * inverse, inverse


def normalize_back(upstream, scaled, inverse, gain):
    gain_grad = jnp.sum(upstream * scaled, axis=0)
    shift_grad = jnp.sum(upstream, axis=0)
    inner_grad = upstream * gain
    lowered = inverse * (
        inner_grad
        - jnp.mean(inner_grad, axis=-1, keepdims=True)
        - scaled * jnp.mean(inner_grad * scaled, axis=-1, keepdims=True)
    )
    return (lowered, gain_grad, shift_grad)


def gelu(before):
    return 0.5 * before * (1.0 + lax.erf(before * (1.0 / math.sqrt(2.0))))


def gelu_slope(before):
    return 0.5 * (1.0 + lax.erf(before * (1.0 / math.sqrt(2.0)))) + before * jnp.exp(
        -0.5 * before * before
    ) * (1.0 / math.sqrt(2.0 * math.pi))


def adamw_update(param, gradient, first, second, rate):
    first_new = beta_one * first + (1.0 - beta_one) * gradient
    second_new = beta_two * second + (1.0 - beta_two) * gradient * gradient
    ratio = (
        first_new
        / (1.0 - beta_one**STEP)
        / (jnp.sqrt(second_new / (1.0 - beta_two**STEP)) + adam_eps)
    )
    return (param - rate * (ratio + decay_rate * param), first_new, second_new)


def find_place():
    dp = lax.axis_index("dp")
    t = lax.axis_index("tensor")
    i = lax.rem(dp, GROUP)
    base = dp - i
    c = lax.rem(i, 2)
    x = lax.rem(i // 2, 2)
    y = i // 4
    up = 1 - 2 * c
    level = c * (3 - t) + (1 - c) * t

    def at(cc, xx, yy):
        return base + 4 * yy + 2 * xx + cc

    return SimpleNamespace(
        t=t,
        c=c,
        x=x,
        y=y,
        q=2 * y + x,
        qx=2 * y + 1 - x,
        qy=2 * (1 - y) + x,
        qd=2 * (1 - y) + 1 - x,
        level=level,
        partner=(at(1 - c, x, y), t),
        xn=(at(c, 1 - x, y), t),
        yn=(at(c, x, 1 - y), t),
        above=(dp, t + up),
        below=(dp, t - up),
    )


def greet(p):
    barrier = pltpu.get_barrier_semaphore()

    def signal(device):
        pl.semaphore_signal(barrier, inc=1, device_id=device, device_id_type=MESH)

    signal(p.partner)
    signal(p.xn)
    signal(p.yn)

    @pl.when(p.level < 3)
    def _():
        signal(p.above)

    @pl.when(p.level > 0)
    def _():
        signal(p.below)

    inner = (p.level > 0) & (p.level < 3)

    @pl.when(inner)
    def _():
        pl.semaphore_wait(barrier, 5)

    @pl.when(jnp.logical_not(inner))
    def _():
        pl.semaphore_wait(barrier, 4)


def remote(src, dst, send_sem, recv_sem, device):
    return pltpu.make_async_remote_copy(
        src_ref=src,
        dst_ref=dst,
        send_sem=send_sem,
        recv_sem=recv_sem,
        device_id=device,
        device_id_type=MESH,
    )


def local(src, dst, sem):
    return pltpu.make_async_copy(src, dst, sem)


def forward_kernel(
    frames,
    cotangent,
    wa,
    wm,
    bias,
    vec,
    o_x,
    o_ct,
    o_h,
    o_m,
    o_n1,
    o_n2,
    o_q,
    o_k,
    o_v,
    o_a,
    o_u,
    o_c,
    o_w,
    gathered,
    biases,
    hs,
    ms,
    n1s,
    n2s,
    qs,
    ks,
    vs,
    as_,
    us,
    cs,
    low,
    part,
    other,
    rz,
    sz,
    szd,
    rx,
    sx,
    ry,
    sy,
    rxd,
    sxd,
    ryd,
    syd,
    native,
    first_sem,
    bias_sem,
    swap_sem,
    low_sem,
    mid_sem,
    out_sem,
):
    p = find_place()
    greet(p)
    level = p.level

    def when(cond):
        return pl.when(cond)

    mine = (p.t // 2) == p.c
    clip = lax.rem(p.t, 2)
    inputs = ((frames, hs.at[0], 0), (frames, o_x, 1), (cotangent, o_ct, 2))

    @when(mine)
    def _():
        for source, target, k in inputs:
            local(source.at[clip], target, first_sem.at[k]).start()
            remote(source.at[clip], target, first_sem.at[3 + k], first_sem.at[6 + k], p.partner).start()

    def wait_input(k):
        source, target, _ = inputs[k]

        @when(mine)
        def _():
            local(source.at[clip], target, first_sem.at[k]).wait()
            remote(source.at[clip], target, first_sem.at[3 + k], first_sem.at[6 + k], p.partner).wait_send()

        @when(jnp.logical_not(mine))
        def _():
            remote(source.at[clip], target, first_sem.at[3 + k], first_sem.at[6 + k], p.partner).wait_recv()

    def bias_copy(src, j, k, device):
        return remote(src, biases.at[j], bias_sem.at[k], bias_sem.at[3 + j], device)

    @when(level == 0)
    def _():
        local(bias, biases.at[0], bias_sem.at[5]).start()
        bias_copy(bias, 0, 0, p.above).start()

    @when(level == 1)
    def _():
        local(bias, biases.at[1], bias_sem.at[5]).start()
        bias_copy(bias, 1, 1, p.above).start()
        bias_copy(bias, 1, 2, p.below).start()

    def block(l, i, q=None):
        if i < 2:
            return wa.at[l, i] if q is None else wa.at[l, i, q]
        k, cols = (i - 2) // 2, pl.ds(BLOCK * ((i - 2) % 2), BLOCK)
        return wm.at[l, k, :, :, :, cols] if q is None else wm.at[l, k, q, :, :, cols]

    def z_copy(src, u, j, device, send_sem):
        return remote(src, gathered.at[j, u, p.q], send_sem, rz.at[u, j], device)

    def x_copy(u, j, q):
        return remote(gathered.at[j, u, q], gathered.at[j, u, q], sx.at[u, j], rx.at[u, j], p.xn)

    def y_copy(u, j, q):
        return remote(gathered.at[j, u, q], gathered.at[j, u, q], sy.at[u, j], ry.at[u, j], p.yn)

    def xd_copy(u, j, q):
        return remote(gathered.at[j, u, q, 1], gathered.at[j, u, q, 1], sxd.at[u, j], rxd.at[u, j], p.xn)

    def yd_copy(u, j, q):
        return remote(gathered.at[j, u, q, 0], gathered.at[j, u, q, 0], syd.at[u, j], ryd.at[u, j], p.yn)

    def source(l, i):
        u = UNITS * l + i

        @when(level == 0)
        def _():
            z_copy(block(l, i, p.q), u, 0, p.above, sz.at[u, 0]).start()
            local(block(l, i), gathered.at[0, u], native.at[u]).start()

        @when(level == 1)
        def _():
            z_copy(block(l, i, p.q), u, 1, p.above, sz.at[u, 1]).start()
            z_copy(block(l, i, p.q), u, 1, p.below, szd.at[u]).start()
            local(block(l, i), gathered.at[1, u], native.at[u]).start()

    def stage_one(l, i):
        u = UNITS * l + i
        for j in range(2):

            @when(level != j)
            def _(j=j):
                here = gathered.at[j, u, p.q]
                z_copy(here, u, j, p.above, sz.at[u, j]).wait_recv()

                @when((level == 2) | ((level == 1) if j == 0 else (level == 2)))
                def _():
                    z_copy(here, u, j, p.above, sz.at[u, j]).start()

                x_copy(u, j, p.q).start()
                y_copy(u, j, p.q).start()

    def stage_two(l, i):
        u = UNITS * l + i
        for j in range(2):

            @when(level != j)
            def _(j=j):
                x_copy(u, j, p.qx).wait_recv()
                yd_copy(u, j, p.qx).start()
                y_copy(u, j, p.qy).wait_recv()
                xd_copy(u, j, p.qy).start()

    def finish(l, i):
        u = UNITS * l + i
        for j in range(2):

            @when(level != j)
            def _(j=j):
                yd_copy(u, j, p.qd).wait_recv()
                xd_copy(u, j, p.qd).wait_recv()

            @when(level == j)
            def _(j=j):
                local(block(l, i), gathered.at[j, u], native.at[u]).wait()

    def ahead(step, l, i, by):
        k = i + by
        if k < UNITS:
            step(l, k)
        else:

            @when(l + k // UNITS < LAYERS)
            def _():
                step(l + k // UNITS, k % UNITS)

    def tick(l, i):
        ahead(source, l, i, 3)
        ahead(stage_one, l, i, 2)
        ahead(stage_two, l, i, 1)
        finish(l, i)

    for i in range(3):
        source(0, i)
    bias_wait = bias_copy(bias, 0, 0, p.above)

    @when(level != 0)
    def _():
        bias_wait.wait_recv()

    @when((level == 1) | (level == 2))
    def _():
        bias_copy(biases.at[0], 0, 0, p.above).start()

    @when(level != 1)
    def _():
        bias_copy(bias, 1, 1, p.above).wait_recv()

    @when(level == 2)
    def _():
        bias_copy(biases.at[1], 1, 1, p.above).start()

    @when(level < 2)
    def _():
        local(bias, biases.at[0], bias_sem.at[5]).wait()

    wait_input(0)
    stage_one(0, 0)
    stage_one(0, 1)
    stage_two(0, 0)

    def unit_low(u, j):
        value = gathered[j, u].reshape(WIDTH, BLOCK).astype(bf16)
        return value

    def keep_low(l, i):
        u = UNITS * l + i
        slot = i % 2

        def drain():
            for j in range(2):
                local(low.at[slot, j], o_w.at[j, u], low_sem.at[slot, j]).wait()

        if i >= 2:
            drain()
        else:
            pl.when(l > 0)(drain)
        for j in range(2):
            low[slot, j] = unit_low(u, j)
            local(low.at[slot, j], o_w.at[j, u], low_sem.at[slot, j]).start()
        return low.at[slot]

    def swap(slot):
        copy = remote(part, other.at[slot], swap_sem.at[slot], swap_sem.at[2 + slot], p.partner)
        copy.start()
        copy.wait()

    def out_copies(l):
        return [
            local(hs.at[l + 1], o_h.at[l], out_sem.at[0, l]),
            local(ms.at[l], o_m.at[l], out_sem.at[1, l]),
            local(n1s.at[l], o_n1.at[l], out_sem.at[2, l]),
            local(n2s.at[l], o_n2.at[l], out_sem.at[3, l]),
            local(qs.at[l], o_q.at[l], out_sem.at[4, l]),
            local(ks.at[l], o_k.at[l], out_sem.at[5, l]),
            local(vs.at[l], o_v.at[l], out_sem.at[6, l]),
            local(as_.at[l], o_a.at[l], out_sem.at[7, l]),
        ]

    def mid_copies(l, i):
        k = i - 2
        return [
            local(us.at[:, k], o_u.at[l, :, k], mid_sem.at[0, k]),
            local(cs.at[:, k], o_c.at[l, :, k], mid_sem.at[1, k]),
        ]

    def layer(l, carry):
        params = vec[l]

        tick(l, 0)
        scaled, _ = normalize_parts(hs[l])
        n1s[l] = (scaled * params[0:1] + params[1:2]).astype(bf16)
        weights = keep_low(l, 0)
        for j in range(2):
            both = product(n1s[l], weights[j])
            qs[l, j] = (both[:, :192] + biases[j, pl.ds(3 * l, 1), 0:192]).astype(bf16)
            ks[l, j] = both[:, 192:].astype(bf16)

        tick(l, 1)
        weights = keep_low(l, 1)
        keep = lax.broadcasted_iota(jnp.int32, (128, ROWS), 1) < FRAMES
        for j in range(2):
            vs[l, j] = (
                product(n1s[l], weights[j, :, 0:192]) + biases[j, pl.ds(3 * l, 1), 192:384]
            ).astype(bf16)

            def rows_of(r, carry, j=j):
                rows = pl.ds(pl.multiple_of(r * 128, 128), 128)
                heads = []
                for h in range(HEADS_HERE):
                    cols = slice(HEAD_DIM * h, HEAD_DIM * (h + 1))
                    scores = contract_last(qs[l, j, rows, cols], ks[l, j, :, cols]) * score_scale
                    scores = jnp.where(keep, scores, -1e30)
                    weight = jnp.exp(scores - jnp.max(scores, axis=-1, keepdims=True))
                    weight = weight * (1.0 / jnp.sum(weight, axis=-1, keepdims=True))
                    heads.append(product(weight.astype(bf16), vs[l, j, :, cols]))
                as_[l, j, rows, :] = jnp.concatenate(heads, axis=-1).astype(bf16)
                return carry

            lax.fori_loop(0, ROWS // 128, rows_of, 0)
        part[...] = contract_last(as_[l, 0], weights[0, :, 192:384])
        part[...] += contract_last(as_[l, 1], weights[1, :, 192:384])
        swap(0)
        ms[l] = hs[l] + (part[...] + other[0]) + params[4:5]
        scaled, _ = normalize_parts(ms[l])
        n2s[l] = (scaled * params[2:3] + params[3:4]).astype(bf16)

        for i in (2, 3):
            tick(l, i)
            weights = keep_low(l, i)

            @when(l > 0)
            def _(i=i):
                for copy in mid_copies(l - 1, i):
                    copy.wait()

            for j in range(2):
                before = product(n2s[l], weights[j]) + biases[j, pl.ds(3 * l + i - 1, 1), :]
                us[j, i - 2] = before
                cs[j, i - 2] = gelu(before).astype(bf16)
            for copy in mid_copies(l, i):
                copy.start()

        for i in (4, 5):
            tick(l, i)
            weights = keep_low(l, i)
            for j in range(2):
                term = contract_last(cs[j, i - 4], weights[j])
                if i == 4 and j == 0:
                    part[...] = term
                else:
                    part[...] += term
        swap(1)
        hs[l + 1] = ms[l] + (part[...] + other[1]) + params[5:6]
        for copy in out_copies(l):
            copy.start()
        return carry

    lax.fori_loop(0, LAYERS, layer, 0)

    last = LAYERS - 1
    for i in (2, 3):
        for copy in mid_copies(last, i):
            copy.wait()
    for l in range(LAYERS):
        for copy in out_copies(l):
            copy.wait()
    for slot in range(2):
        for j in range(2):
            local(low.at[slot, j], o_w.at[j, 0], low_sem.at[slot, j]).wait()
    wait_input(1)
    wait_input(2)

    @when(level < 3)
    def _():
        bias_copy(bias, 0, 0, p.above).wait_send()

    @when((level == 1) | (level == 2))
    def _():
        bias_copy(bias, 1, 1, p.above).wait_send()

    @when(level == 1)
    def _():
        bias_copy(bias, 1, 2, p.below).wait_send()

    def drain(u, carry):
        for j in range(2):

            @when((level < 3) if j == 0 else ((level == 1) | (level == 2)))
            def _(j=j):
                z_copy(gathered.at[j, u, p.q], u, j, p.above, sz.at[u, j]).wait_send()

            @when(level != j)
            def _(j=j):
                x_copy(u, j, p.q).wait_send()
                y_copy(u, j, p.q).wait_send()
                yd_copy(u, j, p.qx).wait_send()
                xd_copy(u, j, p.qy).wait_send()

        @when(level == 1)
        def _():
            z_copy(gathered.at[1, u, p.q], u, 1, p.below, szd.at[u]).wait_send()

        return carry

    lax.fori_loop(0, TOTAL, drain, 0)


def run_forward(frames, cotangent, wa, wm, bias, vectors):
    def hbm(shape, kind):
        return jax.ShapeDtypeStruct(shape, kind)

    dma = pltpu.SemaphoreType.DMA
    per_unit = dma((TOTAL, 2))
    return pl.pallas_call(
        forward_kernel,
        out_shape=(
            hbm((ROWS, WIDTH), f32),
            hbm((ROWS, WIDTH), f32),
            hbm((LAYERS, ROWS, WIDTH), f32),
            hbm((LAYERS, ROWS, WIDTH), f32),
            hbm((LAYERS, ROWS, WIDTH), bf16),
            hbm((LAYERS, ROWS, WIDTH), bf16),
            hbm((LAYERS, 2, ROWS, 192), bf16),
            hbm((LAYERS, 2, ROWS, 192), bf16),
            hbm((LAYERS, 2, ROWS, 192), bf16),
            hbm((LAYERS, 2, ROWS, 192), bf16),
            hbm((LAYERS, 2, 2, ROWS, BLOCK), f32),
            hbm((LAYERS, 2, 2, ROWS, BLOCK), bf16),
            hbm((2, TOTAL, WIDTH, BLOCK), bf16),
        ),
        in_specs=[ANY, ANY, ANY, ANY, ANY, VMEM],
        out_specs=(ANY,) * 13,
        scratch_shapes=[
            pltpu.VMEM((2, TOTAL, 4, 2, 96, BLOCK), f32),
            pltpu.VMEM((2, 8, BLOCK), f32),
            pltpu.VMEM((LAYERS + 1, ROWS, WIDTH), f32),
            pltpu.VMEM((LAYERS, ROWS, WIDTH), f32),
            pltpu.VMEM((LAYERS, ROWS, WIDTH), bf16),
            pltpu.VMEM((LAYERS, ROWS, WIDTH), bf16),
            pltpu.VMEM((LAYERS, 2, ROWS, 192), bf16),
            pltpu.VMEM((LAYERS, 2, ROWS, 192), bf16),
            pltpu.VMEM((LAYERS, 2, ROWS, 192), bf16),
            pltpu.VMEM((LAYERS, 2, ROWS, 192), bf16),
            pltpu.VMEM((2, 2, ROWS, BLOCK), f32),
            pltpu.VMEM((2, 2, ROWS, BLOCK), bf16),
            pltpu.VMEM((2, 2, WIDTH, BLOCK), bf16),
            pltpu.VMEM((ROWS, WIDTH), f32),
            pltpu.VMEM((2, ROWS, WIDTH), f32),
            per_unit,
            per_unit,
            dma((TOTAL,)),
            per_unit,
            per_unit,
            per_unit,
            per_unit,
            per_unit,
            per_unit,
            per_unit,
            per_unit,
            dma((TOTAL,)),
            dma((9,)),
            dma((6,)),
            dma((4,)),
            dma((2, 2)),
            dma((2, 2)),
            dma((8, LAYERS)),
        ],
        compiler_params=pltpu.CompilerParams(
            collective_id=0, has_side_effects=True, vmem_limit_bytes=63 << 20
        ),
        name="gather_forward",
    )(frames, cotangent, wa, wm, bias, vectors)


def reduce_kernel(
    grads,
    acts,
    o_fin,
    o_act,
    held,
    x1,
    y1,
    x2,
    y2,
    own,
    zin,
    zup,
    load_sem,
    sx1,
    rx1,
    sy1,
    ry1,
    sx2,
    rx2,
    sy2,
    ry2,
    szd,
    rzd,
    szu,
    rzu,
    sfin,
    rfin,
    lfin,
    act_send,
    act_recv,
    act_sem,
):
    p = find_place()
    greet(p)
    level = p.level
    when = pl.when

    def act_copy(src, j, n, k, device):
        return remote(src, o_act.at[j, n], act_send.at[n, k], act_recv.at[n, j], device)

    for n in range(3):

        @when(level == 0)
        def _(n=n):
            local(acts.at[n], o_act.at[0, n], act_sem.at[n]).start()
            act_copy(acts.at[n], 0, n, 0, p.above).start()

        @when(level == 1)
        def _(n=n):
            local(acts.at[n], o_act.at[1, n], act_sem.at[n]).start()
            act_copy(acts.at[n], 1, n, 1, p.above).start()
            act_copy(acts.at[n], 1, n, 2, p.below).start()

    def load(u):
        return local(grads.at[u], held.at[lax.rem(u, SLOTS)], load_sem.at[lax.rem(u, SLOTS)])

    def x1_copy(w):
        return remote(held.at[w, :, :, 1 - p.x, 0], x1.at[w], sx1.at[w], rx1.at[w], p.xn)

    def y1_copy(w):
        return remote(held.at[w, :, 1 - p.y, :, 1], y1.at[w], sy1.at[w], ry1.at[w], p.yn)

    def x2_copy(w):
        return remote(held.at[w, :, p.y, 1 - p.x, 1], x2.at[w], sx2.at[w], rx2.at[w], p.xn)

    def y2_copy(w):
        return remote(held.at[w, :, 1 - p.y, p.x, 0], y2.at[w], sy2.at[w], ry2.at[w], p.yn)

    def down_copy(u, j):
        return remote(own.at[u, j], zin.at[u, j], szd.at[u, j], rzd.at[u, j], p.below)

    def up_copy(u):
        return remote(own.at[u, 1], zup.at[u], szu.at[u], rzu.at[u], p.above)

    def fin_copy(u, j):
        return remote(own.at[u, j, 1 - p.c], o_fin.at[u], sfin.at[u], rfin.at[u], p.partner)

    def fin_local(u, j):
        return local(own.at[u, j, p.c], o_fin.at[u], lfin.at[u])

    def begin(u):
        w = lax.rem(u, SLOTS)

        @when(u >= SLOTS)
        def _():
            x1_copy(w).wait_send()
            y1_copy(w).wait_send()
            x2_copy(w).wait_send()
            y2_copy(w).wait_send()

        load(u).start()

    def stage_one(u):
        w = lax.rem(u, SLOTS)
        load(u).wait()
        x1_copy(w).start()
        y1_copy(w).start()

    def stage_two(u):
        w = lax.rem(u, SLOTS)
        x1_copy(w).wait_recv()
        held[w, :, 1 - p.y, p.x, 0] += x1[w, :, 1 - p.y]
        held[w, :, p.y, p.x, 0] += x1[w, :, p.y]
        y1_copy(w).wait_recv()
        held[w, :, p.y, 1 - p.x, 1] += y1[w, :, 1 - p.x]
        held[w, :, p.y, p.x, 1] += y1[w, :, p.x]
        y2_copy(w).start()
        x2_copy(w).start()

    def stage_three(u):
        w = lax.rem(u, SLOTS)
        y2_copy(w).wait_recv()
        own[u, :, 0] = held[w, :, p.y, p.x, 0] + y2[w]
        x2_copy(w).wait_recv()
        own[u, :, 1] = held[w, :, p.y, p.x, 1] + x2[w]

        @when(level == 3)
        def _():
            down_copy(u, 0).start()
            down_copy(u, 1).start()

        @when(level == 0)
        def _():
            up_copy(u).start()

    def level_two(u):
        for j in range(2):
            down_copy(u, j).wait_recv()
            own[u, j] += zin[u, j]
            down_copy(u, j).start()

    def level_one(u):
        down_copy(u, 0).wait_recv()
        own[u, 0] += zin[u, 0]
        down_copy(u, 0).start()
        down_copy(u, 1).wait_recv()
        up_copy(u).wait_recv()
        own[u, 1] += zin[u, 1] + zup[u]
        fin_local(u, 1).start()
        fin_copy(u, 1).start()

    def level_zero(u):
        down_copy(u, 0).wait_recv()
        own[u, 0] += zin[u, 0]
        fin_local(u, 0).start()
        fin_copy(u, 0).start()

    def in_range(u):
        return (u >= 0) & (u < TOTAL)

    def tick(s, carry):
        when(in_range(s + 1))(lambda: begin(s + 1))
        when(in_range(s))(lambda: stage_one(s))
        when(in_range(s - 1))(lambda: stage_two(s - 1))
        when(in_range(s - 2))(lambda: stage_three(s - 2))
        when(in_range(s - 3) & (level == 2))(lambda: level_two(s - 3))
        when(in_range(s - 4) & (level == 1))(lambda: level_one(s - 4))
        when(in_range(s - 5) & (level == 0))(lambda: level_zero(s - 5))
        for n in range(3):

            @when((s == 2 + 2 * n) & (level == 1))
            def _(n=n):
                act_copy(acts.at[n], 0, n, 0, p.above).wait_recv()
                act_copy(o_act.at[0, n], 0, n, 0, p.above).start()

            @when((s == 3 + 2 * n) & (level == 2))
            def _(n=n):
                act_copy(acts.at[n], 1, n, 1, p.above).wait_recv()
                act_copy(o_act.at[1, n], 1, n, 1, p.above).start()
                act_copy(acts.at[n], 0, n, 0, p.above).wait_recv()
                act_copy(o_act.at[0, n], 0, n, 0, p.above).start()

        return carry

    begin(0)
    lax.fori_loop(0, TOTAL + 5, tick, 0)

    for w in range(SLOTS):
        x1_copy(w).wait_send()
        y1_copy(w).wait_send()
        x2_copy(w).wait_send()
        y2_copy(w).wait_send()

    def drain(u, carry):
        @when(level > 0)
        def _():
            down_copy(u, 0).wait_send()

        @when(level > 1)
        def _():
            down_copy(u, 1).wait_send()
            fin_copy(u, 0).wait_recv()

        @when(level == 0)
        def _():
            up_copy(u).wait_send()

        @when(level < 2)
        def _():
            fin_local(u, 0).wait()
            fin_copy(u, 0).wait_send()

        return carry

    lax.fori_loop(0, TOTAL, drain, 0)
    for n in range(3):

        @when(level < 3)
        def _(n=n):
            act_copy(acts.at[n], 0, n, 0, p.above).wait_send()

        @when((level == 1) | (level == 2))
        def _(n=n):
            act_copy(acts.at[n], 1, n, 1, p.above).wait_send()

        @when(level == 1)
        def _(n=n):
            act_copy(acts.at[n], 1, n, 2, p.below).wait_send()

        @when(level < 2)
        def _(n=n):
            local(acts.at[n], o_act.at[0, n], act_sem.at[n]).wait()

        @when(level == 3)
        def _(n=n):
            act_copy(acts.at[n], 0, n, 0, p.above).wait_recv()

        @when((level == 0) | (level == 3))
        def _(n=n):
            act_copy(acts.at[n], 1, n, 1, p.above).wait_recv()


def run_reduce(grads, acts):
    dma = pltpu.SemaphoreType.DMA
    slots = dma((SLOTS,))
    units = dma((TOTAL,))
    return pl.pallas_call(
        reduce_kernel,
        out_shape=(
            jax.ShapeDtypeStruct((TOTAL, 96, BLOCK), f32),
            jax.ShapeDtypeStruct((2, 3, ROWS, WIDTH), f32),
        ),
        in_specs=[ANY, ANY],
        out_specs=(ANY, ANY),
        scratch_shapes=[
            pltpu.VMEM((SLOTS, 2, 2, 2, 2, 96, BLOCK), f32),
            pltpu.VMEM((SLOTS, 2, 2, 96, BLOCK), f32),
            pltpu.VMEM((SLOTS, 2, 2, 96, BLOCK), f32),
            pltpu.VMEM((SLOTS, 2, 96, BLOCK), f32),
            pltpu.VMEM((SLOTS, 2, 96, BLOCK), f32),
            pltpu.VMEM((TOTAL, 2, 2, 96, BLOCK), f32),
            pltpu.VMEM((TOTAL, 2, 2, 96, BLOCK), f32),
            pltpu.VMEM((TOTAL, 2, 96, BLOCK), f32),
            slots,
            slots,
            slots,
            slots,
            slots,
            slots,
            slots,
            slots,
            slots,
            dma((TOTAL, 2)),
            dma((TOTAL, 2)),
            units,
            units,
            units,
            units,
            units,
            dma((3, 3)),
            dma((3, 2)),
            dma((3,)),
        ],
        compiler_params=pltpu.CompilerParams(
            collective_id=1, has_side_effects=True, vmem_limit_bytes=60 << 20
        ),
        name="reduce_gradients",
    )(grads, acts)


def sum_cores(value):
    size = lax.axis_size("dp")
    return value + lax.ppermute(value, "dp", [(i, i + 1 - 2 * (i % 2)) for i in range(size)])


def backward(saved, vectors):
    x_in, cotangent, hs, ms, n1s, n2s, qs, ks, vs, as_, us, cs, low = saved
    keep = lax.broadcasted_iota(jnp.int32, (ROWS, ROWS), 1) < FRAMES
    upstream = cotangent
    units = []
    vector_grads = [None] * LAYERS
    head_grads = [None] * LAYERS
    up_grads = [None] * LAYERS
    for l in reversed(range(LAYERS)):
        params = vectors[l]
        base = UNITS * l
        scaled_two, inverse_two = normalize_parts(ms[l])
        scaled_one, inverse_one = normalize_parts(x_in if l == 0 else hs[l - 1])
        output_low = upstream.astype(bf16)
        down_bias_grad = jnp.sum(output_low.astype(f32), axis=0)
        for k in range(2):
            units.append(jnp.stack([contract_rows(output_low, cs[l, j, k]) for j in range(2)]))
        partial = 0.0
        up_rows = [[None, None], [None, None]]
        for k in range(2):
            pair = []
            for j in range(2):
                back = (product(output_low, low[j, base + 4 + k]) * gelu_slope(us[l, j, k])).astype(bf16)
                up_rows[j][k] = jnp.sum(back.astype(f32), axis=0)
                pair.append(contract_rows(n2s[l], back))
                partial = partial + contract_last(back, low[j, base + 2 + k])
            units.append(jnp.stack(pair))
        lowered, gain_two_grad, shift_two_grad = normalize_back(
            sum_cores(partial), scaled_two, inverse_two, params[2]
        )
        upstream = upstream + lowered
        branch_low = upstream.astype(bf16)
        out_bias_grad = jnp.sum(branch_low.astype(f32), axis=0)
        partial = 0.0
        vo_units, qk_units, head_rows = [], [], []
        for j in range(2):
            w_out = low[j, base + 1][:, 192:]
            out_grad = contract_rows(branch_low, as_[l, j])
            mixture_back = product(branch_low, w_out).astype(bf16)
            dq, dk, dv = [], [], []
            for h in range(HEADS_HERE):
                cols = slice(HEAD_DIM * h, HEAD_DIM * (h + 1))
                q, k, v, da = qs[l, j][:, cols], ks[l, j][:, cols], vs[l, j][:, cols], mixture_back[:, cols]
                scores = jnp.where(keep, contract_last(q, k) * score_scale, -1e30)
                weight = jnp.exp(scores - jnp.max(scores, axis=-1, keepdims=True))
                weight = weight * (1.0 / jnp.sum(weight, axis=-1, keepdims=True))
                prob_grad = contract_last(da, v)
                centre = jnp.sum(prob_grad * weight, axis=-1, keepdims=True)
                score_back = (weight * (prob_grad - centre)).astype(bf16)
                dq.append((product(score_back, k) * score_scale).astype(bf16))
                dk.append((contract_rows(score_back, q) * score_scale).astype(bf16))
                dv.append(contract_rows(weight.astype(bf16), da).astype(bf16))
            dq, dk, dv = (jnp.concatenate(parts, axis=-1) for parts in (dq, dk, dv))
            vo_units.append(jnp.concatenate([contract_rows(n1s[l], dv), out_grad], axis=-1))
            qk_units.append(
                jnp.concatenate([contract_rows(n1s[l], dq), contract_rows(n1s[l], dk)], axis=-1)
            )
            partial = (
                partial
                + contract_last(dq, low[j, base][:, :192])
                + contract_last(dk, low[j, base][:, 192:])
                + contract_last(dv, low[j, base + 1][:, :192])
            )
            head_rows.append((jnp.sum(dq.astype(f32), axis=0), jnp.sum(dv.astype(f32), axis=0)))
        units.append(jnp.stack(vo_units))
        units.append(jnp.stack(qk_units))
        lowered, gain_one_grad, shift_one_grad = normalize_back(
            sum_cores(partial), scaled_one, inverse_one, params[0]
        )
        upstream = upstream + lowered
        vector_grads[l] = jnp.stack(
            [gain_one_grad, shift_one_grad, gain_two_grad, shift_two_grad, out_bias_grad, down_bias_grad]
        )
        head_grads[l] = jnp.stack([jnp.stack([head_rows[j][n] for n in range(2)]) for j in range(2)])
        up_grads[l] = jnp.stack([jnp.concatenate(up_rows[j]) for j in range(2)])
    grads = jnp.stack(units).reshape(TOTAL, 2, 2, 2, 2, 96, BLOCK)
    return upstream, grads, jnp.stack(vector_grads), jnp.stack(head_grads), jnp.stack(up_grads)


def per_device(
    frames,
    cotangent,
    w_attn,
    w_mlp,
    vectors,
    head_bias,
    up_bias,
    moment_attn,
    square_attn,
    moment_mlp,
    square_mlp,
    moment_vectors,
    square_vectors,
    moment_head,
    square_head,
    moment_up,
    square_up,
):
    dp = lax.axis_index("dp")
    t = lax.axis_index("tensor")
    core = dp % 2
    dp_size = lax.axis_size("dp")

    def clips_of(block):
        return jnp.pad(block.reshape(2, FRAMES, WIDTH), ((0, 0), (0, ROWS - FRAMES), (0, 0)))

    wa = jnp.stack(
        [
            jnp.concatenate([w_attn[:, 0], w_attn[:, 1]], axis=-1),
            jnp.concatenate([w_attn[:, 2], w_attn[:, 3]], axis=-1),
        ],
        axis=1,
    ).reshape(LAYERS, 2, 4, 2, 96, BLOCK)
    wm = w_mlp.reshape(LAYERS, 2, 4, 2, 96, 2 * BLOCK)
    bias = jnp.concatenate(
        [head_bias.reshape(LAYERS, 1, BLOCK), up_bias.reshape(LAYERS, 2, BLOCK)], axis=1
    ).reshape(3 * LAYERS, BLOCK)
    bias = jnp.pad(bias, ((0, 8 - 3 * LAYERS), (0, 0)))
    saved = run_forward(clips_of(frames), clips_of(cotangent), wa, wm, bias, vectors)

    input_grad, grads, vector_grad, head_grad, up_grad = backward(saved, vectors)

    acts = jnp.concatenate([saved[2], input_grad[None]])
    fin, acts = run_reduce(grads, acts)

    acts = acts[:, :, :FRAMES]
    acts = jnp.where(core == 0, acts, acts[::-1])
    acts = jnp.concatenate([acts[0], acts[1]], axis=1)
    sections, upstream = acts[:2], acts[2]

    def in_order(pair, axis):
        return jnp.where(core == 0, pair, jnp.flip(pair, axis))

    head_grad = in_order(head_grad, 1).transpose(0, 2, 1, 3).reshape(LAYERS, 2, 2 * HEADS_HERE, HEAD_DIM)
    up_grad = in_order(up_grad, 1).reshape(LAYERS, 24, HEAD_DIM)
    head_all = jnp.concatenate(
        [jnp.where(core == k, head_grad, 0.0) for k in range(2)], axis=2
    )
    up_all = jnp.concatenate([jnp.where(core == k, up_grad, 0.0) for k in range(2)], axis=1)
    vector_all = jnp.where(core == 0, vector_grad, 0.0)
    vector_all, head_all, up_all = lax.psum((vector_all, head_all, up_all), ("dp", "tensor"))

    def owned(param, dim):
        size = param.shape[dim] // dp_size
        return lax.dynamic_slice_in_dim(param, dp * size, size, dim)

    head_all = lax.dynamic_slice_in_dim(head_all, t * HEADS_HERE, HEADS_HERE, 2)
    up_all = lax.dynamic_slice_in_dim(up_all, t * 12, 12, 1)

    if dp_size > GROUP:
        rows = jnp.zeros((TOTAL, WIDTH, BLOCK), f32)
        rows = lax.dynamic_update_slice_in_dim(rows, fin, (dp % GROUP) * 96, 1)
        fin = lax.psum_scatter(rows, "dp", scatter_dimension=1, tiled=True)

    def unit(l, k):
        return fin[(LAYERS - 1 - l) * UNITS + k]

    attn_grad = jnp.stack(
        [
            jnp.stack([unit(l, 5)[:, :192], unit(l, 5)[:, 192:], unit(l, 4)[:, :192], unit(l, 4)[:, 192:]])
            for l in range(LAYERS)
        ]
    )
    mlp_grad = jnp.stack(
        [
            jnp.stack(
                [
                    jnp.concatenate([unit(l, 2), unit(l, 3)], axis=-1),
                    jnp.concatenate([unit(l, 0), unit(l, 1)], axis=-1),
                ]
            )
            for l in range(LAYERS)
        ]
    )
    attn = adamw_update(owned(w_attn, 2), attn_grad, moment_attn, square_attn, rate_matrix)
    mlp = adamw_update(owned(w_mlp, 2), mlp_grad, moment_mlp, square_mlp, rate_matrix)
    vector_new = adamw_update(
        owned(vectors, 2), owned(vector_all, 2), moment_vectors, square_vectors, rate_vector
    )
    head = adamw_update(owned(head_bias, 3), owned(head_all, 3), moment_head, square_head, rate_vector)
    upper = adamw_update(owned(up_bias, 2), owned(up_all, 2), moment_up, square_up, rate_vector)
    return (sections, upstream, *attn, *mlp, *vector_new, *head, *upper)


def solution(mesh):
    in_specs = (
        P("dp", None),
        P("dp", None),
        P(None, None, None, "tensor"),
        P(None, None, None, "tensor"),
        P(),
        P(None, None, "tensor", None),
        P(None, "tensor", None),
        P(None, None, "dp", "tensor"),
        P(None, None, "dp", "tensor"),
        P(None, None, "dp", "tensor"),
        P(None, None, "dp", "tensor"),
        P(None, None, "dp"),
        P(None, None, "dp"),
        P(None, None, "tensor", "dp"),
        P(None, None, "tensor", "dp"),
        P(None, "tensor", "dp"),
        P(None, "tensor", "dp"),
    )
    out_specs = (
        P(None, "dp", None),
        P("dp", None),
        P(None, None, "dp", "tensor"),
        P(None, None, "dp", "tensor"),
        P(None, None, "dp", "tensor"),
        P(None, None, "dp", "tensor"),
        P(None, None, "dp", "tensor"),
        P(None, None, "dp", "tensor"),
        P(None, None, "dp"),
        P(None, None, "dp"),
        P(None, None, "dp"),
        P(None, None, "tensor", "dp"),
        P(None, None, "tensor", "dp"),
        P(None, None, "tensor", "dp"),
        P(None, "tensor", "dp"),
        P(None, "tensor", "dp"),
        P(None, "tensor", "dp"),
    )
    return jax.shard_map(
        per_device, mesh=mesh, in_specs=in_specs, out_specs=out_specs, check_vma=False
    )
```

```python
import math
from types import SimpleNamespace

import jax
import jax.numpy as jnp
from jax import lax
from jax.experimental import pallas as pl
from jax.experimental.pallas import tpu as pltpu
from jax.sharding import PartitionSpec as P

HEAD_DIM = 64
FRAMES = 500
ROWS = 512
LAYERS = 2
STEP = 10
WIDTH = 768
BLOCK = 384
UNITS = 6
TOTAL = LAYERS * UNITS
GROUP = 8
HEADS_HERE = 3
SLOTS = 3

ln_eps = 1e-05
beta_one = 0.9
beta_two = 0.999
adam_eps = 1e-08
decay_rate = 0.01
rate_matrix = 0.05
rate_vector = 0.2
score_scale = 1.0 / math.sqrt(HEAD_DIM)
MESH = pl.DeviceIdType.MESH
f32 = jnp.float32
bf16 = jnp.bfloat16
ANY = pl.BlockSpec(memory_space=pl.ANY)
VMEM = pl.BlockSpec(memory_space=pltpu.VMEM)


def product(left, right):
    return jnp.dot(left, right, preferred_element_type=f32)


def contract_last(left, right):
    return lax.dot_general(left, right, (((1,), (1,)), ((), ())), preferred_element_type=f32)


def contract_rows(left, right):
    return lax.dot_general(left, right, (((0,), (0,)), ((), ())), preferred_element_type=f32)


def normalize_parts(inputs):
    centre = jnp.mean(inputs, axis=-1, keepdims=True)
    centred = inputs - centre
    inverse = lax.rsqrt(jnp.mean(centred * centred, axis=-1, keepdims=True) + ln_eps)
    return centred * inverse, inverse


def normalize_back(upstream, scaled, inverse, gain):
    gain_grad = jnp.sum(upstream * scaled, axis=0)
    shift_grad = jnp.sum(upstream, axis=0)
    inner_grad = upstream * gain
    lowered = inverse * (
        inner_grad
        - jnp.mean(inner_grad, axis=-1, keepdims=True)
        - scaled * jnp.mean(inner_grad * scaled, axis=-1, keepdims=True)
    )
    return (lowered, gain_grad, shift_grad)


def gelu(before):
    return 0.5 * before * (1.0 + lax.erf(before * (1.0 / math.sqrt(2.0))))


def gelu_slope(before):
    return 0.5 * (1.0 + lax.erf(before * (1.0 / math.sqrt(2.0)))) + before * jnp.exp(
        -0.5 * before * before
    ) * (1.0 / math.sqrt(2.0 * math.pi))


def adamw_update(param, gradient, first, second, rate):
    first_new = beta_one * first + (1.0 - beta_one) * gradient
    second_new = beta_two * second + (1.0 - beta_two) * gradient * gradient
    ratio = (
        first_new
        / (1.0 - beta_one**STEP)
        / (jnp.sqrt(second_new / (1.0 - beta_two**STEP)) + adam_eps)
    )
    return (param - rate * (ratio + decay_rate * param), first_new, second_new)


def find_place():
    dp = lax.axis_index("dp")
    t = lax.axis_index("tensor")
    i = lax.rem(dp, GROUP)
    base = dp - i
    c = lax.rem(i, 2)
    x = lax.rem(i // 2, 2)
    y = i // 4
    up = 1 - 2 * c
    level = c * (3 - t) + (1 - c) * t

    def at(cc, xx, yy):
        return base + 4 * yy + 2 * xx + cc

    return SimpleNamespace(
        t=t,
        c=c,
        x=x,
        y=y,
        q=2 * y + x,
        qx=2 * y + 1 - x,
        qy=2 * (1 - y) + x,
        qd=2 * (1 - y) + 1 - x,
        level=level,
        partner=(at(1 - c, x, y), t),
        xn=(at(c, 1 - x, y), t),
        yn=(at(c, x, 1 - y), t),
        above=(dp, t + up),
        below=(dp, t - up),
    )


def greet(p):
    barrier = pltpu.get_barrier_semaphore()

    def signal(device):
        pl.semaphore_signal(barrier, inc=1, device_id=device, device_id_type=MESH)

    signal(p.partner)
    signal(p.xn)
    signal(p.yn)

    @pl.when(p.level < 3)
    def _():
        signal(p.above)

    @pl.when(p.level > 0)
    def _():
        signal(p.below)

    inner = (p.level > 0) & (p.level < 3)

    @pl.when(inner)
    def _():
        pl.semaphore_wait(barrier, 5)

    @pl.when(jnp.logical_not(inner))
    def _():
        pl.semaphore_wait(barrier, 4)


def remote(src, dst, send_sem, recv_sem, device):
    return pltpu.make_async_remote_copy(
        src_ref=src,
        dst_ref=dst,
        send_sem=send_sem,
        recv_sem=recv_sem,
        device_id=device,
        device_id_type=MESH,
    )


def local(src, dst, sem):
    return pltpu.make_async_copy(src, dst, sem)


def forward_kernel(
    frames,
    cotangent,
    wa,
    wm,
    bias,
    vec,
    o_ct,
    o_h,
    o_m,
    o_n1,
    o_n2,
    o_q,
    o_k,
    o_v,
    o_a,
    o_u,
    o_c,
    o_w,
    gathered,
    biases,
    hs,
    ms,
    n1s,
    n2s,
    qs,
    ks,
    vs,
    as_,
    us,
    cs,
    low,
    part,
    other,
    rz,
    sz,
    szd,
    rx,
    sx,
    ry,
    sy,
    rxd,
    sxd,
    ryd,
    syd,
    native,
    first_sem,
    bias_sem,
    swap_sem,
    low_sem,
    mid_sem,
    out_sem,
):
    p = find_place()
    greet(p)
    level = p.level

    def when(cond):
        return pl.when(cond)

    mine = (p.t // 2) == p.c
    clip = lax.rem(p.t, 2)
    inputs = ((frames, hs.at[0], 0), (frames, o_h.at[0], 1), (cotangent, o_ct, 2))

    @when(mine)
    def _():
        for source, target, k in inputs:
            local(source.at[clip], target, first_sem.at[k]).start()
            remote(source.at[clip], target, first_sem.at[3 + k], first_sem.at[6 + k], p.partner).start()

    def wait_input(k):
        source, target, _ = inputs[k]

        @when(mine)
        def _():
            local(source.at[clip], target, first_sem.at[k]).wait()
            remote(source.at[clip], target, first_sem.at[3 + k], first_sem.at[6 + k], p.partner).wait_send()

        @when(jnp.logical_not(mine))
        def _():
            remote(source.at[clip], target, first_sem.at[3 + k], first_sem.at[6 + k], p.partner).wait_recv()

    def bias_copy(src, j, k, device):
        return remote(src, biases.at[j], bias_sem.at[k], bias_sem.at[3 + j], device)

    @when(level == 0)
    def _():
        local(bias, biases.at[0], bias_sem.at[5]).start()
        bias_copy(bias, 0, 0, p.above).start()

    @when(level == 1)
    def _():
        local(bias, biases.at[1], bias_sem.at[5]).start()
        bias_copy(bias, 1, 1, p.above).start()
        bias_copy(bias, 1, 2, p.below).start()

    def block(l, i, q=None):
        if i < 2:
            return wa.at[l, i] if q is None else wa.at[l, i, q]
        k, cols = (i - 2) // 2, pl.ds(BLOCK * ((i - 2) % 2), BLOCK)
        return wm.at[l, k, :, :, :, cols] if q is None else wm.at[l, k, q, :, :, cols]

    def z_copy(src, u, j, device, send_sem):
        return remote(src, gathered.at[j, u, p.q], send_sem, rz.at[u, j], device)

    def x_copy(u, j, q):
        return remote(gathered.at[j, u, q], gathered.at[j, u, q], sx.at[u, j], rx.at[u, j], p.xn)

    def y_copy(u, j, q):
        return remote(gathered.at[j, u, q], gathered.at[j, u, q], sy.at[u, j], ry.at[u, j], p.yn)

    def xd_copy(u, j, q):
        return remote(gathered.at[j, u, q, 1], gathered.at[j, u, q, 1], sxd.at[u, j], rxd.at[u, j], p.xn)

    def yd_copy(u, j, q):
        return remote(gathered.at[j, u, q, 0], gathered.at[j, u, q, 0], syd.at[u, j], ryd.at[u, j], p.yn)

    def source(l, i):
        u = UNITS * l + i

        @when(level == 0)
        def _():
            z_copy(block(l, i, p.q), u, 0, p.above, sz.at[u, 0]).start()
            local(block(l, i), gathered.at[0, u], native.at[u]).start()

        @when(level == 1)
        def _():
            z_copy(block(l, i, p.q), u, 1, p.above, sz.at[u, 1]).start()
            z_copy(block(l, i, p.q), u, 1, p.below, szd.at[u]).start()
            local(block(l, i), gathered.at[1, u], native.at[u]).start()

    def stage_one(l, i):
        u = UNITS * l + i
        for j in range(2):

            @when(level != j)
            def _(j=j):
                here = gathered.at[j, u, p.q]
                z_copy(here, u, j, p.above, sz.at[u, j]).wait_recv()

                @when((level == 2) | ((level == 1) if j == 0 else (level == 2)))
                def _():
                    z_copy(here, u, j, p.above, sz.at[u, j]).start()

                x_copy(u, j, p.q).start()
                y_copy(u, j, p.q).start()

    def stage_two(l, i):
        u = UNITS * l + i
        for j in range(2):

            @when(level != j)
            def _(j=j):
                x_copy(u, j, p.qx).wait_recv()
                yd_copy(u, j, p.qx).start()
                y_copy(u, j, p.qy).wait_recv()
                xd_copy(u, j, p.qy).start()

    def finish(l, i):
        u = UNITS * l + i
        for j in range(2):

            @when(level != j)
            def _(j=j):
                yd_copy(u, j, p.qd).wait_recv()
                xd_copy(u, j, p.qd).wait_recv()

            @when(level == j)
            def _(j=j):
                local(block(l, i), gathered.at[j, u], native.at[u]).wait()

    def ahead(step, l, i, by):
        k = i + by
        if k < UNITS:
            step(l, k)
        else:

            @when(l + k // UNITS < LAYERS)
            def _():
                step(l + k // UNITS, k % UNITS)

    def tick(l, i):
        ahead(source, l, i, 3)
        ahead(stage_one, l, i, 2)
        ahead(stage_two, l, i, 1)
        finish(l, i)

    for i in range(3):
        source(0, i)
    bias_wait = bias_copy(bias, 0, 0, p.above)

    @when(level != 0)
    def _():
        bias_wait.wait_recv()

    @when((level == 1) | (level == 2))
    def _():
        bias_copy(biases.at[0], 0, 0, p.above).start()

    @when(level != 1)
    def _():
        bias_copy(bias, 1, 1, p.above).wait_recv()

    @when(level == 2)
    def _():
        bias_copy(biases.at[1], 1, 1, p.above).start()

    @when(level < 2)
    def _():
        local(bias, biases.at[0], bias_sem.at[5]).wait()

    wait_input(0)
    stage_one(0, 0)
    stage_one(0, 1)
    stage_two(0, 0)

    def unit_low(u, j):
        value = gathered[j, u].reshape(WIDTH, BLOCK).astype(bf16)
        return value

    def keep_low(l, i):
        u = UNITS * l + i
        slot = i % 2

        def drain():
            for j in range(2):
                local(low.at[slot, j], o_w.at[j, u], low_sem.at[slot, j]).wait()

        if i >= 2:
            drain()
        else:
            pl.when(l > 0)(drain)
        for j in range(2):
            low[slot, j] = unit_low(u, j)
            local(low.at[slot, j], o_w.at[j, u], low_sem.at[slot, j]).start()
        return low.at[slot]

    def swap(slot):
        copy = remote(part, other.at[slot], swap_sem.at[slot], swap_sem.at[2 + slot], p.partner)
        copy.start()
        copy.wait()

    def out_copies(l):
        return [
            local(hs.at[l + 1], o_h.at[l + 1], out_sem.at[0, l]),
            local(ms.at[l], o_m.at[l], out_sem.at[1, l]),
            local(n1s.at[l], o_n1.at[l], out_sem.at[2, l]),
            local(n2s.at[l], o_n2.at[l], out_sem.at[3, l]),
            local(qs.at[l], o_q.at[l], out_sem.at[4, l]),
            local(ks.at[l], o_k.at[l], out_sem.at[5, l]),
            local(vs.at[l], o_v.at[l], out_sem.at[6, l]),
            local(as_.at[l], o_a.at[l], out_sem.at[7, l]),
        ]

    def mid_copies(l, i):
        k = i - 2
        return [
            local(us.at[:, k], o_u.at[l, :, k], mid_sem.at[0, k]),
            local(cs.at[:, k], o_c.at[l, :, k], mid_sem.at[1, k]),
        ]

    def layer(l, carry):
        params = vec[l]

        tick(l, 0)
        scaled, _ = normalize_parts(hs[l])
        n1s[l] = (scaled * params[0:1] + params[1:2]).astype(bf16)
        weights = keep_low(l, 0)
        for j in range(2):
            both = product(n1s[l], weights[j])
            qs[l, j] = (both[:, :192] + biases[j, pl.ds(3 * l, 1), 0:192]).astype(bf16)
            ks[l, j] = both[:, 192:].astype(bf16)

        tick(l, 1)
        weights = keep_low(l, 1)
        keep = lax.broadcasted_iota(jnp.int32, (128, ROWS), 1) < FRAMES
        for j in range(2):
            vs[l, j] = (
                product(n1s[l], weights[j, :, 0:192]) + biases[j, pl.ds(3 * l, 1), 192:384]
            ).astype(bf16)

            def rows_of(r, carry, j=j):
                rows = pl.ds(pl.multiple_of(r * 128, 128), 128)
                heads = []
                for h in range(HEADS_HERE):
                    cols = slice(HEAD_DIM * h, HEAD_DIM * (h + 1))
                    scores = contract_last(qs[l, j, rows, cols], ks[l, j, :, cols]) * score_scale
                    scores = jnp.where(keep, scores, -1e30)
                    weight = jnp.exp(scores - jnp.max(scores, axis=-1, keepdims=True))
                    weight = weight * (1.0 / jnp.sum(weight, axis=-1, keepdims=True))
                    heads.append(product(weight.astype(bf16), vs[l, j, :, cols]))
                as_[l, j, rows, :] = jnp.concatenate(heads, axis=-1).astype(bf16)
                return carry

            lax.fori_loop(0, ROWS // 128, rows_of, 0)
        part[...] = contract_last(as_[l, 0], weights[0, :, 192:384])
        part[...] += contract_last(as_[l, 1], weights[1, :, 192:384])
        swap(0)
        ms[l] = hs[l] + (part[...] + other[0]) + params[4:5]
        scaled, _ = normalize_parts(ms[l])
        n2s[l] = (scaled * params[2:3] + params[3:4]).astype(bf16)

        for i in (2, 3):
            tick(l, i)
            weights = keep_low(l, i)

            @when(l > 0)
            def _(i=i):
                for copy in mid_copies(l - 1, i):
                    copy.wait()

            for j in range(2):
                before = product(n2s[l], weights[j]) + biases[j, pl.ds(3 * l + i - 1, 1), :]
                us[j, i - 2] = before
                cs[j, i - 2] = gelu(before).astype(bf16)
            for copy in mid_copies(l, i):
                copy.start()

        for i in (4, 5):
            tick(l, i)
            weights = keep_low(l, i)
            for j in range(2):
                term = contract_last(cs[j, i - 4], weights[j])
                if i == 4 and j == 0:
                    part[...] = term
                else:
                    part[...] += term
        swap(1)
        hs[l + 1] = ms[l] + (part[...] + other[1]) + params[5:6]
        for copy in out_copies(l):
            copy.start()
        return carry

    lax.fori_loop(0, LAYERS, layer, 0)

    last = LAYERS - 1
    for i in (2, 3):
        for copy in mid_copies(last, i):
            copy.wait()
    for l in range(LAYERS):
        for copy in out_copies(l):
            copy.wait()
    for slot in range(2):
        for j in range(2):
            local(low.at[slot, j], o_w.at[j, 0], low_sem.at[slot, j]).wait()
    wait_input(1)
    wait_input(2)

    @when(level < 3)
    def _():
        bias_copy(bias, 0, 0, p.above).wait_send()

    @when((level == 1) | (level == 2))
    def _():
        bias_copy(bias, 1, 1, p.above).wait_send()

    @when(level == 1)
    def _():
        bias_copy(bias, 1, 2, p.below).wait_send()

    def drain(u, carry):
        for j in range(2):

            @when((level < 3) if j == 0 else ((level == 1) | (level == 2)))
            def _(j=j):
                z_copy(gathered.at[j, u, p.q], u, j, p.above, sz.at[u, j]).wait_send()

            @when(level != j)
            def _(j=j):
                x_copy(u, j, p.q).wait_send()
                y_copy(u, j, p.q).wait_send()
                yd_copy(u, j, p.qx).wait_send()
                xd_copy(u, j, p.qy).wait_send()

        @when(level == 1)
        def _():
            z_copy(gathered.at[1, u, p.q], u, 1, p.below, szd.at[u]).wait_send()

        return carry

    lax.fori_loop(0, TOTAL, drain, 0)


def run_forward(frames, cotangent, wa, wm, bias, vectors):
    def hbm(shape, kind):
        return jax.ShapeDtypeStruct(shape, kind)

    dma = pltpu.SemaphoreType.DMA
    per_unit = dma((TOTAL, 2))
    return pl.pallas_call(
        forward_kernel,
        out_shape=(
            hbm((ROWS, WIDTH), f32),
            hbm((LAYERS + 1, ROWS, WIDTH), f32),
            hbm((LAYERS, ROWS, WIDTH), f32),
            hbm((LAYERS, ROWS, WIDTH), bf16),
            hbm((LAYERS, ROWS, WIDTH), bf16),
            hbm((LAYERS, 2, ROWS, 192), bf16),
            hbm((LAYERS, 2, ROWS, 192), bf16),
            hbm((LAYERS, 2, ROWS, 192), bf16),
            hbm((LAYERS, 2, ROWS, 192), bf16),
            hbm((LAYERS, 2, 2, ROWS, BLOCK), f32),
            hbm((LAYERS, 2, 2, ROWS, BLOCK), bf16),
            hbm((2, TOTAL, WIDTH, BLOCK), bf16),
        ),
        in_specs=[ANY, ANY, ANY, ANY, ANY, VMEM],
        out_specs=(ANY,) * 12,
        scratch_shapes=[
            pltpu.VMEM((2, TOTAL, 4, 2, 96, BLOCK), f32),
            pltpu.VMEM((2, 8, BLOCK), f32),
            pltpu.VMEM((LAYERS + 1, ROWS, WIDTH), f32),
            pltpu.VMEM((LAYERS, ROWS, WIDTH), f32),
            pltpu.VMEM((LAYERS, ROWS, WIDTH), bf16),
            pltpu.VMEM((LAYERS, ROWS, WIDTH), bf16),
            pltpu.VMEM((LAYERS, 2, ROWS, 192), bf16),
            pltpu.VMEM((LAYERS, 2, ROWS, 192), bf16),
            pltpu.VMEM((LAYERS, 2, ROWS, 192), bf16),
            pltpu.VMEM((LAYERS, 2, ROWS, 192), bf16),
            pltpu.VMEM((2, 2, ROWS, BLOCK), f32),
            pltpu.VMEM((2, 2, ROWS, BLOCK), bf16),
            pltpu.VMEM((2, 2, WIDTH, BLOCK), bf16),
            pltpu.VMEM((ROWS, WIDTH), f32),
            pltpu.VMEM((2, ROWS, WIDTH), f32),
            per_unit,
            per_unit,
            dma((TOTAL,)),
            per_unit,
            per_unit,
            per_unit,
            per_unit,
            per_unit,
            per_unit,
            per_unit,
            per_unit,
            dma((TOTAL,)),
            dma((9,)),
            dma((6,)),
            dma((4,)),
            dma((2, 2)),
            dma((2, 2)),
            dma((8, LAYERS)),
        ],
        compiler_params=pltpu.CompilerParams(
            collective_id=0, has_side_effects=True, vmem_limit_bytes=63 << 20
        ),
        name="gather_forward",
    )(frames, cotangent, wa, wm, bias, vectors)


def backward_kernel(
    i_ct,
    i_h,
    i_m,
    i_n1,
    i_n2,
    i_q,
    i_k,
    i_v,
    i_a,
    i_u,
    i_c,
    i_w,
    vec,
    o_fin,
    o_act,
    o_small,
    held,
    x1,
    y1,
    x2,
    y2,
    own,
    zin,
    zup,
    grad,
    part,
    other,
    h_in,
    m_in,
    n1,
    n2,
    q,
    k,
    v,
    a,
    u_in,
    c_in,
    w_in,
    low,
    dqk,
    dv,
    small,
    small_in,
    sx1,
    rx1,
    sy1,
    ry1,
    sx2,
    rx2,
    sy2,
    ry2,
    szd,
    rzd,
    szu,
    rzu,
    sfin,
    rfin,
    lfin,
    act_send,
    act_recv,
    act_sem,
    load_sem,
    unit_sem,
    swap_sem,
    small_send,
    small_recv,
    ct_sem,
):
    p = find_place()
    greet(p)
    level = p.level
    when = pl.when

    def act_copy(src, j, n, m, device):
        return remote(src, o_act.at[j, n], act_send.at[n, m], act_recv.at[n, j], device)

    def act_source(n):
        return i_h.at[n + 1] if n < LAYERS else grad

    def act_begin(n):
        src = act_source(n)

        @when(level == 0)
        def _():
            local(src, o_act.at[0, n], act_sem.at[n]).start()
            act_copy(src, 0, n, 0, p.above).start()

        @when(level == 1)
        def _():
            local(src, o_act.at[1, n], act_sem.at[n]).start()
            act_copy(src, 1, n, 1, p.above).start()
            act_copy(src, 1, n, 2, p.below).start()

    def act_pass(n, at, s):
        src = act_source(n)

        @when((s == at) & (level == 1))
        def _():
            act_copy(src, 0, n, 0, p.above).wait_recv()
            act_copy(o_act.at[0, n], 0, n, 0, p.above).start()

        @when((s == at + 1) & (level == 2))
        def _():
            act_copy(src, 1, n, 1, p.above).wait_recv()
            act_copy(o_act.at[1, n], 1, n, 1, p.above).start()
            act_copy(src, 0, n, 0, p.above).wait_recv()
            act_copy(o_act.at[0, n], 0, n, 0, p.above).start()

    def x1_copy(w):
        return remote(held.at[w, :, :, 1 - p.x, 0], x1.at[w], sx1.at[w], rx1.at[w], p.xn)

    def y1_copy(w):
        return remote(held.at[w, :, 1 - p.y, :, 1], y1.at[w], sy1.at[w], ry1.at[w], p.yn)

    def x2_copy(w):
        return remote(held.at[w, :, p.y, 1 - p.x, 1], x2.at[w], sx2.at[w], rx2.at[w], p.xn)

    def y2_copy(w):
        return remote(held.at[w, :, 1 - p.y, p.x, 0], y2.at[w], sy2.at[w], ry2.at[w], p.yn)

    def down_copy(u, j):
        return remote(own.at[u, j], zin.at[u, j], szd.at[u, j], rzd.at[u, j], p.below)

    def up_copy(u):
        return remote(own.at[u, 1], zup.at[u], szu.at[u], rzu.at[u], p.above)

    def fin_copy(u, j):
        return remote(own.at[u, j, 1 - p.c], o_fin.at[u], sfin.at[u], rfin.at[u], p.partner)

    def fin_local(u, j):
        return local(own.at[u, j, p.c], o_fin.at[u], lfin.at[u])

    def sent(w):
        x1_copy(w).wait_send()
        y1_copy(w).wait_send()
        x2_copy(w).wait_send()
        y2_copy(w).wait_send()

    def stage_one(w):
        x1_copy(w).start()
        y1_copy(w).start()

    def stage_two(w):
        x1_copy(w).wait_recv()
        held[w, :, 1 - p.y, p.x, 0] += x1[w, :, 1 - p.y]
        held[w, :, p.y, p.x, 0] += x1[w, :, p.y]
        y1_copy(w).wait_recv()
        held[w, :, p.y, 1 - p.x, 1] += y1[w, :, 1 - p.x]
        held[w, :, p.y, p.x, 1] += y1[w, :, p.x]
        y2_copy(w).start()
        x2_copy(w).start()

    def stage_three(u, w):
        y2_copy(w).wait_recv()
        own[u, :, 0] = held[w, :, p.y, p.x, 0] + y2[w]
        x2_copy(w).wait_recv()
        own[u, :, 1] = held[w, :, p.y, p.x, 1] + x2[w]

        @when(level == 3)
        def _():
            down_copy(u, 0).start()
            down_copy(u, 1).start()

        @when(level == 0)
        def _():
            up_copy(u).start()

    def level_two(u):
        for j in range(2):
            down_copy(u, j).wait_recv()
            own[u, j] += zin[u, j]
            down_copy(u, j).start()

    def level_one(u):
        down_copy(u, 0).wait_recv()
        own[u, 0] += zin[u, 0]
        down_copy(u, 0).start()
        down_copy(u, 1).wait_recv()
        up_copy(u).wait_recv()
        own[u, 1] += zin[u, 1] + zup[u]
        fin_local(u, 1).start()
        fin_copy(u, 1).start()

    def level_zero(u):
        down_copy(u, 0).wait_recv()
        own[u, 0] += zin[u, 0]
        fin_local(u, 0).start()
        fin_copy(u, 0).start()

    def service(s, i):
        if isinstance(s, int):

            def guard(ok, step):
                if ok:
                    step()
        else:

            def guard(ok, step):
                when(ok)(step)

        if isinstance(s, int):
            assert s >= TOTAL
        else:
            stage_one(i % SLOTS)
        guard((s >= 1) & (s - 1 < TOTAL), lambda: stage_two((i - 1) % SLOTS))
        guard((s >= 2) & (s - 2 < TOTAL), lambda: stage_three(s - 2, (i - 2) % SLOTS))
        guard((s >= 3) & (s - 3 < TOTAL), lambda: when(level == 2)(lambda: level_two(s - 3)))
        guard((s >= 4) & (s - 4 < TOTAL), lambda: when(level == 1)(lambda: level_one(s - 4)))
        guard((s >= 5) & (s - 5 < TOTAL), lambda: when(level == 0)(lambda: level_zero(s - 5)))

    def loads(l):
        whole = (
            (i_c, c_in),
            (i_u, u_in),
            (i_n2, n2),
            (i_m, m_in),
            (i_a, a),
            (i_q, q),
            (i_k, k),
            (i_v, v),
            (i_n1, n1),
            (i_h, h_in),
        )
        return [local(src.at[l], dst, load_sem.at[n]) for n, (src, dst) in enumerate(whole)]

    def unit_load(l, i):
        return local(i_w.at[:, UNITS * l + i], w_in.at[:, i], unit_sem.at[i])

    def swap(slot):
        copy = remote(part, other.at[slot], swap_sem.at[slot], swap_sem.at[2 + slot], p.partner)
        copy.start()
        copy.wait()

    def put(w, j, value):
        held[w, j] = value.reshape(2, 2, 2, 96, BLOCK)

    def small_row(l, row, value):
        small[l, row : row + 1] = value[:, :BLOCK]
        small[l, row + 1 : row + 2] = value[:, BLOCK:]

    def norm_back(slot, l, source, gain, first):
        def rows_of(r, carry):
            rows = pl.ds(pl.multiple_of(r * 128, 128), 128)
            upstream = part[rows] + other[slot, rows]
            scaled, inverse = normalize_parts(source[rows])
            lowered, gain_grad, shift_grad = normalize_back(upstream, scaled, inverse, gain)
            value = grad[rows] + lowered
            grad[rows] = value
            rounded = value.astype(bf16)
            low[rows] = rounded
            bias_grad = jnp.sum(rounded.astype(f32), axis=0)
            return (
                carry[0] + gain_grad.reshape(1, WIDTH),
                carry[1] + shift_grad.reshape(1, WIDTH),
                carry[2] + bias_grad.reshape(1, WIDTH),
            )

        zero = jnp.zeros((1, WIDTH), f32)
        sums = lax.fori_loop(0, ROWS // 128, rows_of, (zero, zero, zero))
        small_row(l, first, sums[0])
        small_row(l, first + 2, sums[1])
        return sums[2]

    keep = lax.broadcasted_iota(jnp.int32, (ROWS, ROWS), 1) < FRAMES

    def attention_back(j, carry):
        mixture_back = product(low[...], w_in[j, 1, :, 192:384]).astype(bf16)
        parts = ([], [], [])
        for h in range(HEADS_HERE):
            cols = slice(HEAD_DIM * h, HEAD_DIM * (h + 1))
            qh, kh, vh, dah = q[j, :, cols], k[j, :, cols], v[j, :, cols], mixture_back[:, cols]
            scores = jnp.where(keep, contract_last(qh, kh) * score_scale, -1e30)
            weight = jnp.exp(scores - jnp.max(scores, axis=-1, keepdims=True))
            weight = weight * (1.0 / jnp.sum(weight, axis=-1, keepdims=True))
            prob_grad = contract_last(dah, vh)
            centre = jnp.sum(prob_grad * weight, axis=-1, keepdims=True)
            score_back = (weight * (prob_grad - centre)).astype(bf16)
            parts[0].append((product(score_back, kh) * score_scale).astype(bf16))
            parts[1].append((contract_rows(score_back, qh) * score_scale).astype(bf16))
            parts[2].append(contract_rows(weight.astype(bf16), dah).astype(bf16))
        dqk[j] = jnp.concatenate(parts[0] + parts[1], axis=-1)
        dv[j] = jnp.concatenate(parts[2], axis=-1)
        return carry

    local(i_ct, grad, ct_sem.at[0]).start()

    def layer(step, carry):
        l = LAYERS - 1 - step
        s0 = UNITS * step
        params = vec[l]
        fetch = loads(l)
        for copy in fetch[:2]:
            copy.start()
        for i in (4, 5, 2, 3):
            unit_load(l, i).start()
        for copy in fetch[2:]:
            copy.start()
        for i in (1, 0):
            unit_load(l, i).start()

        def free(s, w):
            when(s >= SLOTS)(lambda: sent(w))

        @when(step == 0)
        def _():
            local(i_ct, grad, ct_sem.at[0]).wait()
            low[...] = grad[...].astype(bf16)
            small_row(l, 10, jnp.sum(low[...].astype(f32), axis=0, keepdims=True))

        fetch[0].wait()
        for i in (0, 1):
            free(s0 + i, i)
            for j in range(2):
                put(i, j, contract_rows(low[...], c_in[j, i]))
            service(s0 + i, i)
            if i == 0:

                @when(step == 0)
                def _():
                    act_begin(0)
                    act_begin(1)

        fetch[1].wait()
        fetch[2].wait()
        for i in (2, 3):
            h = i - 2
            unit_load(l, 4 + h).wait()
            unit_load(l, 2 + h).wait()
            w = i % SLOTS
            free(s0 + i, w)
            for j in range(2):
                back = (product(low[...], w_in[j, 4 + h]) * gelu_slope(u_in[j, h])).astype(bf16)
                row = 14 + 2 * j + h
                small[l, row : row + 1] = jnp.sum(back.astype(f32), axis=0, keepdims=True)
                put(w, j, contract_rows(n2[...], back))
                term = contract_last(back, w_in[j, 2 + h])
                if h == 0 and j == 0:
                    part[...] = term
                else:
                    part[...] += term
            service(s0 + i, i)
        swap(0)
        fetch[3].wait()
        small_row(l, 8, norm_back(0, l, m_in, params[2:3], 4))

        for copy in fetch[4:]:
            copy.wait()
        unit_load(l, 1).wait()
        unit_load(l, 0).wait()
        lax.fori_loop(0, 2, attention_back, 0)
        free(s0 + 4, 4 % SLOTS)
        for j in range(2):
            held[4 % SLOTS, j, :, :, :, :, 0:192] = contract_rows(n1[...], dv[j]).reshape(2, 2, 2, 96, 192)
            held[4 % SLOTS, j, :, :, :, :, 192:384] = contract_rows(low[...], a[j]).reshape(2, 2, 2, 96, 192)
        service(s0 + 4, 4)
        free(s0 + 5, 5 % SLOTS)
        for j in range(2):
            put(5 % SLOTS, j, contract_rows(n1[...], dqk[j]))
            sums = jnp.sum(dqk[j].astype(f32), axis=0, keepdims=True)
            small[l, 12 + j : 13 + j, 0:192] = sums[:, 0:192]
            small[l, 12 + j : 13 + j, 192:384] = jnp.sum(dv[j].astype(f32), axis=0, keepdims=True)
            term = contract_last(dqk[j], w_in[j, 0]) + contract_last(dv[j], w_in[j, 1, :, 0:192])
            if j == 0:
                part[...] = term
            else:
                part[...] += term
        service(s0 + 5, 5)
        swap(1)
        down_sum = norm_back(1, l, h_in, params[0:1], 0)

        @when(l > 0)
        def _():
            small_row(l - 1, 10, down_sum)

        for n in range(LAYERS):
            act_pass(n, 0, step - n)

        return carry

    small[...] = jnp.zeros_like(small)
    lax.fori_loop(0, LAYERS, layer, 0)

    def small_copy(m, device):
        return remote(small, small_in.at[m], small_send.at[m], small_recv.at[m], device)

    def small_step(m, device):
        copy = small_copy(m, device)
        copy.start()
        return copy

    act_begin(2)
    act_pass(1, -1, 0)
    small_copy(0, p.xn).start()
    service(TOTAL, 0)
    small_copy(0, p.xn).wait()
    small[...] += small_in[0]
    small_copy(1, p.yn).start()
    act_pass(2, 0, 0)
    service(TOTAL + 1, 1)
    small_copy(1, p.yn).wait()
    small[...] += small_in[1]

    @when((level == 0) | (level == 2))
    def _():
        small_copy(2, p.above).start()

    @when((level == 1) | (level == 3))
    def _():
        small_copy(2, p.below).start()

    act_pass(2, -1, 0)
    service(TOTAL + 2, 2)
    small_copy(2, p.above).wait()
    small[...] += small_in[2]

    @when(level == 1)
    def _():
        small_copy(3, p.above).start()

    @when(level == 2)
    def _():
        small_copy(3, p.below).start()

    service(TOTAL + 3, 3)

    @when(level == 1)
    def _():
        small_copy(3, p.above).wait()
        small[...] += small_in[3]
        small_copy(4, p.below).start()
        small_copy(4, p.below).wait_send()

    @when(level == 2)
    def _():
        small_copy(3, p.below).wait()
        small[...] += small_in[3]
        small_copy(4, p.above).start()
        small_copy(4, p.above).wait_send()

    service(TOTAL + 4, 4)

    @when((level == 0) | (level == 3))
    def _():
        small_copy(4, p.above).wait_recv()
        small[...] = small_in[4]

    small_copy(5, p.partner).start()
    local(small, o_small.at[0], ct_sem.at[1]).start()
    small_copy(5, p.partner).wait()
    local(small_in.at[5], o_small.at[1], ct_sem.at[2]).start()

    for w in range(SLOTS):
        sent(w)

    def drain(u, carry):
        @when(level > 0)
        def _():
            down_copy(u, 0).wait_send()

        @when(level > 1)
        def _():
            down_copy(u, 1).wait_send()
            fin_copy(u, 0).wait_recv()

        @when(level == 0)
        def _():
            up_copy(u).wait_send()

        @when(level < 2)
        def _():
            fin_local(u, 0).wait()
            fin_copy(u, 0).wait_send()

        return carry

    lax.fori_loop(0, TOTAL, drain, 0)
    for n in range(3):
        src = act_source(n)

        @when(level < 3)
        def _(n=n, src=src):
            act_copy(src, 0, n, 0, p.above).wait_send()

        @when((level == 1) | (level == 2))
        def _(n=n, src=src):
            act_copy(src, 1, n, 1, p.above).wait_send()

        @when(level == 1)
        def _(n=n, src=src):
            act_copy(src, 1, n, 2, p.below).wait_send()

        @when(level < 2)
        def _(n=n, src=src):
            local(src, o_act.at[0, n], act_sem.at[n]).wait()

        @when(level == 3)
        def _(n=n, src=src):
            act_copy(src, 0, n, 0, p.above).wait_recv()

        @when((level == 0) | (level == 3))
        def _(n=n, src=src):
            act_copy(src, 1, n, 1, p.above).wait_recv()

    local(small, o_small.at[0], ct_sem.at[1]).wait()
    local(small_in.at[5], o_small.at[1], ct_sem.at[2]).wait()


SMALL = (LAYERS, 24, BLOCK)


def run_backward(saved, vectors):
    dma = pltpu.SemaphoreType.DMA
    slots = dma((SLOTS,))
    units = dma((TOTAL,))
    pair = dma((TOTAL, 2))
    return pl.pallas_call(
        backward_kernel,
        out_shape=(
            jax.ShapeDtypeStruct((TOTAL, 96, BLOCK), f32),
            jax.ShapeDtypeStruct((2, 3, ROWS, WIDTH), f32),
            jax.ShapeDtypeStruct((2, *SMALL), f32),
        ),
        in_specs=[ANY] * 12 + [VMEM],
        out_specs=(ANY,) * 3,
        scratch_shapes=[
            pltpu.VMEM((SLOTS, 2, 2, 2, 2, 96, BLOCK), f32),
            pltpu.VMEM((SLOTS, 2, 2, 96, BLOCK), f32),
            pltpu.VMEM((SLOTS, 2, 2, 96, BLOCK), f32),
            pltpu.VMEM((SLOTS, 2, 96, BLOCK), f32),
            pltpu.VMEM((SLOTS, 2, 96, BLOCK), f32),
            pltpu.VMEM((TOTAL, 2, 2, 96, BLOCK), f32),
            pltpu.VMEM((TOTAL, 2, 2, 96, BLOCK), f32),
            pltpu.VMEM((TOTAL, 2, 96, BLOCK), f32),
            pltpu.VMEM((ROWS, WIDTH), f32),
            pltpu.VMEM((ROWS, WIDTH), f32),
            pltpu.VMEM((2, ROWS, WIDTH), f32),
            pltpu.VMEM((ROWS, WIDTH), f32),
            pltpu.VMEM((ROWS, WIDTH), f32),
            pltpu.VMEM((ROWS, WIDTH), bf16),
            pltpu.VMEM((ROWS, WIDTH), bf16),
            pltpu.VMEM((2, ROWS, 192), bf16),
            pltpu.VMEM((2, ROWS, 192), bf16),
            pltpu.VMEM((2, ROWS, 192), bf16),
            pltpu.VMEM((2, ROWS, 192), bf16),
            pltpu.VMEM((2, 2, ROWS, BLOCK), f32),
            pltpu.VMEM((2, 2, ROWS, BLOCK), bf16),
            pltpu.VMEM((2, UNITS, WIDTH, BLOCK), bf16),
            pltpu.VMEM((ROWS, WIDTH), bf16),
            pltpu.VMEM((2, ROWS, BLOCK), bf16),
            pltpu.VMEM((2, ROWS, 192), bf16),
            pltpu.VMEM(SMALL, f32),
            pltpu.VMEM((6, *SMALL), f32),
            slots,
            slots,
            slots,
            slots,
            slots,
            slots,
            slots,
            slots,
            pair,
            pair,
            units,
            units,
            units,
            units,
            units,
            dma((3, 3)),
            dma((3, 2)),
            dma((3,)),
            dma((10,)),
            dma((UNITS,)),
            dma((4,)),
            dma((6,)),
            dma((6,)),
            dma((3,)),
        ],
        compiler_params=pltpu.CompilerParams(
            collective_id=1, has_side_effects=True, vmem_limit_bytes=63 << 20
        ),
        name="backward_reduce",
    )(*saved, vectors)


def per_device(
    frames,
    cotangent,
    w_attn,
    w_mlp,
    vectors,
    head_bias,
    up_bias,
    moment_attn,
    square_attn,
    moment_mlp,
    square_mlp,
    moment_vectors,
    square_vectors,
    moment_head,
    square_head,
    moment_up,
    square_up,
):
    dp = lax.axis_index("dp")
    t = lax.axis_index("tensor")
    core = dp % 2
    dp_size = lax.axis_size("dp")

    def clips_of(block):
        return jnp.pad(block.reshape(2, FRAMES, WIDTH), ((0, 0), (0, ROWS - FRAMES), (0, 0)))

    wa = jnp.stack(
        [
            jnp.concatenate([w_attn[:, 0], w_attn[:, 1]], axis=-1),
            jnp.concatenate([w_attn[:, 2], w_attn[:, 3]], axis=-1),
        ],
        axis=1,
    ).reshape(LAYERS, 2, 4, 2, 96, BLOCK)
    wm = w_mlp.reshape(LAYERS, 2, 4, 2, 96, 2 * BLOCK)
    bias = jnp.concatenate(
        [head_bias.reshape(LAYERS, 1, BLOCK), up_bias.reshape(LAYERS, 2, BLOCK)], axis=1
    ).reshape(3 * LAYERS, BLOCK)
    bias = jnp.pad(bias, ((0, 8 - 3 * LAYERS), (0, 0)))
    saved = run_forward(clips_of(frames), clips_of(cotangent), wa, wm, bias, vectors)

    fin, acts, small = run_backward(saved, vectors)

    acts = acts[:, :, :FRAMES]
    acts = jnp.where(core == 0, acts, acts[::-1])
    acts = jnp.concatenate([acts[0], acts[1]], axis=1)
    sections, upstream = acts[:2], acts[2]

    if dp_size > GROUP:
        groups = [[i + GROUP * o for o in range(dp_size // GROUP)] for i in range(GROUP)]
        small = lax.psum(small, "dp", axis_index_groups=groups)
    vector_all = small[0, :, :12].reshape(LAYERS, 6, WIDTH)
    owner = t // 2
    here = jnp.where(owner == core, small[0], small[1])
    second = jnp.where(owner == 0, t % 2, 1 - t % 2)
    head_all = jnp.where(second == 0, here[:, 12], here[:, 13]).reshape(LAYERS, 2, HEADS_HERE, HEAD_DIM)
    up_all = jnp.where(second == 0, here[:, 14:16], here[:, 16:18]).reshape(LAYERS, 12, HEAD_DIM)

    def owned(param, dim):
        size = param.shape[dim] // dp_size
        return lax.dynamic_slice_in_dim(param, dp * size, size, dim)

    if dp_size > GROUP:
        rows = jnp.zeros((TOTAL, WIDTH, BLOCK), f32)
        rows = lax.dynamic_update_slice_in_dim(rows, fin, (dp % GROUP) * 96, 1)
        fin = lax.psum_scatter(rows, "dp", scatter_dimension=1, tiled=True)

    def unit(l, k):
        return fin[(LAYERS - 1 - l) * UNITS + k]

    attn_grad = jnp.stack(
        [
            jnp.stack([unit(l, 5)[:, :192], unit(l, 5)[:, 192:], unit(l, 4)[:, :192], unit(l, 4)[:, 192:]])
            for l in range(LAYERS)
        ]
    )
    mlp_grad = jnp.stack(
        [
            jnp.stack(
                [
                    jnp.concatenate([unit(l, 2), unit(l, 3)], axis=-1),
                    jnp.concatenate([unit(l, 0), unit(l, 1)], axis=-1),
                ]
            )
            for l in range(LAYERS)
        ]
    )
    attn = adamw_update(owned(w_attn, 2), attn_grad, moment_attn, square_attn, rate_matrix)
    mlp = adamw_update(owned(w_mlp, 2), mlp_grad, moment_mlp, square_mlp, rate_matrix)
    vector_new = adamw_update(
        owned(vectors, 2), owned(vector_all, 2), moment_vectors, square_vectors, rate_vector
    )
    head = adamw_update(owned(head_bias, 3), owned(head_all, 3), moment_head, square_head, rate_vector)
    upper = adamw_update(owned(up_bias, 2), owned(up_all, 2), moment_up, square_up, rate_vector)
    return (sections, upstream, *attn, *mlp, *vector_new, *head, *upper)


def solution(mesh):
    in_specs = (
        P("dp", None),
        P("dp", None),
        P(None, None, None, "tensor"),
        P(None, None, None, "tensor"),
        P(),
        P(None, None, "tensor", None),
        P(None, "tensor", None),
        P(None, None, "dp", "tensor"),
        P(None, None, "dp", "tensor"),
        P(None, None, "dp", "tensor"),
        P(None, None, "dp", "tensor"),
        P(None, None, "dp"),
        P(None, None, "dp"),
        P(None, None, "tensor", "dp"),
        P(None, None, "tensor", "dp"),
        P(None, "tensor", "dp"),
        P(None, "tensor", "dp"),
    )
    out_specs = (
        P(None, "dp", None),
        P("dp", None),
        P(None, None, "dp", "tensor"),
        P(None, None, "dp", "tensor"),
        P(None, None, "dp", "tensor"),
        P(None, None, "dp", "tensor"),
        P(None, None, "dp", "tensor"),
        P(None, None, "dp", "tensor"),
        P(None, None, "dp"),
        P(None, None, "dp"),
        P(None, None, "dp"),
        P(None, None, "tensor", "dp"),
        P(None, None, "tensor", "dp"),
        P(None, None, "tensor", "dp"),
        P(None, "tensor", "dp"),
        P(None, "tensor", "dp"),
        P(None, "tensor", "dp"),
    )
    return jax.shard_map(
        per_device, mesh=mesh, in_specs=in_specs, out_specs=out_specs, check_vma=False
    )
```

```python
import math
from types import SimpleNamespace

import jax
import jax.numpy as jnp
from jax import lax
from jax.experimental import pallas as pl
from jax.experimental.pallas import tpu as pltpu
from jax.sharding import PartitionSpec as P

HEAD_DIM = 64
FRAMES = 500
ROWS = 512
LAYERS = 2
STEP = 10
WIDTH = 768
BLOCK = 384
UNITS = 6
TOTAL = LAYERS * UNITS
GROUP = 8
HEADS_HERE = 3
SLOTS = 3
SPAN = 504
SECOND = 496
CHUNK = 128

ln_eps = 1e-05
beta_one = 0.9
beta_two = 0.999
adam_eps = 1e-08
decay_rate = 0.01
rate_matrix = 0.05
rate_vector = 0.2
score_scale = 1.0 / math.sqrt(HEAD_DIM)
MESH = pl.DeviceIdType.MESH
f32 = jnp.float32
bf16 = jnp.bfloat16
ANY = pl.BlockSpec(memory_space=pl.ANY)
VMEM = pl.BlockSpec(memory_space=pltpu.VMEM)


def product(left, right):
    return jnp.dot(left, right, preferred_element_type=f32)


def contract_last(left, right):
    return lax.dot_general(left, right, (((1,), (1,)), ((), ())), preferred_element_type=f32)


def contract_rows(left, right):
    return lax.dot_general(left, right, (((0,), (0,)), ((), ())), preferred_element_type=f32)


def normalize_parts(inputs):
    centre = jnp.mean(inputs, axis=-1, keepdims=True)
    centred = inputs - centre
    inverse = lax.rsqrt(jnp.mean(centred * centred, axis=-1, keepdims=True) + ln_eps)
    return centred * inverse, inverse


def normalize_back(upstream, scaled, inverse, gain):
    gain_grad = jnp.sum(upstream * scaled, axis=0)
    shift_grad = jnp.sum(upstream, axis=0)
    inner_grad = upstream * gain
    lowered = inverse * (
        inner_grad
        - jnp.mean(inner_grad, axis=-1, keepdims=True)
        - scaled * jnp.mean(inner_grad * scaled, axis=-1, keepdims=True)
    )
    return (lowered, gain_grad, shift_grad)


def gelu(before):
    return 0.5 * before * (1.0 + lax.erf(before * (1.0 / math.sqrt(2.0))))


def gelu_slope(before):
    return 0.5 * (1.0 + lax.erf(before * (1.0 / math.sqrt(2.0)))) + before * jnp.exp(
        -0.5 * before * before
    ) * (1.0 / math.sqrt(2.0 * math.pi))


def adamw_update(param, gradient, first, second, rate):
    first_new = beta_one * first + (1.0 - beta_one) * gradient
    second_new = beta_two * second + (1.0 - beta_two) * gradient * gradient
    ratio = (
        first_new
        / (1.0 - beta_one**STEP)
        / (jnp.sqrt(second_new / (1.0 - beta_two**STEP)) + adam_eps)
    )
    return (param - rate * (ratio + decay_rate * param), first_new, second_new)


def find_place():
    dp = lax.axis_index("dp")
    t = lax.axis_index("tensor")
    i = lax.rem(dp, GROUP)
    base = dp - i
    c = lax.rem(i, 2)
    x = lax.rem(i // 2, 2)
    y = i // 4
    up = 1 - 2 * c
    level = c * (3 - t) + (1 - c) * t

    def at(cc, xx, yy):
        return base + 4 * yy + 2 * xx + cc

    return SimpleNamespace(
        t=t,
        c=c,
        x=x,
        y=y,
        q=2 * y + x,
        qx=2 * y + 1 - x,
        qy=2 * (1 - y) + x,
        qd=2 * (1 - y) + 1 - x,
        level=level,
        partner=(at(1 - c, x, y), t),
        xn=(at(c, 1 - x, y), t),
        yn=(at(c, x, 1 - y), t),
        above=(dp, t + up),
        below=(dp, t - up),
    )


def greet(p):
    barrier = pltpu.get_barrier_semaphore()

    def signal(device):
        pl.semaphore_signal(barrier, inc=1, device_id=device, device_id_type=MESH)

    signal(p.partner)
    signal(p.xn)
    signal(p.yn)

    @pl.when(p.level < 3)
    def _():
        signal(p.above)

    @pl.when(p.level > 0)
    def _():
        signal(p.below)

    inner = (p.level > 0) & (p.level < 3)

    @pl.when(inner)
    def _():
        pl.semaphore_wait(barrier, 5)

    @pl.when(jnp.logical_not(inner))
    def _():
        pl.semaphore_wait(barrier, 4)


def remote(src, dst, send_sem, recv_sem, device):
    return pltpu.make_async_remote_copy(
        src_ref=src,
        dst_ref=dst,
        send_sem=send_sem,
        recv_sem=recv_sem,
        device_id=device,
        device_id_type=MESH,
    )


def local(src, dst, sem):
    return pltpu.make_async_copy(src, dst, sem)


def forward_kernel(
    frames,
    cotangent,
    wa,
    wm,
    head_bias,
    up_bias,
    vec,
    o_ct,
    o_h,
    o_m,
    o_n1,
    o_n2,
    o_qk,
    o_v,
    o_a,
    o_u,
    o_c,
    o_wa,
    o_wm,
    ga,
    gm,
    hb,
    ub,
    hs,
    ms,
    n1s,
    n2s,
    qks,
    vs,
    as_,
    us,
    cs,
    low_a,
    low_m,
    part,
    other,
    rz,
    sz,
    szd,
    rx,
    sx,
    ry,
    sy,
    rxd,
    sxd,
    ryd,
    syd,
    native,
    first_sem,
    bias_local,
    bias_send,
    bias_recv,
    swap_sem,
    low_sem,
    mid_sem,
    out_sem,
):
    p = find_place()
    greet(p)
    level = p.level
    when = pl.when

    def quarter(ref, i, q, h=None):
        lead = (slice(None), q) if i < 2 else (q,)
        return ref.at[lead if h is None else (*lead, h)]

    def block(l, i):
        if i < 2:
            return wa.at[l, pl.ds(2 * i, 2)]
        return wm.at[l, (i - 2) // 2, :, :, :, pl.ds(BLOCK * (i % 2), BLOCK)]

    def block_quarter(l, i):
        if i < 2:
            return wa.at[l, pl.ds(2 * i, 2), p.q]
        return wm.at[l, (i - 2) // 2, p.q, :, :, pl.ds(BLOCK * (i % 2), BLOCK)]

    def held(l, i, j):
        return ga.at[j, l, i] if i < 2 else gm.at[j, l, i - 2]

    def z_copy(src, l, i, j, device, send_sem):
        return remote(src, quarter(held(l, i, j), i, p.q), send_sem, rz.at[UNITS * l + i, j], device)

    def plane_copy(l, i, j, q, h, send_sem, recv_sem, device):
        here = quarter(held(l, i, j), i, q, h)
        u = UNITS * l + i
        return remote(here, here, send_sem.at[u, j], recv_sem.at[u, j], device)

    def x_copy(l, i, j, q):
        return plane_copy(l, i, j, q, None, sx, rx, p.xn)

    def y_copy(l, i, j, q):
        return plane_copy(l, i, j, q, None, sy, ry, p.yn)

    def xd_copy(l, i, j, q):
        return plane_copy(l, i, j, q, 1, sxd, rxd, p.xn)

    def yd_copy(l, i, j, q):
        return plane_copy(l, i, j, q, 0, syd, ryd, p.yn)

    def source(l, i):
        u = UNITS * l + i

        @when(level == 0)
        def _():
            z_copy(block_quarter(l, i), l, i, 0, p.above, sz.at[u, 0]).start()
            local(block(l, i), held(l, i, 0), native.at[u]).start()

        @when(level == 1)
        def _():
            z_copy(block_quarter(l, i), l, i, 1, p.above, sz.at[u, 1]).start()
            z_copy(block_quarter(l, i), l, i, 1, p.below, szd.at[u]).start()
            local(block(l, i), held(l, i, 1), native.at[u]).start()

    def stage_one(l, i):
        u = UNITS * l + i
        for j in range(2):

            @when(level != j)
            def _(j=j):
                here = quarter(held(l, i, j), i, p.q)
                z_copy(here, l, i, j, p.above, sz.at[u, j]).wait_recv()

                @when((level == 2) | ((level == 1) if j == 0 else (level == 2)))
                def _():
                    z_copy(here, l, i, j, p.above, sz.at[u, j]).start()

                x_copy(l, i, j, p.q).start()
                y_copy(l, i, j, p.q).start()

    def stage_two(l, i):
        for j in range(2):

            @when(level != j)
            def _(j=j):
                x_copy(l, i, j, p.qx).wait_recv()
                yd_copy(l, i, j, p.qx).start()
                y_copy(l, i, j, p.qy).wait_recv()
                xd_copy(l, i, j, p.qy).start()

    def finish(l, i):
        u = UNITS * l + i
        for j in range(2):

            @when(level != j)
            def _(j=j):
                yd_copy(l, i, j, p.qd).wait_recv()
                xd_copy(l, i, j, p.qd).wait_recv()

            @when(level == j)
            def _(j=j):
                local(block(l, i), held(l, i, j), native.at[u]).wait()

    def ahead(step, l, i, by):
        k = i + by
        if k < UNITS:
            step(l, k)
        else:

            @when(l + k // UNITS < LAYERS)
            def _():
                step(l + k // UNITS, k % UNITS)

    def tick(l, i):
        ahead(source, l, i, 3)
        ahead(stage_one, l, i, 2)
        ahead(stage_two, l, i, 1)
        finish(l, i)

    mine = (p.t // 2) == p.c
    clip = lax.rem(p.t, 2)
    span = pl.ds(pl.multiple_of(clip * SECOND, 8), SPAN)
    inputs = (
        (frames.at[span], part.at[pl.ds(0, SPAN)]),
        (cotangent.at[span], ms.at[1, pl.ds(0, SPAN)]),
    )

    def input_copies(k):
        src, dst = inputs[k]
        return (
            local(src, dst, first_sem.at[k]),
            remote(src, dst, first_sem.at[2 + k], first_sem.at[4 + k], p.partner),
        )

    def wait_input(k):
        here, there = input_copies(k)

        @when(mine)
        def _():
            here.wait()
            there.wait_send()

        @when(jnp.logical_not(mine))
        def _():
            there.wait_recv()

    def take_clip(target, raw):
        @when(clip == 0)
        def _():
            target[0:FRAMES] = raw[0:FRAMES]

        @when(clip == 1)
        def _():
            target[0:FRAMES] = raw[FRAMES - SECOND : SPAN]

        target[FRAMES:ROWS] = jnp.zeros((ROWS - FRAMES, WIDTH), f32)

    kept_biases = ((head_bias, hb), (up_bias, ub))

    def bias_copy(src, n, j, m, device):
        return remote(src, kept_biases[n][1].at[j], bias_send.at[n, m], bias_recv.at[n, j], device)

    def bias_source():
        for n, (src, dst) in enumerate(kept_biases):

            @when(level == 0)
            def _(n=n, src=src, dst=dst):
                local(src, dst.at[0], bias_local.at[n]).start()
                bias_copy(src, n, 0, 0, p.above).start()

            @when(level == 1)
            def _(n=n, src=src, dst=dst):
                local(src, dst.at[1], bias_local.at[n]).start()
                bias_copy(src, n, 1, 1, p.above).start()
                bias_copy(src, n, 1, 2, p.below).start()

    def bias_pass():
        for n, (src, dst) in enumerate(kept_biases):

            @when(level != 0)
            def _(n=n, src=src):
                bias_copy(src, n, 0, 0, p.above).wait_recv()

            @when((level == 1) | (level == 2))
            def _(n=n, dst=dst):
                bias_copy(dst.at[0], n, 0, 0, p.above).start()

            @when(level != 1)
            def _(n=n, src=src):
                bias_copy(src, n, 1, 1, p.above).wait_recv()

            @when(level == 2)
            def _(n=n, dst=dst):
                bias_copy(dst.at[1], n, 1, 1, p.above).start()

            @when(level < 2)
            def _(n=n, src=src, dst=dst):
                local(src, dst.at[0], bias_local.at[n]).wait()

    def bias_drain():
        for n, (src, dst) in enumerate(kept_biases):

            @when(level < 3)
            def _(n=n, src=src):
                bias_copy(src, n, 0, 0, p.above).wait_send()

            @when((level == 1) | (level == 2))
            def _(n=n, src=src):
                bias_copy(src, n, 1, 1, p.above).wait_send()

            @when(level == 1)
            def _(n=n, src=src):
                bias_copy(src, n, 1, 2, p.below).wait_send()

    def row_of(ref, rows):
        return jnp.concatenate([ref[r : r + 1, :] for r in rows], axis=-1)

    @when(mine)
    def _():
        for copy in input_copies(0):
            copy.start()

    bias_source()
    for i in range(3):
        source(0, i)

    @when(mine)
    def _():
        for copy in input_copies(1):
            copy.start()

    bias_pass()
    stage_one(0, 0)
    wait_input(0)
    take_clip(hs.at[0], part)
    stage_one(0, 1)
    stage_two(0, 0)
    wait_input(1)
    take_clip(part, ms.at[1])
    keep_cotangent = local(part, o_ct, out_sem.at[0, 1])
    keep_cotangent.start()
    keep_cotangent.wait()

    def keep_low(l, i):
        if i < 2:
            slots, slot, target = low_a, 0, lambda j: o_wa.at[j, l, i]
        else:
            slots, slot, target = low_m, i % 2, lambda j: o_wm.at[j, l, i - 2]
        sems = 0 if i < 2 else 1 + i % 2

        def copy(j):
            return local(slots.at[slot, j], target(j), low_sem.at[sems, j])

        def drain():
            for j in range(2):
                copy(j).wait()

        if i in (1, 4, 5):
            drain()
        else:
            when(l > 0)(drain)
        for j in range(2):
            if i < 2:
                slots[slot, j] = ga[j, l, i].reshape(BLOCK, WIDTH).astype(bf16)
            else:
                slots[slot, j] = gm[j, l, i - 2].reshape(WIDTH, BLOCK).astype(bf16)
            copy(j).start()
        return slots.at[slot]

    def swap(slot):
        copy = remote(part, other.at[slot], swap_sem.at[slot], swap_sem.at[2 + slot], p.partner)
        copy.start()
        copy.wait()

    def out_copies(l):
        return [
            local(hs.at[l], o_h.at[l], out_sem.at[0, l]),
            local(ms.at[l], o_m.at[l], out_sem.at[1, l]),
            local(n1s.at[l], o_n1.at[l], out_sem.at[2, l]),
            local(n2s.at[l], o_n2.at[l], out_sem.at[3, l]),
            local(qks.at[l], o_qk.at[l], out_sem.at[4, l]),
            local(vs.at[l], o_v.at[l], out_sem.at[5, l]),
            local(as_.at[l], o_a.at[l], out_sem.at[6, l]),
        ]

    def mid_copies(l, i):
        k = i - 2
        return [
            local(us.at[:, k], o_u.at[l, :, k], mid_sem.at[0, k]),
            local(cs.at[:, k], o_c.at[l, :, k], mid_sem.at[1, k]),
        ]

    def layer(l, carry):
        params = vec[l]

        tick(l, 0)
        scaled, _ = normalize_parts(hs[l])
        n1s[l] = (scaled * params[0:1] + params[1:2]).astype(bf16)
        weights = keep_low(l, 0)
        for j in range(2):
            both = contract_last(n1s[l], weights[j])
            shift = jnp.concatenate([row_of(hb.at[j, l, 0], range(HEADS_HERE)), jnp.zeros((1, 192), f32)], axis=-1)
            qks[l, j] = (both + shift).astype(bf16)

        tick(l, 1)
        weights = keep_low(l, 1)
        keep = lax.broadcasted_iota(jnp.int32, (128, ROWS), 1) < FRAMES
        for j in range(2):
            vs[l, j] = (
                contract_last(n1s[l], weights[j, 0:192]) + row_of(hb.at[j, l, 1], range(HEADS_HERE))
            ).astype(bf16)

            def rows_of(r, carry, j=j):
                rows = pl.ds(pl.multiple_of(r * 128, 128), 128)
                heads = []
                for h in range(HEADS_HERE):
                    cols = slice(HEAD_DIM * h, HEAD_DIM * (h + 1))
                    k_cols = slice(192 + HEAD_DIM * h, 192 + HEAD_DIM * (h + 1))
                    scores = contract_last(qks[l, j, rows, cols], qks[l, j, :, k_cols]) * score_scale
                    scores = jnp.where(keep, scores, -1e30)
                    weight = jnp.exp(scores - jnp.max(scores, axis=-1, keepdims=True))
                    weight = weight * (1.0 / jnp.sum(weight, axis=-1, keepdims=True))
                    heads.append(product(weight.astype(bf16), vs[l, j, :, cols]))
                as_[l, j, rows, :] = jnp.concatenate(heads, axis=-1).astype(bf16)
                return carry

            lax.fori_loop(0, ROWS // 128, rows_of, 0)
        part[...] = product(as_[l, 0], weights[0, 192:384])
        part[...] += product(as_[l, 1], weights[1, 192:384])
        swap(0)
        ms[l] = hs[l] + (part[...] + other[0]) + params[4:5]
        scaled, _ = normalize_parts(ms[l])
        n2s[l] = (scaled * params[2:3] + params[3:4]).astype(bf16)
        for copy in out_copies(l):
            copy.start()

        for i in (2, 3):
            tick(l, i)
            weights = keep_low(l, i)

            @when(l > 0)
            def _(i=i):
                for copy in mid_copies(l - 1, i):
                    copy.wait()

            for j in range(2):
                shift = row_of(ub.at[j, l], range(6 * (i - 2), 6 * (i - 1)))
                before = product(n2s[l], weights[j]) + shift
                us[j, i - 2] = before
                cs[j, i - 2] = gelu(before).astype(bf16)
            for copy in mid_copies(l, i):
                copy.start()

        for i in (4, 5):
            tick(l, i)
            weights = keep_low(l, i)

            @when(l < LAYERS - 1)
            def _(i=i, weights=weights):
                for j in range(2):
                    term = contract_last(cs[j, i - 4], weights[j])
                    if i == 4 and j == 0:
                        part[...] = term
                    else:
                        part[...] += term

        @when(l < LAYERS - 1)
        def _():
            swap(1)
            hs[l + 1] = ms[l] + (part[...] + other[1]) + params[5:6]

        return carry

    lax.fori_loop(0, LAYERS, layer, 0)

    last = LAYERS - 1
    for i in (2, 3):
        for copy in mid_copies(last, i):
            copy.wait()
    for l in range(LAYERS):
        for copy in out_copies(l):
            copy.wait()
    for j in range(2):
        local(low_a.at[0, j], o_wa.at[j, last, 1], low_sem.at[0, j]).wait()
        for slot in range(2):
            local(low_m.at[slot, j], o_wm.at[j, last, 2 + slot], low_sem.at[1 + slot, j]).wait()
    bias_drain()

    def drain(u, carry):
        l = u // UNITS
        for j in range(2):

            @when((level < 3) if j == 0 else ((level == 1) | (level == 2)))
            def _(j=j):
                z_copy(gm.at[j, l, 0, p.q], l, 2, j, p.above, sz.at[u, j]).wait_send()

            @when(level != j)
            def _(j=j):
                whole, half = gm.at[j, l, 0, p.q], gm.at[j, l, 0, p.q, 0]
                remote(whole, whole, sx.at[u, j], rx.at[u, j], p.xn).wait_send()
                remote(whole, whole, sy.at[u, j], ry.at[u, j], p.yn).wait_send()
                remote(half, half, sxd.at[u, j], rxd.at[u, j], p.xn).wait_send()
                remote(half, half, syd.at[u, j], ryd.at[u, j], p.yn).wait_send()

        @when(level == 1)
        def _():
            z_copy(gm.at[1, l, 0, p.q], l, 2, 1, p.below, szd.at[u]).wait_send()

        return carry

    lax.fori_loop(0, TOTAL, drain, 0)


def run_forward(frames, cotangent, wa, wm, head_bias, up_bias, vectors):
    def hbm(shape, kind):
        return jax.ShapeDtypeStruct(shape, kind)

    dma = pltpu.SemaphoreType.DMA
    per_unit = dma((TOTAL, 2))
    return pl.pallas_call(
        forward_kernel,
        out_shape=(
            hbm((ROWS, WIDTH), f32),
            hbm((LAYERS, ROWS, WIDTH), f32),
            hbm((LAYERS, ROWS, WIDTH), f32),
            hbm((LAYERS, ROWS, WIDTH), bf16),
            hbm((LAYERS, ROWS, WIDTH), bf16),
            hbm((LAYERS, 2, ROWS, BLOCK), bf16),
            hbm((LAYERS, 2, ROWS, 192), bf16),
            hbm((LAYERS, 2, ROWS, 192), bf16),
            hbm((LAYERS, 2, 2, ROWS, BLOCK), f32),
            hbm((LAYERS, 2, 2, ROWS, BLOCK), bf16),
            hbm((2, LAYERS, 2, BLOCK, WIDTH), bf16),
            hbm((2, LAYERS, 4, WIDTH, BLOCK), bf16),
        ),
        in_specs=[ANY, ANY, ANY, ANY, ANY, ANY, VMEM],
        out_specs=(ANY,) * 12,
        scratch_shapes=[
            pltpu.VMEM((2, LAYERS, 2, 2, 4, 2, 24, WIDTH), f32),
            pltpu.VMEM((2, LAYERS, 4, 4, 2, 96, BLOCK), f32),
            pltpu.VMEM((2, *head_bias.shape), f32),
            pltpu.VMEM((2, *up_bias.shape), f32),
            pltpu.VMEM((LAYERS, ROWS, WIDTH), f32),
            pltpu.VMEM((LAYERS, ROWS, WIDTH), f32),
            pltpu.VMEM((LAYERS, ROWS, WIDTH), bf16),
            pltpu.VMEM((LAYERS, ROWS, WIDTH), bf16),
            pltpu.VMEM((LAYERS, 2, ROWS, BLOCK), bf16),
            pltpu.VMEM((LAYERS, 2, ROWS, 192), bf16),
            pltpu.VMEM((LAYERS, 2, ROWS, 192), bf16),
            pltpu.VMEM((2, 2, ROWS, BLOCK), f32),
            pltpu.VMEM((2, 2, ROWS, BLOCK), bf16),
            pltpu.VMEM((1, 2, BLOCK, WIDTH), bf16),
            pltpu.VMEM((2, 2, WIDTH, BLOCK), bf16),
            pltpu.VMEM((ROWS, WIDTH), f32),
            pltpu.VMEM((2, ROWS, WIDTH), f32),
            per_unit,
            per_unit,
            dma((TOTAL,)),
            per_unit,
            per_unit,
            per_unit,
            per_unit,
            per_unit,
            per_unit,
            per_unit,
            per_unit,
            dma((TOTAL,)),
            dma((6,)),
            dma((2,)),
            dma((2, 3)),
            dma((2, 2)),
            dma((4,)),
            dma((3, 2)),
            dma((2, 2)),
            dma((7, LAYERS)),
        ],
        compiler_params=pltpu.CompilerParams(
            collective_id=0, has_side_effects=True, vmem_limit_bytes=63 << 20
        ),
        name="gather_forward",
    )(frames, cotangent, wa, wm, head_bias, up_bias, vectors)


def backward_kernel(
    i_ct,
    i_h,
    i_m,
    i_n1,
    i_n2,
    i_qk,
    i_v,
    i_a,
    i_u,
    i_c,
    i_wa,
    i_wm,
    vec,
    o_fin,
    o_act,
    o_small,
    o_src,
    o_grads,
    held,
    x1,
    y1,
    x2,
    y2,
    own,
    zin,
    zup,
    stage,
    grad,
    part,
    other,
    h_in,
    m_in,
    n1,
    n2,
    qk,
    v,
    a,
    u_in,
    c_in,
    wa,
    wm,
    low,
    dqk,
    dv,
    small,
    small_in,
    sx1,
    rx1,
    sy1,
    ry1,
    sx2,
    rx2,
    sy2,
    ry2,
    szd,
    rzd,
    szu,
    rzu,
    sfin,
    rfin,
    lfin,
    act_send,
    act_recv,
    act_sem,
    load_sem,
    unit_sem,
    stage_sem,
    held_sem,
    swap_sem,
    small_send,
    small_recv,
    once_sem,
):
    p = find_place()
    greet(p)
    level = p.level
    when = pl.when

    chunks = ROWS // CHUNK
    n_chunks = 3 * chunks
    slot_of = (p.c, 1 - p.c)

    def act_part(ref, k):
        return ref.at[pl.ds(pl.multiple_of(lax.rem(k, chunks) * CHUNK, CHUNK), CHUNK)]

    def act_own(k):
        return act_part(o_src.at[k // chunks - 1], k)

    def act_there(j, k):
        return act_part(o_act.at[k // chunks, slot_of[j]], k)

    def act_copy(src, j, k, m, device):
        return remote(src, act_there(j, k), act_send.at[k, m], act_recv.at[k, j], device)

    def act_step(s):
        def between(k):
            return (k >= 0) & (k < n_chunks)

        def set_out(src):
            @when(level == 0)
            def _():
                act_copy(src, 0, s, 0, p.above).start()

            @when(level == 1)
            def _():
                act_copy(src, 1, s, 1, p.above).start()
                act_copy(src, 1, s, 2, p.below).start()

        when(between(s) & (s < chunks))(lambda: set_out(act_part(i_h.at[1], s)))
        when(between(s) & (s >= chunks))(lambda: set_out(act_own(s)))

        @when(between(s - 1) & (level == 1))
        def _():
            k = s - 1
            act_copy(act_there(0, k), 0, k, 0, p.above).wait_recv()
            act_copy(act_there(0, k), 0, k, 0, p.above).start()

        @when(between(s - 2) & (level == 2))
        def _():
            k = s - 2
            for j in (1, 0):
                act_copy(act_there(j, k), j, k, j, p.above).wait_recv()
                act_copy(act_there(j, k), j, k, j, p.above).start()

    def act_drain(k):
        @when(level < 3)
        def _():
            act_copy(act_there(0, k), 0, k, 0, p.above).wait_send()

        @when((level == 1) | (level == 2))
        def _():
            act_copy(act_there(1, k), 1, k, 1, p.above).wait_send()

        @when(level == 1)
        def _():
            act_copy(act_there(1, k), 1, k, 2, p.below).wait_send()

        @when(level == 3)
        def _():
            act_copy(act_there(0, k), 0, k, 0, p.above).wait_recv()

        @when((level == 0) | (level == 3))
        def _():
            act_copy(act_there(1, k), 1, k, 1, p.above).wait_recv()

    def act_local(src, n, method):
        for j in range(2):

            @when(level == j)
            def _(j=j):
                getattr(local(src, o_act.at[n, slot_of[j]], act_sem.at[n]), method)()

    def x1_copy(w):
        return remote(held.at[w, :, :, 1 - p.x, 0], x1.at[w], sx1.at[w], rx1.at[w], p.xn)

    def y1_copy(w):
        return remote(held.at[w, :, 1 - p.y, :, 1], y1.at[w], sy1.at[w], ry1.at[w], p.yn)

    def x2_copy(w):
        return remote(held.at[w, :, p.y, 1 - p.x, 1], x2.at[w], sx2.at[w], rx2.at[w], p.xn)

    def y2_copy(w):
        return remote(held.at[w, :, 1 - p.y, p.x, 0], y2.at[w], sy2.at[w], ry2.at[w], p.yn)

    def down_copy(u, j):
        return remote(own.at[u, j], zin.at[u, j], szd.at[u, j], rzd.at[u, j], p.below)

    def up_copy(u):
        return remote(own.at[u, 1], zup.at[u], szu.at[u], rzu.at[u], p.above)

    def fin_copy(u, j):
        return remote(own.at[u, j, 1 - p.c], o_fin.at[u], sfin.at[u], rfin.at[u], p.partner)

    def fin_local(u, j):
        return local(own.at[u, j, p.c], o_fin.at[u], lfin.at[u])

    def sent(w):
        x1_copy(w).wait_send()
        y1_copy(w).wait_send()
        x2_copy(w).wait_send()
        y2_copy(w).wait_send()

    def stage_one(u):
        w = lax.rem(u, SLOTS)
        when(u >= SLOTS)(lambda: sent(w))
        load = local(o_grads.at[u], held.at[w], held_sem.at[0])
        load.start()
        load.wait()
        x1_copy(w).start()
        y1_copy(w).start()

    def stage_two(u):
        w = lax.rem(u, SLOTS)
        x1_copy(w).wait_recv()
        held[w, :, 1 - p.y, p.x, 0] += x1[w, :, 1 - p.y]
        held[w, :, p.y, p.x, 0] += x1[w, :, p.y]
        y1_copy(w).wait_recv()
        held[w, :, p.y, 1 - p.x, 1] += y1[w, :, 1 - p.x]
        held[w, :, p.y, p.x, 1] += y1[w, :, p.x]
        y2_copy(w).start()
        x2_copy(w).start()

    def stage_three(u):
        w = lax.rem(u, SLOTS)
        y2_copy(w).wait_recv()
        own[u, :, 0] = held[w, :, p.y, p.x, 0] + y2[w]
        x2_copy(w).wait_recv()
        own[u, :, 1] = held[w, :, p.y, p.x, 1] + x2[w]

        @when(level == 3)
        def _():
            down_copy(u, 0).start()
            down_copy(u, 1).start()

        @when(level == 0)
        def _():
            up_copy(u).start()

    def level_two(u):
        for j in range(2):
            down_copy(u, j).wait_recv()
            own[u, j] += zin[u, j]
            down_copy(u, j).start()

    def level_one(u):
        down_copy(u, 0).wait_recv()
        own[u, 0] += zin[u, 0]
        down_copy(u, 0).start()
        down_copy(u, 1).wait_recv()
        up_copy(u).wait_recv()
        own[u, 1] += zin[u, 1] + zup[u]
        fin_local(u, 1).start()
        fin_copy(u, 1).start()

    def level_zero(u):
        down_copy(u, 0).wait_recv()
        own[u, 0] += zin[u, 0]
        fin_local(u, 0).start()
        fin_copy(u, 0).start()

    def service(s):
        def unit(k, step, extra=True):
            when((k >= 0) & (k < TOTAL) & extra)(lambda: step(k))

        unit(s, stage_one)
        unit(s - 1, stage_two)
        unit(s - 2, stage_three)
        unit(s - 3, level_two, level == 2)
        unit(s - 4, level_one, level == 1)
        unit(s - 5, level_zero, level == 0)
        act_step(s)

    def loads(l):
        whole = (
            (i_c, c_in),
            (i_u, u_in),
            (i_n2, n2),
            (i_m, m_in),
            (i_a, a),
            (i_qk, qk),
            (i_v, v),
            (i_n1, n1),
            (i_h, h_in),
        )
        return [local(src.at[l], dst, load_sem.at[n]) for n, (src, dst) in enumerate(whole)]

    def load_a(l):
        return local(i_wa.at[:, l], wa, unit_sem.at[4])

    def load_m(l, i):
        return local(i_wm.at[:, l, i], wm.at[:, i], unit_sem.at[i])

    def swap(slot):
        copy = remote(part, other.at[slot], swap_sem.at[slot], swap_sem.at[2 + slot], p.partner)
        copy.start()
        copy.wait()

    def put(u, j, value):
        stage[j] = value.reshape(2, 2, 2, 96, BLOCK)
        local(stage.at[j], o_grads.at[u, j], stage_sem.at[j]).start()

    def put_done(u):
        for j in range(2):
            local(stage.at[j], o_grads.at[u, j], stage_sem.at[j]).wait()

    def small_row(l, row, value):
        small[l, row : row + 1] = value[:, :BLOCK]
        small[l, row + 1 : row + 2] = value[:, BLOCK:]

    def norm_back(slot, l, source, gain, first):
        def rows_of(r, carry):
            rows = pl.ds(pl.multiple_of(r * 128, 128), 128)
            upstream = part[rows] + other[slot, rows]
            scaled, inverse = normalize_parts(source[rows])
            lowered, gain_grad, shift_grad = normalize_back(upstream, scaled, inverse, gain)
            value = grad[rows] + lowered
            grad[rows] = value
            rounded = value.astype(bf16)
            low[rows] = rounded
            bias_grad = jnp.sum(rounded.astype(f32), axis=0)
            return (
                carry[0] + gain_grad.reshape(1, WIDTH),
                carry[1] + shift_grad.reshape(1, WIDTH),
                carry[2] + bias_grad.reshape(1, WIDTH),
            )

        zero = jnp.zeros((1, WIDTH), f32)
        sums = lax.fori_loop(0, ROWS // 128, rows_of, (zero, zero, zero))
        small_row(l, first, sums[0])
        small_row(l, first + 2, sums[1])
        return sums[2]

    keep = lax.broadcasted_iota(jnp.int32, (ROWS, ROWS), 1) < FRAMES

    def attention_back(j, carry):
        mixture_back = contract_last(low[...], wa[j, 1, 192:384]).astype(bf16)
        parts = ([], [], [])
        for h in range(HEADS_HERE):
            cols = slice(HEAD_DIM * h, HEAD_DIM * (h + 1))
            k_cols = slice(192 + HEAD_DIM * h, 192 + HEAD_DIM * (h + 1))
            qh, kh, vh, dah = qk[j, :, cols], qk[j, :, k_cols], v[j, :, cols], mixture_back[:, cols]
            scores = jnp.where(keep, contract_last(qh, kh) * score_scale, -1e30)
            weight = jnp.exp(scores - jnp.max(scores, axis=-1, keepdims=True))
            weight = weight * (1.0 / jnp.sum(weight, axis=-1, keepdims=True))
            prob_grad = contract_last(dah, vh)
            centre = jnp.sum(prob_grad * weight, axis=-1, keepdims=True)
            score_back = (weight * (prob_grad - centre)).astype(bf16)
            parts[0].append((product(score_back, kh) * score_scale).astype(bf16))
            parts[1].append((contract_rows(score_back, qh) * score_scale).astype(bf16))
            parts[2].append(contract_rows(weight.astype(bf16), dah).astype(bf16))
        dqk[j] = jnp.concatenate(parts[0] + parts[1], axis=-1)
        dv[j] = jnp.concatenate(parts[2], axis=-1)
        return carry

    local(i_ct, grad, once_sem.at[0]).start()
    small[...] = jnp.zeros_like(small)

    def layer(step, carry):
        l = LAYERS - 1 - step
        u0 = UNITS * step
        s0 = 4 * step
        params = vec[l]
        fetch = loads(l)
        for copy in fetch[:2]:
            copy.start()
        for i in (2, 3, 0, 1):
            load_m(l, i).start()
        for copy in fetch[2:]:
            copy.start()
        load_a(l).start()

        @when(step == 0)
        def _():
            local(i_ct, grad, once_sem.at[0]).wait()
            low[...] = grad[...].astype(bf16)
            small_row(l, 10, jnp.sum(low[...].astype(f32), axis=0, keepdims=True))

        fetch[0].wait()
        for i in (0, 1):
            for j in range(2):
                put(u0 + i, j, contract_rows(low[...], c_in[j, i]))
            put_done(u0 + i)
            if i == 0:
                service(s0)
            else:
                when(step == 0)(lambda: service(1))
        for i in range(2):
            load_m(l, 2 + i).wait()

        @when(step == 0)
        def _():
            for h in range(2):
                for j in range(2):
                    term = contract_last(c_in[j, h], wm[j, 2 + h])
                    if h == 0 and j == 0:
                        part[...] = term
                    else:
                        part[...] += term
            swap(1)
            fetch[3].wait()
            part[...] = m_in[...] + (part[...] + other[1]) + params[5:6]
            keep_top = local(part, o_src.at[0], once_sem.at[1])
            keep_top.start()
            act_local(part, 1, "start")
            keep_top.wait()
            act_local(part, 1, "wait")

        fetch[1].wait()
        fetch[2].wait()
        for i in (2, 3):
            h = i - 2
            load_m(l, h).wait()
            for j in range(2):
                back = (product(low[...], wm[j, 2 + h]) * gelu_slope(u_in[j, h])).astype(bf16)
                row = 14 + 2 * j + h
                small[l, row : row + 1] = jnp.sum(back.astype(f32), axis=0, keepdims=True)
                put(u0 + i, j, contract_rows(n2[...], back))
                term = contract_last(back, wm[j, h])
                if h == 0 and j == 0:
                    part[...] = term
                else:
                    part[...] += term
            put_done(u0 + i)
        service(s0 + 2 - step)
        swap(0)

        @when(step > 0)
        def _():
            fetch[3].wait()

        small_row(l, 8, norm_back(0, l, m_in, params[2:3], 4))

        for copy in fetch[4:]:
            copy.wait()
        load_a(l).wait()
        when(step == 0)(lambda: act_local(h_in, 0, "start"))
        lax.fori_loop(0, 2, attention_back, 0)
        service(s0 + 3 - step)
        for j in range(2):
            stage[j, :, :, :, :, 0:192] = contract_rows(n1[...], dv[j]).reshape(2, 2, 2, 96, 192)
            stage[j, :, :, :, :, 192:384] = contract_rows(low[...], a[j]).reshape(2, 2, 2, 96, 192)
            local(stage.at[j], o_grads.at[u0 + 4, j], stage_sem.at[j]).start()
        put_done(u0 + 4)
        for j in range(2):
            put(u0 + 5, j, contract_rows(n1[...], dqk[j]))
            sums = jnp.sum(dqk[j].astype(f32), axis=0, keepdims=True)
            small[l, 12 + j : 13 + j, 0:192] = sums[:, 0:192]
            small[l, 12 + j : 13 + j, 192:384] = jnp.sum(dv[j].astype(f32), axis=0, keepdims=True)
            term = product(dqk[j], wa[j, 0]) + product(dv[j], wa[j, 1, 0:192])
            if j == 0:
                part[...] = term
            else:
                part[...] += term
        put_done(u0 + 5)
        swap(1)
        down_sum = norm_back(1, l, h_in, params[0:1], 0)

        @when(l > 0)
        def _():
            small_row(l - 1, 10, down_sum)

        when(step == 0)(lambda: act_local(h_in, 0, "wait"))
        return carry

    lax.fori_loop(0, LAYERS, layer, 0)
    keep_grad = local(grad, o_src.at[1], once_sem.at[1])
    keep_grad.start()
    act_local(grad, 2, "start")
    keep_grad.wait()

    def small_copy(m, device):
        return remote(small, small_in.at[m], small_send.at[m], small_recv.at[m], device)

    def small_add(m, device):
        small_copy(m, device).wait()
        small[...] += small_in[m]

    first = STEPS_INSIDE

    def small_step(s):
        @when(s == first)
        def _():
            small_copy(0, p.xn).start()

        @when(s == first + 1)
        def _():
            small_add(0, p.xn)
            small_copy(1, p.yn).start()

        @when(s == first + 2)
        def _():
            small_add(1, p.yn)

            @when((level == 0) | (level == 2))
            def _():
                small_copy(2, p.above).start()

            @when((level == 1) | (level == 3))
            def _():
                small_copy(2, p.below).start()

        @when(s == first + 3)
        def _():
            small_add(2, p.above)

            @when(level == 1)
            def _():
                small_copy(3, p.above).start()

            @when(level == 2)
            def _():
                small_copy(3, p.below).start()

        @when(s == first + 4)
        def _():
            @when((level == 1) | (level == 2))
            def _():
                small_add(3, p.above)

            @when(level == 1)
            def _():
                small_copy(4, p.below).start()

            @when(level == 2)
            def _():
                small_copy(4, p.above).start()

        @when(s == first + 5)
        def _():
            @when((level == 0) | (level == 3))
            def _():
                small_copy(4, p.above).wait_recv()
                small[...] = small_in[4]

            small_copy(5, p.partner).start()
            local(small, o_small.at[0], once_sem.at[2]).start()

        @when(s == first + 6)
        def _():
            small_copy(5, p.partner).wait()
            local(small_in.at[5], o_small.at[1], once_sem.at[3]).start()

            @when((level == 1) | (level == 2))
            def _():
                small_copy(4, p.above).wait_send()

    def step_after(s, carry):
        small_step(s)
        service(s)
        return carry

    lax.fori_loop(first, TOTAL + 5, step_after, 0)

    for w in range(SLOTS):
        sent(w)

    def drain(u, carry):
        @when(level > 0)
        def _():
            down_copy(u, 0).wait_send()

        @when(level > 1)
        def _():
            down_copy(u, 1).wait_send()
            fin_copy(u, 0).wait_recv()

        @when(level == 0)
        def _():
            up_copy(u).wait_send()

        @when(level < 2)
        def _():
            fin_local(u, 0).wait()
            fin_copy(u, 0).wait_send()

        act_drain(u)
        return carry

    assert n_chunks == TOTAL
    lax.fori_loop(0, TOTAL, drain, 0)

    act_local(grad, 2, "wait")
    local(small, o_small.at[0], once_sem.at[2]).wait()
    local(small_in.at[5], o_small.at[1], once_sem.at[3]).wait()


STEPS_INSIDE = 4 + 3
SMALL = (LAYERS, 24, BLOCK)


def run_backward(saved, vectors):
    dma = pltpu.SemaphoreType.DMA
    slots = dma((SLOTS,))
    units = dma((TOTAL,))
    pair = dma((TOTAL, 2))
    return pl.pallas_call(
        backward_kernel,
        out_shape=(
            jax.ShapeDtypeStruct((TOTAL, 96, BLOCK), f32),
            jax.ShapeDtypeStruct((3, 2, ROWS, WIDTH), f32),
            jax.ShapeDtypeStruct((2, *SMALL), f32),
            jax.ShapeDtypeStruct((2, ROWS, WIDTH), f32),
            jax.ShapeDtypeStruct((TOTAL, 2, 2, 2, 2, 96, BLOCK), f32),
        ),
        in_specs=[ANY] * 12 + [VMEM],
        out_specs=(ANY,) * 5,
        scratch_shapes=[
            pltpu.VMEM((SLOTS, 2, 2, 2, 2, 96, BLOCK), f32),
            pltpu.VMEM((SLOTS, 2, 2, 96, BLOCK), f32),
            pltpu.VMEM((SLOTS, 2, 2, 96, BLOCK), f32),
            pltpu.VMEM((SLOTS, 2, 96, BLOCK), f32),
            pltpu.VMEM((SLOTS, 2, 96, BLOCK), f32),
            pltpu.VMEM((TOTAL, 2, 2, 96, BLOCK), f32),
            pltpu.VMEM((TOTAL, 2, 2, 96, BLOCK), f32),
            pltpu.VMEM((TOTAL, 2, 96, BLOCK), f32),
            pltpu.VMEM((2, 2, 2, 2, 96, BLOCK), f32),
            pltpu.VMEM((ROWS, WIDTH), f32),
            pltpu.VMEM((ROWS, WIDTH), f32),
            pltpu.VMEM((2, ROWS, WIDTH), f32),
            pltpu.VMEM((ROWS, WIDTH), f32),
            pltpu.VMEM((ROWS, WIDTH), f32),
            pltpu.VMEM((ROWS, WIDTH), bf16),
            pltpu.VMEM((ROWS, WIDTH), bf16),
            pltpu.VMEM((2, ROWS, BLOCK), bf16),
            pltpu.VMEM((2, ROWS, 192), bf16),
            pltpu.VMEM((2, ROWS, 192), bf16),
            pltpu.VMEM((2, 2, ROWS, BLOCK), f32),
            pltpu.VMEM((2, 2, ROWS, BLOCK), bf16),
            pltpu.VMEM((2, 2, BLOCK, WIDTH), bf16),
            pltpu.VMEM((2, 4, WIDTH, BLOCK), bf16),
            pltpu.VMEM((ROWS, WIDTH), bf16),
            pltpu.VMEM((2, ROWS, BLOCK), bf16),
            pltpu.VMEM((2, ROWS, 192), bf16),
            pltpu.VMEM(SMALL, f32),
            pltpu.VMEM((6, *SMALL), f32),
            slots,
            slots,
            slots,
            slots,
            slots,
            slots,
            slots,
            slots,
            pair,
            pair,
            units,
            units,
            units,
            units,
            units,
            dma((TOTAL, 3)),
            dma((TOTAL, 2)),
            dma((3,)),
            dma((9,)),
            dma((5,)),
            dma((2,)),
            dma((1,)),
            dma((4,)),
            dma((6,)),
            dma((6,)),
            dma((4,)),
        ],
        compiler_params=pltpu.CompilerParams(
            collective_id=1, has_side_effects=True, vmem_limit_bytes=63 << 20
        ),
        name="backward_reduce",
    )(*saved, vectors)


def per_device(
    frames,
    cotangent,
    w_attn,
    w_mlp,
    vectors,
    head_bias,
    up_bias,
    moment_attn,
    square_attn,
    moment_mlp,
    square_mlp,
    moment_vectors,
    square_vectors,
    moment_head,
    square_head,
    moment_up,
    square_up,
):
    dp = lax.axis_index("dp")
    t = lax.axis_index("tensor")
    core = dp % 2
    dp_size = lax.axis_size("dp")

    wa = jnp.swapaxes(w_attn, 2, 3).reshape(LAYERS, 4, 4, 2, 24, WIDTH)
    wm = w_mlp.reshape(LAYERS, 2, 4, 2, 96, 2 * BLOCK)
    saved = run_forward(frames, cotangent, wa, wm, head_bias, up_bias, vectors)
    fin, acts, small, _, _ = run_backward(saved, vectors)
    sections = jnp.concatenate([acts[:2, 0, :FRAMES], acts[:2, 1, :FRAMES]], axis=1)
    upstream = jnp.concatenate([acts[2, 0, :FRAMES], acts[2, 1, :FRAMES]], axis=0)

    if dp_size > GROUP:
        groups = [[i + GROUP * o for o in range(dp_size // GROUP)] for i in range(GROUP)]
        small = lax.psum(small, "dp", axis_index_groups=groups)
    vector_all = small[0, :, :12].reshape(LAYERS, 6, WIDTH)
    owner = t // 2
    here = jnp.where(owner == core, small[0], small[1])
    second = jnp.where(owner == 0, t % 2, 1 - t % 2)
    head_all = jnp.where(second == 0, here[:, 12], here[:, 13]).reshape(LAYERS, 2, HEADS_HERE, HEAD_DIM)
    up_all = jnp.where(second == 0, here[:, 14:16], here[:, 16:18]).reshape(LAYERS, 12, HEAD_DIM)

    def owned(param, dim):
        size = param.shape[dim] // dp_size
        return lax.dynamic_slice_in_dim(param, dp * size, size, dim)

    if dp_size > GROUP:
        rows = jnp.zeros((TOTAL, WIDTH, BLOCK), f32)
        rows = lax.dynamic_update_slice_in_dim(rows, fin, (dp % GROUP) * 96, 1)
        fin = lax.psum_scatter(rows, "dp", scatter_dimension=1, tiled=True)

    def unit(l, k):
        return fin[(LAYERS - 1 - l) * UNITS + k]

    attn_grad = jnp.stack(
        [
            jnp.stack([unit(l, 5)[:, :192], unit(l, 5)[:, 192:], unit(l, 4)[:, :192], unit(l, 4)[:, 192:]])
            for l in range(LAYERS)
        ]
    )
    mlp_grad = jnp.stack(
        [
            jnp.stack(
                [
                    jnp.concatenate([unit(l, 2), unit(l, 3)], axis=-1),
                    jnp.concatenate([unit(l, 0), unit(l, 1)], axis=-1),
                ]
            )
            for l in range(LAYERS)
        ]
    )
    attn = adamw_update(owned(w_attn, 2), attn_grad, moment_attn, square_attn, rate_matrix)
    mlp = adamw_update(owned(w_mlp, 2), mlp_grad, moment_mlp, square_mlp, rate_matrix)
    vector_new = adamw_update(
        owned(vectors, 2), owned(vector_all, 2), moment_vectors, square_vectors, rate_vector
    )
    head = adamw_update(owned(head_bias, 3), owned(head_all, 3), moment_head, square_head, rate_vector)
    upper = adamw_update(owned(up_bias, 2), owned(up_all, 2), moment_up, square_up, rate_vector)
    return (sections, upstream, *attn, *mlp, *vector_new, *head, *upper)


def solution(mesh):
    in_specs = (
        P("dp", None),
        P("dp", None),
        P(None, None, None, "tensor"),
        P(None, None, None, "tensor"),
        P(),
        P(None, None, "tensor", None),
        P(None, "tensor", None),
        P(None, None, "dp", "tensor"),
        P(None, None, "dp", "tensor"),
        P(None, None, "dp", "tensor"),
        P(None, None, "dp", "tensor"),
        P(None, None, "dp"),
        P(None, None, "dp"),
        P(None, None, "tensor", "dp"),
        P(None, None, "tensor", "dp"),
        P(None, "tensor", "dp"),
        P(None, "tensor", "dp"),
    )
    out_specs = (
        P(None, "dp", None),
        P("dp", None),
        P(None, None, "dp", "tensor"),
        P(None, None, "dp", "tensor"),
        P(None, None, "dp", "tensor"),
        P(None, None, "dp", "tensor"),
        P(None, None, "dp", "tensor"),
        P(None, None, "dp", "tensor"),
        P(None, None, "dp"),
        P(None, None, "dp"),
        P(None, None, "dp"),
        P(None, None, "tensor", "dp"),
        P(None, None, "tensor", "dp"),
        P(None, None, "tensor", "dp"),
        P(None, "tensor", "dp"),
        P(None, "tensor", "dp"),
        P(None, "tensor", "dp"),
    )
    return jax.shard_map(
        per_device, mesh=mesh, in_specs=in_specs, out_specs=out_specs, check_vma=False
    )
```

```python
import math
from types import SimpleNamespace

import jax
import jax.numpy as jnp
from jax import lax
from jax.experimental import pallas as pl
from jax.experimental.pallas import tpu as pltpu
from jax.sharding import PartitionSpec as P

HEAD_DIM = 64
FRAMES = 500
ROWS = 512
LAYERS = 2
STEP = 10
WIDTH = 768
BLOCK = 384
UNITS = 6
TOTAL = LAYERS * UNITS
GROUP = 8
HEADS_HERE = 3
SLOTS = 3
LEAD = 2
SOURCE_LEAD = 5
SPAN = 504
SECOND = 496
CHUNK = 128

ln_eps = 1e-05
beta_one = 0.9
beta_two = 0.999
adam_eps = 1e-08
decay_rate = 0.01
rate_matrix = 0.05
rate_vector = 0.2
score_scale = 1.0 / math.sqrt(HEAD_DIM)
MESH = pl.DeviceIdType.MESH
f32 = jnp.float32
bf16 = jnp.bfloat16
ANY = pl.BlockSpec(memory_space=pl.ANY)
VMEM = pl.BlockSpec(memory_space=pltpu.VMEM)


def product(left, right):
    return jnp.dot(left, right, preferred_element_type=f32)


def contract_last(left, right):
    return lax.dot_general(left, right, (((1,), (1,)), ((), ())), preferred_element_type=f32)


def contract_rows(left, right):
    return lax.dot_general(left, right, (((0,), (0,)), ((), ())), preferred_element_type=f32)


def normalize_parts(inputs):
    centre = jnp.mean(inputs, axis=-1, keepdims=True)
    centred = inputs - centre
    inverse = lax.rsqrt(jnp.mean(centred * centred, axis=-1, keepdims=True) + ln_eps)
    return centred * inverse, inverse


def normalize_back(upstream, scaled, inverse, gain):
    gain_grad = jnp.sum(upstream * scaled, axis=0)
    shift_grad = jnp.sum(upstream, axis=0)
    inner_grad = upstream * gain
    lowered = inverse * (
        inner_grad
        - jnp.mean(inner_grad, axis=-1, keepdims=True)
        - scaled * jnp.mean(inner_grad * scaled, axis=-1, keepdims=True)
    )
    return (lowered, gain_grad, shift_grad)


def gelu(before):
    return 0.5 * before * (1.0 + lax.erf(before * (1.0 / math.sqrt(2.0))))


def gelu_slope(before):
    return 0.5 * (1.0 + lax.erf(before * (1.0 / math.sqrt(2.0)))) + before * jnp.exp(
        -0.5 * before * before
    ) * (1.0 / math.sqrt(2.0 * math.pi))


def adamw_update(param, gradient, first, second, rate):
    first_new = beta_one * first + (1.0 - beta_one) * gradient
    second_new = beta_two * second + (1.0 - beta_two) * gradient * gradient
    ratio = (
        first_new
        / (1.0 - beta_one**STEP)
        / (jnp.sqrt(second_new / (1.0 - beta_two**STEP)) + adam_eps)
    )
    return (param - rate * (ratio + decay_rate * param), first_new, second_new)


def find_place():
    dp = lax.axis_index("dp")
    t = lax.axis_index("tensor")
    i = lax.rem(dp, GROUP)
    base = dp - i
    c = lax.rem(i, 2)
    x = lax.rem(i // 2, 2)
    y = i // 4
    up = 1 - 2 * c
    level = c * (3 - t) + (1 - c) * t

    def at(cc, xx, yy):
        return base + 4 * yy + 2 * xx + cc

    return SimpleNamespace(
        t=t,
        c=c,
        x=x,
        y=y,
        q=2 * y + x,
        qx=2 * y + 1 - x,
        qy=2 * (1 - y) + x,
        qd=2 * (1 - y) + 1 - x,
        level=level,
        partner=(at(1 - c, x, y), t),
        xn=(at(c, 1 - x, y), t),
        yn=(at(c, x, 1 - y), t),
        above=(dp, t + up),
        below=(dp, t - up),
    )


def greet(p):
    barrier = pltpu.get_barrier_semaphore()

    def signal(device):
        pl.semaphore_signal(barrier, inc=1, device_id=device, device_id_type=MESH)

    signal(p.partner)
    signal(p.xn)
    signal(p.yn)

    @pl.when(p.level < 3)
    def _():
        signal(p.above)

    @pl.when(p.level > 0)
    def _():
        signal(p.below)

    inner = (p.level > 0) & (p.level < 3)

    @pl.when(inner)
    def _():
        pl.semaphore_wait(barrier, 5)

    @pl.when(jnp.logical_not(inner))
    def _():
        pl.semaphore_wait(barrier, 4)


def remote(src, dst, send_sem, recv_sem, device):
    return pltpu.make_async_remote_copy(
        src_ref=src,
        dst_ref=dst,
        send_sem=send_sem,
        recv_sem=recv_sem,
        device_id=device,
        device_id_type=MESH,
    )


def local(src, dst, sem):
    return pltpu.make_async_copy(src, dst, sem)


def forward_kernel(
    frames,
    cotangent,
    wa,
    wm,
    head_bias,
    up_bias,
    vec,
    o_ct,
    o_h,
    o_m,
    o_n1,
    o_n2,
    o_qk,
    o_v,
    o_a,
    o_u,
    o_c,
    o_wa,
    o_wm,
    o_first,
    ga,
    gm,
    hb,
    ub,
    hs,
    ms,
    n1s,
    n2s,
    qks,
    vs,
    as_,
    us,
    cs,
    low_a,
    low_m,
    low_ct,
    part,
    other,
    rz,
    sz,
    szd,
    rx,
    sx,
    ry,
    sy,
    rxd,
    sxd,
    ryd,
    syd,
    native,
    rc,
    sc,
    scd,
    first_sem,
    bias_local,
    bias_send,
    bias_recv,
    swap_sem,
    low_sem,
    mid_sem,
    out_sem,
    grad_sem,
):
    p = find_place()
    greet(p)
    level = p.level
    when = pl.when

    def quarter(ref, i, q, h=None):
        lead = (slice(None), q) if i < 2 else (q,)
        return ref.at[lead if h is None else (*lead, h)]

    def block(l, i):
        if i < 2:
            return wa.at[l, pl.ds(2 * i, 2)]
        return wm.at[l, (i - 2) // 2, :, :, :, pl.ds(BLOCK * (i % 2), BLOCK)]

    def block_quarter(l, i):
        if i < 2:
            return wa.at[l, pl.ds(2 * i, 2), p.q]
        return wm.at[l, (i - 2) // 2, p.q, :, :, pl.ds(BLOCK * (i % 2), BLOCK)]

    def held(l, i, j):
        return ga.at[j, l, i] if i < 2 else gm.at[j, l, i - 2]

    def z_copy(src, l, i, j, device, send_sem):
        return remote(src, quarter(held(l, i, j), i, p.q), send_sem, rz.at[UNITS * l + i, j], device)

    def plane_copy(l, i, j, q, h, send_sem, recv_sem, device):
        here = quarter(held(l, i, j), i, q, h)
        u = UNITS * l + i
        return remote(here, here, send_sem.at[u, j], recv_sem.at[u, j], device)

    def x_copy(l, i, j, q):
        return plane_copy(l, i, j, q, None, sx, rx, p.xn)

    def y_copy(l, i, j, q):
        return plane_copy(l, i, j, q, None, sy, ry, p.yn)

    def xd_copy(l, i, j, q):
        return plane_copy(l, i, j, q, 1, sxd, rxd, p.xn)

    def yd_copy(l, i, j, q):
        return plane_copy(l, i, j, q, 0, syd, ryd, p.yn)

    def source(l, i):
        u = UNITS * l + i

        @when(level == 0)
        def _():
            z_copy(block_quarter(l, i), l, i, 0, p.above, sz.at[u, 0]).start()
            local(block(l, i), held(l, i, 0), native.at[u]).start()

        @when(level == 1)
        def _():
            z_copy(block_quarter(l, i), l, i, 1, p.above, sz.at[u, 1]).start()
            z_copy(block_quarter(l, i), l, i, 1, p.below, szd.at[u]).start()
            local(block(l, i), held(l, i, 1), native.at[u]).start()

    def stage_one(l, i):
        u = UNITS * l + i
        for j in range(2):

            @when(level != j)
            def _(j=j):
                here = quarter(held(l, i, j), i, p.q)
                z_copy(here, l, i, j, p.above, sz.at[u, j]).wait_recv()

                @when((level == 2) | ((level == 1) if j == 0 else (level == 2)))
                def _():
                    z_copy(here, l, i, j, p.above, sz.at[u, j]).start()

                x_copy(l, i, j, p.q).start()
                y_copy(l, i, j, p.q).start()

    def stage_two(l, i):
        for j in range(2):

            @when(level != j)
            def _(j=j):
                x_copy(l, i, j, p.qx).wait_recv()
                yd_copy(l, i, j, p.qx).start()
                y_copy(l, i, j, p.qy).wait_recv()
                xd_copy(l, i, j, p.qy).start()

    def finish(l, i):
        u = UNITS * l + i
        for j in range(2):

            @when(level != j)
            def _(j=j):
                yd_copy(l, i, j, p.qd).wait_recv()
                xd_copy(l, i, j, p.qd).wait_recv()

            @when(level == j)
            def _(j=j):
                local(block(l, i), held(l, i, j), native.at[u]).wait()

    last = LAYERS - 1
    alone = UNITS - 1

    def chunk_copy(src, q, j, device, send_sem):
        return remote(src, held(last, alone, j).at[q], send_sem, rc.at[q, j], device)

    def chunk_source(q):
        here = wm.at[last, 1, q, :, :, pl.ds(BLOCK, BLOCK)]

        @when(level == 0)
        def _():
            chunk_copy(here, q, 0, p.above, sc.at[q, 0]).start()

        @when(level == 1)
        def _():
            chunk_copy(here, q, 1, p.above, sc.at[q, 1]).start()
            chunk_copy(here, q, 1, p.below, scd.at[q]).start()

    def chunk_pass(q, at, j):
        @when(level == at)
        def _():
            here = held(last, alone, j).at[q]
            chunk_copy(here, q, j, p.above, sc.at[q, j]).wait_recv()
            chunk_copy(here, q, j, p.above, sc.at[q, j]).start()

    def chunk_native(method):
        for j in range(2):

            @when(level == j)
            def _(j=j):
                getattr(local(block(last, alone), held(last, alone, j), native.at[TOTAL - 1]), method)()

    def chunk_finish():
        for q in range(4):
            here = held(last, alone, 0).at[q]

            @when((level == 3))
            def _(q=q, here=here):
                chunk_copy(here, q, 0, p.above, sc.at[q, 0]).wait_recv()

            @when((level == 3) | (level == 0))
            def _(q=q, here=here):
                chunk_copy(here, q, 1, p.above, sc.at[q, 1]).wait_recv()

        chunk_native("wait")

    def chunk_drain():
        for q in range(4):
            here = held(last, alone, 0).at[q]

            @when(level < 3)
            def _(q=q, here=here):
                chunk_copy(here, q, 0, p.above, sc.at[q, 0]).wait_send()

            @when((level == 1) | (level == 2))
            def _(q=q, here=here):
                chunk_copy(here, q, 1, p.above, sc.at[q, 1]).wait_send()

            @when(level == 1)
            def _(q=q, here=here):
                chunk_copy(here, q, 1, p.below, scd.at[q]).wait_send()

    def chunk_step(l, i):
        def at_chunk(q, step):
            when((q >= 0) & (q < 4))(lambda: step(q))

        half = l * (UNITS // 2) + i // 2
        if i % 2 == 0:
            at_chunk(half, chunk_source)

            def on(q):
                chunk_pass(q, 2, 1)
                chunk_pass(q, 2, 0)

            at_chunk(half - 1, on)
        else:
            at_chunk(half, lambda q: chunk_pass(q, 1, 0))

    def ahead(step, l, i, by):
        k = i + by
        there = l + k // UNITS
        if k % UNITS == alone:
            when(there < last)(lambda: step(there, alone))
        elif k < UNITS:
            step(l, k)
        else:
            when(there < LAYERS)(lambda: step(there, k % UNITS))

    def serve(l, k):
        ahead(source, l, k, SOURCE_LEAD)
        ahead(stage_one, l, k, LEAD)
        ahead(stage_two, l, k, LEAD - 1)

    def tick(l, i):
        if i < 2:
            serve(l, i)
        elif i < UNITS - 1:
            serve(l, i + 1)
        chunk_step(l, i)
        if i == alone:
            when(l < last)(lambda: finish(l, i))
            when(l == last)(chunk_finish)
        else:
            finish(l, i)

    mine = (p.t // 2) == p.c
    clip = lax.rem(p.t, 2)
    span = pl.ds(pl.multiple_of(clip * SECOND, 8), SPAN)
    inputs = (
        (frames.at[span], part.at[pl.ds(0, SPAN)]),
        (cotangent.at[span], ms.at[1, pl.ds(0, SPAN)]),
    )

    def input_copies(k):
        src, dst = inputs[k]
        return (
            local(src, dst, first_sem.at[k]),
            remote(src, dst, first_sem.at[2 + k], first_sem.at[4 + k], p.partner),
        )

    def wait_input(k):
        here, there = input_copies(k)

        @when(mine)
        def _():
            here.wait()
            there.wait_send()

        @when(jnp.logical_not(mine))
        def _():
            there.wait_recv()

    def take_clip(target, raw):
        @when(clip == 0)
        def _():
            target[0:FRAMES] = raw[0:FRAMES]

        @when(clip == 1)
        def _():
            target[0:FRAMES] = raw[FRAMES - SECOND : SPAN]

        target[FRAMES:ROWS] = jnp.zeros((ROWS - FRAMES, WIDTH), f32)

    kept_biases = ((head_bias, hb), (up_bias, ub))

    def bias_copy(src, n, j, m, device):
        return remote(src, kept_biases[n][1].at[j], bias_send.at[n, m], bias_recv.at[n, j], device)

    def bias_source():
        for n, (src, dst) in enumerate(kept_biases):

            @when(level == 0)
            def _(n=n, src=src, dst=dst):
                local(src, dst.at[0], bias_local.at[n]).start()
                bias_copy(src, n, 0, 0, p.above).start()

            @when(level == 1)
            def _(n=n, src=src, dst=dst):
                local(src, dst.at[1], bias_local.at[n]).start()
                bias_copy(src, n, 1, 1, p.above).start()
                bias_copy(src, n, 1, 2, p.below).start()

    def bias_pass():
        for n, (src, dst) in enumerate(kept_biases):

            @when(level != 0)
            def _(n=n, src=src):
                bias_copy(src, n, 0, 0, p.above).wait_recv()

            @when((level == 1) | (level == 2))
            def _(n=n, dst=dst):
                bias_copy(dst.at[0], n, 0, 0, p.above).start()

            @when(level != 1)
            def _(n=n, src=src):
                bias_copy(src, n, 1, 1, p.above).wait_recv()

            @when(level == 2)
            def _(n=n, dst=dst):
                bias_copy(dst.at[1], n, 1, 1, p.above).start()

            @when(level < 2)
            def _(n=n, src=src, dst=dst):
                local(src, dst.at[0], bias_local.at[n]).wait()

    def bias_drain():
        for n, (src, dst) in enumerate(kept_biases):

            @when(level < 3)
            def _(n=n, src=src):
                bias_copy(src, n, 0, 0, p.above).wait_send()

            @when((level == 1) | (level == 2))
            def _(n=n, src=src):
                bias_copy(src, n, 1, 1, p.above).wait_send()

            @when(level == 1)
            def _(n=n, src=src):
                bias_copy(src, n, 1, 2, p.below).wait_send()

    def row_of(ref, rows):
        return jnp.concatenate([ref[r : r + 1, :] for r in rows], axis=-1)

    @when(mine)
    def _():
        for copy in input_copies(0):
            copy.start()

    bias_source()
    for i in range(SOURCE_LEAD):
        source(0, i)

    @when(mine)
    def _():
        for copy in input_copies(1):
            copy.start()

    bias_pass()
    chunk_native("start")
    stage_one(0, 0)
    wait_input(0)
    take_clip(hs.at[0], part)
    for i in range(1, LEAD):
        stage_one(0, i)
        stage_two(0, i - 1)
    wait_input(1)
    take_clip(part, ms.at[1])
    keep_cotangent = local(part, o_ct, out_sem.at[0, 1])
    keep_cotangent.start()
    low_ct[...] = part[...].astype(bf16)
    keep_cotangent.wait()

    def keep_low(l, i):
        if i < 2:
            slots, slot, target = low_a, 0, lambda j: o_wa.at[j, l, i]
        else:
            slots, slot, target = low_m, i % 2, lambda j: o_wm.at[j, l, i - 2]
        sems = 0 if i < 2 else 1 + i % 2

        def copy(j):
            return local(slots.at[slot, j], target(j), low_sem.at[sems, j])

        def drain():
            for j in range(2):
                copy(j).wait()

        if i in (1, 4, 5):
            drain()
        else:
            when(l > 0)(drain)
        for j in range(2):
            if i < 2:
                slots[slot, j] = ga[j, l, i].reshape(BLOCK, WIDTH).astype(bf16)
            else:
                slots[slot, j] = gm[j, l, i - 2].reshape(WIDTH, BLOCK).astype(bf16)
            copy(j).start()
        return slots.at[slot]

    def swap(slot):
        copy = remote(part, other.at[slot], swap_sem.at[slot], swap_sem.at[2 + slot], p.partner)
        copy.start()
        copy.wait()

    def out_copies(l):
        return [
            local(hs.at[l], o_h.at[l], out_sem.at[0, l]),
            local(ms.at[l], o_m.at[l], out_sem.at[1, l]),
            local(n1s.at[l], o_n1.at[l], out_sem.at[2, l]),
            local(n2s.at[l], o_n2.at[l], out_sem.at[3, l]),
            local(qks.at[l], o_qk.at[l], out_sem.at[4, l]),
            local(vs.at[l], o_v.at[l], out_sem.at[5, l]),
            local(as_.at[l], o_a.at[l], out_sem.at[6, l]),
        ]

    def mid_copies(l, i):
        k = i - 2
        return [
            local(us.at[:, k], o_u.at[l, :, k], mid_sem.at[0, k]),
            local(cs.at[:, k], o_c.at[l, :, k], mid_sem.at[1, k]),
        ]

    def drain(u, carry):
        l = u // UNITS
        for j in range(2):

            @when((level < 3) if j == 0 else ((level == 1) | (level == 2)))
            def _(j=j):
                z_copy(gm.at[j, l, 0, p.q], l, 2, j, p.above, sz.at[u, j]).wait_send()

            @when(level != j)
            def _(j=j):
                whole, half = gm.at[j, l, 0, p.q], gm.at[j, l, 0, p.q, 0]
                remote(whole, whole, sx.at[u, j], rx.at[u, j], p.xn).wait_send()
                remote(whole, whole, sy.at[u, j], ry.at[u, j], p.yn).wait_send()
                remote(half, half, sxd.at[u, j], rxd.at[u, j], p.xn).wait_send()
                remote(half, half, syd.at[u, j], ryd.at[u, j], p.yn).wait_send()

        @when(level == 1)
        def _():
            z_copy(gm.at[1, l, 0, p.q], l, 2, 1, p.below, szd.at[u]).wait_send()

        return carry

    def grad_copy(k, j):
        return local(gm.at[j, 0, k], o_first.at[k, j], grad_sem.at[k, j])

    def layer(l, carry):
        params = vec[l]

        tick(l, 0)
        scaled, _ = normalize_parts(hs[l])
        n1s[l] = (scaled * params[0:1] + params[1:2]).astype(bf16)
        weights = keep_low(l, 0)
        for j in range(2):
            both = contract_last(n1s[l], weights[j])
            shift = jnp.concatenate([row_of(hb.at[j, l, 0], range(HEADS_HERE)), jnp.zeros((1, 192), f32)], axis=-1)
            qks[l, j] = (both + shift).astype(bf16)

        tick(l, 1)
        weights = keep_low(l, 1)
        keep = lax.broadcasted_iota(jnp.int32, (128, ROWS), 1) < FRAMES
        for j in range(2):
            vs[l, j] = (
                contract_last(n1s[l], weights[j, 0:192]) + row_of(hb.at[j, l, 1], range(HEADS_HERE))
            ).astype(bf16)

            def rows_of(r, carry, j=j):
                rows = pl.ds(pl.multiple_of(r * 128, 128), 128)
                heads = []
                for h in range(HEADS_HERE):
                    cols = slice(HEAD_DIM * h, HEAD_DIM * (h + 1))
                    k_cols = slice(192 + HEAD_DIM * h, 192 + HEAD_DIM * (h + 1))
                    scores = contract_last(qks[l, j, rows, cols], qks[l, j, :, k_cols]) * score_scale
                    scores = jnp.where(keep, scores, -1e30)
                    weight = jnp.exp(scores - jnp.max(scores, axis=-1, keepdims=True))
                    weight = weight * (1.0 / jnp.sum(weight, axis=-1, keepdims=True))
                    heads.append(product(weight.astype(bf16), vs[l, j, :, cols]))
                as_[l, j, rows, :] = jnp.concatenate(heads, axis=-1).astype(bf16)
                return carry

            lax.fori_loop(0, ROWS // 128, rows_of, 0)
            if j == 0:
                serve(l, 2)
        part[...] = product(as_[l, 0], weights[0, 192:384])
        part[...] += product(as_[l, 1], weights[1, 192:384])
        swap(0)
        ms[l] = hs[l] + (part[...] + other[0]) + params[4:5]
        scaled, _ = normalize_parts(ms[l])
        n2s[l] = (scaled * params[2:3] + params[3:4]).astype(bf16)
        for copy in out_copies(l):
            copy.start()

        for i in (2, 3):
            tick(l, i)
            weights = keep_low(l, i)

            @when(l > 0)
            def _(i=i):
                for copy in mid_copies(l - 1, i):
                    copy.wait()

            for j in range(2):
                shift = row_of(ub.at[j, l], range(6 * (i - 2), 6 * (i - 1)))
                before = product(n2s[l], weights[j]) + shift
                us[j, i - 2] = before
                cs[j, i - 2] = gelu(before).astype(bf16)
            for copy in mid_copies(l, i):
                copy.start()

        for i in (4, 5):
            tick(l, i)
            weights = keep_low(l, i)

            @when(l == last)
            def _(i=i):
                if i == 4:
                    lax.fori_loop(0, UNITS, drain, 0)
                for j in range(2):
                    gm[j, 0, i - 4] = contract_rows(low_ct[...], cs[j, i - 4]).reshape(4, 2, 96, BLOCK)
                    grad_copy(i - 4, j).start()

            @when(l < LAYERS - 1)
            def _(i=i, weights=weights):
                for j in range(2):
                    term = contract_last(cs[j, i - 4], weights[j])
                    if i == 4 and j == 0:
                        part[...] = term
                    else:
                        part[...] += term

        @when(l < LAYERS - 1)
        def _():
            swap(1)
            hs[l + 1] = ms[l] + (part[...] + other[1]) + params[5:6]

        return carry

    lax.fori_loop(0, LAYERS, layer, 0)

    for i in (2, 3):
        for copy in mid_copies(last, i):
            copy.wait()
    for l in range(LAYERS):
        for copy in out_copies(l):
            copy.wait()
    for j in range(2):
        local(low_a.at[0, j], o_wa.at[j, last, 1], low_sem.at[0, j]).wait()
        for slot in range(2):
            local(low_m.at[slot, j], o_wm.at[j, last, 2 + slot], low_sem.at[1 + slot, j]).wait()
    for k in range(2):
        for j in range(2):
            grad_copy(k, j).wait()
    bias_drain()
    chunk_drain()

    lax.fori_loop(UNITS, TOTAL - 1, drain, 0)


def run_forward(frames, cotangent, wa, wm, head_bias, up_bias, vectors):
    def hbm(shape, kind):
        return jax.ShapeDtypeStruct(shape, kind)

    dma = pltpu.SemaphoreType.DMA
    per_unit = dma((TOTAL, 2))
    return pl.pallas_call(
        forward_kernel,
        out_shape=(
            hbm((ROWS, WIDTH), f32),
            hbm((LAYERS, ROWS, WIDTH), f32),
            hbm((LAYERS, ROWS, WIDTH), f32),
            hbm((LAYERS, ROWS, WIDTH), bf16),
            hbm((LAYERS, ROWS, WIDTH), bf16),
            hbm((LAYERS, 2, ROWS, BLOCK), bf16),
            hbm((LAYERS, 2, ROWS, 192), bf16),
            hbm((LAYERS, 2, ROWS, 192), bf16),
            hbm((LAYERS, 2, 2, ROWS, BLOCK), f32),
            hbm((LAYERS, 2, 2, ROWS, BLOCK), bf16),
            hbm((2, LAYERS, 2, BLOCK, WIDTH), bf16),
            hbm((2, LAYERS, 4, WIDTH, BLOCK), bf16),
            hbm((2, 2, 4, 2, 96, BLOCK), f32),
        ),
        in_specs=[ANY, ANY, ANY, ANY, ANY, ANY, VMEM],
        out_specs=(ANY,) * 13,
        scratch_shapes=[
            pltpu.VMEM((2, LAYERS, 2, 2, 4, 2, 24, WIDTH), f32),
            pltpu.VMEM((2, LAYERS, 4, 4, 2, 96, BLOCK), f32),
            pltpu.VMEM((2, *head_bias.shape), f32),
            pltpu.VMEM((2, *up_bias.shape), f32),
            pltpu.VMEM((LAYERS, ROWS, WIDTH), f32),
            pltpu.VMEM((LAYERS, ROWS, WIDTH), f32),
            pltpu.VMEM((LAYERS, ROWS, WIDTH), bf16),
            pltpu.VMEM((LAYERS, ROWS, WIDTH), bf16),
            pltpu.VMEM((LAYERS, 2, ROWS, BLOCK), bf16),
            pltpu.VMEM((LAYERS, 2, ROWS, 192), bf16),
            pltpu.VMEM((LAYERS, 2, ROWS, 192), bf16),
            pltpu.VMEM((2, 2, ROWS, BLOCK), f32),
            pltpu.VMEM((2, 2, ROWS, BLOCK), bf16),
            pltpu.VMEM((1, 2, BLOCK, WIDTH), bf16),
            pltpu.VMEM((2, 2, WIDTH, BLOCK), bf16),
            pltpu.VMEM((ROWS, WIDTH), bf16),
            pltpu.VMEM((ROWS, WIDTH), f32),
            pltpu.VMEM((2, ROWS, WIDTH), f32),
            per_unit,
            per_unit,
            dma((TOTAL,)),
            per_unit,
            per_unit,
            per_unit,
            per_unit,
            per_unit,
            per_unit,
            per_unit,
            per_unit,
            dma((TOTAL,)),
            dma((4, 2)),
            dma((4, 2)),
            dma((4,)),
            dma((6,)),
            dma((2,)),
            dma((2, 3)),
            dma((2, 2)),
            dma((4,)),
            dma((3, 2)),
            dma((2, 2)),
            dma((7, LAYERS)),
            dma((2, 2)),
        ],
        compiler_params=pltpu.CompilerParams(
            collective_id=0, has_side_effects=True, vmem_limit_bytes=63 << 20
        ),
        name="gather_forward",
    )(frames, cotangent, wa, wm, head_bias, up_bias, vectors)


def backward_kernel(
    i_ct,
    i_h,
    i_m,
    i_n1,
    i_n2,
    i_qk,
    i_v,
    i_a,
    i_u,
    i_c,
    i_wa,
    i_wm,
    i_first,
    vec,
    o_fin,
    o_act,
    o_small,
    o_src,
    o_grads,
    held,
    x1,
    y1,
    x2,
    y2,
    own,
    zin,
    zup,
    stage,
    whole_in,
    whole_up,
    grad,
    part,
    other,
    h_in,
    m_in,
    n1,
    n2,
    qk,
    v,
    a,
    u_in,
    c_in,
    wa,
    wm,
    low,
    dqk,
    dv,
    small,
    small_in,
    sx1,
    rx1,
    sy1,
    ry1,
    sx2,
    rx2,
    sy2,
    ry2,
    szd,
    rzd,
    szu,
    rzu,
    sfin,
    rfin,
    lfin,
    act_send,
    act_recv,
    act_sem,
    load_sem,
    unit_sem,
    stage_sem,
    held_sem,
    swap_sem,
    small_send,
    small_recv,
    once_sem,
    whole_send,
    whole_recv,
    whole_send_up,
    whole_recv_up,
):
    p = find_place()
    greet(p)
    level = p.level
    when = pl.when

    chunks = ROWS // CHUNK
    n_chunks = 3 * chunks
    slot_of = (p.c, 1 - p.c)

    def act_part(ref, k):
        return ref.at[pl.ds(pl.multiple_of(k % chunks * CHUNK, CHUNK), CHUNK)]

    def act_own(k):
        return act_part(o_src.at[k // chunks - 1], k)

    def act_there(j, k):
        return act_part(o_act.at[k // chunks, slot_of[j]], k)

    def act_copy(src, j, k, m, device):
        return remote(src, act_there(j, k), act_send.at[k, m], act_recv.at[k, j], device)

    def act_step(s, ticks):
        def set_out(k):
            src = act_part(i_h.at[1], k) if k < chunks else act_own(k)

            @when(level == 0)
            def _():
                act_copy(src, 0, k, 0, p.above).start()

            @when(level == 1)
            def _():
                act_copy(src, 1, k, 1, p.above).start()
                act_copy(src, 1, k, 2, p.below).start()

        def pass_on(k, at, j):
            @when(level == at)
            def _():
                act_copy(act_there(j, k), j, k, j, p.above).wait_recv()
                act_copy(act_there(j, k), j, k, j, p.above).start()

        for t in ticks:
            outs, firsts, seconds = ([k for k in range(n_chunks) if row[k] == t] for row in ACT_TICKS)
            if outs or firsts or seconds:

                @when(s == t)
                def _(outs=outs, firsts=firsts, seconds=seconds):
                    for k in outs:
                        set_out(k)
                    for k in firsts:
                        pass_on(k, 1, 0)
                    for k in seconds:
                        pass_on(k, 2, 1)
                        pass_on(k, 2, 0)

    def act_drain(k):
        @when(level < 3)
        def _():
            act_copy(act_there(0, k), 0, k, 0, p.above).wait_send()

        @when((level == 1) | (level == 2))
        def _():
            act_copy(act_there(1, k), 1, k, 1, p.above).wait_send()

        @when(level == 1)
        def _():
            act_copy(act_there(1, k), 1, k, 2, p.below).wait_send()

        @when(level == 3)
        def _():
            act_copy(act_there(0, k), 0, k, 0, p.above).wait_recv()

        @when((level == 0) | (level == 3))
        def _():
            act_copy(act_there(1, k), 1, k, 1, p.above).wait_recv()

    def act_local(src, n, method):
        for j in range(2):

            @when(level == j)
            def _(j=j):
                getattr(local(src, o_act.at[n, slot_of[j]], act_sem.at[n]), method)()

    def x1_copy(w):
        return remote(held.at[w, :, :, 1 - p.x, 0], x1.at[w], sx1.at[w], rx1.at[w], p.xn)

    def y1_copy(w):
        return remote(held.at[w, :, 1 - p.y, :, 1], y1.at[w], sy1.at[w], ry1.at[w], p.yn)

    def x2_copy(w):
        return remote(held.at[w, :, p.y, 1 - p.x, 1], x2.at[w], sx2.at[w], rx2.at[w], p.xn)

    def y2_copy(w):
        return remote(held.at[w, :, 1 - p.y, p.x, 0], y2.at[w], sy2.at[w], ry2.at[w], p.yn)

    def down_copy(u, j):
        return remote(own.at[u, j], zin.at[u, j], szd.at[u, j], rzd.at[u, j], p.below)

    def up_copy(u):
        return remote(own.at[u, 1], zup.at[u], szu.at[u], rzu.at[u], p.above)

    def fin_copy(u, j):
        return remote(own.at[u, j, 1 - p.c], o_fin.at[u], sfin.at[u], rfin.at[u], p.partner)

    def fin_local(u, j):
        return local(own.at[u, j, p.c], o_fin.at[u], lfin.at[u])

    def sent(w):
        x1_copy(w).wait_send()
        y1_copy(w).wait_send()
        x2_copy(w).wait_send()
        y2_copy(w).wait_send()

    def stage_one(u):
        w = lax.rem(u, SLOTS)
        when(u >= SLOTS)(lambda: sent(w))
        when(u < 2)(lambda: local(i_first.at[u], held.at[w], held_sem.at[0]).start())
        when(u >= 2)(lambda: local(o_grads.at[u - 2], held.at[w], held_sem.at[0]).start())
        local(i_first.at[0], held.at[w], held_sem.at[0]).wait()
        x1_copy(w).start()
        y1_copy(w).start()

    def stage_two(u):
        w = lax.rem(u, SLOTS)
        x1_copy(w).wait_recv()
        held[w, :, 1 - p.y, p.x, 0] += x1[w, :, 1 - p.y]
        held[w, :, p.y, p.x, 0] += x1[w, :, p.y]
        y1_copy(w).wait_recv()
        held[w, :, p.y, 1 - p.x, 1] += y1[w, :, 1 - p.x]
        held[w, :, p.y, p.x, 1] += y1[w, :, p.x]
        y2_copy(w).start()
        x2_copy(w).start()

    def stage_three(u):
        w = lax.rem(u, SLOTS)
        y2_copy(w).wait_recv()
        own[u, :, 0] = held[w, :, p.y, p.x, 0] + y2[w]
        x2_copy(w).wait_recv()
        own[u, :, 1] = held[w, :, p.y, p.x, 1] + x2[w]

        @when(level == 3)
        def _():
            down_copy(u, 0).start()
            down_copy(u, 1).start()

        @when(level == 0)
        def _():
            up_copy(u).start()

    def level_two(u):
        for j in range(2):
            down_copy(u, j).wait_recv()
            own[u, j] += zin[u, j]
            down_copy(u, j).start()

    def level_one(u):
        down_copy(u, 0).wait_recv()
        own[u, 0] += zin[u, 0]
        down_copy(u, 0).start()
        down_copy(u, 1).wait_recv()
        up_copy(u).wait_recv()
        own[u, 1] += zin[u, 1] + zup[u]
        fin_local(u, 1).start()
        fin_copy(u, 1).start()

    def level_zero(u):
        down_copy(u, 0).wait_recv()
        own[u, 0] += zin[u, 0]
        fin_local(u, 0).start()
        fin_copy(u, 0).start()

    def whole_part(ref, e):
        return ref.at[e // 2, e % 2]

    def whole_copy(e, j):
        here, there = whole_part(stage.at[j], e), whole_part(whole_in.at[j], e)
        return remote(here, there, whole_send.at[e, j], whole_recv.at[e, j], p.below)

    def whole_copy_up(e):
        here, there = whole_part(stage.at[1], e), whole_part(whole_up, e)
        return remote(here, there, whole_send_up.at[e], whole_recv_up.at[e], p.above)

    def whole_add(e, j):
        whole_copy(e, j).wait_recv()
        stage[j, e // 2, e % 2] += whole_in[j, e // 2, e % 2]

    lane = (TOTAL - 1) % SLOTS

    def plane_copies(j):
        return (
            remote(stage.at[j, :, 1 - p.x, 0], x1.at[lane, 0], sx1.at[lane], rx1.at[lane], p.xn),
            remote(stage.at[j, 1 - p.y, :, 1], y1.at[lane, 0], sy1.at[lane], ry1.at[lane], p.yn),
            remote(stage.at[j, p.y, 1 - p.x, 1], x2.at[lane, 0], sx2.at[lane], rx2.at[lane], p.xn),
            remote(stage.at[j, 1 - p.y, p.x, 0], y2.at[lane, 0], sy2.at[lane], ry2.at[lane], p.yn),
        )

    def whole_fin(j):
        u = TOTAL - 1
        return (
            local(stage.at[j, p.y, p.x, p.c], o_fin.at[u], lfin.at[u]),
            remote(stage.at[j, p.y, p.x, 1 - p.c], o_fin.at[u], sfin.at[u], rfin.at[u], p.partner),
        )

    def whole_step(s):
        first = STEPS_INSIDE

        for e in range(4):

            @when((s == first + e) & (level == 0))
            def _(e=e):
                whole_copy_up(e).start()

            @when((s == first + e) & (level == 3))
            def _(e=e):
                whole_copy(e, 0).start()
                whole_copy(e, 1).start()

            @when((s == first + e + 1) & (level == 2))
            def _(e=e):
                for j in range(2):
                    whole_add(e, j)
                    whole_copy(e, j).start()

            @when((s == first + e + 2) & (level == 1))
            def _(e=e):
                whole_add(e, 0)
                whole_copy(e, 0).start()
                whole_add(e, 1)
                whole_copy_up(e).wait_recv()
                stage[1, e // 2, e % 2] += whole_up[e // 2, e % 2]

            @when((s == first + e + 3) & (level == 0))
            def _(e=e):
                whole_add(e, 0)

        for j in range(2):
            a1, b1, a2, b2 = plane_copies(j)

            @when((s == first + 6) & (level == j))
            def _(a1=a1, b1=b1):
                sent(lane)
                a1.start()
                b1.start()

            @when((s == first + 7) & (level == j))
            def _(j=j, a1=a1, b1=b1, a2=a2, b2=b2):
                a1.wait()
                stage[j, 1 - p.y, p.x, 0] += x1[lane, 0, 1 - p.y]
                stage[j, p.y, p.x, 0] += x1[lane, 0, p.y]
                b1.wait()
                stage[j, p.y, 1 - p.x, 1] += y1[lane, 0, 1 - p.x]
                stage[j, p.y, p.x, 1] += y1[lane, 0, p.x]
                a2.start()
                b2.start()

            @when((s == first + 8) & (level == j))
            def _(j=j, a2=a2, b2=b2):
                b2.wait()
                stage[j, p.y, p.x, 0] += y2[lane, 0]
                a2.wait()
                stage[j, p.y, p.x, 1] += x2[lane, 0]
                for copy in whole_fin(j):
                    copy.start()

    def whole_drain():
        for e in range(4):

            @when(level > 0)
            def _(e=e):
                whole_copy(e, 0).wait_send()

            @when(level > 1)
            def _(e=e):
                whole_copy(e, 1).wait_send()

            @when(level == 0)
            def _(e=e):
                whole_copy_up(e).wait_send()

        here, there = whole_fin(0)

        @when(level < 2)
        def _():
            here.wait()
            there.wait_send()

        @when(level > 1)
        def _():
            sent(lane)
            there.wait_recv()

    def service(s, ticks):
        def unit(k, step, extra=True):
            when((k >= 0) & (k < TOTAL - 1) & extra)(lambda: step(k))

        unit(s - 1, stage_two)
        unit(s - 2, stage_three)
        unit(s + 1, stage_one)
        for at, step, (least, slack, until) in zip((2, 1, 0), (level_two, level_one, level_zero), Z_TICKS):

            def done(t):
                late = jnp.where(t < until, slack, 0)
                return jnp.clip(t + 1 - least - late, 0, TOTAL - 1)

            def one(u, carry, step=step):
                step(u)
                return carry

            @when(level == at)
            def _(done=done, one=one):
                lax.fori_loop(done(s - 1), done(s), one, 0)

        act_step(s, ticks)

    def loads(l):
        whole = (
            (i_c, c_in),
            (i_n2, n2),
            (i_m, m_in),
            (i_a, a),
            (i_qk, qk),
            (i_v, v),
            (i_n1, n1),
            (i_h, h_in),
        )
        return [local(src.at[l], dst, load_sem.at[n]) for n, (src, dst) in enumerate(whole)]

    def load_u(l, h):
        return local(i_u.at[l, :, h], u_in, unit_sem.at[5])

    def load_a(l):
        return local(i_wa.at[:, l], wa, unit_sem.at[4])

    def load_m(l, i):
        return local(i_wm.at[:, l, i], wm.at[:, i], unit_sem.at[i])

    def swap(slot):
        copy = remote(part, other.at[slot], swap_sem.at[slot], swap_sem.at[2 + slot], p.partner)
        copy.start()
        copy.wait()

    def put(u, j, value):
        stage[j] = value.reshape(2, 2, 2, 96, BLOCK)
        when(u < TOTAL - 1)(lambda: local(stage.at[j], o_grads.at[u - 2, j], stage_sem.at[j]).start())

    def put_done(u):
        @when(u < TOTAL - 1)
        def _():
            for j in range(2):
                local(stage.at[j], o_grads.at[u - 2, j], stage_sem.at[j]).wait()

    def small_row(l, row, value):
        small[l, row : row + 1] = value[:, :BLOCK]
        small[l, row + 1 : row + 2] = value[:, BLOCK:]

    def norm_back(slot, l, source, gain, first):
        def rows_of(r, carry):
            rows = pl.ds(pl.multiple_of(r * 128, 128), 128)
            upstream = part[rows] + other[slot, rows]
            scaled, inverse = normalize_parts(source[rows])
            lowered, gain_grad, shift_grad = normalize_back(upstream, scaled, inverse, gain)
            value = grad[rows] + lowered
            grad[rows] = value
            rounded = value.astype(bf16)
            low[rows] = rounded
            bias_grad = jnp.sum(rounded.astype(f32), axis=0)
            return (
                carry[0] + gain_grad.reshape(1, WIDTH),
                carry[1] + shift_grad.reshape(1, WIDTH),
                carry[2] + bias_grad.reshape(1, WIDTH),
            )

        zero = jnp.zeros((1, WIDTH), f32)
        sums = lax.fori_loop(0, ROWS // 128, rows_of, (zero, zero, zero))
        small_row(l, first, sums[0])
        small_row(l, first + 2, sums[1])
        return sums[2]

    keep = lax.broadcasted_iota(jnp.int32, (ROWS, ROWS), 1) < FRAMES

    def attention_back(j, carry):
        mixture_back = contract_last(low[...], wa[j, 1, 192:384]).astype(bf16)
        parts = ([], [], [])
        for h in range(HEADS_HERE):
            cols = slice(HEAD_DIM * h, HEAD_DIM * (h + 1))
            k_cols = slice(192 + HEAD_DIM * h, 192 + HEAD_DIM * (h + 1))
            qh, kh, vh, dah = qk[j, :, cols], qk[j, :, k_cols], v[j, :, cols], mixture_back[:, cols]
            scores = jnp.where(keep, contract_last(qh, kh) * score_scale, -1e30)
            weight = jnp.exp(scores - jnp.max(scores, axis=-1, keepdims=True))
            weight = weight * (1.0 / jnp.sum(weight, axis=-1, keepdims=True))
            prob_grad = contract_last(dah, vh)
            centre = jnp.sum(prob_grad * weight, axis=-1, keepdims=True)
            score_back = (weight * (prob_grad - centre)).astype(bf16)
            parts[0].append((product(score_back, kh) * score_scale).astype(bf16))
            parts[1].append((contract_rows(score_back, qh) * score_scale).astype(bf16))
            parts[2].append(contract_rows(weight.astype(bf16), dah).astype(bf16))
        dqk[j] = jnp.concatenate(parts[0] + parts[1], axis=-1)
        dv[j] = jnp.concatenate(parts[2], axis=-1)
        return carry

    stage_one(0)
    service(jnp.int32(0), (0,))
    local(i_ct, grad, once_sem.at[0]).start()
    small[...] = jnp.zeros_like(small)

    def layer(step, carry):
        l = LAYERS - 1 - step
        u0 = UNITS * step
        s0 = 3 * step
        params = vec[l]
        fetch = loads(l)
        fetch[0].start()
        load_u(l, 0).start()
        for i in (2, 3, 0, 1):
            load_m(l, i).start()
        for copy in fetch[1:]:
            copy.start()
        load_a(l).start()

        @when(step == 0)
        def _():
            local(i_ct, grad, once_sem.at[0]).wait()
            low[...] = grad[...].astype(bf16)
            small_row(l, 10, jnp.sum(low[...].astype(f32), axis=0, keepdims=True))

        fetch[0].wait()

        @when(step > 0)
        def _():
            for i in (0, 1):
                for j in range(2):
                    put(u0 + i, j, contract_rows(low[...], c_in[j, i]))
                put_done(u0 + i)
            service(s0, (3,))

        for i in range(2):
            load_m(l, 2 + i).wait()

        @when(step == 0)
        def _():
            for h in range(2):
                for j in range(2):
                    term = contract_last(c_in[j, h], wm[j, 2 + h])
                    if h == 0 and j == 0:
                        part[...] = term
                    else:
                        part[...] += term
            swap(1)
            fetch[2].wait()
            part[...] = m_in[...] + (part[...] + other[1]) + params[5:6]
            keep_top = local(part, o_src.at[0], once_sem.at[1])
            keep_top.start()
            act_local(part, 1, "start")
            keep_top.wait()
            act_local(part, 1, "wait")

        fetch[1].wait()
        for i in (2, 3):
            h = i - 2
            load_m(l, h).wait()
            load_u(l, h).wait()
            for j in range(2):
                back = (product(low[...], wm[j, 2 + h]) * gelu_slope(u_in[j])).astype(bf16)
                row = 14 + 2 * j + h
                small[l, row : row + 1] = jnp.sum(back.astype(f32), axis=0, keepdims=True)
                put(u0 + i, j, contract_rows(n2[...], back))
                term = contract_last(back, wm[j, h])
                if h == 0 and j == 0:
                    part[...] = term
                else:
                    part[...] += term
            if h == 0:
                load_u(l, 1).start()
            put_done(u0 + i)
        service(s0 + 1, (1, 4))
        swap(0)

        @when(step > 0)
        def _():
            fetch[2].wait()

        small_row(l, 8, norm_back(0, l, m_in, params[2:3], 4))

        for copy in fetch[3:]:
            copy.wait()
        load_a(l).wait()
        when(step == 0)(lambda: act_local(h_in, 0, "start"))
        lax.fori_loop(0, 2, attention_back, 0)
        service(s0 + 2, (2, 5))
        for j in range(2):
            stage[j, :, :, :, :, 0:192] = contract_rows(n1[...], dv[j]).reshape(2, 2, 2, 96, 192)
            stage[j, :, :, :, :, 192:384] = contract_rows(low[...], a[j]).reshape(2, 2, 2, 96, 192)
            local(stage.at[j], o_grads.at[u0 + 2, j], stage_sem.at[j]).start()
        put_done(u0 + 4)
        for j in range(2):
            put(u0 + 5, j, contract_rows(n1[...], dqk[j]))
            sums = jnp.sum(dqk[j].astype(f32), axis=0, keepdims=True)
            small[l, 12 + j : 13 + j, 0:192] = sums[:, 0:192]
            small[l, 12 + j : 13 + j, 192:384] = jnp.sum(dv[j].astype(f32), axis=0, keepdims=True)
            term = product(dqk[j], wa[j, 0]) + product(dv[j], wa[j, 1, 0:192])
            if j == 0:
                part[...] = term
            else:
                part[...] += term
        put_done(u0 + 5)
        swap(1)
        down_sum = norm_back(1, l, h_in, params[0:1], 0)

        @when(l > 0)
        def _():
            small_row(l - 1, 10, down_sum)

        when(step == 0)(lambda: act_local(h_in, 0, "wait"))
        return carry

    lax.fori_loop(0, LAYERS, layer, 0)
    keep_grad = local(grad, o_src.at[1], once_sem.at[1])
    keep_grad.start()
    act_local(grad, 2, "start")
    keep_grad.wait()

    def small_copy(m, device):
        return remote(small, small_in.at[m], small_send.at[m], small_recv.at[m], device)

    def small_add(m, device):
        small_copy(m, device).wait()
        small[...] += small_in[m]

    first = STEPS_INSIDE

    def small_step(s):
        @when(s == first)
        def _():
            small_copy(0, p.xn).start()

        @when(s == first + 1)
        def _():
            small_add(0, p.xn)
            small_copy(1, p.yn).start()

        @when(s == first + 2)
        def _():
            small_add(1, p.yn)

            @when((level == 0) | (level == 2))
            def _():
                small_copy(2, p.above).start()

            @when((level == 1) | (level == 3))
            def _():
                small_copy(2, p.below).start()

        @when(s == first + 3)
        def _():
            small_add(2, p.above)

            @when(level == 1)
            def _():
                small_copy(3, p.above).start()

            @when(level == 2)
            def _():
                small_copy(3, p.below).start()

        @when(s == first + 4)
        def _():
            @when((level == 1) | (level == 2))
            def _():
                small_add(3, p.above)

            @when(level == 1)
            def _():
                small_copy(4, p.below).start()

            @when(level == 2)
            def _():
                small_copy(4, p.above).start()

        @when(s == first + 5)
        def _():
            @when((level == 0) | (level == 3))
            def _():
                small_copy(4, p.above).wait_recv()
                small[...] = small_in[4]

            small_copy(5, p.partner).start()
            local(small, o_small.at[0], once_sem.at[2]).start()

        @when(s == first + 6)
        def _():
            small_copy(5, p.partner).wait()
            local(small_in.at[5], o_small.at[1], once_sem.at[3]).start()

            @when((level == 1) | (level == 2))
            def _():
                small_copy(4, p.above).wait_send()

    def step_after(s, carry):
        small_step(s)
        service(s, range(STEPS_INSIDE, LAST_TICK))
        whole_step(s)
        return carry

    lax.fori_loop(first, LAST_TICK, step_after, 0)

    for w in range(SLOTS):
        if w != lane:
            sent(w)
    whole_drain()

    def drain(u, carry):
        @when(level > 0)
        def _():
            down_copy(u, 0).wait_send()

        @when(level > 1)
        def _():
            down_copy(u, 1).wait_send()
            fin_copy(u, 0).wait_recv()

        @when(level == 0)
        def _():
            up_copy(u).wait_send()

        @when(level < 2)
        def _():
            fin_local(u, 0).wait()
            fin_copy(u, 0).wait_send()

        return carry

    lax.fori_loop(0, TOTAL - 1, drain, 0)
    for k in range(n_chunks):
        act_drain(k)

    act_local(grad, 2, "wait")
    local(small, o_small.at[0], once_sem.at[2]).wait()
    local(small_in.at[5], o_small.at[1], once_sem.at[3]).wait()


LAST_TICK = TOTAL + 4
ACT_TICKS = ((0, 0, 0, 0, 2, 2, 3, 3, 6, 6, 7, 7), (1, 1, 2, 2, 3, 3, 4, 4, 7, 7, 8, 8), (2, 2, 3, 3, 4, 4, 5, 5, 8, 8, 9, 9))
Z_TICKS = ((3, 0, 0), (4, 0, 0), (5, 0, 0))
STEPS_INSIDE = 1 + 2 + 3
SMALL = (LAYERS, 24, BLOCK)


def run_backward(saved, vectors):
    dma = pltpu.SemaphoreType.DMA
    slots = dma((SLOTS,))
    units = dma((TOTAL,))
    pair = dma((TOTAL, 2))
    return pl.pallas_call(
        backward_kernel,
        out_shape=(
            jax.ShapeDtypeStruct((TOTAL, 96, BLOCK), f32),
            jax.ShapeDtypeStruct((3, 2, ROWS, WIDTH), f32),
            jax.ShapeDtypeStruct((2, *SMALL), f32),
            jax.ShapeDtypeStruct((2, ROWS, WIDTH), f32),
            jax.ShapeDtypeStruct((TOTAL - 3, 2, 2, 2, 2, 96, BLOCK), f32),
        ),
        in_specs=[ANY] * 13 + [VMEM],
        out_specs=(ANY,) * 5,
        scratch_shapes=[
            pltpu.VMEM((SLOTS, 2, 2, 2, 2, 96, BLOCK), f32),
            pltpu.VMEM((SLOTS, 2, 2, 96, BLOCK), f32),
            pltpu.VMEM((SLOTS, 2, 2, 96, BLOCK), f32),
            pltpu.VMEM((SLOTS, 2, 96, BLOCK), f32),
            pltpu.VMEM((SLOTS, 2, 96, BLOCK), f32),
            pltpu.VMEM((TOTAL - 1, 2, 2, 96, BLOCK), f32),
            pltpu.VMEM((TOTAL - 1, 2, 2, 96, BLOCK), f32),
            pltpu.VMEM((TOTAL - 1, 2, 96, BLOCK), f32),
            pltpu.VMEM((2, 2, 2, 2, 96, BLOCK), f32),
            pltpu.VMEM((2, 2, 2, 2, 96, BLOCK), f32),
            pltpu.VMEM((2, 2, 2, 96, BLOCK), f32),
            pltpu.VMEM((ROWS, WIDTH), f32),
            pltpu.VMEM((ROWS, WIDTH), f32),
            pltpu.VMEM((2, ROWS, WIDTH), f32),
            pltpu.VMEM((ROWS, WIDTH), f32),
            pltpu.VMEM((ROWS, WIDTH), f32),
            pltpu.VMEM((ROWS, WIDTH), bf16),
            pltpu.VMEM((ROWS, WIDTH), bf16),
            pltpu.VMEM((2, ROWS, BLOCK), bf16),
            pltpu.VMEM((2, ROWS, 192), bf16),
            pltpu.VMEM((2, ROWS, 192), bf16),
            pltpu.VMEM((2, ROWS, BLOCK), f32),
            pltpu.VMEM((2, 2, ROWS, BLOCK), bf16),
            pltpu.VMEM((2, 2, BLOCK, WIDTH), bf16),
            pltpu.VMEM((2, 4, WIDTH, BLOCK), bf16),
            pltpu.VMEM((ROWS, WIDTH), bf16),
            pltpu.VMEM((2, ROWS, BLOCK), bf16),
            pltpu.VMEM((2, ROWS, 192), bf16),
            pltpu.VMEM(SMALL, f32),
            pltpu.VMEM((6, *SMALL), f32),
            slots,
            slots,
            slots,
            slots,
            slots,
            slots,
            slots,
            slots,
            pair,
            pair,
            units,
            units,
            units,
            units,
            units,
            dma((TOTAL, 3)),
            dma((TOTAL, 2)),
            dma((3,)),
            dma((8,)),
            dma((6,)),
            dma((2,)),
            dma((1,)),
            dma((4,)),
            dma((6,)),
            dma((6,)),
            dma((4,)),
            dma((4, 2)),
            dma((4, 2)),
            dma((4,)),
            dma((4,)),
        ],
        compiler_params=pltpu.CompilerParams(
            collective_id=1, has_side_effects=True, vmem_limit_bytes=63 << 20
        ),
        name="backward_reduce",
    )(*saved, vectors)


def per_device(
    frames,
    cotangent,
    w_attn,
    w_mlp,
    vectors,
    head_bias,
    up_bias,
    moment_attn,
    square_attn,
    moment_mlp,
    square_mlp,
    moment_vectors,
    square_vectors,
    moment_head,
    square_head,
    moment_up,
    square_up,
):
    dp = lax.axis_index("dp")
    t = lax.axis_index("tensor")
    core = dp % 2
    dp_size = lax.axis_size("dp")

    wa = jnp.swapaxes(w_attn, 2, 3).reshape(LAYERS, 4, 4, 2, 24, WIDTH)
    wm = w_mlp.reshape(LAYERS, 2, 4, 2, 96, 2 * BLOCK)
    saved = run_forward(frames, cotangent, wa, wm, head_bias, up_bias, vectors)
    saved = (*saved[:-1], saved[-1].reshape(2, 2, 2, 2, 2, 96, BLOCK))
    fin, acts, small, _, _ = run_backward(saved, vectors)
    sections = jnp.concatenate([acts[:2, 0, :FRAMES], acts[:2, 1, :FRAMES]], axis=1)
    upstream = jnp.concatenate([acts[2, 0, :FRAMES], acts[2, 1, :FRAMES]], axis=0)

    if dp_size > GROUP:
        groups = [[i + GROUP * o for o in range(dp_size // GROUP)] for i in range(GROUP)]
        small = lax.psum(small, "dp", axis_index_groups=groups)
    vector_all = small[0, :, :12].reshape(LAYERS, 6, WIDTH)
    owner = t // 2
    here = jnp.where(owner == core, small[0], small[1])
    second = jnp.where(owner == 0, t % 2, 1 - t % 2)
    head_all = jnp.where(second == 0, here[:, 12], here[:, 13]).reshape(LAYERS, 2, HEADS_HERE, HEAD_DIM)
    up_all = jnp.where(second == 0, here[:, 14:16], here[:, 16:18]).reshape(LAYERS, 12, HEAD_DIM)

    def owned(param, dim):
        size = param.shape[dim] // dp_size
        return lax.dynamic_slice_in_dim(param, dp * size, size, dim)

    if dp_size > GROUP:
        rows = jnp.zeros((TOTAL, WIDTH, BLOCK), f32)
        rows = lax.dynamic_update_slice_in_dim(rows, fin, (dp % GROUP) * 96, 1)
        fin = lax.psum_scatter(rows, "dp", scatter_dimension=1, tiled=True)

    def unit(l, k):
        return fin[(LAYERS - 1 - l) * UNITS + k]

    attn_grad = jnp.stack(
        [
            jnp.stack([unit(l, 5)[:, :192], unit(l, 5)[:, 192:], unit(l, 4)[:, :192], unit(l, 4)[:, 192:]])
            for l in range(LAYERS)
        ]
    )
    mlp_grad = jnp.stack(
        [
            jnp.stack(
                [
                    jnp.concatenate([unit(l, 2), unit(l, 3)], axis=-1),
                    jnp.concatenate([unit(l, 0), unit(l, 1)], axis=-1),
                ]
            )
            for l in range(LAYERS)
        ]
    )
    attn = adamw_update(owned(w_attn, 2), attn_grad, moment_attn, square_attn, rate_matrix)
    mlp = adamw_update(owned(w_mlp, 2), mlp_grad, moment_mlp, square_mlp, rate_matrix)
    vector_new = adamw_update(
        owned(vectors, 2), owned(vector_all, 2), moment_vectors, square_vectors, rate_vector
    )
    head = adamw_update(owned(head_bias, 3), owned(head_all, 3), moment_head, square_head, rate_vector)
    upper = adamw_update(owned(up_bias, 2), owned(up_all, 2), moment_up, square_up, rate_vector)
    return (sections, upstream, *attn, *mlp, *vector_new, *head, *upper)


def solution(mesh):
    in_specs = (
        P("dp", None),
        P("dp", None),
        P(None, None, None, "tensor"),
        P(None, None, None, "tensor"),
        P(),
        P(None, None, "tensor", None),
        P(None, "tensor", None),
        P(None, None, "dp", "tensor"),
        P(None, None, "dp", "tensor"),
        P(None, None, "dp", "tensor"),
        P(None, None, "dp", "tensor"),
        P(None, None, "dp"),
        P(None, None, "dp"),
        P(None, None, "tensor", "dp"),
        P(None, None, "tensor", "dp"),
        P(None, "tensor", "dp"),
        P(None, "tensor", "dp"),
    )
    out_specs = (
        P(None, "dp", None),
        P("dp", None),
        P(None, None, "dp", "tensor"),
        P(None, None, "dp", "tensor"),
        P(None, None, "dp", "tensor"),
        P(None, None, "dp", "tensor"),
        P(None, None, "dp", "tensor"),
        P(None, None, "dp", "tensor"),
        P(None, None, "dp"),
        P(None, None, "dp"),
        P(None, None, "dp"),
        P(None, None, "tensor", "dp"),
        P(None, None, "tensor", "dp"),
        P(None, None, "tensor", "dp"),
        P(None, "tensor", "dp"),
        P(None, "tensor", "dp"),
        P(None, "tensor", "dp"),
    )
    return jax.shard_map(
        per_device, mesh=mesh, in_specs=in_specs, out_specs=out_specs, check_vma=False
    )
```

```python
import math
from types import SimpleNamespace

import jax
import jax.numpy as jnp
from jax import lax
from jax.experimental import pallas as pl
from jax.experimental.pallas import tpu as pltpu
from jax.sharding import PartitionSpec as P

HEAD_DIM = 64
FRAMES = 500
ROWS = 512
LAYERS = 2
STEP = 10
WIDTH = 768
BLOCK = 384
UNITS = 6
TOTAL = LAYERS * UNITS
GROUP = 8
HEADS_HERE = 3
SLOTS = 3
LEAD = 2
SOURCE_LEAD = 5
CHUNK_TICKS = ((2, 4, 5, 7), (3, 5, 6, 8), (4, 6, 7, 9))
SPAN = 504
SECOND = 496
CHUNK = 128

ln_eps = 1e-05
beta_one = 0.9
beta_two = 0.999
adam_eps = 1e-08
decay_rate = 0.01
rate_matrix = 0.05
rate_vector = 0.2
score_scale = 1.0 / math.sqrt(HEAD_DIM)
MESH = pl.DeviceIdType.MESH
f32 = jnp.float32
bf16 = jnp.bfloat16
ANY = pl.BlockSpec(memory_space=pl.ANY)
VMEM = pl.BlockSpec(memory_space=pltpu.VMEM)


def product(left, right):
    return jnp.dot(left, right, preferred_element_type=f32)


def contract_last(left, right):
    return lax.dot_general(left, right, (((1,), (1,)), ((), ())), preferred_element_type=f32)


def contract_rows(left, right):
    return lax.dot_general(left, right, (((0,), (0,)), ((), ())), preferred_element_type=f32)


def normalize_parts(inputs):
    centre = jnp.mean(inputs, axis=-1, keepdims=True)
    centred = inputs - centre
    inverse = lax.rsqrt(jnp.mean(centred * centred, axis=-1, keepdims=True) + ln_eps)
    return centred * inverse, inverse


def normalize_back(upstream, scaled, inverse, gain):
    gain_grad = jnp.sum(upstream * scaled, axis=0)
    shift_grad = jnp.sum(upstream, axis=0)
    inner_grad = upstream * gain
    lowered = inverse * (
        inner_grad
        - jnp.mean(inner_grad, axis=-1, keepdims=True)
        - scaled * jnp.mean(inner_grad * scaled, axis=-1, keepdims=True)
    )
    return (lowered, gain_grad, shift_grad)


def gelu(before):
    return 0.5 * before * (1.0 + lax.erf(before * (1.0 / math.sqrt(2.0))))


def gelu_slope(before):
    return 0.5 * (1.0 + lax.erf(before * (1.0 / math.sqrt(2.0)))) + before * jnp.exp(
        -0.5 * before * before
    ) * (1.0 / math.sqrt(2.0 * math.pi))


def adamw_update(param, gradient, first, second, rate):
    first_new = beta_one * first + (1.0 - beta_one) * gradient
    second_new = beta_two * second + (1.0 - beta_two) * gradient * gradient
    ratio = (
        first_new
        / (1.0 - beta_one**STEP)
        / (jnp.sqrt(second_new / (1.0 - beta_two**STEP)) + adam_eps)
    )
    return (param - rate * (ratio + decay_rate * param), first_new, second_new)


def find_place():
    dp = lax.axis_index("dp")
    t = lax.axis_index("tensor")
    i = lax.rem(dp, GROUP)
    base = dp - i
    c = lax.rem(i, 2)
    x = lax.rem(i // 2, 2)
    y = i // 4
    up = 1 - 2 * c
    level = c * (3 - t) + (1 - c) * t

    def at(cc, xx, yy):
        return base + 4 * yy + 2 * xx + cc

    return SimpleNamespace(
        t=t,
        c=c,
        x=x,
        y=y,
        q=2 * y + x,
        qx=2 * y + 1 - x,
        qy=2 * (1 - y) + x,
        qd=2 * (1 - y) + 1 - x,
        level=level,
        partner=(at(1 - c, x, y), t),
        xn=(at(c, 1 - x, y), t),
        yn=(at(c, x, 1 - y), t),
        above=(dp, t + up),
        below=(dp, t - up),
    )


def greet(p):
    barrier = pltpu.get_barrier_semaphore()

    def signal(device):
        pl.semaphore_signal(barrier, inc=1, device_id=device, device_id_type=MESH)

    signal(p.partner)
    signal(p.xn)
    signal(p.yn)

    @pl.when(p.level < 3)
    def _():
        signal(p.above)

    @pl.when(p.level > 0)
    def _():
        signal(p.below)

    inner = (p.level > 0) & (p.level < 3)

    @pl.when(inner)
    def _():
        pl.semaphore_wait(barrier, 5)

    @pl.when(jnp.logical_not(inner))
    def _():
        pl.semaphore_wait(barrier, 4)


def remote(src, dst, send_sem, recv_sem, device):
    return pltpu.make_async_remote_copy(
        src_ref=src,
        dst_ref=dst,
        send_sem=send_sem,
        recv_sem=recv_sem,
        device_id=device,
        device_id_type=MESH,
    )


def local(src, dst, sem):
    return pltpu.make_async_copy(src, dst, sem)


def forward_kernel(
    frames,
    cotangent,
    wa,
    wm,
    head_bias,
    up_bias,
    vec,
    o_ct,
    o_h,
    o_m,
    o_n1,
    o_n2,
    o_qk,
    o_v,
    o_a,
    o_u,
    o_c,
    o_wa,
    o_wm,
    o_first,
    ga,
    gm,
    hb,
    ub,
    hs,
    ms,
    n1s,
    n2s,
    qks,
    vs,
    as_,
    us,
    cs,
    low_a,
    low_m,
    low_ct,
    part,
    other,
    rz,
    sz,
    szd,
    rx,
    sx,
    ry,
    sy,
    rxd,
    sxd,
    ryd,
    syd,
    native,
    rc,
    sc,
    scd,
    first_sem,
    bias_local,
    bias_send,
    bias_recv,
    swap_sem,
    low_sem,
    mid_sem,
    out_sem,
    grad_sem,
):
    p = find_place()
    greet(p)
    level = p.level
    when = pl.when

    def quarter(ref, i, q, h=None):
        lead = (slice(None), q) if i < 2 else (q,)
        return ref.at[lead if h is None else (*lead, h)]

    def block(l, i):
        if i < 2:
            return wa.at[l, pl.ds(2 * i, 2)]
        return wm.at[l, (i - 2) // 2, :, :, :, pl.ds(BLOCK * (i % 2), BLOCK)]

    def block_quarter(l, i):
        if i < 2:
            return wa.at[l, pl.ds(2 * i, 2), p.q]
        return wm.at[l, (i - 2) // 2, p.q, :, :, pl.ds(BLOCK * (i % 2), BLOCK)]

    def held(l, i, j):
        return ga.at[j, l, i] if i < 2 else gm.at[j, l, i - 2]

    def z_copy(src, l, i, j, device, send_sem):
        return remote(src, quarter(held(l, i, j), i, p.q), send_sem, rz.at[UNITS * l + i, j], device)

    def plane_copy(l, i, j, q, h, send_sem, recv_sem, device):
        here = quarter(held(l, i, j), i, q, h)
        u = UNITS * l + i
        return remote(here, here, send_sem.at[u, j], recv_sem.at[u, j], device)

    def x_copy(l, i, j, q):
        return plane_copy(l, i, j, q, None, sx, rx, p.xn)

    def y_copy(l, i, j, q):
        return plane_copy(l, i, j, q, None, sy, ry, p.yn)

    def xd_copy(l, i, j, q):
        return plane_copy(l, i, j, q, 1, sxd, rxd, p.xn)

    def yd_copy(l, i, j, q):
        return plane_copy(l, i, j, q, 0, syd, ryd, p.yn)

    def source(l, i):
        u = UNITS * l + i

        @when(level == 0)
        def _():
            z_copy(block_quarter(l, i), l, i, 0, p.above, sz.at[u, 0]).start()
            local(block(l, i), held(l, i, 0), native.at[u]).start()

        @when(level == 1)
        def _():
            z_copy(block_quarter(l, i), l, i, 1, p.above, sz.at[u, 1]).start()
            z_copy(block_quarter(l, i), l, i, 1, p.below, szd.at[u]).start()
            local(block(l, i), held(l, i, 1), native.at[u]).start()

    def stage_one(l, i):
        u = UNITS * l + i
        for j in range(2):

            @when(level != j)
            def _(j=j):
                here = quarter(held(l, i, j), i, p.q)
                z_copy(here, l, i, j, p.above, sz.at[u, j]).wait_recv()

                @when((level == 2) | ((level == 1) if j == 0 else (level == 2)))
                def _():
                    z_copy(here, l, i, j, p.above, sz.at[u, j]).start()

                x_copy(l, i, j, p.q).start()
                y_copy(l, i, j, p.q).start()

    def stage_two(l, i):
        for j in range(2):

            @when(level != j)
            def _(j=j):
                x_copy(l, i, j, p.qx).wait_recv()
                yd_copy(l, i, j, p.qx).start()
                y_copy(l, i, j, p.qy).wait_recv()
                xd_copy(l, i, j, p.qy).start()

    def finish(l, i):
        u = UNITS * l + i
        for j in range(2):

            @when(level != j)
            def _(j=j):
                yd_copy(l, i, j, p.qd).wait_recv()
                xd_copy(l, i, j, p.qd).wait_recv()

            @when(level == j)
            def _(j=j):
                local(block(l, i), held(l, i, j), native.at[u]).wait()

    last = LAYERS - 1
    alone = UNITS - 1

    def chunk_copy(src, q, j, device, send_sem):
        return remote(src, held(last, alone, j).at[q], send_sem, rc.at[q, j], device)

    def chunk_source(q):
        here = wm.at[last, 1, q, :, :, pl.ds(BLOCK, BLOCK)]

        @when(level == 0)
        def _():
            chunk_copy(here, q, 0, p.above, sc.at[q, 0]).start()

        @when(level == 1)
        def _():
            chunk_copy(here, q, 1, p.above, sc.at[q, 1]).start()
            chunk_copy(here, q, 1, p.below, scd.at[q]).start()

    def chunk_pass(q, at, j):
        @when(level == at)
        def _():
            here = held(last, alone, j).at[q]
            chunk_copy(here, q, j, p.above, sc.at[q, j]).wait_recv()
            chunk_copy(here, q, j, p.above, sc.at[q, j]).start()

    def chunk_native(method):
        for j in range(2):

            @when(level == j)
            def _(j=j):
                getattr(local(block(last, alone), held(last, alone, j), native.at[TOTAL - 1]), method)()

    def chunk_finish():
        for q in range(4):
            here = held(last, alone, 0).at[q]

            @when((level == 3))
            def _(q=q, here=here):
                chunk_copy(here, q, 0, p.above, sc.at[q, 0]).wait_recv()

            @when((level == 3) | (level == 0))
            def _(q=q, here=here):
                chunk_copy(here, q, 1, p.above, sc.at[q, 1]).wait_recv()

        chunk_native("wait")

    def chunk_drain():
        for q in range(4):
            here = held(last, alone, 0).at[q]

            @when(level < 3)
            def _(q=q, here=here):
                chunk_copy(here, q, 0, p.above, sc.at[q, 0]).wait_send()

            @when((level == 1) | (level == 2))
            def _(q=q, here=here):
                chunk_copy(here, q, 1, p.above, sc.at[q, 1]).wait_send()

            @when(level == 1)
            def _(q=q, here=here):
                chunk_copy(here, q, 1, p.below, scd.at[q]).wait_send()

    def chunk_step(l, i):
        for q in range(4):
            for at, tick_of in enumerate(CHUNK_TICKS):
                there, k = divmod(tick_of[q], UNITS)
                if k == i:

                    @when(l == there)
                    def _(q=q, at=at):
                        if at == 0:
                            chunk_source(q)
                        elif at == 1:
                            chunk_pass(q, 1, 0)
                        else:
                            chunk_pass(q, 2, 1)
                            chunk_pass(q, 2, 0)

    def ahead(step, l, i, by):
        k = i + by
        there = l + k // UNITS
        if k % UNITS == alone:
            when(there < last)(lambda: step(there, alone))
        elif k < UNITS:
            step(l, k)
        else:
            when(there < LAYERS)(lambda: step(there, k % UNITS))

    def serve(l, k):
        ahead(source, l, k, SOURCE_LEAD)
        ahead(stage_one, l, k, LEAD)
        ahead(stage_two, l, k, LEAD - 1)

    def tick(l, i):
        if i < 2:
            serve(l, i)
        elif i < UNITS - 1:
            serve(l, i + 1)
        chunk_step(l, i)
        if i == alone:
            when(l < last)(lambda: finish(l, i))
            when(l == last)(chunk_finish)
        else:
            finish(l, i)

    mine = (p.t // 2) == p.c
    clip = lax.rem(p.t, 2)
    span = pl.ds(pl.multiple_of(clip * SECOND, 8), SPAN)
    inputs = (
        (frames.at[span], part.at[pl.ds(0, SPAN)]),
        (cotangent.at[span], ms.at[1, pl.ds(0, SPAN)]),
    )

    def input_copies(k):
        src, dst = inputs[k]
        return (
            local(src, dst, first_sem.at[k]),
            remote(src, dst, first_sem.at[2 + k], first_sem.at[4 + k], p.partner),
        )

    def wait_input(k):
        here, there = input_copies(k)

        @when(mine)
        def _():
            here.wait()
            there.wait_send()

        @when(jnp.logical_not(mine))
        def _():
            there.wait_recv()

    def take_clip(target, raw):
        @when(clip == 0)
        def _():
            target[0:FRAMES] = raw[0:FRAMES]

        @when(clip == 1)
        def _():
            target[0:FRAMES] = raw[FRAMES - SECOND : SPAN]

        target[FRAMES:ROWS] = jnp.zeros((ROWS - FRAMES, WIDTH), f32)

    kept_biases = ((head_bias, hb), (up_bias, ub))

    def bias_copy(src, n, j, m, device):
        return remote(src, kept_biases[n][1].at[j], bias_send.at[n, m], bias_recv.at[n, j], device)

    def bias_source():
        for n, (src, dst) in enumerate(kept_biases):

            @when(level == 0)
            def _(n=n, src=src, dst=dst):
                local(src, dst.at[0], bias_local.at[n]).start()
                bias_copy(src, n, 0, 0, p.above).start()

            @when(level == 1)
            def _(n=n, src=src, dst=dst):
                local(src, dst.at[1], bias_local.at[n]).start()
                bias_copy(src, n, 1, 1, p.above).start()
                bias_copy(src, n, 1, 2, p.below).start()

    def bias_pass():
        for n, (src, dst) in enumerate(kept_biases):

            @when(level != 0)
            def _(n=n, src=src):
                bias_copy(src, n, 0, 0, p.above).wait_recv()

            @when((level == 1) | (level == 2))
            def _(n=n, dst=dst):
                bias_copy(dst.at[0], n, 0, 0, p.above).start()

            @when(level != 1)
            def _(n=n, src=src):
                bias_copy(src, n, 1, 1, p.above).wait_recv()

            @when(level == 2)
            def _(n=n, dst=dst):
                bias_copy(dst.at[1], n, 1, 1, p.above).start()

            @when(level < 2)
            def _(n=n, src=src, dst=dst):
                local(src, dst.at[0], bias_local.at[n]).wait()

    def bias_drain():
        for n, (src, dst) in enumerate(kept_biases):

            @when(level < 3)
            def _(n=n, src=src):
                bias_copy(src, n, 0, 0, p.above).wait_send()

            @when((level == 1) | (level == 2))
            def _(n=n, src=src):
                bias_copy(src, n, 1, 1, p.above).wait_send()

            @when(level == 1)
            def _(n=n, src=src):
                bias_copy(src, n, 1, 2, p.below).wait_send()

    def head_row(j, l, n):
        return jnp.concatenate([hb[j, l, h, n : n + 1, :] for h in range(HEADS_HERE)], axis=-1)

    def up_row(j, l, k):
        return jnp.concatenate([ub[j, r, pl.ds(l, 1), :] for r in range(6 * k, 6 * k + 6)], axis=-1)

    @when(mine)
    def _():
        for copy in input_copies(0):
            copy.start()

    bias_source()
    for i in range(SOURCE_LEAD):
        source(0, i)

    @when(mine)
    def _():
        for copy in input_copies(1):
            copy.start()

    bias_pass()
    chunk_native("start")
    stage_one(0, 0)
    wait_input(0)
    take_clip(hs.at[0], part)
    for i in range(1, LEAD):
        stage_one(0, i)
        stage_two(0, i - 1)
    wait_input(1)
    take_clip(part, ms.at[1])
    keep_cotangent = local(part, o_ct, out_sem.at[0, 1])
    keep_cotangent.start()
    low_ct[...] = part[...].astype(bf16)
    keep_cotangent.wait()

    def keep_low(l, i):
        if i < 2:
            slots, slot, target = low_a, 0, lambda j: o_wa.at[j, l, i]
        else:
            slots, slot, target = low_m, i % 2, lambda j: o_wm.at[j, l, i - 2]
        sems = 0 if i < 2 else 1 + i % 2

        def copy(j):
            return local(slots.at[slot, j], target(j), low_sem.at[sems, j])

        def drain():
            for j in range(2):
                copy(j).wait()

        if i in (1, 4, 5):
            drain()
        else:
            when(l > 0)(drain)
        for j in range(2):
            if i < 2:
                slots[slot, j] = ga[j, l, i].reshape(BLOCK, WIDTH).astype(bf16)
            else:
                slots[slot, j] = gm[j, l, i - 2].reshape(WIDTH, BLOCK).astype(bf16)
            copy(j).start()
        return slots.at[slot]

    def swap(slot):
        copy = remote(part, other.at[slot], swap_sem.at[slot], swap_sem.at[2 + slot], p.partner)
        copy.start()
        copy.wait()

    def out_copies(l):
        return [
            local(hs.at[l], o_h.at[l], out_sem.at[0, l]),
            local(ms.at[l], o_m.at[l], out_sem.at[1, l]),
            local(n1s.at[l], o_n1.at[l], out_sem.at[2, l]),
            local(n2s.at[l], o_n2.at[l], out_sem.at[3, l]),
            local(qks.at[l], o_qk.at[l], out_sem.at[4, l]),
            local(vs.at[l], o_v.at[l], out_sem.at[5, l]),
            local(as_.at[l], o_a.at[l], out_sem.at[6, l]),
        ]

    def mid_copies(l, i):
        k = i - 2
        return [
            local(us.at[:, k], o_u.at[l, :, k], mid_sem.at[0, k]),
            local(cs.at[:, k], o_c.at[l, :, k], mid_sem.at[1, k]),
        ]

    def drain(u, carry):
        l = u // UNITS
        for j in range(2):

            @when((level < 3) if j == 0 else ((level == 1) | (level == 2)))
            def _(j=j):
                z_copy(gm.at[j, l, 0, p.q], l, 2, j, p.above, sz.at[u, j]).wait_send()

            @when(level != j)
            def _(j=j):
                whole, half = gm.at[j, l, 0, p.q], gm.at[j, l, 0, p.q, 0]
                remote(whole, whole, sx.at[u, j], rx.at[u, j], p.xn).wait_send()
                remote(whole, whole, sy.at[u, j], ry.at[u, j], p.yn).wait_send()
                remote(half, half, sxd.at[u, j], rxd.at[u, j], p.xn).wait_send()
                remote(half, half, syd.at[u, j], ryd.at[u, j], p.yn).wait_send()

        @when(level == 1)
        def _():
            z_copy(gm.at[1, l, 0, p.q], l, 2, 1, p.below, szd.at[u]).wait_send()

        return carry

    def grad_copy(k, j):
        return local(gm.at[j, 0, k], o_first.at[k, j], grad_sem.at[k, j])

    def layer(l, carry):
        params = [vec[k, pl.ds(l, 1)] for k in range(6)]

        tick(l, 0)
        scaled, _ = normalize_parts(hs[l])
        n1s[l] = (scaled * params[0] + params[1]).astype(bf16)
        weights = keep_low(l, 0)
        for j in range(2):
            both = contract_last(n1s[l], weights[j])
            shift = jnp.concatenate([head_row(j, l, 0), jnp.zeros((1, 192), f32)], axis=-1)
            qks[l, j] = (both + shift).astype(bf16)

        tick(l, 1)
        weights = keep_low(l, 1)
        keep = lax.broadcasted_iota(jnp.int32, (128, ROWS), 1) < FRAMES
        for j in range(2):
            vs[l, j] = (
                contract_last(n1s[l], weights[j, 0:192]) + head_row(j, l, 1)
            ).astype(bf16)

            def rows_of(r, carry, j=j):
                rows = pl.ds(pl.multiple_of(r * 128, 128), 128)
                heads = []
                for h in range(HEADS_HERE):
                    cols = slice(HEAD_DIM * h, HEAD_DIM * (h + 1))
                    k_cols = slice(192 + HEAD_DIM * h, 192 + HEAD_DIM * (h + 1))
                    scores = contract_last(qks[l, j, rows, cols], qks[l, j, :, k_cols]) * score_scale
                    scores = jnp.where(keep, scores, -1e30)
                    weight = jnp.exp(scores - jnp.max(scores, axis=-1, keepdims=True))
                    weight = weight * (1.0 / jnp.sum(weight, axis=-1, keepdims=True))
                    heads.append(product(weight.astype(bf16), vs[l, j, :, cols]))
                as_[l, j, rows, :] = jnp.concatenate(heads, axis=-1).astype(bf16)
                return carry

            lax.fori_loop(0, ROWS // 128, rows_of, 0)
            if j == 0:
                serve(l, 2)
        part[...] = product(as_[l, 0], weights[0, 192:384])
        part[...] += product(as_[l, 1], weights[1, 192:384])
        swap(0)
        ms[l] = hs[l] + (part[...] + other[0]) + params[4]
        scaled, _ = normalize_parts(ms[l])
        n2s[l] = (scaled * params[2] + params[3]).astype(bf16)
        for copy in out_copies(l):
            copy.start()

        for i in (2, 3):
            tick(l, i)
            weights = keep_low(l, i)

            @when(l > 0)
            def _(i=i):
                for copy in mid_copies(l - 1, i):
                    copy.wait()

            for j in range(2):
                before = product(n2s[l], weights[j]) + up_row(j, l, i - 2)
                us[j, i - 2] = before
                cs[j, i - 2] = gelu(before).astype(bf16)
            for copy in mid_copies(l, i):
                copy.start()

        for i in (4, 5):
            tick(l, i)
            weights = keep_low(l, i)

            @when(l == last)
            def _(i=i):
                if i == 4:
                    lax.fori_loop(0, UNITS, drain, 0)
                for j in range(2):
                    gm[j, 0, i - 4] = contract_rows(low_ct[...], cs[j, i - 4]).reshape(4, 2, 96, BLOCK)
                    grad_copy(i - 4, j).start()

            @when(l < LAYERS - 1)
            def _(i=i, weights=weights):
                for j in range(2):
                    term = contract_last(cs[j, i - 4], weights[j])
                    if i == 4 and j == 0:
                        part[...] = term
                    else:
                        part[...] += term

        @when(l < LAYERS - 1)
        def _():
            swap(1)
            hs[l + 1] = ms[l] + (part[...] + other[1]) + params[5]

        return carry

    lax.fori_loop(0, LAYERS, layer, 0)

    for i in (2, 3):
        for copy in mid_copies(last, i):
            copy.wait()
    for l in range(LAYERS):
        for copy in out_copies(l):
            copy.wait()
    for j in range(2):
        local(low_a.at[0, j], o_wa.at[j, last, 1], low_sem.at[0, j]).wait()
        for slot in range(2):
            local(low_m.at[slot, j], o_wm.at[j, last, 2 + slot], low_sem.at[1 + slot, j]).wait()
    for k in range(2):
        for j in range(2):
            grad_copy(k, j).wait()
    bias_drain()
    chunk_drain()

    lax.fori_loop(UNITS, TOTAL - 1, drain, 0)


def run_forward(frames, cotangent, wa, wm, head_bias, up_bias, vectors):
    def hbm(shape, kind):
        return jax.ShapeDtypeStruct(shape, kind)

    dma = pltpu.SemaphoreType.DMA
    per_unit = dma((TOTAL, 2))
    return pl.pallas_call(
        forward_kernel,
        out_shape=(
            hbm((ROWS, WIDTH), f32),
            hbm((LAYERS, ROWS, WIDTH), f32),
            hbm((LAYERS, ROWS, WIDTH), f32),
            hbm((LAYERS, ROWS, WIDTH), bf16),
            hbm((LAYERS, ROWS, WIDTH), bf16),
            hbm((LAYERS, 2, ROWS, BLOCK), bf16),
            hbm((LAYERS, 2, ROWS, 192), bf16),
            hbm((LAYERS, 2, ROWS, 192), bf16),
            hbm((LAYERS, 2, 2, ROWS, BLOCK), f32),
            hbm((LAYERS, 2, 2, ROWS, BLOCK), bf16),
            hbm((2, LAYERS, 2, BLOCK, WIDTH), bf16),
            hbm((2, LAYERS, 4, WIDTH, BLOCK), bf16),
            hbm((2, 2, 4, 2, 96, BLOCK), f32),
        ),
        in_specs=[ANY, ANY, ANY, ANY, ANY, ANY, VMEM],
        out_specs=(ANY,) * 13,
        scratch_shapes=[
            pltpu.VMEM((2, LAYERS, 2, 2, 4, 2, 24, WIDTH), f32),
            pltpu.VMEM((2, LAYERS, 4, 4, 2, 96, BLOCK), f32),
            pltpu.VMEM((2, *head_bias.shape), f32),
            pltpu.VMEM((2, *up_bias.shape), f32),
            pltpu.VMEM((LAYERS, ROWS, WIDTH), f32),
            pltpu.VMEM((LAYERS, ROWS, WIDTH), f32),
            pltpu.VMEM((LAYERS, ROWS, WIDTH), bf16),
            pltpu.VMEM((LAYERS, ROWS, WIDTH), bf16),
            pltpu.VMEM((LAYERS, 2, ROWS, BLOCK), bf16),
            pltpu.VMEM((LAYERS, 2, ROWS, 192), bf16),
            pltpu.VMEM((LAYERS, 2, ROWS, 192), bf16),
            pltpu.VMEM((2, 2, ROWS, BLOCK), f32),
            pltpu.VMEM((2, 2, ROWS, BLOCK), bf16),
            pltpu.VMEM((1, 2, BLOCK, WIDTH), bf16),
            pltpu.VMEM((2, 2, WIDTH, BLOCK), bf16),
            pltpu.VMEM((ROWS, WIDTH), bf16),
            pltpu.VMEM((ROWS, WIDTH), f32),
            pltpu.VMEM((2, ROWS, WIDTH), f32),
            per_unit,
            per_unit,
            dma((TOTAL,)),
            per_unit,
            per_unit,
            per_unit,
            per_unit,
            per_unit,
            per_unit,
            per_unit,
            per_unit,
            dma((TOTAL,)),
            dma((4, 2)),
            dma((4, 2)),
            dma((4,)),
            dma((6,)),
            dma((2,)),
            dma((2, 3)),
            dma((2, 2)),
            dma((4,)),
            dma((3, 2)),
            dma((2, 2)),
            dma((7, LAYERS)),
            dma((2, 2)),
        ],
        compiler_params=pltpu.CompilerParams(
            collective_id=0, has_side_effects=True, vmem_limit_bytes=63 << 20
        ),
        name="gather_forward",
    )(frames, cotangent, wa, wm, head_bias, up_bias, vectors)


def backward_kernel(
    i_ct,
    i_h,
    i_m,
    i_n1,
    i_n2,
    i_qk,
    i_v,
    i_a,
    i_u,
    i_c,
    i_wa,
    i_wm,
    i_first,
    vec,
    o_fin,
    o_top,
    o_input,
    o_small,
    o_src,
    o_grads,
    held,
    x1,
    y1,
    x2,
    y2,
    own,
    zin,
    zup,
    stage,
    whole_in,
    whole_up,
    grad,
    part,
    other,
    h_in,
    m_in,
    n1,
    n2,
    qk,
    v,
    a,
    u_in,
    c_in,
    wa,
    wm,
    low,
    dqk,
    dv,
    small,
    small_in,
    sx1,
    rx1,
    sy1,
    ry1,
    sx2,
    rx2,
    sy2,
    ry2,
    szd,
    rzd,
    szu,
    rzu,
    sfin,
    rfin,
    lfin,
    act_send,
    act_recv,
    act_sem,
    load_sem,
    unit_sem,
    stage_sem,
    held_sem,
    swap_sem,
    small_send,
    small_recv,
    once_sem,
    whole_send,
    whole_recv,
    whole_send_up,
    whole_recv_up,
):
    p = find_place()
    level = p.level
    when = pl.when

    chunks = ROWS // CHUNK
    n_chunks = 3 * chunks
    slot_of = (p.c, 1 - p.c)

    def act_part(ref, k):
        return ref.at[pl.ds(pl.multiple_of(k % chunks * CHUNK, CHUNK), CHUNK)]

    def act_all(n, j):
        return o_top.at[n, slot_of[j]] if n < LAYERS else o_input.at[slot_of[j]]

    def act_own(k):
        return act_part(o_src.at[k // chunks - 1], k)

    def act_there(j, k):
        return act_part(act_all(k // chunks, j), k)

    def act_copy(src, j, k, m, device):
        return remote(src, act_there(j, k), act_send.at[k, m], act_recv.at[k, j], device)

    def act_step(s, ticks):
        def set_out(k):
            src = act_part(i_h.at[1], k) if k < chunks else act_own(k)

            @when(level == 0)
            def _():
                act_copy(src, 0, k, 0, p.above).start()

            @when(level == 1)
            def _():
                act_copy(src, 1, k, 1, p.above).start()
                act_copy(src, 1, k, 2, p.below).start()

        def pass_on(k, at, j):
            @when(level == at)
            def _():
                act_copy(act_there(j, k), j, k, j, p.above).wait_recv()
                act_copy(act_there(j, k), j, k, j, p.above).start()

        for t in ticks:
            outs, firsts, seconds = ([k for k in range(n_chunks) if row[k] == t] for row in ACT_TICKS)
            if outs or firsts or seconds:

                @when(s == t)
                def _(outs=outs, firsts=firsts, seconds=seconds):
                    for k in outs:
                        set_out(k)
                    for k in firsts:
                        pass_on(k, 1, 0)
                    for k in seconds:
                        pass_on(k, 2, 1)
                        pass_on(k, 2, 0)

    def act_drain(k):
        @when(level < 3)
        def _():
            act_copy(act_there(0, k), 0, k, 0, p.above).wait_send()

        @when((level == 1) | (level == 2))
        def _():
            act_copy(act_there(1, k), 1, k, 1, p.above).wait_send()

        @when(level == 1)
        def _():
            act_copy(act_there(1, k), 1, k, 2, p.below).wait_send()

        @when(level == 3)
        def _():
            act_copy(act_there(0, k), 0, k, 0, p.above).wait_recv()

        @when((level == 0) | (level == 3))
        def _():
            act_copy(act_there(1, k), 1, k, 1, p.above).wait_recv()

    def act_local(src, n, method):
        for j in range(2):

            @when(level == j)
            def _(j=j):
                getattr(local(src, act_all(n, j), act_sem.at[n]), method)()

    def x1_copy(w):
        return remote(held.at[w, :, :, 1 - p.x, 0], x1.at[w], sx1.at[w], rx1.at[w], p.xn)

    def y1_copy(w):
        return remote(held.at[w, :, 1 - p.y, :, 1], y1.at[w], sy1.at[w], ry1.at[w], p.yn)

    def x2_copy(w):
        return remote(held.at[w, :, p.y, 1 - p.x, 1], x2.at[w], sx2.at[w], rx2.at[w], p.xn)

    def y2_copy(w):
        return remote(held.at[w, :, 1 - p.y, p.x, 0], y2.at[w], sy2.at[w], ry2.at[w], p.yn)

    def down_copy(u, j):
        return remote(own.at[u, j], zin.at[u, j], szd.at[u, j], rzd.at[u, j], p.below)

    def up_copy(u):
        return remote(own.at[u, 1], zup.at[u], szu.at[u], rzu.at[u], p.above)

    def fin_copy(u, j):
        return remote(own.at[u, j, 1 - p.c], o_fin.at[u], sfin.at[u], rfin.at[u], p.partner)

    def fin_local(u, j):
        return local(own.at[u, j, p.c], o_fin.at[u], lfin.at[u])

    def sent(w):
        x1_copy(w).wait_send()
        y1_copy(w).wait_send()
        x2_copy(w).wait_send()
        y2_copy(w).wait_send()

    def stage_one(u):
        w = lax.rem(u, SLOTS)
        when(u >= SLOTS)(lambda: sent(w))
        when(u < 2)(lambda: local(i_first.at[u], held.at[w], held_sem.at[0]).start())
        when(u >= 2)(lambda: local(o_grads.at[u - 2], held.at[w], held_sem.at[0]).start())
        local(i_first.at[0], held.at[w], held_sem.at[0]).wait()
        x1_copy(w).start()
        y1_copy(w).start()

    def stage_two(u):
        w = lax.rem(u, SLOTS)
        x1_copy(w).wait_recv()
        held[w, :, 1 - p.y, p.x, 0] += x1[w, :, 1 - p.y]
        held[w, :, p.y, p.x, 0] += x1[w, :, p.y]
        y1_copy(w).wait_recv()
        held[w, :, p.y, 1 - p.x, 1] += y1[w, :, 1 - p.x]
        held[w, :, p.y, p.x, 1] += y1[w, :, p.x]
        y2_copy(w).start()
        x2_copy(w).start()

    def stage_three(u):
        w = lax.rem(u, SLOTS)
        y2_copy(w).wait_recv()
        own[u, :, 0] = held[w, :, p.y, p.x, 0] + y2[w]
        x2_copy(w).wait_recv()
        own[u, :, 1] = held[w, :, p.y, p.x, 1] + x2[w]

        @when(level == 3)
        def _():
            down_copy(u, 0).start()
            down_copy(u, 1).start()

        @when(level == 0)
        def _():
            up_copy(u).start()

    def level_two(u):
        for j in range(2):
            down_copy(u, j).wait_recv()
            own[u, j] += zin[u, j]
            down_copy(u, j).start()

    def level_one(u):
        down_copy(u, 0).wait_recv()
        own[u, 0] += zin[u, 0]
        down_copy(u, 0).start()
        down_copy(u, 1).wait_recv()
        up_copy(u).wait_recv()
        own[u, 1] += zin[u, 1] + zup[u]
        fin_local(u, 1).start()
        fin_copy(u, 1).start()

    def level_zero(u):
        down_copy(u, 0).wait_recv()
        own[u, 0] += zin[u, 0]
        fin_local(u, 0).start()
        fin_copy(u, 0).start()

    def whole_part(ref, e):
        return ref.at[e // 2, e % 2]

    def whole_copy(e, j):
        here, there = whole_part(stage.at[j], e), whole_part(whole_in.at[j], e)
        return remote(here, there, whole_send.at[e, j], whole_recv.at[e, j], p.below)

    def whole_copy_up(e):
        here, there = whole_part(stage.at[1], e), whole_part(whole_up, e)
        return remote(here, there, whole_send_up.at[e], whole_recv_up.at[e], p.above)

    def whole_add(e, j):
        whole_copy(e, j).wait_recv()
        stage[j, e // 2, e % 2] += whole_in[j, e // 2, e % 2]

    lane = (TOTAL - 1) % SLOTS

    def plane_copies(j):
        return (
            remote(stage.at[j, :, 1 - p.x, 0], x1.at[lane, 0], sx1.at[lane], rx1.at[lane], p.xn),
            remote(stage.at[j, 1 - p.y, :, 1], y1.at[lane, 0], sy1.at[lane], ry1.at[lane], p.yn),
            remote(stage.at[j, p.y, 1 - p.x, 1], x2.at[lane, 0], sx2.at[lane], rx2.at[lane], p.xn),
            remote(stage.at[j, 1 - p.y, p.x, 0], y2.at[lane, 0], sy2.at[lane], ry2.at[lane], p.yn),
        )

    def whole_fin(j):
        u = TOTAL - 1
        return (
            local(stage.at[j, p.y, p.x, p.c], o_fin.at[u], lfin.at[u]),
            remote(stage.at[j, p.y, p.x, 1 - p.c], o_fin.at[u], sfin.at[u], rfin.at[u], p.partner),
        )

    def whole_step(s):
        first = STEPS_INSIDE

        for e in range(4):

            @when((s == first + e) & (level == 0))
            def _(e=e):
                whole_copy_up(e).start()

            @when((s == first + e) & (level == 3))
            def _(e=e):
                whole_copy(e, 0).start()
                whole_copy(e, 1).start()

            @when((s == first + e + 1) & (level == 2))
            def _(e=e):
                for j in range(2):
                    whole_add(e, j)
                    whole_copy(e, j).start()

            @when((s == first + e + 2) & (level == 1))
            def _(e=e):
                whole_add(e, 0)
                whole_copy(e, 0).start()
                whole_add(e, 1)
                whole_copy_up(e).wait_recv()
                stage[1, e // 2, e % 2] += whole_up[e // 2, e % 2]

            @when((s == first + e + 3) & (level == 0))
            def _(e=e):
                whole_add(e, 0)

        for j in range(2):
            a1, b1, a2, b2 = plane_copies(j)

            @when((s == first + 6) & (level == j))
            def _(a1=a1, b1=b1):
                sent(lane)
                a1.start()
                b1.start()

            @when((s == first + 7) & (level == j))
            def _(j=j, a1=a1, b1=b1, a2=a2, b2=b2):
                a1.wait()
                stage[j, 1 - p.y, p.x, 0] += x1[lane, 0, 1 - p.y]
                stage[j, p.y, p.x, 0] += x1[lane, 0, p.y]
                b1.wait()
                stage[j, p.y, 1 - p.x, 1] += y1[lane, 0, 1 - p.x]
                stage[j, p.y, p.x, 1] += y1[lane, 0, p.x]
                a2.start()
                b2.start()

            @when((s == first + 8) & (level == j))
            def _(j=j, a2=a2, b2=b2):
                b2.wait()
                stage[j, p.y, p.x, 0] += y2[lane, 0]
                a2.wait()
                stage[j, p.y, p.x, 1] += x2[lane, 0]
                for copy in whole_fin(j):
                    copy.start()

    def whole_drain():
        for e in range(4):

            @when(level > 0)
            def _(e=e):
                whole_copy(e, 0).wait_send()

            @when(level > 1)
            def _(e=e):
                whole_copy(e, 1).wait_send()

            @when(level == 0)
            def _(e=e):
                whole_copy_up(e).wait_send()

        here, there = whole_fin(0)

        @when(level < 2)
        def _():
            here.wait()
            there.wait_send()

        @when(level > 1)
        def _():
            sent(lane)
            there.wait_recv()

    def service(s, ticks):
        def unit(k, step, extra=True):
            when((k >= 0) & (k < TOTAL - 1) & extra)(lambda: step(k))

        unit(s - 1, stage_two)
        unit(s - 2, stage_three)
        unit(s + 1, stage_one)
        for at, step, (least, slack, until) in zip((2, 1, 0), (level_two, level_one, level_zero), Z_TICKS):

            def done(t):
                late = jnp.where(t < until, slack, 0)
                return jnp.clip(t + 1 - least - late, 0, TOTAL - 1)

            def one(u, carry, step=step):
                step(u)
                return carry

            @when(level == at)
            def _(done=done, one=one):
                lax.fori_loop(done(s - 1), done(s), one, 0)

        act_step(s, ticks)

    def loads(l):
        whole = (
            (i_c, c_in),
            (i_n2, n2),
            (i_m, m_in),
            (i_a, a),
            (i_qk, qk),
            (i_v, v),
            (i_n1, n1),
            (i_h, h_in),
        )
        return [local(src.at[l], dst, load_sem.at[n]) for n, (src, dst) in enumerate(whole)]

    def load_u(l, h):
        return local(i_u.at[l, :, h], u_in, unit_sem.at[5])

    def load_a(l):
        return local(i_wa.at[:, l], wa, unit_sem.at[4])

    def load_m(l, i):
        return local(i_wm.at[:, l, i], wm.at[:, i], unit_sem.at[i])

    def start_loads(l):
        fetch = loads(l)
        load_u(l, 0).start()
        for i in (2, 0, 3, 1):
            load_m(l, i).start()
        for copy in fetch:
            copy.start()
        load_a(l).start()

    def swap(slot):
        copy = remote(part, other.at[slot], swap_sem.at[slot], swap_sem.at[2 + slot], p.partner)
        copy.start()
        copy.wait()

    def put(u, j, value):
        stage[j] = value.reshape(2, 2, 2, 96, BLOCK)
        when(u < TOTAL - 1)(lambda: local(stage.at[j], o_grads.at[u - 2, j], stage_sem.at[j]).start())

    def put_done(u):
        @when(u < TOTAL - 1)
        def _():
            for j in range(2):
                local(stage.at[j], o_grads.at[u - 2, j], stage_sem.at[j]).wait()

    def small_row(l, row, value):
        small[l, row : row + 1] = value[:, :BLOCK]
        small[l, row + 1 : row + 2] = value[:, BLOCK:]

    def norm_back(slot, l, source, gain, first):
        def rows_of(r, carry):
            rows = pl.ds(pl.multiple_of(r * 128, 128), 128)
            upstream = part[rows] + other[slot, rows]
            scaled, inverse = normalize_parts(source[rows])
            lowered, gain_grad, shift_grad = normalize_back(upstream, scaled, inverse, gain)
            value = grad[rows] + lowered
            grad[rows] = value
            rounded = value.astype(bf16)
            low[rows] = rounded
            bias_grad = jnp.sum(rounded.astype(f32), axis=0)
            return (
                carry[0] + gain_grad.reshape(1, WIDTH),
                carry[1] + shift_grad.reshape(1, WIDTH),
                carry[2] + bias_grad.reshape(1, WIDTH),
            )

        zero = jnp.zeros((1, WIDTH), f32)
        sums = lax.fori_loop(0, ROWS // 128, rows_of, (zero, zero, zero))
        small_row(l, first, sums[0])
        small_row(l, first + 2, sums[1])
        return sums[2]

    keep = lax.broadcasted_iota(jnp.int32, (ROWS, ROWS), 1) < FRAMES

    def attention_back(j, carry):
        mixture_back = contract_last(low[...], wa[j, 1, 192:384]).astype(bf16)
        parts = ([], [], [])
        for h in range(HEADS_HERE):
            cols = slice(HEAD_DIM * h, HEAD_DIM * (h + 1))
            k_cols = slice(192 + HEAD_DIM * h, 192 + HEAD_DIM * (h + 1))
            qh, kh, vh, dah = qk[j, :, cols], qk[j, :, k_cols], v[j, :, cols], mixture_back[:, cols]
            scores = jnp.where(keep, contract_last(qh, kh) * score_scale, -1e30)
            weight = jnp.exp(scores - jnp.max(scores, axis=-1, keepdims=True))
            weight = weight * (1.0 / jnp.sum(weight, axis=-1, keepdims=True))
            prob_grad = contract_last(dah, vh)
            centre = jnp.sum(prob_grad * weight, axis=-1, keepdims=True)
            score_back = (weight * (prob_grad - centre)).astype(bf16)
            parts[0].append((product(score_back, kh) * score_scale).astype(bf16))
            parts[1].append((contract_rows(score_back, qh) * score_scale).astype(bf16))
            parts[2].append(contract_rows(weight.astype(bf16), dah).astype(bf16))
        dqk[j] = jnp.concatenate(parts[0] + parts[1], axis=-1)
        dv[j] = jnp.concatenate(parts[2], axis=-1)
        return carry

    local(i_ct, grad, once_sem.at[0]).start()
    start_loads(LAYERS - 1)
    greet(p)
    stage_one(0)
    service(0, (0,))
    small[...] = jnp.zeros_like(small)

    def layer(step, carry):
        l = LAYERS - 1 - step
        u0 = UNITS * step
        params = [vec[k, pl.ds(l, 1)] for k in range(6)]
        fetch = loads(l)

        @when(step == 0)
        def _():
            local(i_ct, grad, once_sem.at[0]).wait()
            low[...] = grad[...].astype(bf16)
            small_row(l, 10, jnp.sum(low[...].astype(f32), axis=0, keepdims=True))

        fetch[0].wait()

        @when(step > 0)
        def _():
            for i in (0, 1):
                for j in range(2):
                    put(u0 + i, j, contract_rows(low[...], c_in[j, i]))
                put_done(u0 + i)
            service(3, (3,))

        fetch[1].wait()
        for i in (2, 3):
            h = i - 2
            load_m(l, 2 + h).wait()
            load_m(l, h).wait()
            load_u(l, h).wait()
            for j in range(2):
                back = (product(low[...], wm[j, 2 + h]) * gelu_slope(u_in[j])).astype(bf16)
                row = 14 + 2 * j + h
                small[l, row : row + 1] = jnp.sum(back.astype(f32), axis=0, keepdims=True)
                put(u0 + i, j, contract_rows(n2[...], back))
                term = contract_last(back, wm[j, h])
                if h == 0 and j == 0:
                    part[...] = term
                else:
                    part[...] += term
            if h == 0:
                load_u(l, 1).start()
            put_done(u0 + i)
            if i == 2:
                when(step == 0)(lambda: service(1, (1,)))
            else:
                when(step > 0)(lambda: service(4, (4,)))
        swap(step)
        fetch[2].wait()
        small_row(l, 8, norm_back(step, l, m_in, params[2], 4))

        @when(step == 0)
        def _():
            for h in range(2):
                for j in range(2):
                    term = contract_last(c_in[j, h], wm[j, 2 + h])
                    if h == 0 and j == 0:
                        part[...] = term
                    else:
                        part[...] += term
            swap(1)
            part[...] = m_in[...] + (part[...] + other[1]) + params[5]
            keep_top = local(part, o_src.at[0], once_sem.at[1])
            keep_top.start()
            act_local(part, 1, "start")
            keep_top.wait()
            act_local(part, 1, "wait")
            service(2, (2,))

        for copy in fetch[3:]:
            copy.wait()
        load_a(l).wait()
        when(step == 0)(lambda: act_local(h_in, 0, "start"))
        lax.fori_loop(0, 2, attention_back, 0)
        when(step > 0)(lambda: service(5, (5,)))
        for j in range(2):
            stage[j, :, :, :, :, 0:192] = contract_rows(n1[...], dv[j]).reshape(2, 2, 2, 96, 192)
            stage[j, :, :, :, :, 192:384] = contract_rows(low[...], a[j]).reshape(2, 2, 2, 96, 192)
            local(stage.at[j], o_grads.at[u0 + 2, j], stage_sem.at[j]).start()
        put_done(u0 + 4)
        for j in range(2):
            put(u0 + 5, j, contract_rows(n1[...], dqk[j]))
            sums = jnp.sum(dqk[j].astype(f32), axis=0, keepdims=True)
            small[l, 12 + j : 13 + j, 0:192] = sums[:, 0:192]
            small[l, 12 + j : 13 + j, 192:384] = jnp.sum(dv[j].astype(f32), axis=0, keepdims=True)
            term = product(dqk[j], wa[j, 0]) + product(dv[j], wa[j, 1, 0:192])
            if j == 0:
                part[...] = term
            else:
                part[...] += term
        put_done(u0 + 5)
        swap(0)
        down_sum = norm_back(0, l, h_in, params[0], 0)

        @when(l > 0)
        def _():
            small_row(l - 1, 10, down_sum)

        @when(step == 0)
        def _():
            act_local(h_in, 0, "wait")
            start_loads(LAYERS - 2)

        return carry

    lax.fori_loop(0, LAYERS, layer, 0)
    keep_grad = local(grad, o_src.at[1], once_sem.at[1])
    keep_grad.start()
    act_local(grad, 2, "start")
    keep_grad.wait()

    def small_copy(m, device):
        return remote(small, small_in.at[m], small_send.at[m], small_recv.at[m], device)

    def small_add(m, device):
        small_copy(m, device).wait()
        small[...] += small_in[m]

    first = STEPS_INSIDE

    def small_step(s):
        @when(s == first)
        def _():
            small_copy(0, p.xn).start()

        @when(s == first + 1)
        def _():
            small_add(0, p.xn)
            small_copy(1, p.yn).start()

        @when(s == first + 2)
        def _():
            small_add(1, p.yn)

            @when((level == 0) | (level == 2))
            def _():
                small_copy(2, p.above).start()

            @when((level == 1) | (level == 3))
            def _():
                small_copy(2, p.below).start()

        @when(s == first + 3)
        def _():
            small_add(2, p.above)

            @when(level == 1)
            def _():
                small_copy(3, p.above).start()

            @when(level == 2)
            def _():
                small_copy(3, p.below).start()

        @when(s == first + 4)
        def _():
            @when((level == 1) | (level == 2))
            def _():
                small_add(3, p.above)

            @when(level == 1)
            def _():
                small_copy(4, p.below).start()

            @when(level == 2)
            def _():
                small_copy(4, p.above).start()

        @when(s == first + 5)
        def _():
            @when((level == 0) | (level == 3))
            def _():
                small_copy(4, p.above).wait_recv()
                small[...] = small_in[4]

            small_copy(5, p.partner).start()
            local(small, o_small.at[0], once_sem.at[2]).start()

        @when(s == first + 6)
        def _():
            small_copy(5, p.partner).wait()
            local(small_in.at[5], o_small.at[1], once_sem.at[3]).start()

            @when((level == 1) | (level == 2))
            def _():
                small_copy(4, p.above).wait_send()

    def step_after(s, carry):
        small_step(s)
        service(s, range(STEPS_INSIDE, LAST_TICK))
        whole_step(s)
        return carry

    lax.fori_loop(first, LAST_TICK, step_after, 0)

    for w in range(SLOTS):
        if w != lane:
            sent(w)
    whole_drain()

    def drain(u, carry):
        @when(level > 0)
        def _():
            down_copy(u, 0).wait_send()

        @when(level > 1)
        def _():
            down_copy(u, 1).wait_send()
            fin_copy(u, 0).wait_recv()

        @when(level == 0)
        def _():
            up_copy(u).wait_send()

        @when(level < 2)
        def _():
            fin_local(u, 0).wait()
            fin_copy(u, 0).wait_send()

        return carry

    lax.fori_loop(0, TOTAL - 1, drain, 0)
    for k in range(n_chunks):
        act_drain(k)

    act_local(grad, 2, "wait")
    local(small, o_small.at[0], once_sem.at[2]).wait()
    local(small_in.at[5], o_small.at[1], once_sem.at[3]).wait()


LAST_TICK = TOTAL + 4
ACT_TICKS = ((0, 0, 0, 0, 2, 2, 3, 3, 6, 6, 6, 6), (1, 1, 1, 1, 3, 3, 4, 4, 7, 7, 7, 7), (2, 2, 2, 2, 4, 4, 5, 5, 8, 8, 8, 8))
Z_TICKS = ((3, 0, 0), (4, 0, 0), (5, 0, 0))
STEPS_INSIDE = 1 + 2 + 3
SMALL = (LAYERS, 24, BLOCK)


def run_backward(saved, vectors):
    dma = pltpu.SemaphoreType.DMA
    slots = dma((SLOTS,))
    units = dma((TOTAL,))
    pair = dma((TOTAL, 2))
    return pl.pallas_call(
        backward_kernel,
        out_shape=(
            jax.ShapeDtypeStruct((TOTAL, 96, BLOCK), f32),
            jax.ShapeDtypeStruct((LAYERS, 2, ROWS, WIDTH), f32),
            jax.ShapeDtypeStruct((2, ROWS, WIDTH), f32),
            jax.ShapeDtypeStruct((2, *SMALL), f32),
            jax.ShapeDtypeStruct((2, ROWS, WIDTH), f32),
            jax.ShapeDtypeStruct((TOTAL - 3, 2, 2, 2, 2, 96, BLOCK), f32),
        ),
        in_specs=[ANY] * 13 + [VMEM],
        out_specs=(ANY,) * 6,
        scratch_shapes=[
            pltpu.VMEM((SLOTS, 2, 2, 2, 2, 96, BLOCK), f32),
            pltpu.VMEM((SLOTS, 2, 2, 96, BLOCK), f32),
            pltpu.VMEM((SLOTS, 2, 2, 96, BLOCK), f32),
            pltpu.VMEM((SLOTS, 2, 96, BLOCK), f32),
            pltpu.VMEM((SLOTS, 2, 96, BLOCK), f32),
            pltpu.VMEM((TOTAL - 1, 2, 2, 96, BLOCK), f32),
            pltpu.VMEM((TOTAL - 1, 2, 2, 96, BLOCK), f32),
            pltpu.VMEM((TOTAL - 1, 2, 96, BLOCK), f32),
            pltpu.VMEM((2, 2, 2, 2, 96, BLOCK), f32),
            pltpu.VMEM((2, 2, 2, 2, 96, BLOCK), f32),
            pltpu.VMEM((2, 2, 2, 96, BLOCK), f32),
            pltpu.VMEM((ROWS, WIDTH), f32),
            pltpu.VMEM((ROWS, WIDTH), f32),
            pltpu.VMEM((2, ROWS, WIDTH), f32),
            pltpu.VMEM((ROWS, WIDTH), f32),
            pltpu.VMEM((ROWS, WIDTH), f32),
            pltpu.VMEM((ROWS, WIDTH), bf16),
            pltpu.VMEM((ROWS, WIDTH), bf16),
            pltpu.VMEM((2, ROWS, BLOCK), bf16),
            pltpu.VMEM((2, ROWS, 192), bf16),
            pltpu.VMEM((2, ROWS, 192), bf16),
            pltpu.VMEM((2, ROWS, BLOCK), f32),
            pltpu.VMEM((2, 2, ROWS, BLOCK), bf16),
            pltpu.VMEM((2, 2, BLOCK, WIDTH), bf16),
            pltpu.VMEM((2, 4, WIDTH, BLOCK), bf16),
            pltpu.VMEM((ROWS, WIDTH), bf16),
            pltpu.VMEM((2, ROWS, BLOCK), bf16),
            pltpu.VMEM((2, ROWS, 192), bf16),
            pltpu.VMEM(SMALL, f32),
            pltpu.VMEM((6, *SMALL), f32),
            slots,
            slots,
            slots,
            slots,
            slots,
            slots,
            slots,
            slots,
            pair,
            pair,
            units,
            units,
            units,
            units,
            units,
            dma((TOTAL, 3)),
            dma((TOTAL, 2)),
            dma((3,)),
            dma((8,)),
            dma((6,)),
            dma((2,)),
            dma((1,)),
            dma((4,)),
            dma((6,)),
            dma((6,)),
            dma((4,)),
            dma((4, 2)),
            dma((4, 2)),
            dma((4,)),
            dma((4,)),
        ],
        compiler_params=pltpu.CompilerParams(
            collective_id=1, has_side_effects=True, vmem_limit_bytes=63 << 20
        ),
        name="backward_reduce",
    )(*saved, vectors)


def update_kernel(dp, fin, pa, ma, sa, pm, mm, sm, tops, inputs, *refs):
    smalls, (na, fa, va, nm, fm, vm, sections, upstream), small_outs = refs[:12], refs[12:20], refs[20:]
    step = pl.program_id(0)

    def join(clips, target):
        target[:FRAMES] = clips[0, :FRAMES]
        target[FRAMES:] = clips[1, :FRAMES]

    @pl.when(step < LAYERS)
    def _():
        for k in range(4):
            grad = fin[5 - k // 2, :, 192 * (k % 2) : 192 * (k % 2 + 1)]
            na[0, k], fa[0, k], va[0, k] = adamw_update(pa[0, k].T, grad, ma[0, k], sa[0, k], rate_matrix)
        for k in range(2):
            for h in range(2):
                cols = slice(BLOCK * h, BLOCK * (h + 1))
                grad = fin[2 - 2 * k + h]
                nm[0, k, :, cols], fm[0, k, :, cols], vm[0, k, :, cols] = adamw_update(
                    pm[0, k, :, cols], grad, mm[0, k, :, cols], sm[0, k, :, cols], rate_matrix
                )
        join(tops.at[0], sections.at[0])

    @pl.when(step == LAYERS)
    def _():
        join(inputs, upstream)
        for k in range(3):
            done = adamw_update(*(ref[...] for ref in smalls[4 * k : 4 * k + 4]), rate_vector)
            for ref, value in zip(small_outs[3 * k : 3 * k + 3], done):
                ref[...] = value


def run_update(dp, fin, w_attn, moment_attn, square_attn, w_mlp, moment_mlp, square_mlp, tops, inputs, smalls):
    rows = fin.shape[1]

    def layer(l):
        return jnp.minimum(l, LAYERS - 1)

    def whole(part):
        return pl.BlockSpec(part.shape, lambda l, dp: (0,) * part.ndim)

    attn = pl.BlockSpec((1, 4, rows, 192), lambda l, dp: (layer(l), 0, 0, 0))
    mlp = pl.BlockSpec((1, 2, rows, WIDTH), lambda l, dp: (layer(l), 0, 0, 0))
    return pl.pallas_call(
        update_kernel,
        grid_spec=pltpu.PrefetchScalarGridSpec(
            num_scalar_prefetch=1,
            grid=(LAYERS + 1,),
            in_specs=[
                pl.BlockSpec((UNITS, rows, BLOCK), lambda l, dp: (LAYERS - 1 - layer(l), 0, 0)),
                pl.BlockSpec((1, 4, 192, rows), lambda l, dp: (layer(l), 0, 0, 0)),
                attn,
                attn,
                pl.BlockSpec((1, 2, rows, WIDTH), lambda l, dp: (layer(l), 0, dp[0], 0)),
                mlp,
                mlp,
                pl.BlockSpec((1, 2, ROWS, WIDTH), lambda l, dp: (layer(l), 0, 0, 0)),
                pl.BlockSpec((2, ROWS, WIDTH), lambda l, dp: (0, 0, 0)),
            ]
            + [whole(part) for part in smalls],
            out_specs=(attn,) * 3
            + (mlp,) * 3
            + (
                pl.BlockSpec((1, 2 * FRAMES, WIDTH), lambda l, dp: (layer(l), 0, 0)),
                pl.BlockSpec((2 * FRAMES, WIDTH), lambda l, dp: (0, 0)),
            )
            + tuple(whole(smalls[4 * k]) for k in range(3) for _ in range(3)),
        ),
        out_shape=(jax.ShapeDtypeStruct(moment_attn.shape, f32),) * 3
        + (jax.ShapeDtypeStruct(moment_mlp.shape, f32),) * 3
        + (
            jax.ShapeDtypeStruct((LAYERS, 2 * FRAMES, WIDTH), f32),
            jax.ShapeDtypeStruct((2 * FRAMES, WIDTH), f32),
        )
        + tuple(jax.ShapeDtypeStruct(smalls[4 * k].shape, f32) for k in range(3) for _ in range(3)),
        compiler_params=pltpu.CompilerParams(vmem_limit_bytes=60 << 20),
        name="update",
    )(dp.reshape(1), fin, w_attn, moment_attn, square_attn, w_mlp, moment_mlp, square_mlp, tops, inputs, *smalls)


def per_device(
    frames,
    cotangent,
    w_attn,
    w_mlp,
    vectors,
    head_bias,
    up_bias,
    moment_attn,
    square_attn,
    moment_mlp,
    square_mlp,
    moment_vectors,
    square_vectors,
    moment_head,
    square_head,
    moment_up,
    square_up,
):
    dp = lax.axis_index("dp")
    t = lax.axis_index("tensor")
    core = dp % 2
    dp_size = lax.axis_size("dp")

    wa = jnp.swapaxes(w_attn, 2, 3).reshape(LAYERS, 4, 4, 2, 24, WIDTH)
    wm = w_mlp.reshape(LAYERS, 2, 4, 2, 96, 2 * BLOCK)
    rows_first = jnp.swapaxes(vectors, 0, 1)
    saved = run_forward(
        frames, cotangent, wa, wm, jnp.swapaxes(head_bias, 1, 2), jnp.swapaxes(up_bias, 0, 1), rows_first
    )
    saved = (*saved[:-1], saved[-1].reshape(2, 2, 2, 2, 2, 96, BLOCK))
    fin, tops, inputs, small, _, _ = run_backward(saved, rows_first)

    if dp_size > GROUP:
        groups = [[i + GROUP * o for o in range(dp_size // GROUP)] for i in range(GROUP)]
        small = lax.psum(small, "dp", axis_index_groups=groups)
    vector_all = small[0, :, :12].reshape(LAYERS, 6, WIDTH)
    owner = t // 2
    here = jnp.where(owner == core, small[0], small[1])
    second = jnp.where(owner == 0, t % 2, 1 - t % 2)
    head_all = jnp.where(second == 0, here[:, 12], here[:, 13]).reshape(LAYERS, 2, HEADS_HERE, HEAD_DIM)
    up_all = jnp.where(second == 0, here[:, 14:16], here[:, 16:18]).reshape(LAYERS, 12, HEAD_DIM)

    def owned(param, dim):
        size = param.shape[dim] // dp_size
        return lax.dynamic_slice_in_dim(param, dp * size, size, dim)

    if dp_size > GROUP:
        rows = jnp.zeros((TOTAL, WIDTH, BLOCK), f32)
        rows = lax.dynamic_update_slice_in_dim(rows, fin, (dp % GROUP) * 96, 1)
        fin = lax.psum_scatter(rows, "dp", scatter_dimension=1, tiled=True)

    own_attn = jnp.swapaxes(owned(w_attn, 2), 2, 3)
    def swapped(axis, parts):
        return [jnp.swapaxes(part, axis, axis + 1) for part in parts]

    smalls = (
        swapped(0, (owned(vectors, 2), owned(vector_all, 2), moment_vectors, square_vectors))
        + swapped(1, (owned(head_bias, 3), owned(head_all, 3), moment_head, square_head))
        + swapped(1, (owned(up_bias, 2), owned(up_all, 2), moment_up, square_up))
    )
    done = run_update(
        dp, fin, own_attn, moment_attn, square_attn, w_mlp, moment_mlp, square_mlp, tops, inputs, smalls
    )
    matrices, (sections, upstream), done = done[:6], done[6:8], done[8:]
    done = swapped(0, done[:3]) + swapped(1, done[3:])
    return (sections, upstream, *matrices, *done)


def solution(mesh):
    in_specs = (
        P("dp", None),
        P("dp", None),
        P(None, None, None, "tensor"),
        P(None, None, None, "tensor"),
        P(),
        P(None, None, "tensor", None),
        P(None, "tensor", None),
        P(None, None, "dp", "tensor"),
        P(None, None, "dp", "tensor"),
        P(None, None, "dp", "tensor"),
        P(None, None, "dp", "tensor"),
        P(None, None, "dp"),
        P(None, None, "dp"),
        P(None, None, "tensor", "dp"),
        P(None, None, "tensor", "dp"),
        P(None, "tensor", "dp"),
        P(None, "tensor", "dp"),
    )
    out_specs = (
        P(None, "dp", None),
        P("dp", None),
        P(None, None, "dp", "tensor"),
        P(None, None, "dp", "tensor"),
        P(None, None, "dp", "tensor"),
        P(None, None, "dp", "tensor"),
        P(None, None, "dp", "tensor"),
        P(None, None, "dp", "tensor"),
        P(None, None, "dp"),
        P(None, None, "dp"),
        P(None, None, "dp"),
        P(None, None, "tensor", "dp"),
        P(None, None, "tensor", "dp"),
        P(None, None, "tensor", "dp"),
        P(None, "tensor", "dp"),
        P(None, "tensor", "dp"),
        P(None, "tensor", "dp"),
    )
    return jax.shard_map(
        per_device, mesh=mesh, in_specs=in_specs, out_specs=out_specs, check_vma=False
    )
```

```python
import math
from types import SimpleNamespace

import jax
import jax.numpy as jnp
from jax import lax
from jax.experimental import pallas as pl
from jax.experimental.pallas import tpu as pltpu
from jax.sharding import PartitionSpec as P

HEAD_DIM = 64
FRAMES = 500
ROWS = 512
LAYERS = 2
STEP = 10
WIDTH = 768
BLOCK = 384
UNITS = 6
TOTAL = LAYERS * UNITS
GROUP = 8
HEADS_HERE = 3
SLOTS = 3
LEAD = 2
SOURCE_LEAD = 5
CHUNK_TICKS = ((2, 4, 5, 7), (3, 5, 6, 8), (4, 6, 7, 9))
SPAN = 504
SECOND = 496
CHUNK = 128

ln_eps = 1e-05
beta_one = 0.9
beta_two = 0.999
adam_eps = 1e-08
decay_rate = 0.01
rate_matrix = 0.05
rate_vector = 0.2
score_scale = 1.0 / math.sqrt(HEAD_DIM)
MESH = pl.DeviceIdType.MESH
f32 = jnp.float32
bf16 = jnp.bfloat16
ANY = pl.BlockSpec(memory_space=pl.ANY)
VMEM = pl.BlockSpec(memory_space=pltpu.VMEM)


def product(left, right):
    return jnp.dot(left, right, preferred_element_type=f32)


def contract_last(left, right):
    return lax.dot_general(left, right, (((1,), (1,)), ((), ())), preferred_element_type=f32)


def contract_rows(left, right):
    return lax.dot_general(left, right, (((0,), (0,)), ((), ())), preferred_element_type=f32)


def normalize_parts(inputs):
    centre = jnp.mean(inputs, axis=-1, keepdims=True)
    centred = inputs - centre
    inverse = lax.rsqrt(jnp.mean(centred * centred, axis=-1, keepdims=True) + ln_eps)
    return centred * inverse, inverse


def normalize_back(upstream, scaled, inverse, gain):
    gain_grad = jnp.sum(upstream * scaled, axis=0)
    shift_grad = jnp.sum(upstream, axis=0)
    inner_grad = upstream * gain
    lowered = inverse * (
        inner_grad
        - jnp.mean(inner_grad, axis=-1, keepdims=True)
        - scaled * jnp.mean(inner_grad * scaled, axis=-1, keepdims=True)
    )
    return (lowered, gain_grad, shift_grad)


def gelu(before):
    return 0.5 * before * (1.0 + lax.erf(before * (1.0 / math.sqrt(2.0))))


def gelu_slope(before):
    return 0.5 * (1.0 + lax.erf(before * (1.0 / math.sqrt(2.0)))) + before * jnp.exp(
        -0.5 * before * before
    ) * (1.0 / math.sqrt(2.0 * math.pi))


def adamw_update(param, gradient, first, second, rate):
    first_new = beta_one * first + (1.0 - beta_one) * gradient
    second_new = beta_two * second + (1.0 - beta_two) * gradient * gradient
    ratio = (
        first_new
        / (1.0 - beta_one**STEP)
        / (jnp.sqrt(second_new / (1.0 - beta_two**STEP)) + adam_eps)
    )
    return (param - rate * (ratio + decay_rate * param), first_new, second_new)


def find_place():
    dp = lax.axis_index("dp")
    t = lax.axis_index("tensor")
    i = lax.rem(dp, GROUP)
    base = dp - i
    c = lax.rem(i, 2)
    x = lax.rem(i // 2, 2)
    y = i // 4
    up = 1 - 2 * c
    level = c * (3 - t) + (1 - c) * t

    def at(cc, xx, yy):
        return base + 4 * yy + 2 * xx + cc

    return SimpleNamespace(
        t=t,
        c=c,
        x=x,
        y=y,
        q=2 * y + x,
        qx=2 * y + 1 - x,
        qy=2 * (1 - y) + x,
        qd=2 * (1 - y) + 1 - x,
        level=level,
        partner=(at(1 - c, x, y), t),
        xn=(at(c, 1 - x, y), t),
        yn=(at(c, x, 1 - y), t),
        above=(dp, t + up),
        below=(dp, t - up),
    )


def greet(p):
    barrier = pltpu.get_barrier_semaphore()

    def signal(device):
        pl.semaphore_signal(barrier, inc=1, device_id=device, device_id_type=MESH)

    signal(p.partner)
    signal(p.xn)
    signal(p.yn)

    @pl.when(p.level < 3)
    def _():
        signal(p.above)

    @pl.when(p.level > 0)
    def _():
        signal(p.below)

    inner = (p.level > 0) & (p.level < 3)

    @pl.when(inner)
    def _():
        pl.semaphore_wait(barrier, 5)

    @pl.when(jnp.logical_not(inner))
    def _():
        pl.semaphore_wait(barrier, 4)


def remote(src, dst, send_sem, recv_sem, device):
    return pltpu.make_async_remote_copy(
        src_ref=src,
        dst_ref=dst,
        send_sem=send_sem,
        recv_sem=recv_sem,
        device_id=device,
        device_id_type=MESH,
    )


def local(src, dst, sem):
    return pltpu.make_async_copy(src, dst, sem)


def forward_kernel(
    frames,
    cotangent,
    wa,
    wm,
    head_bias,
    up_bias,
    vec,
    o_ct,
    o_h,
    o_m,
    o_n1,
    o_n2,
    o_qk,
    o_v,
    o_a,
    o_u,
    o_c,
    o_wa,
    o_wm,
    o_first,
    ga,
    gm,
    hb,
    ub,
    hs,
    ms,
    n1s,
    n2s,
    qks,
    vs,
    as_,
    us,
    cs,
    low_a,
    low_m,
    low_ct,
    part,
    other,
    rz,
    sz,
    szd,
    rx,
    sx,
    ry,
    sy,
    rxd,
    sxd,
    ryd,
    syd,
    native,
    rc,
    sc,
    scd,
    first_sem,
    bias_local,
    bias_send,
    bias_recv,
    swap_sem,
    low_sem,
    mid_sem,
    out_sem,
    grad_sem,
):
    p = find_place()
    greet(p)
    level = p.level
    when = pl.when

    def quarter(ref, i, q, h=None):
        lead = (slice(None), q) if i < 2 else (q,)
        return ref.at[lead if h is None else (*lead, h)]

    def block(l, i):
        if i < 2:
            return wa.at[l, pl.ds(2 * i, 2)]
        return wm.at[l, (i - 2) // 2, :, :, :, pl.ds(BLOCK * (i % 2), BLOCK)]

    def block_quarter(l, i):
        if i < 2:
            return wa.at[l, pl.ds(2 * i, 2), p.q]
        return wm.at[l, (i - 2) // 2, p.q, :, :, pl.ds(BLOCK * (i % 2), BLOCK)]

    def held(l, i, j):
        return ga.at[j, l, i] if i < 2 else gm.at[j, l, i - 2]

    def z_copy(src, l, i, j, device, send_sem):
        return remote(src, quarter(held(l, i, j), i, p.q), send_sem, rz.at[UNITS * l + i, j], device)

    def plane_copy(l, i, j, q, h, send_sem, recv_sem, device):
        here = quarter(held(l, i, j), i, q, h)
        u = UNITS * l + i
        return remote(here, here, send_sem.at[u, j], recv_sem.at[u, j], device)

    def x_copy(l, i, j, q):
        return plane_copy(l, i, j, q, None, sx, rx, p.xn)

    def y_copy(l, i, j, q):
        return plane_copy(l, i, j, q, None, sy, ry, p.yn)

    def xd_copy(l, i, j, q):
        return plane_copy(l, i, j, q, 1, sxd, rxd, p.xn)

    def yd_copy(l, i, j, q):
        return plane_copy(l, i, j, q, 0, syd, ryd, p.yn)

    def source(l, i):
        u = UNITS * l + i

        @when(level == 0)
        def _():
            z_copy(block_quarter(l, i), l, i, 0, p.above, sz.at[u, 0]).start()
            local(block(l, i), held(l, i, 0), native.at[u]).start()

        @when(level == 1)
        def _():
            z_copy(block_quarter(l, i), l, i, 1, p.above, sz.at[u, 1]).start()
            z_copy(block_quarter(l, i), l, i, 1, p.below, szd.at[u]).start()
            local(block(l, i), held(l, i, 1), native.at[u]).start()

    def stage_one(l, i):
        u = UNITS * l + i
        for j in (1, 0):

            @when(level != j)
            def _(j=j):
                here = quarter(held(l, i, j), i, p.q)
                z_copy(here, l, i, j, p.above, sz.at[u, j]).wait_recv()

                @when((level == 2) | ((level == 1) if j == 0 else (level == 2)))
                def _():
                    z_copy(here, l, i, j, p.above, sz.at[u, j]).start()

                x_copy(l, i, j, p.q).start()
                y_copy(l, i, j, p.q).start()

    def stage_two(l, i):
        for j in (1, 0):

            @when(level != j)
            def _(j=j):
                x_copy(l, i, j, p.qx).wait_recv()
                yd_copy(l, i, j, p.qx).start()
                y_copy(l, i, j, p.qy).wait_recv()
                xd_copy(l, i, j, p.qy).start()

    def finish(l, i):
        u = UNITS * l + i
        for j in range(2):

            @when(level != j)
            def _(j=j):
                yd_copy(l, i, j, p.qd).wait_recv()
                xd_copy(l, i, j, p.qd).wait_recv()

            @when(level == j)
            def _(j=j):
                local(block(l, i), held(l, i, j), native.at[u]).wait()

    last = LAYERS - 1
    alone = UNITS - 1

    def chunk_copy(src, q, j, device, send_sem):
        return remote(src, held(last, alone, j).at[q], send_sem, rc.at[q, j], device)

    def chunk_source(q):
        here = wm.at[last, 1, q, :, :, pl.ds(BLOCK, BLOCK)]

        @when(level == 0)
        def _():
            chunk_copy(here, q, 0, p.above, sc.at[q, 0]).start()

        @when(level == 1)
        def _():
            chunk_copy(here, q, 1, p.above, sc.at[q, 1]).start()
            chunk_copy(here, q, 1, p.below, scd.at[q]).start()

    def chunk_pass(q, at, j):
        @when(level == at)
        def _():
            here = held(last, alone, j).at[q]
            chunk_copy(here, q, j, p.above, sc.at[q, j]).wait_recv()
            chunk_copy(here, q, j, p.above, sc.at[q, j]).start()

    def chunk_native(method):
        for j in range(2):

            @when(level == j)
            def _(j=j):
                getattr(local(block(last, alone), held(last, alone, j), native.at[TOTAL - 1]), method)()

    def chunk_finish():
        for q in range(4):
            here = held(last, alone, 0).at[q]

            @when((level == 3))
            def _(q=q, here=here):
                chunk_copy(here, q, 0, p.above, sc.at[q, 0]).wait_recv()

            @when((level == 3) | (level == 0))
            def _(q=q, here=here):
                chunk_copy(here, q, 1, p.above, sc.at[q, 1]).wait_recv()

        chunk_native("wait")

    def chunk_drain():
        for q in range(4):
            here = held(last, alone, 0).at[q]

            @when(level < 3)
            def _(q=q, here=here):
                chunk_copy(here, q, 0, p.above, sc.at[q, 0]).wait_send()

            @when((level == 1) | (level == 2))
            def _(q=q, here=here):
                chunk_copy(here, q, 1, p.above, sc.at[q, 1]).wait_send()

            @when(level == 1)
            def _(q=q, here=here):
                chunk_copy(here, q, 1, p.below, scd.at[q]).wait_send()

    def chunk_step(l, i):
        for q in range(4):
            for at, tick_of in enumerate(CHUNK_TICKS):
                there, k = divmod(tick_of[q], UNITS)
                if k == i:

                    @when(l == there)
                    def _(q=q, at=at):
                        if at == 0:
                            chunk_source(q)
                        elif at == 1:
                            chunk_pass(q, 1, 0)
                        else:
                            chunk_pass(q, 2, 1)
                            chunk_pass(q, 2, 0)

    def ahead(step, l, i, by):
        k = i + by
        there = l + k // UNITS
        if k % UNITS == alone:
            when(there < last)(lambda: step(there, alone))
        elif k < UNITS:
            step(l, k)
        else:
            when(there < LAYERS)(lambda: step(there, k % UNITS))

    def serve(l, k):
        ahead(source, l, k, SOURCE_LEAD)
        ahead(stage_one, l, k, LEAD)
        ahead(stage_two, l, k, LEAD - 1)

    def tick(l, i):
        if i < 2:
            serve(l, i)
        elif i < UNITS - 1:
            serve(l, i + 1)
        chunk_step(l, i)
        if i == alone:
            when(l < last)(lambda: finish(l, i))
            when(l == last)(chunk_finish)
        else:
            finish(l, i)

    mine = (p.t // 2) == p.c
    clip = lax.rem(p.t, 2)
    span = pl.ds(pl.multiple_of(clip * SECOND, 8), SPAN)
    inputs = (
        (frames.at[span], part.at[pl.ds(0, SPAN)]),
        (cotangent.at[span], ms.at[1, pl.ds(0, SPAN)]),
    )

    def input_copies(k):
        src, dst = inputs[k]
        return (
            local(src, dst, first_sem.at[k]),
            remote(src, dst, first_sem.at[2 + k], first_sem.at[4 + k], p.partner),
        )

    def wait_input(k):
        here, there = input_copies(k)

        @when(mine)
        def _():
            here.wait()
            there.wait_send()

        @when(jnp.logical_not(mine))
        def _():
            there.wait_recv()

    def take_clip(target, raw):
        @when(clip == 0)
        def _():
            target[0:FRAMES] = raw[0:FRAMES]

        @when(clip == 1)
        def _():
            target[0:FRAMES] = raw[FRAMES - SECOND : SPAN]

        target[FRAMES:ROWS] = jnp.zeros((ROWS - FRAMES, WIDTH), f32)

    kept_biases = ((head_bias, hb), (up_bias, ub))

    def bias_copy(src, n, j, m, device):
        return remote(src, kept_biases[n][1].at[j], bias_send.at[n, m], bias_recv.at[n, j], device)

    def bias_source():
        for n, (src, dst) in enumerate(kept_biases):

            @when(level == 0)
            def _(n=n, src=src, dst=dst):
                local(src, dst.at[0], bias_local.at[n]).start()
                bias_copy(src, n, 0, 0, p.above).start()

            @when(level == 1)
            def _(n=n, src=src, dst=dst):
                local(src, dst.at[1], bias_local.at[n]).start()
                bias_copy(src, n, 1, 1, p.above).start()
                bias_copy(src, n, 1, 2, p.below).start()

    def bias_pass():
        for n, (src, dst) in enumerate(kept_biases):

            @when(level != 0)
            def _(n=n, src=src):
                bias_copy(src, n, 0, 0, p.above).wait_recv()

            @when((level == 1) | (level == 2))
            def _(n=n, dst=dst):
                bias_copy(dst.at[0], n, 0, 0, p.above).start()

            @when(level != 1)
            def _(n=n, src=src):
                bias_copy(src, n, 1, 1, p.above).wait_recv()

            @when(level == 2)
            def _(n=n, dst=dst):
                bias_copy(dst.at[1], n, 1, 1, p.above).start()

            @when(level < 2)
            def _(n=n, src=src, dst=dst):
                local(src, dst.at[0], bias_local.at[n]).wait()

    def bias_drain():
        for n, (src, dst) in enumerate(kept_biases):

            @when(level < 3)
            def _(n=n, src=src):
                bias_copy(src, n, 0, 0, p.above).wait_send()

            @when((level == 1) | (level == 2))
            def _(n=n, src=src):
                bias_copy(src, n, 1, 1, p.above).wait_send()

            @when(level == 1)
            def _(n=n, src=src):
                bias_copy(src, n, 1, 2, p.below).wait_send()

    def head_row(j, l, n):
        return jnp.concatenate([hb[j, l, h, n : n + 1, :] for h in range(HEADS_HERE)], axis=-1)

    def up_row(j, l, k):
        return jnp.concatenate([ub[j, r, pl.ds(l, 1), :] for r in range(6 * k, 6 * k + 6)], axis=-1)

    @when(mine)
    def _():
        for copy in input_copies(0):
            copy.start()

    bias_source()
    for i in range(SOURCE_LEAD):
        source(0, i)

    @when(mine)
    def _():
        for copy in input_copies(1):
            copy.start()

    chunk_native("start")
    stage_one(0, 0)
    wait_input(0)
    take_clip(hs.at[0], part)
    for i in range(1, LEAD):
        stage_one(0, i)
        stage_two(0, i - 1)
    bias_pass()
    wait_input(1)
    take_clip(part, ms.at[1])
    keep_cotangent = local(part, o_ct, out_sem.at[0, 1])
    keep_cotangent.start()
    low_ct[...] = part[...].astype(bf16)
    keep_cotangent.wait()

    def keep_low(l, i):
        if i < 2:
            slots, slot, target = low_a, 0, lambda j: o_wa.at[j, l, i]
        else:
            slots, slot, target = low_m, i % 2, lambda j: o_wm.at[j, l, i - 2]
        sems = 0 if i < 2 else 1 + i % 2

        def copy(j):
            return local(slots.at[slot, j], target(j), low_sem.at[sems, j])

        def drain():
            for j in range(2):
                copy(j).wait()

        if i in (1, 4, 5):
            drain()
        else:
            when(l > 0)(drain)
        for j in range(2):
            if i < 2:
                slots[slot, j] = ga[j, l, i].reshape(BLOCK, WIDTH).astype(bf16)
            else:
                slots[slot, j] = gm[j, l, i - 2].reshape(WIDTH, BLOCK).astype(bf16)
            copy(j).start()
        return slots.at[slot]

    def swap(slot):
        copy = remote(part, other.at[slot], swap_sem.at[slot], swap_sem.at[2 + slot], p.partner)
        copy.start()
        copy.wait()

    def out_copies(l):
        return [
            local(hs.at[l], o_h.at[l], out_sem.at[0, l]),
            local(ms.at[l], o_m.at[l], out_sem.at[1, l]),
            local(n1s.at[l], o_n1.at[l], out_sem.at[2, l]),
            local(n2s.at[l], o_n2.at[l], out_sem.at[3, l]),
            local(qks.at[l], o_qk.at[l], out_sem.at[4, l]),
            local(vs.at[l], o_v.at[l], out_sem.at[5, l]),
            local(as_.at[l], o_a.at[l], out_sem.at[6, l]),
        ]

    def mid_copies(l, i):
        k = i - 2
        return [
            local(us.at[:, k], o_u.at[l, :, k], mid_sem.at[0, k]),
            local(cs.at[:, k], o_c.at[l, :, k], mid_sem.at[1, k]),
        ]

    def drain(u, carry):
        l = u // UNITS
        for j in range(2):

            @when((level < 3) if j == 0 else ((level == 1) | (level == 2)))
            def _(j=j):
                z_copy(gm.at[j, l, 0, p.q], l, 2, j, p.above, sz.at[u, j]).wait_send()

            @when(level != j)
            def _(j=j):
                whole, half = gm.at[j, l, 0, p.q], gm.at[j, l, 0, p.q, 0]
                remote(whole, whole, sx.at[u, j], rx.at[u, j], p.xn).wait_send()
                remote(whole, whole, sy.at[u, j], ry.at[u, j], p.yn).wait_send()
                remote(half, half, sxd.at[u, j], rxd.at[u, j], p.xn).wait_send()
                remote(half, half, syd.at[u, j], ryd.at[u, j], p.yn).wait_send()

        @when(level == 1)
        def _():
            z_copy(gm.at[1, l, 0, p.q], l, 2, 1, p.below, szd.at[u]).wait_send()

        return carry

    def grad_copy(k, j):
        return local(gm.at[j, 0, k], o_first.at[k, j], grad_sem.at[k, j])

    def layer(l, carry):
        params = [vec[k, pl.ds(l, 1)] for k in range(6)]

        tick(l, 0)
        scaled, _ = normalize_parts(hs[l])
        n1s[l] = (scaled * params[0] + params[1]).astype(bf16)
        weights = keep_low(l, 0)
        for j in range(2):
            both = contract_last(n1s[l], weights[j])
            shift = jnp.concatenate([head_row(j, l, 0), jnp.zeros((1, 192), f32)], axis=-1)
            qks[l, j] = (both + shift).astype(bf16)

        tick(l, 1)
        weights = keep_low(l, 1)
        keep = lax.broadcasted_iota(jnp.int32, (ROWS, ROWS), 1) < FRAMES
        for j in range(2):
            vs[l, j] = (
                contract_last(n1s[l], weights[j, 0:192]) + head_row(j, l, 1)
            ).astype(bf16)

            heads = []
            for h in range(HEADS_HERE):
                cols = slice(HEAD_DIM * h, HEAD_DIM * (h + 1))
                k_cols = slice(192 + HEAD_DIM * h, 192 + HEAD_DIM * (h + 1))
                scores = contract_last(qks[l, j, :, cols], qks[l, j, :, k_cols]) * score_scale
                scores = jnp.where(keep, scores, -1e30)
                weight = jnp.exp(scores - jnp.max(scores, axis=-1, keepdims=True))
                weight = weight * (1.0 / jnp.sum(weight, axis=-1, keepdims=True))
                heads.append(product(weight.astype(bf16), vs[l, j, :, cols]))
            as_[l, j] = jnp.concatenate(heads, axis=-1).astype(bf16)
            if j == 0:
                serve(l, 2)
        part[...] = product(as_[l, 0], weights[0, 192:384])
        part[...] += product(as_[l, 1], weights[1, 192:384])
        swap(0)
        ms[l] = hs[l] + (part[...] + other[0]) + params[4]
        scaled, _ = normalize_parts(ms[l])
        n2s[l] = (scaled * params[2] + params[3]).astype(bf16)
        for copy in out_copies(l):
            copy.start()

        for i in (2, 3):
            tick(l, i)
            weights = keep_low(l, i)

            @when(l > 0)
            def _(i=i):
                for copy in mid_copies(l - 1, i):
                    copy.wait()

            for j in range(2):
                before = product(n2s[l], weights[j]) + up_row(j, l, i - 2)
                us[j, i - 2] = before
                cs[j, i - 2] = gelu(before).astype(bf16)
            for copy in mid_copies(l, i):
                copy.start()

        for i in (4, 5):
            tick(l, i)
            weights = keep_low(l, i)

            @when(l == last)
            def _(i=i):
                if i == 4:
                    lax.fori_loop(0, UNITS, drain, 0)
                for j in range(2):
                    gm[j, 0, i - 4] = contract_rows(low_ct[...], cs[j, i - 4]).reshape(4, 2, 96, BLOCK)
                    grad_copy(i - 4, j).start()

            @when(l < LAYERS - 1)
            def _(i=i, weights=weights):
                for j in range(2):
                    term = contract_last(cs[j, i - 4], weights[j])
                    if i == 4 and j == 0:
                        part[...] = term
                    else:
                        part[...] += term

        @when(l < LAYERS - 1)
        def _():
            swap(1)
            hs[l + 1] = ms[l] + (part[...] + other[1]) + params[5]

        return carry

    lax.fori_loop(0, LAYERS, layer, 0)

    for i in (2, 3):
        for copy in mid_copies(last, i):
            copy.wait()
    for l in range(LAYERS):
        for copy in out_copies(l):
            copy.wait()
    for j in range(2):
        local(low_a.at[0, j], o_wa.at[j, last, 1], low_sem.at[0, j]).wait()
        for slot in range(2):
            local(low_m.at[slot, j], o_wm.at[j, last, 2 + slot], low_sem.at[1 + slot, j]).wait()
    for k in range(2):
        for j in range(2):
            grad_copy(k, j).wait()
    bias_drain()
    chunk_drain()

    lax.fori_loop(UNITS, TOTAL - 1, drain, 0)


def run_forward(frames, cotangent, wa, wm, head_bias, up_bias, vectors):
    def hbm(shape, kind):
        return jax.ShapeDtypeStruct(shape, kind)

    dma = pltpu.SemaphoreType.DMA
    per_unit = dma((TOTAL, 2))
    return pl.pallas_call(
        forward_kernel,
        out_shape=(
            hbm((ROWS, WIDTH), f32),
            hbm((LAYERS, ROWS, WIDTH), f32),
            hbm((LAYERS, ROWS, WIDTH), f32),
            hbm((LAYERS, ROWS, WIDTH), bf16),
            hbm((LAYERS, ROWS, WIDTH), bf16),
            hbm((LAYERS, 2, ROWS, BLOCK), bf16),
            hbm((LAYERS, 2, ROWS, 192), bf16),
            hbm((LAYERS, 2, ROWS, 192), bf16),
            hbm((LAYERS, 2, 2, ROWS, BLOCK), f32),
            hbm((LAYERS, 2, 2, ROWS, BLOCK), bf16),
            hbm((2, LAYERS, 2, BLOCK, WIDTH), bf16),
            hbm((2, LAYERS, 4, WIDTH, BLOCK), bf16),
            hbm((2, 2, 4, 2, 96, BLOCK), f32),
        ),
        in_specs=[ANY, ANY, ANY, ANY, ANY, ANY, VMEM],
        out_specs=(ANY,) * 13,
        scratch_shapes=[
            pltpu.VMEM((2, LAYERS, 2, 2, 4, 2, 24, WIDTH), f32),
            pltpu.VMEM((2, LAYERS, 4, 4, 2, 96, BLOCK), f32),
            pltpu.VMEM((2, *head_bias.shape), f32),
            pltpu.VMEM((2, *up_bias.shape), f32),
            pltpu.VMEM((LAYERS, ROWS, WIDTH), f32),
            pltpu.VMEM((LAYERS, ROWS, WIDTH), f32),
            pltpu.VMEM((LAYERS, ROWS, WIDTH), bf16),
            pltpu.VMEM((LAYERS, ROWS, WIDTH), bf16),
            pltpu.VMEM((LAYERS, 2, ROWS, BLOCK), bf16),
            pltpu.VMEM((LAYERS, 2, ROWS, 192), bf16),
            pltpu.VMEM((LAYERS, 2, ROWS, 192), bf16),
            pltpu.VMEM((2, 2, ROWS, BLOCK), f32),
            pltpu.VMEM((2, 2, ROWS, BLOCK), bf16),
            pltpu.VMEM((1, 2, BLOCK, WIDTH), bf16),
            pltpu.VMEM((2, 2, WIDTH, BLOCK), bf16),
            pltpu.VMEM((ROWS, WIDTH), bf16),
            pltpu.VMEM((ROWS, WIDTH), f32),
            pltpu.VMEM((2, ROWS, WIDTH), f32),
            per_unit,
            per_unit,
            dma((TOTAL,)),
            per_unit,
            per_unit,
            per_unit,
            per_unit,
            per_unit,
            per_unit,
            per_unit,
            per_unit,
            dma((TOTAL,)),
            dma((4, 2)),
            dma((4, 2)),
            dma((4,)),
            dma((6,)),
            dma((2,)),
            dma((2, 3)),
            dma((2, 2)),
            dma((4,)),
            dma((3, 2)),
            dma((2, 2)),
            dma((7, LAYERS)),
            dma((2, 2)),
        ],
        compiler_params=pltpu.CompilerParams(
            collective_id=0, has_side_effects=True, vmem_limit_bytes=63 << 20
        ),
        name="gather_forward",
    )(frames, cotangent, wa, wm, head_bias, up_bias, vectors)


def backward_kernel(
    i_ct,
    i_h,
    i_m,
    i_n1,
    i_n2,
    i_qk,
    i_v,
    i_a,
    i_u,
    i_c,
    i_wa,
    i_wm,
    i_first,
    vec,
    o_fin,
    o_top,
    o_input,
    o_small,
    o_src,
    o_grads,
    held,
    x1,
    y1,
    x2,
    y2,
    own,
    zin,
    zup,
    stage,
    whole_in,
    whole_up,
    grad,
    part,
    other,
    h_in,
    m_in,
    n1,
    n2,
    qk,
    v,
    a,
    u_in,
    c_in,
    wa,
    wm,
    low,
    dqk,
    dv,
    small,
    small_in,
    sx1,
    rx1,
    sy1,
    ry1,
    sx2,
    rx2,
    sy2,
    ry2,
    szd,
    rzd,
    szu,
    rzu,
    sfin,
    rfin,
    lfin,
    act_send,
    act_recv,
    act_sem,
    load_sem,
    unit_sem,
    stage_sem,
    held_sem,
    swap_sem,
    small_send,
    small_recv,
    once_sem,
    whole_send,
    whole_recv,
    whole_send_up,
    whole_recv_up,
):
    p = find_place()
    level = p.level
    when = pl.when

    chunks = ROWS // CHUNK
    n_chunks = 3 * chunks
    slot_of = (p.c, 1 - p.c)

    def act_part(ref, k):
        return ref.at[pl.ds(pl.multiple_of(k % chunks * CHUNK, CHUNK), CHUNK)]

    def act_all(n, j):
        return o_top.at[n, slot_of[j]] if n < LAYERS else o_input.at[slot_of[j]]

    def act_own(k):
        return act_part(o_src.at[k // chunks - 1], k)

    def act_there(j, k):
        return act_part(act_all(k // chunks, j), k)

    def act_copy(src, j, k, m, device):
        return remote(src, act_there(j, k), act_send.at[k, m], act_recv.at[k, j], device)

    def act_step(s, ticks):
        def set_out(k):
            src = act_part(i_h.at[1], k) if k < chunks else act_own(k)

            @when(level == 0)
            def _():
                act_copy(src, 0, k, 0, p.above).start()

            @when(level == 1)
            def _():
                act_copy(src, 1, k, 1, p.above).start()
                act_copy(src, 1, k, 2, p.below).start()

        def pass_on(k, at, j):
            @when(level == at)
            def _():
                act_copy(act_there(j, k), j, k, j, p.above).wait_recv()
                act_copy(act_there(j, k), j, k, j, p.above).start()

        for t in ticks:
            outs, firsts, seconds = ([k for k in range(n_chunks) if row[k] == t] for row in ACT_TICKS)
            if outs or firsts or seconds:

                @when(s == t)
                def _(outs=outs, firsts=firsts, seconds=seconds):
                    for k in outs:
                        set_out(k)
                    for k in firsts:
                        pass_on(k, 1, 0)
                    for k in seconds:
                        pass_on(k, 2, 1)
                        pass_on(k, 2, 0)

    def act_drain(k):
        @when(level < 3)
        def _():
            act_copy(act_there(0, k), 0, k, 0, p.above).wait_send()

        @when((level == 1) | (level == 2))
        def _():
            act_copy(act_there(1, k), 1, k, 1, p.above).wait_send()

        @when(level == 1)
        def _():
            act_copy(act_there(1, k), 1, k, 2, p.below).wait_send()

        @when(level == 3)
        def _():
            act_copy(act_there(0, k), 0, k, 0, p.above).wait_recv()

        @when((level == 0) | (level == 3))
        def _():
            act_copy(act_there(1, k), 1, k, 1, p.above).wait_recv()

    def act_local(src, n, method):
        for j in range(2):

            @when(level == j)
            def _(j=j):
                getattr(local(src, act_all(n, j), act_sem.at[n]), method)()

    def x1_copy(w):
        return remote(held.at[w, :, :, 1 - p.x, 0], x1.at[w], sx1.at[w], rx1.at[w], p.xn)

    def y1_copy(w):
        return remote(held.at[w, :, 1 - p.y, :, 1], y1.at[w], sy1.at[w], ry1.at[w], p.yn)

    def x2_copy(w):
        return remote(held.at[w, :, p.y, 1 - p.x, 1], x2.at[w], sx2.at[w], rx2.at[w], p.xn)

    def y2_copy(w):
        return remote(held.at[w, :, 1 - p.y, p.x, 0], y2.at[w], sy2.at[w], ry2.at[w], p.yn)

    def down_copy(u, j):
        return remote(own.at[u, j], zin.at[u, j], szd.at[u, j], rzd.at[u, j], p.below)

    def up_copy(u):
        return remote(own.at[u, 1], zup.at[u], szu.at[u], rzu.at[u], p.above)

    def fin_copy(u, j):
        return remote(own.at[u, j, 1 - p.c], o_fin.at[u], sfin.at[u], rfin.at[u], p.partner)

    def fin_local(u, j):
        return local(own.at[u, j, p.c], o_fin.at[u], lfin.at[u])

    def sent(w):
        x1_copy(w).wait_send()
        y1_copy(w).wait_send()
        x2_copy(w).wait_send()
        y2_copy(w).wait_send()

    def stage_one(u):
        w = lax.rem(u, SLOTS)
        when(u >= SLOTS)(lambda: sent(w))
        when(u >= 2)(lambda: local(o_grads.at[u - 2], held.at[w], held_sem.at[w]).start())
        local(i_first.at[0], held.at[w], held_sem.at[w]).wait()
        x1_copy(w).start()
        y1_copy(w).start()

    def stage_two(u):
        w = lax.rem(u, SLOTS)
        x1_copy(w).wait_recv()
        held[w, :, 1 - p.y, p.x, 0] += x1[w, :, 1 - p.y]
        held[w, :, p.y, p.x, 0] += x1[w, :, p.y]
        y1_copy(w).wait_recv()
        held[w, :, p.y, 1 - p.x, 1] += y1[w, :, 1 - p.x]
        held[w, :, p.y, p.x, 1] += y1[w, :, p.x]
        y2_copy(w).start()
        x2_copy(w).start()

    def stage_three(u):
        w = lax.rem(u, SLOTS)
        y2_copy(w).wait_recv()
        own[u, :, 0] = held[w, :, p.y, p.x, 0] + y2[w]
        x2_copy(w).wait_recv()
        own[u, :, 1] = held[w, :, p.y, p.x, 1] + x2[w]

        @when(level == 3)
        def _():
            down_copy(u, 0).start()
            down_copy(u, 1).start()

        @when(level == 0)
        def _():
            up_copy(u).start()

    def level_two(u):
        for j in range(2):
            down_copy(u, j).wait_recv()
            own[u, j] += zin[u, j]
            down_copy(u, j).start()

    def level_one(u):
        down_copy(u, 0).wait_recv()
        own[u, 0] += zin[u, 0]
        down_copy(u, 0).start()
        down_copy(u, 1).wait_recv()
        up_copy(u).wait_recv()
        own[u, 1] += zin[u, 1] + zup[u]
        fin_local(u, 1).start()
        fin_copy(u, 1).start()

    def level_zero(u):
        down_copy(u, 0).wait_recv()
        own[u, 0] += zin[u, 0]
        fin_local(u, 0).start()
        fin_copy(u, 0).start()

    def whole_part(ref, e):
        return ref.at[e // 2, e % 2]

    def whole_copy(e, j):
        here, there = whole_part(stage.at[j], e), whole_part(whole_in.at[j], e)
        return remote(here, there, whole_send.at[e, j], whole_recv.at[e, j], p.below)

    def whole_copy_up(e):
        here, there = whole_part(stage.at[1], e), whole_part(whole_up, e)
        return remote(here, there, whole_send_up.at[e], whole_recv_up.at[e], p.above)

    def whole_add(e, j):
        whole_copy(e, j).wait_recv()
        stage[j, e // 2, e % 2] += whole_in[j, e // 2, e % 2]

    lane = (TOTAL - 1) % SLOTS

    def plane_copies(j):
        return (
            remote(stage.at[j, :, 1 - p.x, 0], x1.at[lane, 0], sx1.at[lane], rx1.at[lane], p.xn),
            remote(stage.at[j, 1 - p.y, :, 1], y1.at[lane, 0], sy1.at[lane], ry1.at[lane], p.yn),
            remote(stage.at[j, p.y, 1 - p.x, 1], x2.at[lane, 0], sx2.at[lane], rx2.at[lane], p.xn),
            remote(stage.at[j, 1 - p.y, p.x, 0], y2.at[lane, 0], sy2.at[lane], ry2.at[lane], p.yn),
        )

    def whole_fin(j):
        u = TOTAL - 1
        return (
            local(stage.at[j, p.y, p.x, p.c], o_fin.at[u], lfin.at[u]),
            remote(stage.at[j, p.y, p.x, 1 - p.c], o_fin.at[u], sfin.at[u], rfin.at[u], p.partner),
        )

    def whole_step(s):
        first = STEPS_INSIDE

        for e in range(4):

            @when((s == first + e) & (level == 0))
            def _(e=e):
                whole_copy_up(e).start()

            @when((s == first + e) & (level == 3))
            def _(e=e):
                whole_copy(e, 0).start()
                whole_copy(e, 1).start()

            @when((s == first + e + 1) & (level == 2))
            def _(e=e):
                for j in range(2):
                    whole_add(e, j)
                    whole_copy(e, j).start()

            @when((s == first + e + 2) & (level == 1))
            def _(e=e):
                whole_add(e, 0)
                whole_copy(e, 0).start()
                whole_add(e, 1)
                whole_copy_up(e).wait_recv()
                stage[1, e // 2, e % 2] += whole_up[e // 2, e % 2]

            @when((s == first + e + 3) & (level == 0))
            def _(e=e):
                whole_add(e, 0)

        for j in range(2):
            a1, b1, a2, b2 = plane_copies(j)

            @when((s == first + 6) & (level == j))
            def _(a1=a1, b1=b1):
                sent(lane)
                a1.start()
                b1.start()

            @when((s == first + 7) & (level == j))
            def _(j=j, a1=a1, b1=b1, a2=a2, b2=b2):
                a1.wait()
                stage[j, 1 - p.y, p.x, 0] += x1[lane, 0, 1 - p.y]
                stage[j, p.y, p.x, 0] += x1[lane, 0, p.y]
                b1.wait()
                stage[j, p.y, 1 - p.x, 1] += y1[lane, 0, 1 - p.x]
                stage[j, p.y, p.x, 1] += y1[lane, 0, p.x]
                a2.start()
                b2.start()

            @when((s == first + 8) & (level == j))
            def _(j=j, a2=a2, b2=b2):
                b2.wait()
                stage[j, p.y, p.x, 0] += y2[lane, 0]
                a2.wait()
                stage[j, p.y, p.x, 1] += x2[lane, 0]
                for copy in whole_fin(j):
                    copy.start()

    def whole_drain():
        for e in range(4):

            @when(level > 0)
            def _(e=e):
                whole_copy(e, 0).wait_send()

            @when(level > 1)
            def _(e=e):
                whole_copy(e, 1).wait_send()

            @when(level == 0)
            def _(e=e):
                whole_copy_up(e).wait_send()

        here, there = whole_fin(0)

        @when(level < 2)
        def _():
            here.wait()
            there.wait_send()

        @when(level > 1)
        def _():
            sent(lane)
            there.wait_recv()

    def service(s, ticks):
        def unit(k, step, extra=True):
            when((k >= 0) & (k < TOTAL - 1) & extra)(lambda: step(k))

        unit(s - 1, stage_two)
        unit(s - 2, stage_three)
        unit(s + 1, stage_one)
        for at, step, (least, slack, until) in zip((2, 1, 0), (level_two, level_one, level_zero), Z_TICKS):

            def done(t):
                late = jnp.where(t < until, slack, 0)
                return jnp.clip(t + 1 - least - late, 0, TOTAL - 1)

            def one(u, carry, step=step):
                step(u)
                return carry

            @when(level == at)
            def _(done=done, one=one):
                lax.fori_loop(done(s - 1), done(s), one, 0)

        act_step(s, ticks)

    def loads(l):
        whole = (
            (i_c, c_in),
            (i_n2, n2),
            (i_m, m_in),
            (i_a, a),
            (i_qk, qk),
            (i_v, v),
            (i_n1, n1),
            (i_h, h_in),
        )
        return [local(src.at[l], dst, load_sem.at[n]) for n, (src, dst) in enumerate(whole)]

    def load_u(l, h):
        return local(i_u.at[l, :, h], u_in, unit_sem.at[5])

    def load_a(l):
        return local(i_wa.at[:, l], wa, unit_sem.at[4])

    def load_m(l, i):
        return local(i_wm.at[:, l, i], wm.at[:, i], unit_sem.at[i])

    def start_loads(l):
        fetch = loads(l)
        load_u(l, 0).start()
        for i in (2, 0, 3, 1):
            load_m(l, i).start()
        for copy in fetch:
            copy.start()
        load_a(l).start()

    def swap(slot):
        copy = remote(part, other.at[slot], swap_sem.at[slot], swap_sem.at[2 + slot], p.partner)
        copy.start()
        copy.wait()

    def put(u, j, value):
        stage[j] = value.reshape(2, 2, 2, 96, BLOCK)
        when(u < TOTAL - 1)(lambda: local(stage.at[j], o_grads.at[u - 2, j], stage_sem.at[j]).start())

    def put_done(u):
        @when(u < TOTAL - 1)
        def _():
            for j in range(2):
                local(stage.at[j], o_grads.at[u - 2, j], stage_sem.at[j]).wait()

    def small_row(l, row, value):
        small[l, row : row + 1] = value[:, :BLOCK]
        small[l, row + 1 : row + 2] = value[:, BLOCK:]

    def norm_back(slot, l, source, gain, first):
        def rows_of(r, carry):
            rows = pl.ds(pl.multiple_of(r * 128, 128), 128)
            upstream = part[rows] + other[slot, rows]
            scaled, inverse = normalize_parts(source[rows])
            lowered, gain_grad, shift_grad = normalize_back(upstream, scaled, inverse, gain)
            value = grad[rows] + lowered
            grad[rows] = value
            rounded = value.astype(bf16)
            low[rows] = rounded
            bias_grad = jnp.sum(rounded.astype(f32), axis=0)
            return (
                carry[0] + gain_grad.reshape(1, WIDTH),
                carry[1] + shift_grad.reshape(1, WIDTH),
                carry[2] + bias_grad.reshape(1, WIDTH),
            )

        zero = jnp.zeros((1, WIDTH), f32)
        sums = lax.fori_loop(0, ROWS // 128, rows_of, (zero, zero, zero))
        small_row(l, first, sums[0])
        small_row(l, first + 2, sums[1])
        return sums[2]

    keep = lax.broadcasted_iota(jnp.int32, (ROWS, ROWS), 1) < FRAMES

    def attention_back(j, carry):
        mixture_back = contract_last(low[...], wa[j, 1, 192:384]).astype(bf16)
        parts = ([], [], [])
        for h in range(HEADS_HERE):
            cols = slice(HEAD_DIM * h, HEAD_DIM * (h + 1))
            k_cols = slice(192 + HEAD_DIM * h, 192 + HEAD_DIM * (h + 1))
            qh, kh, vh, dah = qk[j, :, cols], qk[j, :, k_cols], v[j, :, cols], mixture_back[:, cols]
            scores = jnp.where(keep, contract_last(qh, kh) * score_scale, -1e30)
            weight = jnp.exp(scores - jnp.max(scores, axis=-1, keepdims=True))
            weight = weight * (1.0 / jnp.sum(weight, axis=-1, keepdims=True))
            prob_grad = contract_last(dah, vh)
            centre = jnp.sum(prob_grad * weight, axis=-1, keepdims=True)
            score_back = (weight * (prob_grad - centre)).astype(bf16)
            parts[0].append((product(score_back, kh) * score_scale).astype(bf16))
            parts[1].append((contract_rows(score_back, qh) * score_scale).astype(bf16))
            parts[2].append(contract_rows(weight.astype(bf16), dah).astype(bf16))
        dqk[j] = jnp.concatenate(parts[0] + parts[1], axis=-1)
        dv[j] = jnp.concatenate(parts[2], axis=-1)
        return carry

    for u in range(2):
        local(i_first.at[u], held.at[u], held_sem.at[u]).start()
    local(i_ct, grad, once_sem.at[0]).start()
    start_loads(LAYERS - 1)
    greet(p)
    stage_one(0)
    service(0, (0,))
    small[...] = jnp.zeros_like(small)

    def layer(step, carry):
        l = LAYERS - 1 - step
        u0 = UNITS * step
        params = [vec[k, pl.ds(l, 1)] for k in range(6)]
        fetch = loads(l)

        @when(step == 0)
        def _():
            local(i_ct, grad, once_sem.at[0]).wait()
            low[...] = grad[...].astype(bf16)
            small_row(l, 10, jnp.sum(low[...].astype(f32), axis=0, keepdims=True))

        fetch[0].wait()

        @when(step > 0)
        def _():
            for i in (0, 1):
                for j in range(2):
                    put(u0 + i, j, contract_rows(low[...], c_in[j, i]))
                put_done(u0 + i)
            service(3, (3,))

        fetch[1].wait()
        for i in (2, 3):
            h = i - 2
            load_m(l, 2 + h).wait()
            load_m(l, h).wait()
            load_u(l, h).wait()
            for j in range(2):
                back = (product(low[...], wm[j, 2 + h]) * gelu_slope(u_in[j])).astype(bf16)
                row = 14 + 2 * j + h
                small[l, row : row + 1] = jnp.sum(back.astype(f32), axis=0, keepdims=True)
                put(u0 + i, j, contract_rows(n2[...], back))
                term = contract_last(back, wm[j, h])
                if h == 0 and j == 0:
                    part[...] = term
                else:
                    part[...] += term
            if h == 0:
                load_u(l, 1).start()
            put_done(u0 + i)
            if i == 2:
                when(step == 0)(lambda: service(1, (1,)))
            else:
                when(step > 0)(lambda: service(4, (4,)))
        swap(step)
        fetch[2].wait()
        small_row(l, 8, norm_back(step, l, m_in, params[2], 4))

        @when(step == 0)
        def _():
            for h in range(2):
                for j in range(2):
                    term = contract_last(c_in[j, h], wm[j, 2 + h])
                    if h == 0 and j == 0:
                        part[...] = term
                    else:
                        part[...] += term
            swap(1)
            part[...] = m_in[...] + (part[...] + other[1]) + params[5]
            keep_top = local(part, o_src.at[0], once_sem.at[1])
            keep_top.start()
            act_local(part, 1, "start")
            keep_top.wait()
            act_local(part, 1, "wait")
            service(2, (2,))

        for copy in fetch[3:]:
            copy.wait()
        load_a(l).wait()
        when(step == 0)(lambda: act_local(h_in, 0, "start"))
        lax.fori_loop(0, 2, attention_back, 0)
        when(step > 0)(lambda: service(5, (5,)))
        for j in range(2):
            stage[j, :, :, :, :, 0:192] = contract_rows(n1[...], dv[j]).reshape(2, 2, 2, 96, 192)
            stage[j, :, :, :, :, 192:384] = contract_rows(low[...], a[j]).reshape(2, 2, 2, 96, 192)
            local(stage.at[j], o_grads.at[u0 + 2, j], stage_sem.at[j]).start()
        put_done(u0 + 4)
        for j in range(2):
            put(u0 + 5, j, contract_rows(n1[...], dqk[j]))
            sums = jnp.sum(dqk[j].astype(f32), axis=0, keepdims=True)
            small[l, 12 + j : 13 + j, 0:192] = sums[:, 0:192]
            small[l, 12 + j : 13 + j, 192:384] = jnp.sum(dv[j].astype(f32), axis=0, keepdims=True)
            term = product(dqk[j], wa[j, 0]) + product(dv[j], wa[j, 1, 0:192])
            if j == 0:
                part[...] = term
            else:
                part[...] += term
        put_done(u0 + 5)
        swap(0)
        down_sum = norm_back(0, l, h_in, params[0], 0)

        @when(l > 0)
        def _():
            small_row(l - 1, 10, down_sum)

        @when(step == 0)
        def _():
            act_local(h_in, 0, "wait")
            start_loads(LAYERS - 2)

        return carry

    lax.fori_loop(0, LAYERS, layer, 0)
    keep_grad = local(grad, o_src.at[1], once_sem.at[1])
    keep_grad.start()
    act_local(grad, 2, "start")
    keep_grad.wait()

    def small_copy(m, device):
        return remote(small, small_in.at[m], small_send.at[m], small_recv.at[m], device)

    def small_add(m, device):
        small_copy(m, device).wait()
        small[...] += small_in[m]

    first = STEPS_INSIDE

    def small_step(s):
        @when(s == first)
        def _():
            small_copy(0, p.xn).start()

        @when(s == first + 1)
        def _():
            small_add(0, p.xn)
            small_copy(1, p.yn).start()

        @when(s == first + 2)
        def _():
            small_add(1, p.yn)

            @when((level == 0) | (level == 2))
            def _():
                small_copy(2, p.above).start()

            @when((level == 1) | (level == 3))
            def _():
                small_copy(2, p.below).start()

        @when(s == first + 3)
        def _():
            small_add(2, p.above)

            @when(level == 1)
            def _():
                small_copy(3, p.above).start()

            @when(level == 2)
            def _():
                small_copy(3, p.below).start()

        @when(s == first + 4)
        def _():
            @when((level == 1) | (level == 2))
            def _():
                small_add(3, p.above)

            @when(level == 1)
            def _():
                small_copy(4, p.below).start()

            @when(level == 2)
            def _():
                small_copy(4, p.above).start()

        @when(s == first + 5)
        def _():
            @when((level == 0) | (level == 3))
            def _():
                small_copy(4, p.above).wait_recv()
                small[...] = small_in[4]

            small_copy(5, p.partner).start()
            local(small, o_small.at[0], once_sem.at[2]).start()

        @when(s == first + 6)
        def _():
            small_copy(5, p.partner).wait()
            local(small_in.at[5], o_small.at[1], once_sem.at[3]).start()

            @when((level == 1) | (level == 2))
            def _():
                small_copy(4, p.above).wait_send()

    def step_after(s, carry):
        small_step(s)
        service(s, range(STEPS_INSIDE, LAST_TICK))
        whole_step(s)
        return carry

    lax.fori_loop(first, LAST_TICK, step_after, 0)

    for w in range(SLOTS):
        if w != lane:
            sent(w)
    whole_drain()

    def drain(u, carry):
        @when(level > 0)
        def _():
            down_copy(u, 0).wait_send()

        @when(level > 1)
        def _():
            down_copy(u, 1).wait_send()
            fin_copy(u, 0).wait_recv()

        @when(level == 0)
        def _():
            up_copy(u).wait_send()

        @when(level < 2)
        def _():
            fin_local(u, 0).wait()
            fin_copy(u, 0).wait_send()

        return carry

    lax.fori_loop(0, TOTAL - 1, drain, 0)
    for k in range(n_chunks):
        act_drain(k)

    act_local(grad, 2, "wait")
    local(small, o_small.at[0], once_sem.at[2]).wait()
    local(small_in.at[5], o_small.at[1], once_sem.at[3]).wait()


LAST_TICK = TOTAL + 4
ACT_TICKS = ((0, 0, 0, 0, 2, 2, 3, 3, 6, 6, 6, 6), (1, 1, 1, 1, 3, 3, 4, 4, 7, 7, 7, 7), (2, 2, 2, 2, 4, 4, 5, 5, 8, 8, 8, 8))
Z_TICKS = ((3, 0, 0), (4, 0, 0), (5, 0, 0))
STEPS_INSIDE = 1 + 2 + 3
SMALL = (LAYERS, 24, BLOCK)


def run_backward(saved, vectors):
    dma = pltpu.SemaphoreType.DMA
    slots = dma((SLOTS,))
    units = dma((TOTAL,))
    pair = dma((TOTAL, 2))
    return pl.pallas_call(
        backward_kernel,
        out_shape=(
            jax.ShapeDtypeStruct((TOTAL, 96, BLOCK), f32),
            jax.ShapeDtypeStruct((LAYERS, 2, ROWS, WIDTH), f32),
            jax.ShapeDtypeStruct((2, ROWS, WIDTH), f32),
            jax.ShapeDtypeStruct((2, *SMALL), f32),
            jax.ShapeDtypeStruct((2, ROWS, WIDTH), f32),
            jax.ShapeDtypeStruct((TOTAL - 3, 2, 2, 2, 2, 96, BLOCK), f32),
        ),
        in_specs=[ANY] * 13 + [VMEM],
        out_specs=(ANY,) * 6,
        scratch_shapes=[
            pltpu.VMEM((SLOTS, 2, 2, 2, 2, 96, BLOCK), f32),
            pltpu.VMEM((SLOTS, 2, 2, 96, BLOCK), f32),
            pltpu.VMEM((SLOTS, 2, 2, 96, BLOCK), f32),
            pltpu.VMEM((SLOTS, 2, 96, BLOCK), f32),
            pltpu.VMEM((SLOTS, 2, 96, BLOCK), f32),
            pltpu.VMEM((TOTAL - 1, 2, 2, 96, BLOCK), f32),
            pltpu.VMEM((TOTAL - 1, 2, 2, 96, BLOCK), f32),
            pltpu.VMEM((TOTAL - 1, 2, 96, BLOCK), f32),
            pltpu.VMEM((2, 2, 2, 2, 96, BLOCK), f32),
            pltpu.VMEM((2, 2, 2, 2, 96, BLOCK), f32),
            pltpu.VMEM((2, 2, 2, 96, BLOCK), f32),
            pltpu.VMEM((ROWS, WIDTH), f32),
            pltpu.VMEM((ROWS, WIDTH), f32),
            pltpu.VMEM((2, ROWS, WIDTH), f32),
            pltpu.VMEM((ROWS, WIDTH), f32),
            pltpu.VMEM((ROWS, WIDTH), f32),
            pltpu.VMEM((ROWS, WIDTH), bf16),
            pltpu.VMEM((ROWS, WIDTH), bf16),
            pltpu.VMEM((2, ROWS, BLOCK), bf16),
            pltpu.VMEM((2, ROWS, 192), bf16),
            pltpu.VMEM((2, ROWS, 192), bf16),
            pltpu.VMEM((2, ROWS, BLOCK), f32),
            pltpu.VMEM((2, 2, ROWS, BLOCK), bf16),
            pltpu.VMEM((2, 2, BLOCK, WIDTH), bf16),
            pltpu.VMEM((2, 4, WIDTH, BLOCK), bf16),
            pltpu.VMEM((ROWS, WIDTH), bf16),
            pltpu.VMEM((2, ROWS, BLOCK), bf16),
            pltpu.VMEM((2, ROWS, 192), bf16),
            pltpu.VMEM(SMALL, f32),
            pltpu.VMEM((6, *SMALL), f32),
            slots,
            slots,
            slots,
            slots,
            slots,
            slots,
            slots,
            slots,
            pair,
            pair,
            units,
            units,
            units,
            units,
            units,
            dma((TOTAL, 3)),
            dma((TOTAL, 2)),
            dma((3,)),
            dma((8,)),
            dma((6,)),
            dma((2,)),
            slots,
            dma((4,)),
            dma((6,)),
            dma((6,)),
            dma((4,)),
            dma((4, 2)),
            dma((4, 2)),
            dma((4,)),
            dma((4,)),
        ],
        compiler_params=pltpu.CompilerParams(
            collective_id=1, has_side_effects=True, vmem_limit_bytes=63 << 20
        ),
        name="backward_reduce",
    )(*saved, vectors)


def update_kernel(dp, fin, pa, ma, sa, pm, mm, sm, tops, inputs, *refs):
    smalls, (na, fa, va, nm, fm, vm, sections, upstream), small_outs = refs[:12], refs[12:20], refs[20:]
    step = pl.program_id(0)

    def join(clips, target):
        target[:FRAMES] = clips[0, :FRAMES]
        target[FRAMES:] = clips[1, :FRAMES]

    @pl.when(step < LAYERS)
    def _():
        for k in range(4):
            grad = fin[5 - k // 2, :, 192 * (k % 2) : 192 * (k % 2 + 1)]
            na[0, k], fa[0, k], va[0, k] = adamw_update(pa[0, k].T, grad, ma[0, k], sa[0, k], rate_matrix)
        for k in range(2):
            for h in range(2):
                cols = slice(BLOCK * h, BLOCK * (h + 1))
                grad = fin[2 - 2 * k + h]
                nm[0, k, :, cols], fm[0, k, :, cols], vm[0, k, :, cols] = adamw_update(
                    pm[0, k, :, cols], grad, mm[0, k, :, cols], sm[0, k, :, cols], rate_matrix
                )
        join(tops.at[0], sections.at[0])

    @pl.when(step == LAYERS)
    def _():
        join(inputs, upstream)
        for k in range(3):
            done = adamw_update(*(ref[...] for ref in smalls[4 * k : 4 * k + 4]), rate_vector)
            for ref, value in zip(small_outs[3 * k : 3 * k + 3], done):
                ref[...] = value


def run_update(dp, fin, w_attn, moment_attn, square_attn, w_mlp, moment_mlp, square_mlp, tops, inputs, smalls):
    rows = fin.shape[1]

    def layer(l):
        return jnp.minimum(l, LAYERS - 1)

    def whole(part):
        return pl.BlockSpec(part.shape, lambda l, dp: (0,) * part.ndim)

    attn = pl.BlockSpec((1, 4, rows, 192), lambda l, dp: (layer(l), 0, 0, 0))
    mlp = pl.BlockSpec((1, 2, rows, WIDTH), lambda l, dp: (layer(l), 0, 0, 0))
    return pl.pallas_call(
        update_kernel,
        grid_spec=pltpu.PrefetchScalarGridSpec(
            num_scalar_prefetch=1,
            grid=(LAYERS + 1,),
            in_specs=[
                pl.BlockSpec((UNITS, rows, BLOCK), lambda l, dp: (LAYERS - 1 - layer(l), 0, 0)),
                pl.BlockSpec((1, 4, 192, rows), lambda l, dp: (layer(l), 0, 0, 0)),
                attn,
                attn,
                pl.BlockSpec((1, 2, rows, WIDTH), lambda l, dp: (layer(l), 0, dp[0], 0)),
                mlp,
                mlp,
                pl.BlockSpec((1, 2, ROWS, WIDTH), lambda l, dp: (layer(l), 0, 0, 0)),
                pl.BlockSpec((2, ROWS, WIDTH), lambda l, dp: (0, 0, 0)),
            ]
            + [whole(part) for part in smalls],
            out_specs=(attn,) * 3
            + (mlp,) * 3
            + (
                pl.BlockSpec((1, 2 * FRAMES, WIDTH), lambda l, dp: (layer(l), 0, 0)),
                pl.BlockSpec((2 * FRAMES, WIDTH), lambda l, dp: (0, 0)),
            )
            + tuple(whole(smalls[4 * k]) for k in range(3) for _ in range(3)),
        ),
        out_shape=(jax.ShapeDtypeStruct(moment_attn.shape, f32),) * 3
        + (jax.ShapeDtypeStruct(moment_mlp.shape, f32),) * 3
        + (
            jax.ShapeDtypeStruct((LAYERS, 2 * FRAMES, WIDTH), f32),
            jax.ShapeDtypeStruct((2 * FRAMES, WIDTH), f32),
        )
        + tuple(jax.ShapeDtypeStruct(smalls[4 * k].shape, f32) for k in range(3) for _ in range(3)),
        compiler_params=pltpu.CompilerParams(vmem_limit_bytes=60 << 20),
        name="update",
    )(dp.reshape(1), fin, w_attn, moment_attn, square_attn, w_mlp, moment_mlp, square_mlp, tops, inputs, *smalls)


def per_device(
    frames,
    cotangent,
    w_attn,
    w_mlp,
    vectors,
    head_bias,
    up_bias,
    moment_attn,
    square_attn,
    moment_mlp,
    square_mlp,
    moment_vectors,
    square_vectors,
    moment_head,
    square_head,
    moment_up,
    square_up,
):
    dp = lax.axis_index("dp")
    t = lax.axis_index("tensor")
    core = dp % 2
    dp_size = lax.axis_size("dp")

    wa = jnp.swapaxes(w_attn, 2, 3).reshape(LAYERS, 4, 4, 2, 24, WIDTH)
    wm = w_mlp.reshape(LAYERS, 2, 4, 2, 96, 2 * BLOCK)
    rows_first = jnp.swapaxes(vectors, 0, 1)
    saved = run_forward(
        frames, cotangent, wa, wm, jnp.swapaxes(head_bias, 1, 2), jnp.swapaxes(up_bias, 0, 1), rows_first
    )
    saved = (*saved[:-1], saved[-1].reshape(2, 2, 2, 2, 2, 96, BLOCK))
    fin, tops, inputs, small, _, _ = run_backward(saved, rows_first)

    if dp_size > GROUP:
        groups = [[i + GROUP * o for o in range(dp_size // GROUP)] for i in range(GROUP)]
        small = lax.psum(small, "dp", axis_index_groups=groups)
    vector_all = small[0, :, :12].reshape(LAYERS, 6, WIDTH)
    owner = t // 2
    here = jnp.where(owner == core, small[0], small[1])
    second = jnp.where(owner == 0, t % 2, 1 - t % 2)
    head_all = jnp.where(second == 0, here[:, 12], here[:, 13]).reshape(LAYERS, 2, HEADS_HERE, HEAD_DIM)
    up_all = jnp.where(second == 0, here[:, 14:16], here[:, 16:18]).reshape(LAYERS, 12, HEAD_DIM)

    def owned(param, dim):
        size = param.shape[dim] // dp_size
        return lax.dynamic_slice_in_dim(param, dp * size, size, dim)

    if dp_size > GROUP:
        rows = jnp.zeros((TOTAL, WIDTH, BLOCK), f32)
        rows = lax.dynamic_update_slice_in_dim(rows, fin, (dp % GROUP) * 96, 1)
        fin = lax.psum_scatter(rows, "dp", scatter_dimension=1, tiled=True)

    own_attn = jnp.swapaxes(owned(w_attn, 2), 2, 3)
    def swapped(axis, parts):
        return [jnp.swapaxes(part, axis, axis + 1) for part in parts]

    smalls = (
        swapped(0, (owned(vectors, 2), owned(vector_all, 2), moment_vectors, square_vectors))
        + swapped(1, (owned(head_bias, 3), owned(head_all, 3), moment_head, square_head))
        + swapped(1, (owned(up_bias, 2), owned(up_all, 2), moment_up, square_up))
    )
    done = run_update(
        dp, fin, own_attn, moment_attn, square_attn, w_mlp, moment_mlp, square_mlp, tops, inputs, smalls
    )
    matrices, (sections, upstream), done = done[:6], done[6:8], done[8:]
    done = swapped(0, done[:3]) + swapped(1, done[3:])
    return (sections, upstream, *matrices, *done)


def solution(mesh):
    in_specs = (
        P("dp", None),
        P("dp", None),
        P(None, None, None, "tensor"),
        P(None, None, None, "tensor"),
        P(),
        P(None, None, "tensor", None),
        P(None, "tensor", None),
        P(None, None, "dp", "tensor"),
        P(None, None, "dp", "tensor"),
        P(None, None, "dp", "tensor"),
        P(None, None, "dp", "tensor"),
        P(None, None, "dp"),
        P(None, None, "dp"),
        P(None, None, "tensor", "dp"),
        P(None, None, "tensor", "dp"),
        P(None, "tensor", "dp"),
        P(None, "tensor", "dp"),
    )
    out_specs = (
        P(None, "dp", None),
        P("dp", None),
        P(None, None, "dp", "tensor"),
        P(None, None, "dp", "tensor"),
        P(None, None, "dp", "tensor"),
        P(None, None, "dp", "tensor"),
        P(None, None, "dp", "tensor"),
        P(None, None, "dp", "tensor"),
        P(None, None, "dp"),
        P(None, None, "dp"),
        P(None, None, "dp"),
        P(None, None, "tensor", "dp"),
        P(None, None, "tensor", "dp"),
        P(None, None, "tensor", "dp"),
        P(None, "tensor", "dp"),
        P(None, "tensor", "dp"),
        P(None, "tensor", "dp"),
    )
    return jax.shard_map(
        per_device, mesh=mesh, in_specs=in_specs, out_specs=out_specs, check_vma=False
    )
```

```python
import math
from types import SimpleNamespace

import jax
import jax.numpy as jnp
from jax import lax
from jax.experimental import pallas as pl
from jax.experimental.pallas import tpu as pltpu
from jax.sharding import PartitionSpec as P

HEAD_DIM = 64
FRAMES = 500
ROWS = 512
LAYERS = 2
STEP = 10
WIDTH = 768
BLOCK = 384
UNITS = 6
TOTAL = LAYERS * UNITS
GROUP = 8
HEADS_HERE = 3
SLOTS = 3
LEAD = 2
SOURCE_LEAD = 5
CHUNK_TICKS = ((2, 4, 5, 7), (3, 5, 6, 8), (4, 6, 7, 9))
SPAN = 504
SECOND = 496
CHUNK = 128

ln_eps = 1e-05
beta_one = 0.9
beta_two = 0.999
adam_eps = 1e-08
decay_rate = 0.01
rate_matrix = 0.05
rate_vector = 0.2
score_scale = 1.0 / math.sqrt(HEAD_DIM)
MESH = pl.DeviceIdType.MESH
f32 = jnp.float32
bf16 = jnp.bfloat16
ANY = pl.BlockSpec(memory_space=pl.ANY)
VMEM = pl.BlockSpec(memory_space=pltpu.VMEM)


def product(left, right):
    return jnp.dot(left, right, preferred_element_type=f32)


def contract_last(left, right):
    return lax.dot_general(left, right, (((1,), (1,)), ((), ())), preferred_element_type=f32)


def contract_rows(left, right):
    return lax.dot_general(left, right, (((0,), (0,)), ((), ())), preferred_element_type=f32)


def normalize_parts(inputs):
    centre = jnp.mean(inputs, axis=-1, keepdims=True)
    centred = inputs - centre
    inverse = lax.rsqrt(jnp.mean(centred * centred, axis=-1, keepdims=True) + ln_eps)
    return centred * inverse, inverse


def normalize_back(upstream, scaled, inverse, gain):
    gain_grad = jnp.sum(upstream * scaled, axis=0)
    shift_grad = jnp.sum(upstream, axis=0)
    inner_grad = upstream * gain
    lowered = inverse * (
        inner_grad
        - jnp.mean(inner_grad, axis=-1, keepdims=True)
        - scaled * jnp.mean(inner_grad * scaled, axis=-1, keepdims=True)
    )
    return (lowered, gain_grad, shift_grad)


def gelu(before):
    return 0.5 * before * (1.0 + lax.erf(before * (1.0 / math.sqrt(2.0))))


def gelu_slope(before):
    return 0.5 * (1.0 + lax.erf(before * (1.0 / math.sqrt(2.0)))) + before * jnp.exp(
        -0.5 * before * before
    ) * (1.0 / math.sqrt(2.0 * math.pi))


def adamw_update(param, gradient, first, second, rate):
    first_new = beta_one * first + (1.0 - beta_one) * gradient
    second_new = beta_two * second + (1.0 - beta_two) * gradient * gradient
    ratio = (
        first_new
        / (1.0 - beta_one**STEP)
        / (jnp.sqrt(second_new / (1.0 - beta_two**STEP)) + adam_eps)
    )
    return (param - rate * (ratio + decay_rate * param), first_new, second_new)


def find_place():
    dp = lax.axis_index("dp")
    t = lax.axis_index("tensor")
    i = lax.rem(dp, GROUP)
    base = dp - i
    c = lax.rem(i, 2)
    x = lax.rem(i // 2, 2)
    y = i // 4
    up = 1 - 2 * c
    level = c * (3 - t) + (1 - c) * t

    def at(cc, xx, yy):
        return base + 4 * yy + 2 * xx + cc

    return SimpleNamespace(
        t=t,
        c=c,
        x=x,
        y=y,
        q=2 * y + x,
        qx=2 * y + 1 - x,
        qy=2 * (1 - y) + x,
        qd=2 * (1 - y) + 1 - x,
        level=level,
        partner=(at(1 - c, x, y), t),
        xn=(at(c, 1 - x, y), t),
        yn=(at(c, x, 1 - y), t),
        above=(dp, t + up),
        below=(dp, t - up),
    )


def greet(p):
    barrier = pltpu.get_barrier_semaphore()

    def signal(device):
        pl.semaphore_signal(barrier, inc=1, device_id=device, device_id_type=MESH)

    signal(p.partner)
    signal(p.xn)
    signal(p.yn)

    @pl.when(p.level < 3)
    def _():
        signal(p.above)

    @pl.when(p.level > 0)
    def _():
        signal(p.below)

    inner = (p.level > 0) & (p.level < 3)

    @pl.when(inner)
    def _():
        pl.semaphore_wait(barrier, 5)

    @pl.when(jnp.logical_not(inner))
    def _():
        pl.semaphore_wait(barrier, 4)


def remote(src, dst, send_sem, recv_sem, device):
    return pltpu.make_async_remote_copy(
        src_ref=src,
        dst_ref=dst,
        send_sem=send_sem,
        recv_sem=recv_sem,
        device_id=device,
        device_id_type=MESH,
    )


def local(src, dst, sem):
    return pltpu.make_async_copy(src, dst, sem)


def forward_kernel(
    frames,
    cotangent,
    wa,
    wm,
    head_bias,
    up_bias,
    vec,
    o_ct,
    o_h,
    o_m,
    o_n1,
    o_n2,
    o_qk,
    o_v,
    o_a,
    o_u,
    o_c,
    o_wa,
    o_wm,
    o_first,
    ga,
    gm,
    hb,
    ub,
    hs,
    ms,
    n1s,
    n2s,
    qks,
    vs,
    as_,
    us,
    cs,
    low_a,
    low_m,
    low_ct,
    part,
    other,
    rz,
    sz,
    szd,
    rx,
    sx,
    ry,
    sy,
    rxd,
    sxd,
    ryd,
    syd,
    native,
    rc,
    sc,
    scd,
    first_sem,
    bias_local,
    bias_send,
    bias_recv,
    swap_sem,
    low_sem,
    mid_sem,
    out_sem,
    grad_sem,
):
    p = find_place()
    greet(p)
    level = p.level
    when = pl.when

    def quarter(ref, i, q, h=None):
        lead = (slice(None), q) if i < 2 else (q,)
        return ref.at[lead if h is None else (*lead, h)]

    def block(l, i):
        if i < 2:
            return wa.at[l, pl.ds(2 * i, 2)]
        return wm.at[l, (i - 2) // 2, :, :, :, pl.ds(BLOCK * (i % 2), BLOCK)]

    def block_quarter(l, i):
        if i < 2:
            return wa.at[l, pl.ds(2 * i, 2), p.q]
        return wm.at[l, (i - 2) // 2, p.q, :, :, pl.ds(BLOCK * (i % 2), BLOCK)]

    def held(l, i, j):
        return ga.at[j, l, i] if i < 2 else gm.at[j, l, i - 2]

    def z_copy(src, l, i, j, device, send_sem):
        return remote(src, quarter(held(l, i, j), i, p.q), send_sem, rz.at[UNITS * l + i, j], device)

    def plane_copy(l, i, j, q, h, send_sem, recv_sem, device):
        here = quarter(held(l, i, j), i, q, h)
        u = UNITS * l + i
        return remote(here, here, send_sem.at[u, j], recv_sem.at[u, j], device)

    def x_copy(l, i, j, q):
        return plane_copy(l, i, j, q, None, sx, rx, p.xn)

    def y_copy(l, i, j, q):
        return plane_copy(l, i, j, q, None, sy, ry, p.yn)

    def xd_copy(l, i, j, q):
        return plane_copy(l, i, j, q, 1, sxd, rxd, p.xn)

    def yd_copy(l, i, j, q):
        return plane_copy(l, i, j, q, 0, syd, ryd, p.yn)

    def source(l, i):
        u = UNITS * l + i

        @when(level == 0)
        def _():
            z_copy(block_quarter(l, i), l, i, 0, p.above, sz.at[u, 0]).start()
            local(block(l, i), held(l, i, 0), native.at[u]).start()

        @when(level == 1)
        def _():
            z_copy(block_quarter(l, i), l, i, 1, p.above, sz.at[u, 1]).start()
            z_copy(block_quarter(l, i), l, i, 1, p.below, szd.at[u]).start()
            local(block(l, i), held(l, i, 1), native.at[u]).start()

    def stage_one(l, i):
        u = UNITS * l + i
        for j in (1, 0):

            @when(level != j)
            def _(j=j):
                here = quarter(held(l, i, j), i, p.q)
                z_copy(here, l, i, j, p.above, sz.at[u, j]).wait_recv()

                @when((level == 2) | ((level == 1) if j == 0 else (level == 2)))
                def _():
                    z_copy(here, l, i, j, p.above, sz.at[u, j]).start()

                x_copy(l, i, j, p.q).start()
                y_copy(l, i, j, p.q).start()

    def stage_two(l, i):
        for j in (1, 0):

            @when(level != j)
            def _(j=j):
                x_copy(l, i, j, p.qx).wait_recv()
                yd_copy(l, i, j, p.qx).start()
                y_copy(l, i, j, p.qy).wait_recv()
                xd_copy(l, i, j, p.qy).start()

    def finish(l, i):
        u = UNITS * l + i
        for j in range(2):

            @when(level != j)
            def _(j=j):
                yd_copy(l, i, j, p.qd).wait_recv()
                xd_copy(l, i, j, p.qd).wait_recv()

            @when(level == j)
            def _(j=j):
                local(block(l, i), held(l, i, j), native.at[u]).wait()

    last = LAYERS - 1
    alone = UNITS - 1

    def chunk_copy(src, q, j, device, send_sem):
        return remote(src, held(last, alone, j).at[q], send_sem, rc.at[q, j], device)

    def chunk_source(q):
        here = wm.at[last, 1, q, :, :, pl.ds(BLOCK, BLOCK)]

        @when(level == 0)
        def _():
            chunk_copy(here, q, 0, p.above, sc.at[q, 0]).start()

        @when(level == 1)
        def _():
            chunk_copy(here, q, 1, p.above, sc.at[q, 1]).start()
            chunk_copy(here, q, 1, p.below, scd.at[q]).start()

    def chunk_pass(q, at, j):
        @when(level == at)
        def _():
            here = held(last, alone, j).at[q]
            chunk_copy(here, q, j, p.above, sc.at[q, j]).wait_recv()
            chunk_copy(here, q, j, p.above, sc.at[q, j]).start()

    def chunk_native(method):
        for j in range(2):

            @when(level == j)
            def _(j=j):
                getattr(local(block(last, alone), held(last, alone, j), native.at[TOTAL - 1]), method)()

    def chunk_finish():
        for q in range(4):
            here = held(last, alone, 0).at[q]

            @when((level == 3))
            def _(q=q, here=here):
                chunk_copy(here, q, 0, p.above, sc.at[q, 0]).wait_recv()

            @when((level == 3) | (level == 0))
            def _(q=q, here=here):
                chunk_copy(here, q, 1, p.above, sc.at[q, 1]).wait_recv()

        chunk_native("wait")

    def chunk_drain():
        for q in range(4):
            here = held(last, alone, 0).at[q]

            @when(level < 3)
            def _(q=q, here=here):
                chunk_copy(here, q, 0, p.above, sc.at[q, 0]).wait_send()

            @when((level == 1) | (level == 2))
            def _(q=q, here=here):
                chunk_copy(here, q, 1, p.above, sc.at[q, 1]).wait_send()

            @when(level == 1)
            def _(q=q, here=here):
                chunk_copy(here, q, 1, p.below, scd.at[q]).wait_send()

    def chunk_step(l, i):
        for q in range(4):
            for at, tick_of in enumerate(CHUNK_TICKS):
                there, k = divmod(tick_of[q], UNITS)
                if k == i:

                    @when(l == there)
                    def _(q=q, at=at):
                        if at == 0:
                            chunk_source(q)
                        elif at == 1:
                            chunk_pass(q, 1, 0)
                        else:
                            chunk_pass(q, 2, 1)
                            chunk_pass(q, 2, 0)

    def ahead(step, l, i, by):
        k = i + by
        there = l + k // UNITS
        if k % UNITS == alone:
            when(there < last)(lambda: step(there, alone))
        elif k < UNITS:
            step(l, k)
        else:
            when(there < LAYERS)(lambda: step(there, k % UNITS))

    def serve(l, k):
        ahead(source, l, k, SOURCE_LEAD)
        ahead(stage_one, l, k, LEAD)
        ahead(stage_two, l, k, LEAD - 1)

    def tick(l, i):
        if i < 2:
            serve(l, i)
        elif i < UNITS - 1:
            serve(l, i + 1)
        chunk_step(l, i)
        if i == alone:
            when(l < last)(lambda: finish(l, i))
            when(l == last)(chunk_finish)
        else:
            finish(l, i)

    mine = (p.t // 2) == p.c
    clip = lax.rem(p.t, 2)
    span = pl.ds(pl.multiple_of(clip * SECOND, 8), SPAN)
    inputs = (
        (frames.at[span], part.at[pl.ds(0, SPAN)]),
        (cotangent.at[span], ms.at[1, pl.ds(0, SPAN)]),
    )

    def input_copies(k):
        src, dst = inputs[k]
        return (
            local(src, dst, first_sem.at[k]),
            remote(src, dst, first_sem.at[2 + k], first_sem.at[4 + k], p.partner),
        )

    def wait_input(k):
        here, there = input_copies(k)

        @when(mine)
        def _():
            here.wait()
            there.wait_send()

        @when(jnp.logical_not(mine))
        def _():
            there.wait_recv()

    def take_clip(target, raw):
        @when(clip == 0)
        def _():
            target[0:FRAMES] = raw[0:FRAMES]

        @when(clip == 1)
        def _():
            target[0:FRAMES] = raw[FRAMES - SECOND : SPAN]

        target[FRAMES:ROWS] = jnp.zeros((ROWS - FRAMES, WIDTH), f32)

    kept_biases = ((head_bias, hb), (up_bias, ub))

    def bias_copy(src, n, j, m, device):
        return remote(src, kept_biases[n][1].at[j], bias_send.at[n, m], bias_recv.at[n, j], device)

    def bias_source():
        for n, (src, dst) in enumerate(kept_biases):

            @when(level == 0)
            def _(n=n, src=src, dst=dst):
                local(src, dst.at[0], bias_local.at[n]).start()
                bias_copy(src, n, 0, 0, p.above).start()

            @when(level == 1)
            def _(n=n, src=src, dst=dst):
                local(src, dst.at[1], bias_local.at[n]).start()
                bias_copy(src, n, 1, 1, p.above).start()
                bias_copy(src, n, 1, 2, p.below).start()

    def bias_pass():
        for n, (src, dst) in enumerate(kept_biases):

            @when(level != 0)
            def _(n=n, src=src):
                bias_copy(src, n, 0, 0, p.above).wait_recv()

            @when((level == 1) | (level == 2))
            def _(n=n, dst=dst):
                bias_copy(dst.at[0], n, 0, 0, p.above).start()

            @when(level != 1)
            def _(n=n, src=src):
                bias_copy(src, n, 1, 1, p.above).wait_recv()

            @when(level == 2)
            def _(n=n, dst=dst):
                bias_copy(dst.at[1], n, 1, 1, p.above).start()

            @when(level < 2)
            def _(n=n, src=src, dst=dst):
                local(src, dst.at[0], bias_local.at[n]).wait()

    def bias_drain():
        for n, (src, dst) in enumerate(kept_biases):

            @when(level < 3)
            def _(n=n, src=src):
                bias_copy(src, n, 0, 0, p.above).wait_send()

            @when((level == 1) | (level == 2))
            def _(n=n, src=src):
                bias_copy(src, n, 1, 1, p.above).wait_send()

            @when(level == 1)
            def _(n=n, src=src):
                bias_copy(src, n, 1, 2, p.below).wait_send()

    def head_row(j, l, n):
        return jnp.concatenate([hb[j, l, h, n : n + 1, :] for h in range(HEADS_HERE)], axis=-1)

    def up_row(j, l, k):
        return jnp.concatenate([ub[j, r, pl.ds(l, 1), :] for r in range(6 * k, 6 * k + 6)], axis=-1)

    @when(mine)
    def _():
        for copy in input_copies(0):
            copy.start()

    bias_source()
    for i in range(SOURCE_LEAD):
        source(0, i)

    @when(mine)
    def _():
        for copy in input_copies(1):
            copy.start()

    chunk_native("start")
    stage_one(0, 0)
    wait_input(0)
    take_clip(hs.at[0], part)
    for i in range(1, LEAD):
        stage_one(0, i)
        stage_two(0, i - 1)
    bias_pass()
    wait_input(1)
    take_clip(part, ms.at[1])
    keep_cotangent = local(part, o_ct, out_sem.at[0, 1])
    keep_cotangent.start()
    low_ct[...] = part[...].astype(bf16)
    keep_cotangent.wait()

    def keep_low(l, i):
        if i < 2:
            slots, slot, target = low_a, 0, lambda j: o_wa.at[j, l, i]
        else:
            slots, slot, target = low_m, i % 2, lambda j: o_wm.at[j, l, i - 2]
        sems = 0 if i < 2 else 1 + i % 2

        def copy(j):
            return local(slots.at[slot, j], target(j), low_sem.at[sems, j])

        def drain():
            for j in range(2):
                copy(j).wait()

        if i in (1, 4, 5):
            drain()
        else:
            when(l > 0)(drain)
        for j in range(2):
            if i < 2:
                slots[slot, j] = ga[j, l, i].reshape(BLOCK, WIDTH).astype(bf16)
            else:
                slots[slot, j] = gm[j, l, i - 2].reshape(WIDTH, BLOCK).astype(bf16)
            copy(j).start()
        return slots.at[slot]

    def swap(slot):
        copy = remote(part, other.at[slot], swap_sem.at[slot], swap_sem.at[2 + slot], p.partner)
        copy.start()
        copy.wait()

    def out_copies(l):
        return [
            local(hs.at[l], o_h.at[l], out_sem.at[0, l]),
            local(ms.at[l], o_m.at[l], out_sem.at[1, l]),
            local(n1s.at[l], o_n1.at[l], out_sem.at[2, l]),
            local(n2s.at[l], o_n2.at[l], out_sem.at[3, l]),
            local(qks.at[l], o_qk.at[l], out_sem.at[4, l]),
            local(vs.at[l], o_v.at[l], out_sem.at[5, l]),
            local(as_.at[l], o_a.at[l], out_sem.at[6, l]),
        ]

    def mid_copies(l, i):
        k = i - 2
        return [
            local(us.at[:, k], o_u.at[l, :, k], mid_sem.at[0, k]),
            local(cs.at[:, k], o_c.at[l, :, k], mid_sem.at[1, k]),
        ]

    def drain(u, carry):
        l = u // UNITS
        for j in range(2):

            @when((level < 3) if j == 0 else ((level == 1) | (level == 2)))
            def _(j=j):
                z_copy(gm.at[j, l, 0, p.q], l, 2, j, p.above, sz.at[u, j]).wait_send()

            @when(level != j)
            def _(j=j):
                whole, half = gm.at[j, l, 0, p.q], gm.at[j, l, 0, p.q, 0]
                remote(whole, whole, sx.at[u, j], rx.at[u, j], p.xn).wait_send()
                remote(whole, whole, sy.at[u, j], ry.at[u, j], p.yn).wait_send()
                remote(half, half, sxd.at[u, j], rxd.at[u, j], p.xn).wait_send()
                remote(half, half, syd.at[u, j], ryd.at[u, j], p.yn).wait_send()

        @when(level == 1)
        def _():
            z_copy(gm.at[1, l, 0, p.q], l, 2, 1, p.below, szd.at[u]).wait_send()

        return carry

    def grad_copy(k, j):
        return local(gm.at[j, 0, k], o_first.at[k, j], grad_sem.at[k, j])

    def layer(l, carry):
        params = [vec[k, pl.ds(l, 1)] for k in range(6)]

        tick(l, 0)
        scaled, _ = normalize_parts(hs[l])
        n1s[l] = (scaled * params[0] + params[1]).astype(bf16)
        weights = keep_low(l, 0)
        for j in range(2):
            both = contract_last(n1s[l], weights[j])
            shift = jnp.concatenate([head_row(j, l, 0), jnp.zeros((1, 192), f32)], axis=-1)
            qks[l, j] = (both + shift).astype(bf16)

        tick(l, 1)
        weights = keep_low(l, 1)
        keep = lax.broadcasted_iota(jnp.int32, (ROWS, ROWS), 1) < FRAMES
        def attention(j, carry, weights=weights):
            vs[l, j] = (
                contract_last(n1s[l], weights[j, 0:192]) + head_row(j, l, 1)
            ).astype(bf16)

            heads = []
            for h in range(HEADS_HERE):
                cols = slice(HEAD_DIM * h, HEAD_DIM * (h + 1))
                k_cols = slice(192 + HEAD_DIM * h, 192 + HEAD_DIM * (h + 1))
                scores = contract_last(qks[l, j, :, cols], qks[l, j, :, k_cols]) * score_scale
                scores = jnp.where(keep, scores, -1e30)
                weight = jnp.exp(scores - jnp.max(scores, axis=-1, keepdims=True))
                weight = weight * (1.0 / jnp.sum(weight, axis=-1, keepdims=True))
                heads.append(product(weight.astype(bf16), vs[l, j, :, cols]))
            as_[l, j] = jnp.concatenate(heads, axis=-1).astype(bf16)
            when(j == 0)(lambda: serve(l, 2))
            return carry

        lax.fori_loop(0, 2, attention, 0)
        part[...] = product(as_[l, 0], weights[0, 192:384])
        part[...] += product(as_[l, 1], weights[1, 192:384])
        swap(0)
        ms[l] = hs[l] + (part[...] + other[0]) + params[4]
        scaled, _ = normalize_parts(ms[l])
        n2s[l] = (scaled * params[2] + params[3]).astype(bf16)
        for copy in out_copies(l):
            copy.start()

        for i in (2, 3):
            tick(l, i)
            weights = keep_low(l, i)

            @when(l > 0)
            def _(i=i):
                for copy in mid_copies(l - 1, i):
                    copy.wait()

            def hidden_units(j, carry, i=i, weights=weights):
                before = product(n2s[l], weights[j]) + up_row(j, l, i - 2)
                us[j, i - 2] = before
                cs[j, i - 2] = gelu(before).astype(bf16)
                return carry

            lax.fori_loop(0, 2, hidden_units, 0)
            for copy in mid_copies(l, i):
                copy.start()

        for i in (4, 5):
            tick(l, i)
            weights = keep_low(l, i)

            @when(l == last)
            def _(i=i):
                if i == 4:
                    lax.fori_loop(0, UNITS, drain, 0)
                for j in range(2):
                    gm[j, 0, i - 4] = contract_rows(low_ct[...], cs[j, i - 4]).reshape(4, 2, 96, BLOCK)
                    grad_copy(i - 4, j).start()

            @when(l < LAYERS - 1)
            def _(i=i, weights=weights):
                for j in range(2):
                    term = contract_last(cs[j, i - 4], weights[j])
                    if i == 4 and j == 0:
                        part[...] = term
                    else:
                        part[...] += term

        @when(l < LAYERS - 1)
        def _():
            swap(1)
            hs[l + 1] = ms[l] + (part[...] + other[1]) + params[5]

        return carry

    lax.fori_loop(0, LAYERS, layer, 0)

    for i in (2, 3):
        for copy in mid_copies(last, i):
            copy.wait()
    for l in range(LAYERS):
        for copy in out_copies(l):
            copy.wait()
    for j in range(2):
        local(low_a.at[0, j], o_wa.at[j, last, 1], low_sem.at[0, j]).wait()
        for slot in range(2):
            local(low_m.at[slot, j], o_wm.at[j, last, 2 + slot], low_sem.at[1 + slot, j]).wait()
    for k in range(2):
        for j in range(2):
            grad_copy(k, j).wait()
    bias_drain()
    chunk_drain()

    lax.fori_loop(UNITS, TOTAL - 1, drain, 0)


def run_forward(frames, cotangent, wa, wm, head_bias, up_bias, vectors):
    def hbm(shape, kind):
        return jax.ShapeDtypeStruct(shape, kind)

    dma = pltpu.SemaphoreType.DMA
    per_unit = dma((TOTAL, 2))
    return pl.pallas_call(
        forward_kernel,
        out_shape=(
            hbm((ROWS, WIDTH), f32),
            hbm((LAYERS, ROWS, WIDTH), f32),
            hbm((LAYERS, ROWS, WIDTH), f32),
            hbm((LAYERS, ROWS, WIDTH), bf16),
            hbm((LAYERS, ROWS, WIDTH), bf16),
            hbm((LAYERS, 2, ROWS, BLOCK), bf16),
            hbm((LAYERS, 2, ROWS, 192), bf16),
            hbm((LAYERS, 2, ROWS, 192), bf16),
            hbm((LAYERS, 2, 2, ROWS, BLOCK), f32),
            hbm((LAYERS, 2, 2, ROWS, BLOCK), bf16),
            hbm((2, LAYERS, 2, BLOCK, WIDTH), bf16),
            hbm((2, LAYERS, 4, WIDTH, BLOCK), bf16),
            hbm((2, 2, 4, 2, 96, BLOCK), f32),
        ),
        in_specs=[ANY, ANY, ANY, ANY, ANY, ANY, VMEM],
        out_specs=(ANY,) * 13,
        scratch_shapes=[
            pltpu.VMEM((2, LAYERS, 2, 2, 4, 2, 24, WIDTH), f32),
            pltpu.VMEM((2, LAYERS, 4, 4, 2, 96, BLOCK), f32),
            pltpu.VMEM((2, *head_bias.shape), f32),
            pltpu.VMEM((2, *up_bias.shape), f32),
            pltpu.VMEM((LAYERS, ROWS, WIDTH), f32),
            pltpu.VMEM((LAYERS, ROWS, WIDTH), f32),
            pltpu.VMEM((LAYERS, ROWS, WIDTH), bf16),
            pltpu.VMEM((LAYERS, ROWS, WIDTH), bf16),
            pltpu.VMEM((LAYERS, 2, ROWS, BLOCK), bf16),
            pltpu.VMEM((LAYERS, 2, ROWS, 192), bf16),
            pltpu.VMEM((LAYERS, 2, ROWS, 192), bf16),
            pltpu.VMEM((2, 2, ROWS, BLOCK), f32),
            pltpu.VMEM((2, 2, ROWS, BLOCK), bf16),
            pltpu.VMEM((1, 2, BLOCK, WIDTH), bf16),
            pltpu.VMEM((2, 2, WIDTH, BLOCK), bf16),
            pltpu.VMEM((ROWS, WIDTH), bf16),
            pltpu.VMEM((ROWS, WIDTH), f32),
            pltpu.VMEM((2, ROWS, WIDTH), f32),
            per_unit,
            per_unit,
            dma((TOTAL,)),
            per_unit,
            per_unit,
            per_unit,
            per_unit,
            per_unit,
            per_unit,
            per_unit,
            per_unit,
            dma((TOTAL,)),
            dma((4, 2)),
            dma((4, 2)),
            dma((4,)),
            dma((6,)),
            dma((2,)),
            dma((2, 3)),
            dma((2, 2)),
            dma((4,)),
            dma((3, 2)),
            dma((2, 2)),
            dma((7, LAYERS)),
            dma((2, 2)),
        ],
        compiler_params=pltpu.CompilerParams(
            collective_id=0, has_side_effects=True, vmem_limit_bytes=63 << 20
        ),
        name="gather_forward",
    )(frames, cotangent, wa, wm, head_bias, up_bias, vectors)


def backward_kernel(
    i_ct,
    i_h,
    i_m,
    i_n1,
    i_n2,
    i_qk,
    i_v,
    i_a,
    i_u,
    i_c,
    i_wa,
    i_wm,
    i_first,
    vec,
    o_fin,
    o_top,
    o_input,
    o_small,
    o_src,
    o_grads,
    held,
    x1,
    y1,
    x2,
    y2,
    own,
    zin,
    zup,
    stage,
    whole_in,
    whole_up,
    grad,
    part,
    other,
    h_in,
    m_in,
    n1,
    n2,
    qk,
    v,
    a,
    u_in,
    c_in,
    wa,
    wm,
    low,
    dqk,
    dv,
    small,
    small_in,
    sx1,
    rx1,
    sy1,
    ry1,
    sx2,
    rx2,
    sy2,
    ry2,
    szd,
    rzd,
    szu,
    rzu,
    sfin,
    rfin,
    lfin,
    act_send,
    act_recv,
    act_sem,
    load_sem,
    unit_sem,
    stage_sem,
    held_sem,
    swap_sem,
    small_send,
    small_recv,
    once_sem,
    whole_send,
    whole_recv,
    whole_send_up,
    whole_recv_up,
):
    p = find_place()
    level = p.level
    when = pl.when

    chunks = ROWS // CHUNK
    n_chunks = 3 * chunks
    slot_of = (p.c, 1 - p.c)

    def act_part(ref, k):
        return ref.at[pl.ds(pl.multiple_of(k % chunks * CHUNK, CHUNK), CHUNK)]

    def act_all(n, j):
        return o_top.at[n, slot_of[j]] if n < LAYERS else o_input.at[slot_of[j]]

    def act_own(k):
        return act_part(o_src.at[k // chunks - 1], k)

    def act_there(j, k):
        return act_part(act_all(k // chunks, j), k)

    def act_copy(src, j, k, m, device):
        return remote(src, act_there(j, k), act_send.at[k, m], act_recv.at[k, j], device)

    def act_step(s, ticks):
        def set_out(k):
            src = act_part(i_h.at[1], k) if k < chunks else act_own(k)

            @when(level == 0)
            def _():
                act_copy(src, 0, k, 0, p.above).start()

            @when(level == 1)
            def _():
                act_copy(src, 1, k, 1, p.above).start()
                act_copy(src, 1, k, 2, p.below).start()

        def pass_on(k, at, j):
            @when(level == at)
            def _():
                act_copy(act_there(j, k), j, k, j, p.above).wait_recv()
                act_copy(act_there(j, k), j, k, j, p.above).start()

        for t in ticks:
            outs, firsts, seconds = ([k for k in range(n_chunks) if row[k] == t] for row in ACT_TICKS)
            if outs or firsts or seconds:

                @when(s == t)
                def _(outs=outs, firsts=firsts, seconds=seconds):
                    for k in outs:
                        set_out(k)
                    for k in firsts:
                        pass_on(k, 1, 0)
                    for k in seconds:
                        pass_on(k, 2, 1)
                        pass_on(k, 2, 0)

    def act_drain(k):
        @when(level < 3)
        def _():
            act_copy(act_there(0, k), 0, k, 0, p.above).wait_send()

        @when((level == 1) | (level == 2))
        def _():
            act_copy(act_there(1, k), 1, k, 1, p.above).wait_send()

        @when(level == 1)
        def _():
            act_copy(act_there(1, k), 1, k, 2, p.below).wait_send()

        @when(level == 3)
        def _():
            act_copy(act_there(0, k), 0, k, 0, p.above).wait_recv()

        @when((level == 0) | (level == 3))
        def _():
            act_copy(act_there(1, k), 1, k, 1, p.above).wait_recv()

    def act_local(src, n, method):
        for j in range(2):

            @when(level == j)
            def _(j=j):
                getattr(local(src, act_all(n, j), act_sem.at[n]), method)()

    def x1_copy(w):
        return remote(held.at[w, :, :, 1 - p.x, 0], x1.at[w], sx1.at[w], rx1.at[w], p.xn)

    def y1_copy(w):
        return remote(held.at[w, :, 1 - p.y, :, 1], y1.at[w], sy1.at[w], ry1.at[w], p.yn)

    def x2_copy(w):
        return remote(held.at[w, :, p.y, 1 - p.x, 1], x2.at[w], sx2.at[w], rx2.at[w], p.xn)

    def y2_copy(w):
        return remote(held.at[w, :, 1 - p.y, p.x, 0], y2.at[w], sy2.at[w], ry2.at[w], p.yn)

    def down_copy(u, j):
        return remote(own.at[u, j], zin.at[u, j], szd.at[u, j], rzd.at[u, j], p.below)

    def up_copy(u):
        return remote(own.at[u, 1], zup.at[u], szu.at[u], rzu.at[u], p.above)

    def fin_copy(u, j):
        return remote(own.at[u, j, 1 - p.c], o_fin.at[u], sfin.at[u], rfin.at[u], p.partner)

    def fin_local(u, j):
        return local(own.at[u, j, p.c], o_fin.at[u], lfin.at[u])

    def sent(w):
        x1_copy(w).wait_send()
        y1_copy(w).wait_send()
        x2_copy(w).wait_send()
        y2_copy(w).wait_send()

    def stage_one(u):
        w = lax.rem(u, SLOTS)
        when(u >= SLOTS)(lambda: sent(w))
        when(u >= 2)(lambda: local(o_grads.at[u - 2], held.at[w], held_sem.at[w]).start())
        local(i_first.at[0], held.at[w], held_sem.at[w]).wait()
        x1_copy(w).start()
        y1_copy(w).start()

    def stage_two(u):
        w = lax.rem(u, SLOTS)
        x1_copy(w).wait_recv()
        held[w, :, 1 - p.y, p.x, 0] += x1[w, :, 1 - p.y]
        held[w, :, p.y, p.x, 0] += x1[w, :, p.y]
        y1_copy(w).wait_recv()
        held[w, :, p.y, 1 - p.x, 1] += y1[w, :, 1 - p.x]
        held[w, :, p.y, p.x, 1] += y1[w, :, p.x]
        y2_copy(w).start()
        x2_copy(w).start()

    def stage_three(u):
        w = lax.rem(u, SLOTS)
        y2_copy(w).wait_recv()
        own[u, :, 0] = held[w, :, p.y, p.x, 0] + y2[w]
        x2_copy(w).wait_recv()
        own[u, :, 1] = held[w, :, p.y, p.x, 1] + x2[w]

        @when(level == 3)
        def _():
            down_copy(u, 0).start()
            down_copy(u, 1).start()

        @when(level == 0)
        def _():
            up_copy(u).start()

    def level_two(u):
        for j in range(2):
            down_copy(u, j).wait_recv()
            own[u, j] += zin[u, j]
            down_copy(u, j).start()

    def level_one(u):
        down_copy(u, 0).wait_recv()
        own[u, 0] += zin[u, 0]
        down_copy(u, 0).start()
        down_copy(u, 1).wait_recv()
        up_copy(u).wait_recv()
        own[u, 1] += zin[u, 1] + zup[u]
        fin_local(u, 1).start()
        fin_copy(u, 1).start()

    def level_zero(u):
        down_copy(u, 0).wait_recv()
        own[u, 0] += zin[u, 0]
        fin_local(u, 0).start()
        fin_copy(u, 0).start()

    def whole_part(ref, e):
        return ref.at[e // 2, e % 2]

    def whole_copy(e, j):
        here, there = whole_part(stage.at[j], e), whole_part(whole_in.at[j], e)
        return remote(here, there, whole_send.at[e, j], whole_recv.at[e, j], p.below)

    def whole_copy_up(e):
        here, there = whole_part(stage.at[1], e), whole_part(whole_up, e)
        return remote(here, there, whole_send_up.at[e], whole_recv_up.at[e], p.above)

    def whole_add(e, j):
        whole_copy(e, j).wait_recv()
        stage[j, e // 2, e % 2] += whole_in[j, e // 2, e % 2]

    lane = (TOTAL - 1) % SLOTS

    def plane_copies(j):
        return (
            remote(stage.at[j, :, 1 - p.x, 0], x1.at[lane, 0], sx1.at[lane], rx1.at[lane], p.xn),
            remote(stage.at[j, 1 - p.y, :, 1], y1.at[lane, 0], sy1.at[lane], ry1.at[lane], p.yn),
            remote(stage.at[j, p.y, 1 - p.x, 1], x2.at[lane, 0], sx2.at[lane], rx2.at[lane], p.xn),
            remote(stage.at[j, 1 - p.y, p.x, 0], y2.at[lane, 0], sy2.at[lane], ry2.at[lane], p.yn),
        )

    def whole_fin(j):
        u = TOTAL - 1
        return (
            local(stage.at[j, p.y, p.x, p.c], o_fin.at[u], lfin.at[u]),
            remote(stage.at[j, p.y, p.x, 1 - p.c], o_fin.at[u], sfin.at[u], rfin.at[u], p.partner),
        )

    def whole_step(s):
        first = STEPS_INSIDE

        for e in range(4):

            @when((s == first + e) & (level == 0))
            def _(e=e):
                whole_copy_up(e).start()

            @when((s == first + e) & (level == 3))
            def _(e=e):
                whole_copy(e, 0).start()
                whole_copy(e, 1).start()

            @when((s == first + e + 1) & (level == 2))
            def _(e=e):
                for j in range(2):
                    whole_add(e, j)
                    whole_copy(e, j).start()

            @when((s == first + e + 2) & (level == 1))
            def _(e=e):
                whole_add(e, 0)
                whole_copy(e, 0).start()
                whole_add(e, 1)
                whole_copy_up(e).wait_recv()
                stage[1, e // 2, e % 2] += whole_up[e // 2, e % 2]

            @when((s == first + e + 3) & (level == 0))
            def _(e=e):
                whole_add(e, 0)

        for j in range(2):
            a1, b1, a2, b2 = plane_copies(j)

            @when((s == first + 6) & (level == j))
            def _(a1=a1, b1=b1):
                sent(lane)
                a1.start()
                b1.start()

            @when((s == first + 7) & (level == j))
            def _(j=j, a1=a1, b1=b1, a2=a2, b2=b2):
                a1.wait()
                stage[j, 1 - p.y, p.x, 0] += x1[lane, 0, 1 - p.y]
                stage[j, p.y, p.x, 0] += x1[lane, 0, p.y]
                b1.wait()
                stage[j, p.y, 1 - p.x, 1] += y1[lane, 0, 1 - p.x]
                stage[j, p.y, p.x, 1] += y1[lane, 0, p.x]
                a2.start()
                b2.start()

            @when((s == first + 8) & (level == j))
            def _(j=j, a2=a2, b2=b2):
                b2.wait()
                stage[j, p.y, p.x, 0] += y2[lane, 0]
                a2.wait()
                stage[j, p.y, p.x, 1] += x2[lane, 0]
                for copy in whole_fin(j):
                    copy.start()

    def whole_drain():
        for e in range(4):

            @when(level > 0)
            def _(e=e):
                whole_copy(e, 0).wait_send()

            @when(level > 1)
            def _(e=e):
                whole_copy(e, 1).wait_send()

            @when(level == 0)
            def _(e=e):
                whole_copy_up(e).wait_send()

        here, there = whole_fin(0)

        @when(level < 2)
        def _():
            here.wait()
            there.wait_send()

        @when(level > 1)
        def _():
            sent(lane)
            there.wait_recv()

    def service(s, ticks):
        def unit(k, step, extra=True):
            when((k >= 0) & (k < TOTAL - 1) & extra)(lambda: step(k))

        unit(s - 1, stage_two)
        unit(s - 2, stage_three)
        unit(s + 1, stage_one)
        for at, step, (least, slack, until) in zip((2, 1, 0), (level_two, level_one, level_zero), Z_TICKS):

            def done(t):
                late = jnp.where(t < until, slack, 0)
                return jnp.clip(t + 1 - least - late, 0, TOTAL - 1)

            def one(u, carry, step=step):
                step(u)
                return carry

            @when(level == at)
            def _(done=done, one=one):
                lax.fori_loop(done(s - 1), done(s), one, 0)

        act_step(s, ticks)

    def loads(l):
        whole = (
            (i_c, c_in),
            (i_n2, n2),
            (i_m, m_in),
            (i_a, a),
            (i_qk, qk),
            (i_v, v),
            (i_n1, n1),
            (i_h, h_in),
        )
        return [local(src.at[l], dst, load_sem.at[n]) for n, (src, dst) in enumerate(whole)]

    def load_u(l, h):
        return local(i_u.at[l, :, h], u_in, unit_sem.at[5])

    def load_a(l):
        return local(i_wa.at[:, l], wa, unit_sem.at[4])

    def load_m(l, i):
        return local(i_wm.at[:, l, i], wm.at[:, i], unit_sem.at[i])

    def start_loads(l):
        fetch = loads(l)
        load_u(l, 0).start()
        for i in (2, 0, 3, 1):
            load_m(l, i).start()
        for copy in fetch:
            copy.start()
        load_a(l).start()

    def swap(slot):
        copy = remote(part, other.at[slot], swap_sem.at[slot], swap_sem.at[2 + slot], p.partner)
        copy.start()
        copy.wait()

    def put(u, j, value):
        stage[j] = value.reshape(2, 2, 2, 96, BLOCK)
        when(u < TOTAL - 1)(lambda: local(stage.at[j], o_grads.at[u - 2, j], stage_sem.at[j]).start())

    def put_done(u):
        @when(u < TOTAL - 1)
        def _():
            for j in range(2):
                local(stage.at[j], o_grads.at[u - 2, j], stage_sem.at[j]).wait()

    def small_row(l, row, value):
        small[l, row : row + 1] = value[:, :BLOCK]
        small[l, row + 1 : row + 2] = value[:, BLOCK:]

    def norm_back(slot, l, source, gain, first):
        def rows_of(r, carry):
            rows = pl.ds(pl.multiple_of(r * 128, 128), 128)
            upstream = part[rows] + other[slot, rows]
            scaled, inverse = normalize_parts(source[rows])
            lowered, gain_grad, shift_grad = normalize_back(upstream, scaled, inverse, gain)
            value = grad[rows] + lowered
            grad[rows] = value
            rounded = value.astype(bf16)
            low[rows] = rounded
            bias_grad = jnp.sum(rounded.astype(f32), axis=0)
            return (
                carry[0] + gain_grad.reshape(1, WIDTH),
                carry[1] + shift_grad.reshape(1, WIDTH),
                carry[2] + bias_grad.reshape(1, WIDTH),
            )

        zero = jnp.zeros((1, WIDTH), f32)
        sums = lax.fori_loop(0, ROWS // 128, rows_of, (zero, zero, zero))
        small_row(l, first, sums[0])
        small_row(l, first + 2, sums[1])
        return sums[2]

    keep = lax.broadcasted_iota(jnp.int32, (ROWS, ROWS), 1) < FRAMES

    def attention_back(j, carry):
        mixture_back = contract_last(low[...], wa[j, 1, 192:384]).astype(bf16)
        parts = ([], [], [])
        for h in range(HEADS_HERE):
            cols = slice(HEAD_DIM * h, HEAD_DIM * (h + 1))
            k_cols = slice(192 + HEAD_DIM * h, 192 + HEAD_DIM * (h + 1))
            qh, kh, vh, dah = qk[j, :, cols], qk[j, :, k_cols], v[j, :, cols], mixture_back[:, cols]
            scores = jnp.where(keep, contract_last(qh, kh) * score_scale, -1e30)
            weight = jnp.exp(scores - jnp.max(scores, axis=-1, keepdims=True))
            weight = weight * (1.0 / jnp.sum(weight, axis=-1, keepdims=True))
            prob_grad = contract_last(dah, vh)
            centre = jnp.sum(prob_grad * weight, axis=-1, keepdims=True)
            score_back = (weight * (prob_grad - centre)).astype(bf16)
            parts[0].append((product(score_back, kh) * score_scale).astype(bf16))
            parts[1].append((contract_rows(score_back, qh) * score_scale).astype(bf16))
            parts[2].append(contract_rows(weight.astype(bf16), dah).astype(bf16))
        dqk[j] = jnp.concatenate(parts[0] + parts[1], axis=-1)
        dv[j] = jnp.concatenate(parts[2], axis=-1)
        return carry

    for u in range(2):
        local(i_first.at[u], held.at[u], held_sem.at[u]).start()
    local(i_ct, grad, once_sem.at[0]).start()
    start_loads(LAYERS - 1)
    greet(p)
    stage_one(0)
    service(0, (0,))
    small[...] = jnp.zeros_like(small)

    def layer(step, carry):
        l = LAYERS - 1 - step
        u0 = UNITS * step
        params = [vec[k, pl.ds(l, 1)] for k in range(6)]
        fetch = loads(l)

        @when(step == 0)
        def _():
            local(i_ct, grad, once_sem.at[0]).wait()
            low[...] = grad[...].astype(bf16)
            small_row(l, 10, jnp.sum(low[...].astype(f32), axis=0, keepdims=True))

        fetch[0].wait()

        @when(step > 0)
        def _():
            for i in (0, 1):
                for j in range(2):
                    put(u0 + i, j, contract_rows(low[...], c_in[j, i]))
                put_done(u0 + i)
            service(3, (3,))

        fetch[1].wait()
        for i in (2, 3):
            h = i - 2
            load_m(l, 2 + h).wait()
            load_m(l, h).wait()
            load_u(l, h).wait()
            for j in range(2):
                back = (product(low[...], wm[j, 2 + h]) * gelu_slope(u_in[j])).astype(bf16)
                row = 14 + 2 * j + h
                small[l, row : row + 1] = jnp.sum(back.astype(f32), axis=0, keepdims=True)
                put(u0 + i, j, contract_rows(n2[...], back))
                term = contract_last(back, wm[j, h])
                if h == 0 and j == 0:
                    part[...] = term
                else:
                    part[...] += term
            if h == 0:
                load_u(l, 1).start()
            put_done(u0 + i)
            if i == 2:
                when(step == 0)(lambda: service(1, (1,)))
            else:
                when(step > 0)(lambda: service(4, (4,)))
        swap(step)
        fetch[2].wait()
        small_row(l, 8, norm_back(step, l, m_in, params[2], 4))

        @when(step == 0)
        def _():
            for h in range(2):
                for j in range(2):
                    term = contract_last(c_in[j, h], wm[j, 2 + h])
                    if h == 0 and j == 0:
                        part[...] = term
                    else:
                        part[...] += term
            swap(1)
            part[...] = m_in[...] + (part[...] + other[1]) + params[5]
            keep_top = local(part, o_src.at[0], once_sem.at[1])
            keep_top.start()
            act_local(part, 1, "start")
            keep_top.wait()
            act_local(part, 1, "wait")
            service(2, (2,))

        for copy in fetch[3:]:
            copy.wait()
        load_a(l).wait()
        when(step == 0)(lambda: act_local(h_in, 0, "start"))
        lax.fori_loop(0, 2, attention_back, 0)
        when(step > 0)(lambda: service(5, (5,)))
        for j in range(2):
            stage[j, :, :, :, :, 0:192] = contract_rows(n1[...], dv[j]).reshape(2, 2, 2, 96, 192)
            stage[j, :, :, :, :, 192:384] = contract_rows(low[...], a[j]).reshape(2, 2, 2, 96, 192)
            local(stage.at[j], o_grads.at[u0 + 2, j], stage_sem.at[j]).start()
        put_done(u0 + 4)
        for j in range(2):
            put(u0 + 5, j, contract_rows(n1[...], dqk[j]))
            sums = jnp.sum(dqk[j].astype(f32), axis=0, keepdims=True)
            small[l, 12 + j : 13 + j, 0:192] = sums[:, 0:192]
            small[l, 12 + j : 13 + j, 192:384] = jnp.sum(dv[j].astype(f32), axis=0, keepdims=True)
            term = product(dqk[j], wa[j, 0]) + product(dv[j], wa[j, 1, 0:192])
            if j == 0:
                part[...] = term
            else:
                part[...] += term
        put_done(u0 + 5)
        swap(0)
        down_sum = norm_back(0, l, h_in, params[0], 0)

        @when(l > 0)
        def _():
            small_row(l - 1, 10, down_sum)

        @when(step == 0)
        def _():
            act_local(h_in, 0, "wait")
            start_loads(LAYERS - 2)

        return carry

    lax.fori_loop(0, LAYERS, layer, 0)
    keep_grad = local(grad, o_src.at[1], once_sem.at[1])
    keep_grad.start()
    act_local(grad, 2, "start")
    keep_grad.wait()

    def small_copy(m, device):
        return remote(small, small_in.at[m], small_send.at[m], small_recv.at[m], device)

    def small_add(m, device):
        small_copy(m, device).wait()
        small[...] += small_in[m]

    first = STEPS_INSIDE

    def small_step(s):
        @when(s == first)
        def _():
            small_copy(0, p.xn).start()

        @when(s == first + 1)
        def _():
            small_add(0, p.xn)
            small_copy(1, p.yn).start()

        @when(s == first + 2)
        def _():
            small_add(1, p.yn)

            @when((level == 0) | (level == 2))
            def _():
                small_copy(2, p.above).start()

            @when((level == 1) | (level == 3))
            def _():
                small_copy(2, p.below).start()

        @when(s == first + 3)
        def _():
            small_add(2, p.above)

            @when(level == 1)
            def _():
                small_copy(3, p.above).start()

            @when(level == 2)
            def _():
                small_copy(3, p.below).start()

        @when(s == first + 4)
        def _():
            @when((level == 1) | (level == 2))
            def _():
                small_add(3, p.above)

            @when(level == 1)
            def _():
                small_copy(4, p.below).start()

            @when(level == 2)
            def _():
                small_copy(4, p.above).start()

        @when(s == first + 5)
        def _():
            @when((level == 0) | (level == 3))
            def _():
                small_copy(4, p.above).wait_recv()
                small[...] = small_in[4]

            small_copy(5, p.partner).start()
            local(small, o_small.at[0], once_sem.at[2]).start()

        @when(s == first + 6)
        def _():
            small_copy(5, p.partner).wait()
            local(small_in.at[5], o_small.at[1], once_sem.at[3]).start()

            @when((level == 1) | (level == 2))
            def _():
                small_copy(4, p.above).wait_send()

    def step_after(s, carry):
        small_step(s)
        service(s, range(STEPS_INSIDE, LAST_TICK))
        whole_step(s)
        return carry

    lax.fori_loop(first, LAST_TICK, step_after, 0)

    for w in range(SLOTS):
        if w != lane:
            sent(w)
    whole_drain()

    def drain(u, carry):
        @when(level > 0)
        def _():
            down_copy(u, 0).wait_send()

        @when(level > 1)
        def _():
            down_copy(u, 1).wait_send()
            fin_copy(u, 0).wait_recv()

        @when(level == 0)
        def _():
            up_copy(u).wait_send()

        @when(level < 2)
        def _():
            fin_local(u, 0).wait()
            fin_copy(u, 0).wait_send()

        return carry

    lax.fori_loop(0, TOTAL - 1, drain, 0)
    for k in range(n_chunks):
        act_drain(k)

    act_local(grad, 2, "wait")
    local(small, o_small.at[0], once_sem.at[2]).wait()
    local(small_in.at[5], o_small.at[1], once_sem.at[3]).wait()


LAST_TICK = TOTAL + 4
ACT_TICKS = ((0, 0, 0, 0, 2, 2, 3, 3, 6, 6, 6, 6), (1, 1, 1, 1, 3, 3, 4, 4, 7, 7, 7, 7), (2, 2, 2, 2, 4, 4, 5, 5, 8, 8, 8, 8))
Z_TICKS = ((3, 0, 0), (4, 0, 0), (5, 0, 0))
STEPS_INSIDE = 1 + 2 + 3
SMALL = (LAYERS, 24, BLOCK)


def run_backward(saved, vectors):
    dma = pltpu.SemaphoreType.DMA
    slots = dma((SLOTS,))
    units = dma((TOTAL,))
    pair = dma((TOTAL, 2))
    return pl.pallas_call(
        backward_kernel,
        out_shape=(
            jax.ShapeDtypeStruct((TOTAL, 96, BLOCK), f32),
            jax.ShapeDtypeStruct((LAYERS, 2, ROWS, WIDTH), f32),
            jax.ShapeDtypeStruct((2, ROWS, WIDTH), f32),
            jax.ShapeDtypeStruct((2, *SMALL), f32),
            jax.ShapeDtypeStruct((2, ROWS, WIDTH), f32),
            jax.ShapeDtypeStruct((TOTAL - 3, 2, 2, 2, 2, 96, BLOCK), f32),
        ),
        in_specs=[ANY] * 13 + [VMEM],
        out_specs=(ANY,) * 6,
        scratch_shapes=[
            pltpu.VMEM((SLOTS, 2, 2, 2, 2, 96, BLOCK), f32),
            pltpu.VMEM((SLOTS, 2, 2, 96, BLOCK), f32),
            pltpu.VMEM((SLOTS, 2, 2, 96, BLOCK), f32),
            pltpu.VMEM((SLOTS, 2, 96, BLOCK), f32),
            pltpu.VMEM((SLOTS, 2, 96, BLOCK), f32),
            pltpu.VMEM((TOTAL - 1, 2, 2, 96, BLOCK), f32),
            pltpu.VMEM((TOTAL - 1, 2, 2, 96, BLOCK), f32),
            pltpu.VMEM((TOTAL - 1, 2, 96, BLOCK), f32),
            pltpu.VMEM((2, 2, 2, 2, 96, BLOCK), f32),
            pltpu.VMEM((2, 2, 2, 2, 96, BLOCK), f32),
            pltpu.VMEM((2, 2, 2, 96, BLOCK), f32),
            pltpu.VMEM((ROWS, WIDTH), f32),
            pltpu.VMEM((ROWS, WIDTH), f32),
            pltpu.VMEM((2, ROWS, WIDTH), f32),
            pltpu.VMEM((ROWS, WIDTH), f32),
            pltpu.VMEM((ROWS, WIDTH), f32),
            pltpu.VMEM((ROWS, WIDTH), bf16),
            pltpu.VMEM((ROWS, WIDTH), bf16),
            pltpu.VMEM((2, ROWS, BLOCK), bf16),
            pltpu.VMEM((2, ROWS, 192), bf16),
            pltpu.VMEM((2, ROWS, 192), bf16),
            pltpu.VMEM((2, ROWS, BLOCK), f32),
            pltpu.VMEM((2, 2, ROWS, BLOCK), bf16),
            pltpu.VMEM((2, 2, BLOCK, WIDTH), bf16),
            pltpu.VMEM((2, 4, WIDTH, BLOCK), bf16),
            pltpu.VMEM((ROWS, WIDTH), bf16),
            pltpu.VMEM((2, ROWS, BLOCK), bf16),
            pltpu.VMEM((2, ROWS, 192), bf16),
            pltpu.VMEM(SMALL, f32),
            pltpu.VMEM((6, *SMALL), f32),
            slots,
            slots,
            slots,
            slots,
            slots,
            slots,
            slots,
            slots,
            pair,
            pair,
            units,
            units,
            units,
            units,
            units,
            dma((TOTAL, 3)),
            dma((TOTAL, 2)),
            dma((3,)),
            dma((8,)),
            dma((6,)),
            dma((2,)),
            slots,
            dma((4,)),
            dma((6,)),
            dma((6,)),
            dma((4,)),
            dma((4, 2)),
            dma((4, 2)),
            dma((4,)),
            dma((4,)),
        ],
        compiler_params=pltpu.CompilerParams(
            collective_id=1, has_side_effects=True, vmem_limit_bytes=63 << 20
        ),
        name="backward_reduce",
    )(*saved, vectors)


def update_kernel(dp, fin, pa, ma, sa, pm, mm, sm, tops, inputs, *refs):
    smalls, (na, fa, va, nm, fm, vm, sections, upstream), small_outs = refs[:12], refs[12:20], refs[20:]
    step = pl.program_id(0)

    def join(clips, target):
        target[:FRAMES] = clips[0, :FRAMES]
        target[FRAMES:] = clips[1, :FRAMES]

    @pl.when(step < LAYERS)
    def _():
        for k in range(4):
            grad = fin[5 - k // 2, :, 192 * (k % 2) : 192 * (k % 2 + 1)]
            na[0, k], fa[0, k], va[0, k] = adamw_update(pa[0, k].T, grad, ma[0, k], sa[0, k], rate_matrix)
        for k in range(2):
            for h in range(2):
                cols = slice(BLOCK * h, BLOCK * (h + 1))
                grad = fin[2 - 2 * k + h]
                nm[0, k, :, cols], fm[0, k, :, cols], vm[0, k, :, cols] = adamw_update(
                    pm[0, k, :, cols], grad, mm[0, k, :, cols], sm[0, k, :, cols], rate_matrix
                )
        join(tops.at[0], sections.at[0])

    @pl.when(step == LAYERS)
    def _():
        join(inputs, upstream)
        for k in range(3):
            done = adamw_update(*(ref[...] for ref in smalls[4 * k : 4 * k + 4]), rate_vector)
            for ref, value in zip(small_outs[3 * k : 3 * k + 3], done):
                ref[...] = value


def run_update(dp, fin, w_attn, moment_attn, square_attn, w_mlp, moment_mlp, square_mlp, tops, inputs, smalls):
    rows = fin.shape[1]

    def layer(l):
        return jnp.minimum(l, LAYERS - 1)

    def whole(part):
        return pl.BlockSpec(part.shape, lambda l, dp: (0,) * part.ndim)

    attn = pl.BlockSpec((1, 4, rows, 192), lambda l, dp: (layer(l), 0, 0, 0))
    mlp = pl.BlockSpec((1, 2, rows, WIDTH), lambda l, dp: (layer(l), 0, 0, 0))
    return pl.pallas_call(
        update_kernel,
        grid_spec=pltpu.PrefetchScalarGridSpec(
            num_scalar_prefetch=1,
            grid=(LAYERS + 1,),
            in_specs=[
                pl.BlockSpec((UNITS, rows, BLOCK), lambda l, dp: (LAYERS - 1 - layer(l), 0, 0)),
                pl.BlockSpec((1, 4, 192, rows), lambda l, dp: (layer(l), 0, 0, 0)),
                attn,
                attn,
                pl.BlockSpec((1, 2, rows, WIDTH), lambda l, dp: (layer(l), 0, dp[0], 0)),
                mlp,
                mlp,
                pl.BlockSpec((1, 2, ROWS, WIDTH), lambda l, dp: (layer(l), 0, 0, 0)),
                pl.BlockSpec((2, ROWS, WIDTH), lambda l, dp: (0, 0, 0)),
            ]
            + [whole(part) for part in smalls],
            out_specs=(attn,) * 3
            + (mlp,) * 3
            + (
                pl.BlockSpec((1, 2 * FRAMES, WIDTH), lambda l, dp: (layer(l), 0, 0)),
                pl.BlockSpec((2 * FRAMES, WIDTH), lambda l, dp: (0, 0)),
            )
            + tuple(whole(smalls[4 * k]) for k in range(3) for _ in range(3)),
        ),
        out_shape=(jax.ShapeDtypeStruct(moment_attn.shape, f32),) * 3
        + (jax.ShapeDtypeStruct(moment_mlp.shape, f32),) * 3
        + (
            jax.ShapeDtypeStruct((LAYERS, 2 * FRAMES, WIDTH), f32),
            jax.ShapeDtypeStruct((2 * FRAMES, WIDTH), f32),
        )
        + tuple(jax.ShapeDtypeStruct(smalls[4 * k].shape, f32) for k in range(3) for _ in range(3)),
        compiler_params=pltpu.CompilerParams(vmem_limit_bytes=60 << 20),
        name="update",
    )(dp.reshape(1), fin, w_attn, moment_attn, square_attn, w_mlp, moment_mlp, square_mlp, tops, inputs, *smalls)


def per_device(
    frames,
    cotangent,
    w_attn,
    w_mlp,
    vectors,
    head_bias,
    up_bias,
    moment_attn,
    square_attn,
    moment_mlp,
    square_mlp,
    moment_vectors,
    square_vectors,
    moment_head,
    square_head,
    moment_up,
    square_up,
):
    dp = lax.axis_index("dp")
    t = lax.axis_index("tensor")
    core = dp % 2
    dp_size = lax.axis_size("dp")

    wa = jnp.swapaxes(w_attn, 2, 3).reshape(LAYERS, 4, 4, 2, 24, WIDTH)
    wm = w_mlp.reshape(LAYERS, 2, 4, 2, 96, 2 * BLOCK)
    rows_first = jnp.swapaxes(vectors, 0, 1)
    saved = run_forward(
        frames, cotangent, wa, wm, jnp.swapaxes(head_bias, 1, 2), jnp.swapaxes(up_bias, 0, 1), rows_first
    )
    saved = (*saved[:-1], saved[-1].reshape(2, 2, 2, 2, 2, 96, BLOCK))
    fin, tops, inputs, small, _, _ = run_backward(saved, rows_first)

    if dp_size > GROUP:
        groups = [[i + GROUP * o for o in range(dp_size // GROUP)] for i in range(GROUP)]
        small = lax.psum(small, "dp", axis_index_groups=groups)
    vector_all = small[0, :, :12].reshape(LAYERS, 6, WIDTH)
    owner = t // 2
    here = jnp.where(owner == core, small[0], small[1])
    second = jnp.where(owner == 0, t % 2, 1 - t % 2)
    head_all = jnp.where(second == 0, here[:, 12], here[:, 13]).reshape(LAYERS, 2, HEADS_HERE, HEAD_DIM)
    up_all = jnp.where(second == 0, here[:, 14:16], here[:, 16:18]).reshape(LAYERS, 12, HEAD_DIM)

    def owned(param, dim):
        size = param.shape[dim] // dp_size
        return lax.dynamic_slice_in_dim(param, dp * size, size, dim)

    if dp_size > GROUP:
        rows = jnp.zeros((TOTAL, WIDTH, BLOCK), f32)
        rows = lax.dynamic_update_slice_in_dim(rows, fin, (dp % GROUP) * 96, 1)
        fin = lax.psum_scatter(rows, "dp", scatter_dimension=1, tiled=True)

    own_attn = jnp.swapaxes(owned(w_attn, 2), 2, 3)
    def swapped(axis, parts):
        return [jnp.swapaxes(part, axis, axis + 1) for part in parts]

    smalls = (
        swapped(0, (owned(vectors, 2), owned(vector_all, 2), moment_vectors, square_vectors))
        + swapped(1, (owned(head_bias, 3), owned(head_all, 3), moment_head, square_head))
        + swapped(1, (owned(up_bias, 2), owned(up_all, 2), moment_up, square_up))
    )
    done = run_update(
        dp, fin, own_attn, moment_attn, square_attn, w_mlp, moment_mlp, square_mlp, tops, inputs, smalls
    )
    matrices, (sections, upstream), done = done[:6], done[6:8], done[8:]
    done = swapped(0, done[:3]) + swapped(1, done[3:])
    return (sections, upstream, *matrices, *done)


def solution(mesh):
    in_specs = (
        P("dp", None),
        P("dp", None),
        P(None, None, None, "tensor"),
        P(None, None, None, "tensor"),
        P(),
        P(None, None, "tensor", None),
        P(None, "tensor", None),
        P(None, None, "dp", "tensor"),
        P(None, None, "dp", "tensor"),
        P(None, None, "dp", "tensor"),
        P(None, None, "dp", "tensor"),
        P(None, None, "dp"),
        P(None, None, "dp"),
        P(None, None, "tensor", "dp"),
        P(None, None, "tensor", "dp"),
        P(None, "tensor", "dp"),
        P(None, "tensor", "dp"),
    )
    out_specs = (
        P(None, "dp", None),
        P("dp", None),
        P(None, None, "dp", "tensor"),
        P(None, None, "dp", "tensor"),
        P(None, None, "dp", "tensor"),
        P(None, None, "dp", "tensor"),
        P(None, None, "dp", "tensor"),
        P(None, None, "dp", "tensor"),
        P(None, None, "dp"),
        P(None, None, "dp"),
        P(None, None, "dp"),
        P(None, None, "tensor", "dp"),
        P(None, None, "tensor", "dp"),
        P(None, None, "tensor", "dp"),
        P(None, "tensor", "dp"),
        P(None, "tensor", "dp"),
        P(None, "tensor", "dp"),
    )
    return jax.shard_map(
        per_device, mesh=mesh, in_specs=in_specs, out_specs=out_specs, check_vma=False
    )
```

```python
import math
from types import SimpleNamespace

import jax
import jax.numpy as jnp
from jax import lax
from jax.experimental import pallas as pl
from jax.experimental.pallas import tpu as pltpu
from jax.sharding import PartitionSpec as P

HEAD_DIM = 64
FRAMES = 500
ROWS = 512
LAYERS = 2
STEP = 10
WIDTH = 768
BLOCK = 384
UNITS = 6
TOTAL = LAYERS * UNITS
GROUP = 8
HEADS_HERE = 3
SLOTS = 3
LEAD = 2
SOURCE_LEAD = 5
CHUNK_TICKS = ((2, 4, 5, 7), (3, 5, 6, 8), (4, 6, 7, 9))
SPAN = 504
SECOND = 496
CHUNK = 128

ln_eps = 1e-05
beta_one = 0.9
beta_two = 0.999
adam_eps = 1e-08
decay_rate = 0.01
rate_matrix = 0.05
rate_vector = 0.2
score_scale = 1.0 / math.sqrt(HEAD_DIM)
MESH = pl.DeviceIdType.MESH
f32 = jnp.float32
bf16 = jnp.bfloat16
ANY = pl.BlockSpec(memory_space=pl.ANY)
VMEM = pl.BlockSpec(memory_space=pltpu.VMEM)


def product(left, right):
    return jnp.dot(left, right, preferred_element_type=f32)


def contract_last(left, right):
    return lax.dot_general(left, right, (((1,), (1,)), ((), ())), preferred_element_type=f32)


def contract_rows(left, right):
    return lax.dot_general(left, right, (((0,), (0,)), ((), ())), preferred_element_type=f32)


def normalize_parts(inputs):
    centre = jnp.mean(inputs, axis=-1, keepdims=True)
    centred = inputs - centre
    inverse = lax.rsqrt(jnp.mean(centred * centred, axis=-1, keepdims=True) + ln_eps)
    return centred * inverse, inverse


def normalize_back(upstream, scaled, inverse, gain):
    gain_grad = jnp.sum(upstream * scaled, axis=0)
    shift_grad = jnp.sum(upstream, axis=0)
    inner_grad = upstream * gain
    lowered = inverse * (
        inner_grad
        - jnp.mean(inner_grad, axis=-1, keepdims=True)
        - scaled * jnp.mean(inner_grad * scaled, axis=-1, keepdims=True)
    )
    return (lowered, gain_grad, shift_grad)


def gelu(before):
    return 0.5 * before * (1.0 + lax.erf(before * (1.0 / math.sqrt(2.0))))


def gelu_slope(before):
    return 0.5 * (1.0 + lax.erf(before * (1.0 / math.sqrt(2.0)))) + before * jnp.exp(
        -0.5 * before * before
    ) * (1.0 / math.sqrt(2.0 * math.pi))


def adamw_update(param, gradient, first, second, rate):
    first_new = beta_one * first + (1.0 - beta_one) * gradient
    second_new = beta_two * second + (1.0 - beta_two) * gradient * gradient
    ratio = (
        first_new
        / (1.0 - beta_one**STEP)
        / (jnp.sqrt(second_new / (1.0 - beta_two**STEP)) + adam_eps)
    )
    return (param - rate * (ratio + decay_rate * param), first_new, second_new)


def find_place():
    dp = lax.axis_index("dp")
    t = lax.axis_index("tensor")
    i = lax.rem(dp, GROUP)
    base = dp - i
    c = lax.rem(i, 2)
    x = lax.rem(i // 2, 2)
    y = i // 4
    up = 1 - 2 * c
    level = c * (3 - t) + (1 - c) * t

    def at(cc, xx, yy):
        return base + 4 * yy + 2 * xx + cc

    return SimpleNamespace(
        t=t,
        c=c,
        x=x,
        y=y,
        q=2 * y + x,
        qx=2 * y + 1 - x,
        qy=2 * (1 - y) + x,
        qd=2 * (1 - y) + 1 - x,
        level=level,
        partner=(at(1 - c, x, y), t),
        xn=(at(c, 1 - x, y), t),
        yn=(at(c, x, 1 - y), t),
        above=(dp, t + up),
        below=(dp, t - up),
    )


def hail(p):
    barrier = pltpu.get_barrier_semaphore()

    def signal(device):
        pl.semaphore_signal(barrier, inc=1, device_id=device, device_id_type=MESH)

    signal(p.partner)
    signal(p.xn)
    signal(p.yn)

    @pl.when(p.level < 3)
    def _():
        signal(p.above)

    @pl.when(p.level > 0)
    def _():
        signal(p.below)


def meet(p):
    barrier = pltpu.get_barrier_semaphore()
    inner = (p.level > 0) & (p.level < 3)

    @pl.when(inner)
    def _():
        pl.semaphore_wait(barrier, 5)

    @pl.when(jnp.logical_not(inner))
    def _():
        pl.semaphore_wait(barrier, 4)


def remote(src, dst, send_sem, recv_sem, device):
    return pltpu.make_async_remote_copy(
        src_ref=src,
        dst_ref=dst,
        send_sem=send_sem,
        recv_sem=recv_sem,
        device_id=device,
        device_id_type=MESH,
    )


def local(src, dst, sem):
    return pltpu.make_async_copy(src, dst, sem)


def forward_kernel(
    frames,
    cotangent,
    wa,
    wm,
    head_bias,
    up_bias,
    vec,
    o_ct,
    o_h,
    o_m,
    o_n1,
    o_n2,
    o_qk,
    o_v,
    o_a,
    o_u,
    o_c,
    o_wa,
    o_wm,
    o_first,
    ga,
    gm,
    hb,
    ub,
    hs,
    ms,
    n1s,
    n2s,
    qks,
    vs,
    as_,
    us,
    cs,
    low_a,
    low_m,
    low_ct,
    part,
    other,
    rz,
    sz,
    szd,
    rx,
    sx,
    ry,
    sy,
    rxd,
    sxd,
    ryd,
    syd,
    native,
    rc,
    sc,
    scd,
    first_sem,
    bias_local,
    bias_send,
    bias_recv,
    swap_sem,
    low_sem,
    mid_sem,
    out_sem,
    grad_sem,
):
    p = find_place()
    hail(p)
    level = p.level
    when = pl.when

    def quarter(ref, i, q, h=None):
        lead = (slice(None), q) if i < 2 else (q,)
        return ref.at[lead if h is None else (*lead, h)]

    def block(l, i):
        if i < 2:
            return wa.at[l, pl.ds(2 * i, 2)]
        return wm.at[l, (i - 2) // 2, :, :, :, pl.ds(BLOCK * (i % 2), BLOCK)]

    def block_quarter(l, i):
        if i < 2:
            return wa.at[l, pl.ds(2 * i, 2), p.q]
        return wm.at[l, (i - 2) // 2, p.q, :, :, pl.ds(BLOCK * (i % 2), BLOCK)]

    def held(l, i, j):
        return ga.at[j, l, i] if i < 2 else gm.at[j, l, i - 2]

    def z_copy(src, l, i, j, device, send_sem):
        return remote(src, quarter(held(l, i, j), i, p.q), send_sem, rz.at[UNITS * l + i, j], device)

    def plane_copy(l, i, j, q, h, send_sem, recv_sem, device):
        here = quarter(held(l, i, j), i, q, h)
        u = UNITS * l + i
        return remote(here, here, send_sem.at[u, j], recv_sem.at[u, j], device)

    def x_copy(l, i, j, q):
        return plane_copy(l, i, j, q, None, sx, rx, p.xn)

    def y_copy(l, i, j, q):
        return plane_copy(l, i, j, q, None, sy, ry, p.yn)

    def xd_copy(l, i, j, q):
        return plane_copy(l, i, j, q, 1, sxd, rxd, p.xn)

    def yd_copy(l, i, j, q):
        return plane_copy(l, i, j, q, 0, syd, ryd, p.yn)

    def source(l, i):
        u = UNITS * l + i

        @when(level == 0)
        def _():
            z_copy(block_quarter(l, i), l, i, 0, p.above, sz.at[u, 0]).start()
            local(block(l, i), held(l, i, 0), native.at[u]).start()

        @when(level == 1)
        def _():
            z_copy(block_quarter(l, i), l, i, 1, p.above, sz.at[u, 1]).start()
            z_copy(block_quarter(l, i), l, i, 1, p.below, szd.at[u]).start()
            local(block(l, i), held(l, i, 1), native.at[u]).start()

    def stage_one(l, i):
        u = UNITS * l + i
        for j in (1, 0):

            @when(level != j)
            def _(j=j):
                here = quarter(held(l, i, j), i, p.q)
                z_copy(here, l, i, j, p.above, sz.at[u, j]).wait_recv()

                @when((level == 2) | ((level == 1) if j == 0 else (level == 2)))
                def _():
                    z_copy(here, l, i, j, p.above, sz.at[u, j]).start()

                x_copy(l, i, j, p.q).start()
                y_copy(l, i, j, p.q).start()

    def stage_two(l, i):
        for j in (1, 0):

            @when(level != j)
            def _(j=j):
                x_copy(l, i, j, p.qx).wait_recv()
                yd_copy(l, i, j, p.qx).start()
                y_copy(l, i, j, p.qy).wait_recv()
                xd_copy(l, i, j, p.qy).start()

    def finish(l, i):
        u = UNITS * l + i
        for j in range(2):

            @when(level != j)
            def _(j=j):
                yd_copy(l, i, j, p.qd).wait_recv()
                xd_copy(l, i, j, p.qd).wait_recv()

            @when(level == j)
            def _(j=j):
                local(block(l, i), held(l, i, j), native.at[u]).wait()

    last = LAYERS - 1
    alone = UNITS - 1

    def chunk_copy(src, q, j, device, send_sem):
        return remote(src, held(last, alone, j).at[q], send_sem, rc.at[q, j], device)

    def chunk_source(q):
        here = wm.at[last, 1, q, :, :, pl.ds(BLOCK, BLOCK)]

        @when(level == 0)
        def _():
            chunk_copy(here, q, 0, p.above, sc.at[q, 0]).start()

        @when(level == 1)
        def _():
            chunk_copy(here, q, 1, p.above, sc.at[q, 1]).start()
            chunk_copy(here, q, 1, p.below, scd.at[q]).start()

    def chunk_pass(q, at, j):
        @when(level == at)
        def _():
            here = held(last, alone, j).at[q]
            chunk_copy(here, q, j, p.above, sc.at[q, j]).wait_recv()
            chunk_copy(here, q, j, p.above, sc.at[q, j]).start()

    def chunk_native(method):
        for j in range(2):

            @when(level == j)
            def _(j=j):
                getattr(local(block(last, alone), held(last, alone, j), native.at[TOTAL - 1]), method)()

    def chunk_finish():
        for q in range(4):
            here = held(last, alone, 0).at[q]

            @when((level == 3))
            def _(q=q, here=here):
                chunk_copy(here, q, 0, p.above, sc.at[q, 0]).wait_recv()

            @when((level == 3) | (level == 0))
            def _(q=q, here=here):
                chunk_copy(here, q, 1, p.above, sc.at[q, 1]).wait_recv()

        chunk_native("wait")

    def chunk_drain():
        for q in range(4):
            here = held(last, alone, 0).at[q]

            @when(level < 3)
            def _(q=q, here=here):
                chunk_copy(here, q, 0, p.above, sc.at[q, 0]).wait_send()

            @when((level == 1) | (level == 2))
            def _(q=q, here=here):
                chunk_copy(here, q, 1, p.above, sc.at[q, 1]).wait_send()

            @when(level == 1)
            def _(q=q, here=here):
                chunk_copy(here, q, 1, p.below, scd.at[q]).wait_send()

    def chunk_step(l, i):
        for q in range(4):
            for at, tick_of in enumerate(CHUNK_TICKS):
                there, k = divmod(tick_of[q], UNITS)
                if k == i:

                    @when(l == there)
                    def _(q=q, at=at):
                        if at == 0:
                            chunk_source(q)
                        elif at == 1:
                            chunk_pass(q, 1, 0)
                        else:
                            chunk_pass(q, 2, 1)
                            chunk_pass(q, 2, 0)

    def ahead(step, l, i, by):
        k = i + by
        there = l + k // UNITS
        if k % UNITS == alone:
            when(there < last)(lambda: step(there, alone))
        elif k < UNITS:
            step(l, k)
        else:
            when(there < LAYERS)(lambda: step(there, k % UNITS))

    def serve(l, k):
        ahead(source, l, k, SOURCE_LEAD)
        ahead(stage_one, l, k, LEAD)
        ahead(stage_two, l, k, LEAD - 1)

    def tick(l, i):
        if i < 2:
            serve(l, i)
        elif i < UNITS - 1:
            serve(l, i + 1)
        chunk_step(l, i)
        if i == alone:
            when(l < last)(lambda: finish(l, i))
            when(l == last)(chunk_finish)
        else:
            finish(l, i)

    mine = (p.t // 2) == p.c
    clip = lax.rem(p.t, 2)
    span = pl.ds(pl.multiple_of(clip * SECOND, 8), SPAN)
    inputs = (
        (frames.at[span], part.at[pl.ds(0, SPAN)]),
        (cotangent.at[span], ms.at[1, pl.ds(0, SPAN)]),
    )

    def input_copies(k):
        src, dst = inputs[k]
        return (
            local(src, dst, first_sem.at[k]),
            remote(src, dst, first_sem.at[2 + k], first_sem.at[4 + k], p.partner),
        )

    def wait_input(k):
        here, there = input_copies(k)

        @when(mine)
        def _():
            here.wait()
            there.wait_send()

        @when(jnp.logical_not(mine))
        def _():
            there.wait_recv()

    def take_clip(target, raw):
        @when(clip == 0)
        def _():
            target[0:FRAMES] = raw[0:FRAMES]

        @when(clip == 1)
        def _():
            target[0:FRAMES] = raw[FRAMES - SECOND : SPAN]

        target[FRAMES:ROWS] = jnp.zeros((ROWS - FRAMES, WIDTH), f32)

    kept_biases = ((head_bias, hb), (up_bias, ub))

    def bias_copy(src, n, j, m, device):
        return remote(src, kept_biases[n][1].at[j], bias_send.at[n, m], bias_recv.at[n, j], device)

    def bias_source():
        for n, (src, dst) in enumerate(kept_biases):

            @when(level == 0)
            def _(n=n, src=src, dst=dst):
                local(src, dst.at[0], bias_local.at[n]).start()
                bias_copy(src, n, 0, 0, p.above).start()

            @when(level == 1)
            def _(n=n, src=src, dst=dst):
                local(src, dst.at[1], bias_local.at[n]).start()
                bias_copy(src, n, 1, 1, p.above).start()
                bias_copy(src, n, 1, 2, p.below).start()

    def bias_pass():
        for n, (src, dst) in enumerate(kept_biases):

            @when(level != 0)
            def _(n=n, src=src):
                bias_copy(src, n, 0, 0, p.above).wait_recv()

            @when((level == 1) | (level == 2))
            def _(n=n, dst=dst):
                bias_copy(dst.at[0], n, 0, 0, p.above).start()

            @when(level != 1)
            def _(n=n, src=src):
                bias_copy(src, n, 1, 1, p.above).wait_recv()

            @when(level == 2)
            def _(n=n, dst=dst):
                bias_copy(dst.at[1], n, 1, 1, p.above).start()

            @when(level < 2)
            def _(n=n, src=src, dst=dst):
                local(src, dst.at[0], bias_local.at[n]).wait()

    def bias_drain():
        for n, (src, dst) in enumerate(kept_biases):

            @when(level < 3)
            def _(n=n, src=src):
                bias_copy(src, n, 0, 0, p.above).wait_send()

            @when((level == 1) | (level == 2))
            def _(n=n, src=src):
                bias_copy(src, n, 1, 1, p.above).wait_send()

            @when(level == 1)
            def _(n=n, src=src):
                bias_copy(src, n, 1, 2, p.below).wait_send()

    def head_row(j, l, n):
        return jnp.concatenate([hb[j, l, h, n : n + 1, :] for h in range(HEADS_HERE)], axis=-1)

    def up_row(j, l, k):
        return jnp.concatenate([ub[j, r, pl.ds(l, 1), :] for r in range(6 * k, 6 * k + 6)], axis=-1)

    chunk_native("start")
    meet(p)
    source(0, 0)

    @when(mine)
    def _():
        for copy in input_copies(0):
            copy.start()

    bias_source()
    for i in range(1, SOURCE_LEAD):
        source(0, i)

    @when(mine)
    def _():
        for copy in input_copies(1):
            copy.start()

    stage_one(0, 0)
    wait_input(0)
    take_clip(hs.at[0], part)
    for i in range(1, LEAD):
        stage_one(0, i)
        stage_two(0, i - 1)
    bias_pass()
    wait_input(1)
    take_clip(part, ms.at[1])
    keep_cotangent = local(part, o_ct, out_sem.at[0, 1])
    keep_cotangent.start()
    low_ct[...] = part[...].astype(bf16)
    keep_cotangent.wait()

    def keep_low(l, i):
        if i < 2:
            slots, slot, target = low_a, 0, lambda j: o_wa.at[j, l, i]
        else:
            slots, slot, target = low_m, i % 2, lambda j: o_wm.at[j, l, i - 2]
        sems = 0 if i < 2 else 1 + i % 2

        def copy(j):
            return local(slots.at[slot, j], target(j), low_sem.at[sems, j])

        def drain():
            for j in range(2):
                copy(j).wait()

        if i in (1, 4, 5):
            drain()
        else:
            when(l > 0)(drain)
        for j in range(2):
            if i < 2:
                slots[slot, j] = ga[j, l, i].reshape(BLOCK, WIDTH).astype(bf16)
            else:
                slots[slot, j] = gm[j, l, i - 2].reshape(WIDTH, BLOCK).astype(bf16)
            copy(j).start()
        return slots.at[slot]

    def swap(slot):
        copy = remote(part, other.at[slot], swap_sem.at[slot], swap_sem.at[2 + slot], p.partner)
        copy.start()
        copy.wait()

    def out_copies(l):
        return [
            local(hs.at[l], o_h.at[l], out_sem.at[0, l]),
            local(ms.at[l], o_m.at[l], out_sem.at[1, l]),
            local(n1s.at[l], o_n1.at[l], out_sem.at[2, l]),
            local(n2s.at[l], o_n2.at[l], out_sem.at[3, l]),
            local(qks.at[l], o_qk.at[l], out_sem.at[4, l]),
            local(vs.at[l], o_v.at[l], out_sem.at[5, l]),
            local(as_.at[l], o_a.at[l], out_sem.at[6, l]),
        ]

    def mid_copies(l, i):
        k = i - 2
        return [
            local(us.at[:, k], o_u.at[l, :, k], mid_sem.at[0, k]),
            local(cs.at[:, k], o_c.at[l, :, k], mid_sem.at[1, k]),
        ]

    def drain(u, carry):
        l = u // UNITS
        for j in range(2):

            @when((level < 3) if j == 0 else ((level == 1) | (level == 2)))
            def _(j=j):
                z_copy(gm.at[j, l, 0, p.q], l, 2, j, p.above, sz.at[u, j]).wait_send()

            @when(level != j)
            def _(j=j):
                whole, half = gm.at[j, l, 0, p.q], gm.at[j, l, 0, p.q, 0]
                remote(whole, whole, sx.at[u, j], rx.at[u, j], p.xn).wait_send()
                remote(whole, whole, sy.at[u, j], ry.at[u, j], p.yn).wait_send()
                remote(half, half, sxd.at[u, j], rxd.at[u, j], p.xn).wait_send()
                remote(half, half, syd.at[u, j], ryd.at[u, j], p.yn).wait_send()

        @when(level == 1)
        def _():
            z_copy(gm.at[1, l, 0, p.q], l, 2, 1, p.below, szd.at[u]).wait_send()

        return carry

    def grad_copy(k, j):
        return local(gm.at[j, 0, k], o_first.at[k, j], grad_sem.at[k, j])

    def layer(l, carry):
        params = [vec[k, pl.ds(l, 1)] for k in range(6)]

        tick(l, 0)
        scaled, _ = normalize_parts(hs[l])
        n1s[l] = (scaled * params[0] + params[1]).astype(bf16)
        weights = keep_low(l, 0)
        for j in range(2):
            both = contract_last(n1s[l], weights[j])
            shift = jnp.concatenate([head_row(j, l, 0), jnp.zeros((1, 192), f32)], axis=-1)
            qks[l, j] = (both + shift).astype(bf16)

        tick(l, 1)
        weights = keep_low(l, 1)
        keep = lax.broadcasted_iota(jnp.int32, (ROWS, ROWS), 1) < FRAMES
        def attention(j, carry, weights=weights):
            vs[l, j] = (
                contract_last(n1s[l], weights[j, 0:192]) + head_row(j, l, 1)
            ).astype(bf16)

            heads = []
            for h in range(HEADS_HERE):
                cols = slice(HEAD_DIM * h, HEAD_DIM * (h + 1))
                k_cols = slice(192 + HEAD_DIM * h, 192 + HEAD_DIM * (h + 1))
                scores = contract_last(qks[l, j, :, cols], qks[l, j, :, k_cols]) * score_scale
                scores = jnp.where(keep, scores, -1e30)
                weight = jnp.exp(scores - jnp.max(scores, axis=-1, keepdims=True))
                weight = weight * (1.0 / jnp.sum(weight, axis=-1, keepdims=True))
                heads.append(product(weight.astype(bf16), vs[l, j, :, cols]))
            as_[l, j] = jnp.concatenate(heads, axis=-1).astype(bf16)
            when(j == 0)(lambda: serve(l, 2))
            return carry

        lax.fori_loop(0, 2, attention, 0)
        part[...] = product(as_[l, 0], weights[0, 192:384])
        part[...] += product(as_[l, 1], weights[1, 192:384])
        swap(0)
        ms[l] = hs[l] + (part[...] + other[0]) + params[4]
        scaled, _ = normalize_parts(ms[l])
        n2s[l] = (scaled * params[2] + params[3]).astype(bf16)
        for copy in out_copies(l):
            copy.start()

        for i in (2, 3):
            tick(l, i)
            weights = keep_low(l, i)

            @when(l > 0)
            def _(i=i):
                for copy in mid_copies(l - 1, i):
                    copy.wait()

            def hidden_units(j, carry, i=i, weights=weights):
                before = product(n2s[l], weights[j]) + up_row(j, l, i - 2)
                us[j, i - 2] = before
                cs[j, i - 2] = gelu(before).astype(bf16)
                return carry

            lax.fori_loop(0, 2, hidden_units, 0)
            for copy in mid_copies(l, i):
                copy.start()

        for i in (4, 5):
            tick(l, i)
            weights = keep_low(l, i)

            @when(l == last)
            def _(i=i):
                if i == 4:
                    lax.fori_loop(0, UNITS, drain, 0)
                for j in range(2):
                    gm[j, 0, i - 4] = contract_rows(low_ct[...], cs[j, i - 4]).reshape(4, 2, 96, BLOCK)
                    grad_copy(i - 4, j).start()

            @when(l < LAYERS - 1)
            def _(i=i, weights=weights):
                for j in range(2):
                    term = contract_last(cs[j, i - 4], weights[j])
                    if i == 4 and j == 0:
                        part[...] = term
                    else:
                        part[...] += term

        @when(l < LAYERS - 1)
        def _():
            swap(1)
            hs[l + 1] = ms[l] + (part[...] + other[1]) + params[5]

        return carry

    lax.fori_loop(0, LAYERS, layer, 0)

    for i in (2, 3):
        for copy in mid_copies(last, i):
            copy.wait()
    for l in range(LAYERS):
        for copy in out_copies(l):
            copy.wait()
    for j in range(2):
        local(low_a.at[0, j], o_wa.at[j, last, 1], low_sem.at[0, j]).wait()
        for slot in range(2):
            local(low_m.at[slot, j], o_wm.at[j, last, 2 + slot], low_sem.at[1 + slot, j]).wait()
    for k in range(2):
        for j in range(2):
            grad_copy(k, j).wait()
    bias_drain()
    chunk_drain()

    lax.fori_loop(UNITS, TOTAL - 1, drain, 0)


def run_forward(frames, cotangent, wa, wm, head_bias, up_bias, vectors):
    def hbm(shape, kind):
        return jax.ShapeDtypeStruct(shape, kind)

    dma = pltpu.SemaphoreType.DMA
    per_unit = dma((TOTAL, 2))
    return pl.pallas_call(
        forward_kernel,
        out_shape=(
            hbm((ROWS, WIDTH), f32),
            hbm((LAYERS, ROWS, WIDTH), f32),
            hbm((LAYERS, ROWS, WIDTH), f32),
            hbm((LAYERS, ROWS, WIDTH), bf16),
            hbm((LAYERS, ROWS, WIDTH), bf16),
            hbm((LAYERS, 2, ROWS, BLOCK), bf16),
            hbm((LAYERS, 2, ROWS, 192), bf16),
            hbm((LAYERS, 2, ROWS, 192), bf16),
            hbm((LAYERS, 2, 2, ROWS, BLOCK), f32),
            hbm((LAYERS, 2, 2, ROWS, BLOCK), bf16),
            hbm((2, LAYERS, 2, BLOCK, WIDTH), bf16),
            hbm((2, LAYERS, 4, WIDTH, BLOCK), bf16),
            hbm((2, 2, 4, 2, 96, BLOCK), f32),
        ),
        in_specs=[ANY, ANY, ANY, ANY, ANY, ANY, VMEM],
        out_specs=(ANY,) * 13,
        scratch_shapes=[
            pltpu.VMEM((2, LAYERS, 2, 2, 4, 2, 24, WIDTH), f32),
            pltpu.VMEM((2, LAYERS, 4, 4, 2, 96, BLOCK), f32),
            pltpu.VMEM((2, *head_bias.shape), f32),
            pltpu.VMEM((2, *up_bias.shape), f32),
            pltpu.VMEM((LAYERS, ROWS, WIDTH), f32),
            pltpu.VMEM((LAYERS, ROWS, WIDTH), f32),
            pltpu.VMEM((LAYERS, ROWS, WIDTH), bf16),
            pltpu.VMEM((LAYERS, ROWS, WIDTH), bf16),
            pltpu.VMEM((LAYERS, 2, ROWS, BLOCK), bf16),
            pltpu.VMEM((LAYERS, 2, ROWS, 192), bf16),
            pltpu.VMEM((LAYERS, 2, ROWS, 192), bf16),
            pltpu.VMEM((2, 2, ROWS, BLOCK), f32),
            pltpu.VMEM((2, 2, ROWS, BLOCK), bf16),
            pltpu.VMEM((1, 2, BLOCK, WIDTH), bf16),
            pltpu.VMEM((2, 2, WIDTH, BLOCK), bf16),
            pltpu.VMEM((ROWS, WIDTH), bf16),
            pltpu.VMEM((ROWS, WIDTH), f32),
            pltpu.VMEM((2, ROWS, WIDTH), f32),
            per_unit,
            per_unit,
            dma((TOTAL,)),
            per_unit,
            per_unit,
            per_unit,
            per_unit,
            per_unit,
            per_unit,
            per_unit,
            per_unit,
            dma((TOTAL,)),
            dma((4, 2)),
            dma((4, 2)),
            dma((4,)),
            dma((6,)),
            dma((2,)),
            dma((2, 3)),
            dma((2, 2)),
            dma((4,)),
            dma((3, 2)),
            dma((2, 2)),
            dma((7, LAYERS)),
            dma((2, 2)),
        ],
        compiler_params=pltpu.CompilerParams(
            collective_id=0, has_side_effects=True, vmem_limit_bytes=63 << 20
        ),
        name="gather_forward",
    )(frames, cotangent, wa, wm, head_bias, up_bias, vectors)


def backward_kernel(
    i_ct,
    i_h,
    i_m,
    i_n1,
    i_n2,
    i_qk,
    i_v,
    i_a,
    i_u,
    i_c,
    i_wa,
    i_wm,
    i_first,
    vec,
    o_fin,
    o_top,
    o_input,
    o_small,
    o_src,
    o_grads,
    held,
    x1,
    y1,
    x2,
    y2,
    own,
    zin,
    zup,
    stage,
    whole_in,
    whole_up,
    grad,
    part,
    other,
    h_in,
    m_in,
    n1,
    n2,
    qk,
    v,
    a,
    u_in,
    c_in,
    wa,
    wm,
    low,
    dqk,
    dv,
    small,
    small_in,
    sx1,
    rx1,
    sy1,
    ry1,
    sx2,
    rx2,
    sy2,
    ry2,
    szd,
    rzd,
    szu,
    rzu,
    sfin,
    rfin,
    lfin,
    act_send,
    act_recv,
    act_sem,
    load_sem,
    unit_sem,
    stage_sem,
    held_sem,
    swap_sem,
    small_send,
    small_recv,
    once_sem,
    whole_send,
    whole_recv,
    whole_send_up,
    whole_recv_up,
):
    p = find_place()
    hail(p)
    level = p.level
    when = pl.when

    chunks = ROWS // CHUNK
    n_chunks = 3 * chunks
    slot_of = (p.c, 1 - p.c)

    def act_part(ref, k):
        return ref.at[pl.ds(pl.multiple_of(k % chunks * CHUNK, CHUNK), CHUNK)]

    def act_all(n, j):
        return o_top.at[n, slot_of[j]] if n < LAYERS else o_input.at[slot_of[j]]

    def act_own(k):
        return act_part(o_src.at[k // chunks - 1], k)

    def act_there(j, k):
        return act_part(act_all(k // chunks, j), k)

    def act_copy(src, j, k, m, device):
        return remote(src, act_there(j, k), act_send.at[k, m], act_recv.at[k, j], device)

    def act_step(s, ticks):
        def set_out(k):
            src = act_part(i_h.at[1], k) if k < chunks else act_own(k)

            @when(level == 0)
            def _():
                act_copy(src, 0, k, 0, p.above).start()

            @when(level == 1)
            def _():
                act_copy(src, 1, k, 1, p.above).start()
                act_copy(src, 1, k, 2, p.below).start()

        def pass_on(k, at, j):
            @when(level == at)
            def _():
                act_copy(act_there(j, k), j, k, j, p.above).wait_recv()
                act_copy(act_there(j, k), j, k, j, p.above).start()

        for t in ticks:
            outs, firsts, seconds = ([k for k in range(n_chunks) if row[k] == t] for row in ACT_TICKS)
            if outs or firsts or seconds:

                @when(s == t)
                def _(outs=outs, firsts=firsts, seconds=seconds):
                    for k in outs:
                        set_out(k)
                    for k in firsts:
                        pass_on(k, 1, 0)
                    for k in seconds:
                        pass_on(k, 2, 1)
                        pass_on(k, 2, 0)

    def act_drain(k):
        @when(level < 3)
        def _():
            act_copy(act_there(0, k), 0, k, 0, p.above).wait_send()

        @when((level == 1) | (level == 2))
        def _():
            act_copy(act_there(1, k), 1, k, 1, p.above).wait_send()

        @when(level == 1)
        def _():
            act_copy(act_there(1, k), 1, k, 2, p.below).wait_send()

        @when(level == 3)
        def _():
            act_copy(act_there(0, k), 0, k, 0, p.above).wait_recv()

        @when((level == 0) | (level == 3))
        def _():
            act_copy(act_there(1, k), 1, k, 1, p.above).wait_recv()

    def act_local(src, n, method):
        for j in range(2):

            @when(level == j)
            def _(j=j):
                getattr(local(src, act_all(n, j), act_sem.at[n]), method)()

    def x1_copy(w):
        return remote(held.at[w, :, :, 1 - p.x, 0], x1.at[w], sx1.at[w], rx1.at[w], p.xn)

    def y1_copy(w):
        return remote(held.at[w, :, 1 - p.y, :, 1], y1.at[w], sy1.at[w], ry1.at[w], p.yn)

    def x2_copy(w):
        return remote(held.at[w, :, p.y, 1 - p.x, 1], x2.at[w], sx2.at[w], rx2.at[w], p.xn)

    def y2_copy(w):
        return remote(held.at[w, :, 1 - p.y, p.x, 0], y2.at[w], sy2.at[w], ry2.at[w], p.yn)

    def down_copy(u, j):
        return remote(own.at[u, j], zin.at[u, j], szd.at[u, j], rzd.at[u, j], p.below)

    def up_copy(u):
        return remote(own.at[u, 1], zup.at[u], szu.at[u], rzu.at[u], p.above)

    def fin_copy(u, j):
        return remote(own.at[u, j, 1 - p.c], o_fin.at[u], sfin.at[u], rfin.at[u], p.partner)

    def fin_local(u, j):
        return local(own.at[u, j, p.c], o_fin.at[u], lfin.at[u])

    def sent(w):
        x1_copy(w).wait_send()
        y1_copy(w).wait_send()
        x2_copy(w).wait_send()
        y2_copy(w).wait_send()

    def stage_one(u):
        w = lax.rem(u, SLOTS)
        when(u >= SLOTS)(lambda: sent(w))
        when(u >= 2)(lambda: local(o_grads.at[u - 2], held.at[w], held_sem.at[w]).start())
        local(i_first.at[0], held.at[w], held_sem.at[w]).wait()
        x1_copy(w).start()
        y1_copy(w).start()

    def stage_two(u):
        w = lax.rem(u, SLOTS)
        x1_copy(w).wait_recv()
        held[w, :, 1 - p.y, p.x, 0] += x1[w, :, 1 - p.y]
        held[w, :, p.y, p.x, 0] += x1[w, :, p.y]
        y1_copy(w).wait_recv()
        held[w, :, p.y, 1 - p.x, 1] += y1[w, :, 1 - p.x]
        held[w, :, p.y, p.x, 1] += y1[w, :, p.x]
        y2_copy(w).start()
        x2_copy(w).start()

    def stage_three(u):
        w = lax.rem(u, SLOTS)
        y2_copy(w).wait_recv()
        own[u, :, 0] = held[w, :, p.y, p.x, 0] + y2[w]
        x2_copy(w).wait_recv()
        own[u, :, 1] = held[w, :, p.y, p.x, 1] + x2[w]

        @when(level == 3)
        def _():
            down_copy(u, 0).start()
            down_copy(u, 1).start()

        @when(level == 0)
        def _():
            up_copy(u).start()

    def level_two(u):
        for j in range(2):
            down_copy(u, j).wait_recv()
            own[u, j] += zin[u, j]
            down_copy(u, j).start()

    def level_one(u):
        down_copy(u, 0).wait_recv()
        own[u, 0] += zin[u, 0]
        down_copy(u, 0).start()
        down_copy(u, 1).wait_recv()
        up_copy(u).wait_recv()
        own[u, 1] += zin[u, 1] + zup[u]
        fin_local(u, 1).start()
        fin_copy(u, 1).start()

    def level_zero(u):
        down_copy(u, 0).wait_recv()
        own[u, 0] += zin[u, 0]
        fin_local(u, 0).start()
        fin_copy(u, 0).start()

    def whole_part(ref, e):
        return ref.at[e // 2, e % 2]

    def whole_copy(e, j):
        here, there = whole_part(stage.at[j], e), whole_part(whole_in.at[j], e)
        return remote(here, there, whole_send.at[e, j], whole_recv.at[e, j], p.below)

    def whole_copy_up(e):
        here, there = whole_part(stage.at[1], e), whole_part(whole_up, e)
        return remote(here, there, whole_send_up.at[e], whole_recv_up.at[e], p.above)

    def whole_add(e, j):
        whole_copy(e, j).wait_recv()
        stage[j, e // 2, e % 2] += whole_in[j, e // 2, e % 2]

    lane = (TOTAL - 1) % SLOTS

    def plane_copies(j):
        return (
            remote(stage.at[j, :, 1 - p.x, 0], x1.at[lane, 0], sx1.at[lane], rx1.at[lane], p.xn),
            remote(stage.at[j, 1 - p.y, :, 1], y1.at[lane, 0], sy1.at[lane], ry1.at[lane], p.yn),
            remote(stage.at[j, p.y, 1 - p.x, 1], x2.at[lane, 0], sx2.at[lane], rx2.at[lane], p.xn),
            remote(stage.at[j, 1 - p.y, p.x, 0], y2.at[lane, 0], sy2.at[lane], ry2.at[lane], p.yn),
        )

    def whole_fin(j):
        u = TOTAL - 1
        return (
            local(stage.at[j, p.y, p.x, p.c], o_fin.at[u], lfin.at[u]),
            remote(stage.at[j, p.y, p.x, 1 - p.c], o_fin.at[u], sfin.at[u], rfin.at[u], p.partner),
        )

    def whole_step(s):
        first = STEPS_INSIDE

        for e in range(4):

            @when((s == first + e) & (level == 0))
            def _(e=e):
                whole_copy_up(e).start()

            @when((s == first + e) & (level == 3))
            def _(e=e):
                whole_copy(e, 0).start()
                whole_copy(e, 1).start()

            @when((s == first + e + 1) & (level == 2))
            def _(e=e):
                for j in range(2):
                    whole_add(e, j)
                    whole_copy(e, j).start()

            @when((s == first + e + 2) & (level == 1))
            def _(e=e):
                whole_add(e, 0)
                whole_copy(e, 0).start()
                whole_add(e, 1)
                whole_copy_up(e).wait_recv()
                stage[1, e // 2, e % 2] += whole_up[e // 2, e % 2]

            @when((s == first + e + 3) & (level == 0))
            def _(e=e):
                whole_add(e, 0)

        for j in range(2):
            a1, b1, a2, b2 = plane_copies(j)

            @when((s == first + 6) & (level == j))
            def _(a1=a1, b1=b1):
                sent(lane)
                a1.start()
                b1.start()

            @when((s == first + 7) & (level == j))
            def _(j=j, a1=a1, b1=b1, a2=a2, b2=b2):
                a1.wait()
                stage[j, 1 - p.y, p.x, 0] += x1[lane, 0, 1 - p.y]
                stage[j, p.y, p.x, 0] += x1[lane, 0, p.y]
                b1.wait()
                stage[j, p.y, 1 - p.x, 1] += y1[lane, 0, 1 - p.x]
                stage[j, p.y, p.x, 1] += y1[lane, 0, p.x]
                a2.start()
                b2.start()

            @when((s == first + 8) & (level == j))
            def _(j=j, a2=a2, b2=b2):
                b2.wait()
                stage[j, p.y, p.x, 0] += y2[lane, 0]
                a2.wait()
                stage[j, p.y, p.x, 1] += x2[lane, 0]
                for copy in whole_fin(j):
                    copy.start()

    def whole_drain():
        for e in range(4):

            @when(level > 0)
            def _(e=e):
                whole_copy(e, 0).wait_send()

            @when(level > 1)
            def _(e=e):
                whole_copy(e, 1).wait_send()

            @when(level == 0)
            def _(e=e):
                whole_copy_up(e).wait_send()

        here, there = whole_fin(0)

        @when(level < 2)
        def _():
            here.wait()
            there.wait_send()

        @when(level > 1)
        def _():
            sent(lane)
            there.wait_recv()

    def service(s, ticks):
        def unit(k, step, extra=True):
            when((k >= 0) & (k < TOTAL - 1) & extra)(lambda: step(k))

        unit(s - 1, stage_two)
        unit(s - 2, stage_three)
        unit(s + 1, stage_one)
        for at, step, (least, slack, until) in zip((2, 1, 0), (level_two, level_one, level_zero), Z_TICKS):

            def done(t):
                late = jnp.where(t < until, slack, 0)
                return jnp.clip(t + 1 - least - late, 0, TOTAL - 1)

            def one(u, carry, step=step):
                step(u)
                return carry

            @when(level == at)
            def _(done=done, one=one):
                lax.fori_loop(done(s - 1), done(s), one, 0)

        act_step(s, ticks)

    def loads(l):
        whole = (
            (i_c, c_in),
            (i_n2, n2),
            (i_m, m_in),
            (i_a, a),
            (i_qk, qk),
            (i_v, v),
            (i_n1, n1),
            (i_h, h_in),
        )
        return [local(src.at[l], dst, load_sem.at[n]) for n, (src, dst) in enumerate(whole)]

    def load_u(l, h):
        return local(i_u.at[l, :, h], u_in, unit_sem.at[5])

    def load_a(l):
        return local(i_wa.at[:, l], wa, unit_sem.at[4])

    def load_m(l, i):
        return local(i_wm.at[:, l, i], wm.at[:, i], unit_sem.at[i])

    def start_loads(l):
        fetch = loads(l)
        load_u(l, 0).start()
        for i in (2, 0, 3, 1):
            load_m(l, i).start()
        for copy in fetch:
            copy.start()
        load_a(l).start()

    def swap(slot):
        copy = remote(part, other.at[slot], swap_sem.at[slot], swap_sem.at[2 + slot], p.partner)
        copy.start()
        copy.wait()

    def put(u, j, value):
        stage[j] = value.reshape(2, 2, 2, 96, BLOCK)
        when(u < TOTAL - 1)(lambda: local(stage.at[j], o_grads.at[u - 2, j], stage_sem.at[j]).start())

    def put_done(u):
        @when(u < TOTAL - 1)
        def _():
            for j in range(2):
                local(stage.at[j], o_grads.at[u - 2, j], stage_sem.at[j]).wait()

    def small_row(l, row, value):
        small[l, row : row + 1] = value[:, :BLOCK]
        small[l, row + 1 : row + 2] = value[:, BLOCK:]

    def norm_back(slot, l, source, gain, first):
        def rows_of(r, carry):
            rows = pl.ds(pl.multiple_of(r * 128, 128), 128)
            upstream = part[rows] + other[slot, rows]
            scaled, inverse = normalize_parts(source[rows])
            lowered, gain_grad, shift_grad = normalize_back(upstream, scaled, inverse, gain)
            value = grad[rows] + lowered
            grad[rows] = value
            rounded = value.astype(bf16)
            low[rows] = rounded
            bias_grad = jnp.sum(rounded.astype(f32), axis=0)
            return (
                carry[0] + gain_grad.reshape(1, WIDTH),
                carry[1] + shift_grad.reshape(1, WIDTH),
                carry[2] + bias_grad.reshape(1, WIDTH),
            )

        zero = jnp.zeros((1, WIDTH), f32)
        sums = lax.fori_loop(0, ROWS // 128, rows_of, (zero, zero, zero))
        small_row(l, first, sums[0])
        small_row(l, first + 2, sums[1])
        return sums[2]

    keep = lax.broadcasted_iota(jnp.int32, (ROWS, ROWS), 1) < FRAMES

    def attention_back(j, carry):
        mixture_back = contract_last(low[...], wa[j, 1, 192:384]).astype(bf16)
        parts = ([], [], [])
        for h in range(HEADS_HERE):
            cols = slice(HEAD_DIM * h, HEAD_DIM * (h + 1))
            k_cols = slice(192 + HEAD_DIM * h, 192 + HEAD_DIM * (h + 1))
            qh, kh, vh, dah = qk[j, :, cols], qk[j, :, k_cols], v[j, :, cols], mixture_back[:, cols]
            scores = jnp.where(keep, contract_last(qh, kh) * score_scale, -1e30)
            weight = jnp.exp(scores - jnp.max(scores, axis=-1, keepdims=True))
            weight = weight * (1.0 / jnp.sum(weight, axis=-1, keepdims=True))
            prob_grad = contract_last(dah, vh)
            centre = jnp.sum(prob_grad * weight, axis=-1, keepdims=True)
            score_back = (weight * (prob_grad - centre)).astype(bf16)
            parts[0].append((product(score_back, kh) * score_scale).astype(bf16))
            parts[1].append((contract_rows(score_back, qh) * score_scale).astype(bf16))
            parts[2].append(contract_rows(weight.astype(bf16), dah).astype(bf16))
        dqk[j] = jnp.concatenate(parts[0] + parts[1], axis=-1)
        dv[j] = jnp.concatenate(parts[2], axis=-1)
        return carry

    for u in range(2):
        local(i_first.at[u], held.at[u], held_sem.at[u]).start()
    local(i_ct, grad, once_sem.at[0]).start()
    start_loads(LAYERS - 1)
    meet(p)
    stage_one(0)
    service(0, (0,))
    small[...] = jnp.zeros_like(small)

    def layer(step, carry):
        l = LAYERS - 1 - step
        u0 = UNITS * step
        params = [vec[k, pl.ds(l, 1)] for k in range(6)]
        fetch = loads(l)

        @when(step == 0)
        def _():
            local(i_ct, grad, once_sem.at[0]).wait()
            low[...] = grad[...].astype(bf16)
            small_row(l, 10, jnp.sum(low[...].astype(f32), axis=0, keepdims=True))

        fetch[0].wait()

        @when(step > 0)
        def _():
            for i in (0, 1):
                for j in range(2):
                    put(u0 + i, j, contract_rows(low[...], c_in[j, i]))
                put_done(u0 + i)
            service(3, (3,))

        fetch[1].wait()
        for i in (2, 3):
            h = i - 2
            load_m(l, 2 + h).wait()
            load_m(l, h).wait()
            load_u(l, h).wait()
            for j in range(2):
                back = (product(low[...], wm[j, 2 + h]) * gelu_slope(u_in[j])).astype(bf16)
                row = 14 + 2 * j + h
                small[l, row : row + 1] = jnp.sum(back.astype(f32), axis=0, keepdims=True)
                put(u0 + i, j, contract_rows(n2[...], back))
                term = contract_last(back, wm[j, h])
                if h == 0 and j == 0:
                    part[...] = term
                else:
                    part[...] += term
            if h == 0:
                load_u(l, 1).start()
            put_done(u0 + i)
            if i == 2:
                when(step == 0)(lambda: service(1, (1,)))
            else:
                when(step > 0)(lambda: service(4, (4,)))
        swap(step)
        fetch[2].wait()
        small_row(l, 8, norm_back(step, l, m_in, params[2], 4))

        @when(step == 0)
        def _():
            for h in range(2):
                for j in range(2):
                    term = contract_last(c_in[j, h], wm[j, 2 + h])
                    if h == 0 and j == 0:
                        part[...] = term
                    else:
                        part[...] += term
            swap(1)
            part[...] = m_in[...] + (part[...] + other[1]) + params[5]
            keep_top = local(part, o_src.at[0], once_sem.at[1])
            keep_top.start()
            act_local(part, 1, "start")
            keep_top.wait()
            act_local(part, 1, "wait")
            service(2, (2,))

        for copy in fetch[3:]:
            copy.wait()
        load_a(l).wait()
        when(step == 0)(lambda: act_local(h_in, 0, "start"))
        lax.fori_loop(0, 2, attention_back, 0)
        when(step > 0)(lambda: service(5, (5,)))
        for j in range(2):
            stage[j, :, :, :, :, 0:192] = contract_rows(n1[...], dv[j]).reshape(2, 2, 2, 96, 192)
            stage[j, :, :, :, :, 192:384] = contract_rows(low[...], a[j]).reshape(2, 2, 2, 96, 192)
            local(stage.at[j], o_grads.at[u0 + 2, j], stage_sem.at[j]).start()
        put_done(u0 + 4)
        for j in range(2):
            put(u0 + 5, j, contract_rows(n1[...], dqk[j]))
            sums = jnp.sum(dqk[j].astype(f32), axis=0, keepdims=True)
            small[l, 12 + j : 13 + j, 0:192] = sums[:, 0:192]
            small[l, 12 + j : 13 + j, 192:384] = jnp.sum(dv[j].astype(f32), axis=0, keepdims=True)
            term = product(dqk[j], wa[j, 0]) + product(dv[j], wa[j, 1, 0:192])
            if j == 0:
                part[...] = term
            else:
                part[...] += term
        put_done(u0 + 5)
        swap(0)
        down_sum = norm_back(0, l, h_in, params[0], 0)

        @when(l > 0)
        def _():
            small_row(l - 1, 10, down_sum)

        @when(step == 0)
        def _():
            act_local(h_in, 0, "wait")
            start_loads(LAYERS - 2)

        return carry

    lax.fori_loop(0, LAYERS, layer, 0)
    keep_grad = local(grad, o_src.at[1], once_sem.at[1])
    keep_grad.start()
    act_local(grad, 2, "start")
    keep_grad.wait()

    def small_copy(m, device):
        return remote(small, small_in.at[m], small_send.at[m], small_recv.at[m], device)

    def small_add(m, device):
        small_copy(m, device).wait()
        small[...] += small_in[m]

    first = STEPS_INSIDE

    def small_step(s):
        @when(s == first)
        def _():
            small_copy(0, p.xn).start()

        @when(s == first + 1)
        def _():
            small_add(0, p.xn)
            small_copy(1, p.yn).start()

        @when(s == first + 2)
        def _():
            small_add(1, p.yn)

            @when((level == 0) | (level == 2))
            def _():
                small_copy(2, p.above).start()

            @when((level == 1) | (level == 3))
            def _():
                small_copy(2, p.below).start()

        @when(s == first + 3)
        def _():
            small_add(2, p.above)

            @when(level == 1)
            def _():
                small_copy(3, p.above).start()

            @when(level == 2)
            def _():
                small_copy(3, p.below).start()

        @when(s == first + 4)
        def _():
            @when((level == 1) | (level == 2))
            def _():
                small_add(3, p.above)

            @when(level == 1)
            def _():
                small_copy(4, p.below).start()

            @when(level == 2)
            def _():
                small_copy(4, p.above).start()

        @when(s == first + 5)
        def _():
            @when((level == 0) | (level == 3))
            def _():
                small_copy(4, p.above).wait_recv()
                small[...] = small_in[4]

            small_copy(5, p.partner).start()
            local(small, o_small.at[0], once_sem.at[2]).start()

        @when(s == first + 6)
        def _():
            small_copy(5, p.partner).wait()
            local(small_in.at[5], o_small.at[1], once_sem.at[3]).start()

            @when((level == 1) | (level == 2))
            def _():
                small_copy(4, p.above).wait_send()

    def step_after(s, carry):
        small_step(s)
        service(s, range(STEPS_INSIDE, LAST_TICK))
        whole_step(s)
        return carry

    lax.fori_loop(first, LAST_TICK, step_after, 0)

    for w in range(SLOTS):
        if w != lane:
            sent(w)
    whole_drain()

    def drain(u, carry):
        @when(level > 0)
        def _():
            down_copy(u, 0).wait_send()

        @when(level > 1)
        def _():
            down_copy(u, 1).wait_send()
            fin_copy(u, 0).wait_recv()

        @when(level == 0)
        def _():
            up_copy(u).wait_send()

        @when(level < 2)
        def _():
            fin_local(u, 0).wait()
            fin_copy(u, 0).wait_send()

        return carry

    lax.fori_loop(0, TOTAL - 1, drain, 0)
    for k in range(n_chunks):
        act_drain(k)

    act_local(grad, 2, "wait")
    local(small, o_small.at[0], once_sem.at[2]).wait()
    local(small_in.at[5], o_small.at[1], once_sem.at[3]).wait()


LAST_TICK = TOTAL + 4
ACT_TICKS = ((0, 0, 0, 0, 2, 2, 3, 3, 6, 6, 6, 6), (1, 1, 1, 1, 3, 3, 4, 4, 7, 7, 7, 7), (2, 2, 2, 2, 4, 4, 5, 5, 8, 8, 8, 8))
Z_TICKS = ((3, 0, 0), (4, 0, 0), (5, 0, 0))
STEPS_INSIDE = 1 + 2 + 3
SMALL = (LAYERS, 24, BLOCK)


def run_backward(saved, vectors):
    dma = pltpu.SemaphoreType.DMA
    slots = dma((SLOTS,))
    units = dma((TOTAL,))
    pair = dma((TOTAL, 2))
    return pl.pallas_call(
        backward_kernel,
        out_shape=(
            jax.ShapeDtypeStruct((TOTAL, 96, BLOCK), f32),
            jax.ShapeDtypeStruct((LAYERS, 2, ROWS, WIDTH), f32),
            jax.ShapeDtypeStruct((2, ROWS, WIDTH), f32),
            jax.ShapeDtypeStruct((2, *SMALL), f32),
            jax.ShapeDtypeStruct((2, ROWS, WIDTH), f32),
            jax.ShapeDtypeStruct((TOTAL - 3, 2, 2, 2, 2, 96, BLOCK), f32),
        ),
        in_specs=[ANY] * 13 + [VMEM],
        out_specs=(ANY,) * 6,
        scratch_shapes=[
            pltpu.VMEM((SLOTS, 2, 2, 2, 2, 96, BLOCK), f32),
            pltpu.VMEM((SLOTS, 2, 2, 96, BLOCK), f32),
            pltpu.VMEM((SLOTS, 2, 2, 96, BLOCK), f32),
            pltpu.VMEM((SLOTS, 2, 96, BLOCK), f32),
            pltpu.VMEM((SLOTS, 2, 96, BLOCK), f32),
            pltpu.VMEM((TOTAL - 1, 2, 2, 96, BLOCK), f32),
            pltpu.VMEM((TOTAL - 1, 2, 2, 96, BLOCK), f32),
            pltpu.VMEM((TOTAL - 1, 2, 96, BLOCK), f32),
            pltpu.VMEM((2, 2, 2, 2, 96, BLOCK), f32),
            pltpu.VMEM((2, 2, 2, 2, 96, BLOCK), f32),
            pltpu.VMEM((2, 2, 2, 96, BLOCK), f32),
            pltpu.VMEM((ROWS, WIDTH), f32),
            pltpu.VMEM((ROWS, WIDTH), f32),
            pltpu.VMEM((2, ROWS, WIDTH), f32),
            pltpu.VMEM((ROWS, WIDTH), f32),
            pltpu.VMEM((ROWS, WIDTH), f32),
            pltpu.VMEM((ROWS, WIDTH), bf16),
            pltpu.VMEM((ROWS, WIDTH), bf16),
            pltpu.VMEM((2, ROWS, BLOCK), bf16),
            pltpu.VMEM((2, ROWS, 192), bf16),
            pltpu.VMEM((2, ROWS, 192), bf16),
            pltpu.VMEM((2, ROWS, BLOCK), f32),
            pltpu.VMEM((2, 2, ROWS, BLOCK), bf16),
            pltpu.VMEM((2, 2, BLOCK, WIDTH), bf16),
            pltpu.VMEM((2, 4, WIDTH, BLOCK), bf16),
            pltpu.VMEM((ROWS, WIDTH), bf16),
            pltpu.VMEM((2, ROWS, BLOCK), bf16),
            pltpu.VMEM((2, ROWS, 192), bf16),
            pltpu.VMEM(SMALL, f32),
            pltpu.VMEM((6, *SMALL), f32),
            slots,
            slots,
            slots,
            slots,
            slots,
            slots,
            slots,
            slots,
            pair,
            pair,
            units,
            units,
            units,
            units,
            units,
            dma((TOTAL, 3)),
            dma((TOTAL, 2)),
            dma((3,)),
            dma((8,)),
            dma((6,)),
            dma((2,)),
            slots,
            dma((4,)),
            dma((6,)),
            dma((6,)),
            dma((4,)),
            dma((4, 2)),
            dma((4, 2)),
            dma((4,)),
            dma((4,)),
        ],
        compiler_params=pltpu.CompilerParams(
            collective_id=1, has_side_effects=True, vmem_limit_bytes=63 << 20
        ),
        name="backward_reduce",
    )(*saved, vectors)


def update_kernel(dp, fin, pa, ma, sa, pm, mm, sm, tops, inputs, *refs):
    smalls, (na, fa, va, nm, fm, vm, sections, upstream), small_outs = refs[:12], refs[12:20], refs[20:]
    step = pl.program_id(0)

    def join(clips, target):
        target[:FRAMES] = clips[0, :FRAMES]
        target[FRAMES:] = clips[1, :FRAMES]

    @pl.when(step < LAYERS)
    def _():
        for k in range(4):
            grad = fin[5 - k // 2, :, 192 * (k % 2) : 192 * (k % 2 + 1)]
            na[0, k], fa[0, k], va[0, k] = adamw_update(pa[0, k].T, grad, ma[0, k], sa[0, k], rate_matrix)
        for k in range(2):
            for h in range(2):
                cols = slice(BLOCK * h, BLOCK * (h + 1))
                grad = fin[2 - 2 * k + h]
                nm[0, k, :, cols], fm[0, k, :, cols], vm[0, k, :, cols] = adamw_update(
                    pm[0, k, :, cols], grad, mm[0, k, :, cols], sm[0, k, :, cols], rate_matrix
                )
        join(tops.at[0], sections.at[0])

    @pl.when(step == LAYERS)
    def _():
        join(inputs, upstream)
        for k in range(3):
            done = adamw_update(*(ref[...] for ref in smalls[4 * k : 4 * k + 4]), rate_vector)
            for ref, value in zip(small_outs[3 * k : 3 * k + 3], done):
                ref[...] = value


def run_update(dp, fin, w_attn, moment_attn, square_attn, w_mlp, moment_mlp, square_mlp, tops, inputs, smalls):
    rows = fin.shape[1]

    def layer(l):
        return jnp.minimum(l, LAYERS - 1)

    def whole(part):
        return pl.BlockSpec(part.shape, lambda l, dp: (0,) * part.ndim)

    attn = pl.BlockSpec((1, 4, rows, 192), lambda l, dp: (layer(l), 0, 0, 0))
    mlp = pl.BlockSpec((1, 2, rows, WIDTH), lambda l, dp: (layer(l), 0, 0, 0))
    return pl.pallas_call(
        update_kernel,
        grid_spec=pltpu.PrefetchScalarGridSpec(
            num_scalar_prefetch=1,
            grid=(LAYERS + 1,),
            in_specs=[
                pl.BlockSpec((UNITS, rows, BLOCK), lambda l, dp: (LAYERS - 1 - layer(l), 0, 0)),
                pl.BlockSpec((1, 4, 192, rows), lambda l, dp: (layer(l), 0, 0, 0)),
                attn,
                attn,
                pl.BlockSpec((1, 2, rows, WIDTH), lambda l, dp: (layer(l), 0, dp[0], 0)),
                mlp,
                mlp,
                pl.BlockSpec((1, 2, ROWS, WIDTH), lambda l, dp: (layer(l), 0, 0, 0)),
                pl.BlockSpec((2, ROWS, WIDTH), lambda l, dp: (0, 0, 0)),
            ]
            + [whole(part) for part in smalls],
            out_specs=(attn,) * 3
            + (mlp,) * 3
            + (
                pl.BlockSpec((1, 2 * FRAMES, WIDTH), lambda l, dp: (layer(l), 0, 0)),
                pl.BlockSpec((2 * FRAMES, WIDTH), lambda l, dp: (0, 0)),
            )
            + tuple(whole(smalls[4 * k]) for k in range(3) for _ in range(3)),
        ),
        out_shape=(jax.ShapeDtypeStruct(moment_attn.shape, f32),) * 3
        + (jax.ShapeDtypeStruct(moment_mlp.shape, f32),) * 3
        + (
            jax.ShapeDtypeStruct((LAYERS, 2 * FRAMES, WIDTH), f32),
            jax.ShapeDtypeStruct((2 * FRAMES, WIDTH), f32),
        )
        + tuple(jax.ShapeDtypeStruct(smalls[4 * k].shape, f32) for k in range(3) for _ in range(3)),
        compiler_params=pltpu.CompilerParams(vmem_limit_bytes=60 << 20),
        name="update",
    )(dp.reshape(1), fin, w_attn, moment_attn, square_attn, w_mlp, moment_mlp, square_mlp, tops, inputs, *smalls)


def per_device(
    frames,
    cotangent,
    w_attn,
    w_mlp,
    vectors,
    head_bias,
    up_bias,
    moment_attn,
    square_attn,
    moment_mlp,
    square_mlp,
    moment_vectors,
    square_vectors,
    moment_head,
    square_head,
    moment_up,
    square_up,
):
    dp = lax.axis_index("dp")
    t = lax.axis_index("tensor")
    core = dp % 2
    dp_size = lax.axis_size("dp")

    wa = jnp.swapaxes(w_attn, 2, 3).reshape(LAYERS, 4, 4, 2, 24, WIDTH)
    wm = w_mlp.reshape(LAYERS, 2, 4, 2, 96, 2 * BLOCK)
    rows_first = jnp.swapaxes(vectors, 0, 1)
    saved = run_forward(
        frames, cotangent, wa, wm, jnp.swapaxes(head_bias, 1, 2), jnp.swapaxes(up_bias, 0, 1), rows_first
    )
    saved = (*saved[:-1], saved[-1].reshape(2, 2, 2, 2, 2, 96, BLOCK))
    fin, tops, inputs, small, _, _ = run_backward(saved, rows_first)

    if dp_size > GROUP:
        groups = [[i + GROUP * o for o in range(dp_size // GROUP)] for i in range(GROUP)]
        small = lax.psum(small, "dp", axis_index_groups=groups)
    vector_all = small[0, :, :12].reshape(LAYERS, 6, WIDTH)
    owner = t // 2
    here = jnp.where(owner == core, small[0], small[1])
    second = jnp.where(owner == 0, t % 2, 1 - t % 2)
    head_all = jnp.where(second == 0, here[:, 12], here[:, 13]).reshape(LAYERS, 2, HEADS_HERE, HEAD_DIM)
    up_all = jnp.where(second == 0, here[:, 14:16], here[:, 16:18]).reshape(LAYERS, 12, HEAD_DIM)

    def owned(param, dim):
        size = param.shape[dim] // dp_size
        return lax.dynamic_slice_in_dim(param, dp * size, size, dim)

    if dp_size > GROUP:
        rows = jnp.zeros((TOTAL, WIDTH, BLOCK), f32)
        rows = lax.dynamic_update_slice_in_dim(rows, fin, (dp % GROUP) * 96, 1)
        fin = lax.psum_scatter(rows, "dp", scatter_dimension=1, tiled=True)

    own_attn = jnp.swapaxes(owned(w_attn, 2), 2, 3)
    def swapped(axis, parts):
        return [jnp.swapaxes(part, axis, axis + 1) for part in parts]

    smalls = (
        swapped(0, (owned(vectors, 2), owned(vector_all, 2), moment_vectors, square_vectors))
        + swapped(1, (owned(head_bias, 3), owned(head_all, 3), moment_head, square_head))
        + swapped(1, (owned(up_bias, 2), owned(up_all, 2), moment_up, square_up))
    )
    done = run_update(
        dp, fin, own_attn, moment_attn, square_attn, w_mlp, moment_mlp, square_mlp, tops, inputs, smalls
    )
    matrices, (sections, upstream), done = done[:6], done[6:8], done[8:]
    done = swapped(0, done[:3]) + swapped(1, done[3:])
    return (sections, upstream, *matrices, *done)


def solution(mesh):
    in_specs = (
        P("dp", None),
        P("dp", None),
        P(None, None, None, "tensor"),
        P(None, None, None, "tensor"),
        P(),
        P(None, None, "tensor", None),
        P(None, "tensor", None),
        P(None, None, "dp", "tensor"),
        P(None, None, "dp", "tensor"),
        P(None, None, "dp", "tensor"),
        P(None, None, "dp", "tensor"),
        P(None, None, "dp"),
        P(None, None, "dp"),
        P(None, None, "tensor", "dp"),
        P(None, None, "tensor", "dp"),
        P(None, "tensor", "dp"),
        P(None, "tensor", "dp"),
    )
    out_specs = (
        P(None, "dp", None),
        P("dp", None),
        P(None, None, "dp", "tensor"),
        P(None, None, "dp", "tensor"),
        P(None, None, "dp", "tensor"),
        P(None, None, "dp", "tensor"),
        P(None, None, "dp", "tensor"),
        P(None, None, "dp", "tensor"),
        P(None, None, "dp"),
        P(None, None, "dp"),
        P(None, None, "dp"),
        P(None, None, "tensor", "dp"),
        P(None, None, "tensor", "dp"),
        P(None, None, "tensor", "dp"),
        P(None, "tensor", "dp"),
        P(None, "tensor", "dp"),
        P(None, "tensor", "dp"),
    )
    return jax.shard_map(
        per_device, mesh=mesh, in_specs=in_specs, out_specs=out_specs, check_vma=False
    )
```
